32 devices in a mesh: replica: 4 (over x, core), shard: 8 (over z, y).
Axes of the slice: x: 2, y: 2, z: 4, core: 2. Of those that a mesh axis runs over, the one named last changes fastest.
Arguments:
- tokens: bfloat16 [32, 128, 1536], P(('replica', 'shard')), may hold values from -6 to 6
- segments: int32 [32, 128], P(('replica', 'shard')), may hold values from 0 to 3, never falling along the last dimension, each value on 1 to 64 neighbouring positions
- gain_attn: bfloat16 [1536], P('shard'), may hold values from 0.25 to 1.75
- w_qkv: bfloat16 [1536, 2048], P('shard'), may hold values from -0.15625 to 0.15625
- b_qkv: bfloat16 [2048], P('shard'), may hold values from -3 to 3
- w_out: bfloat16 [1536, 1536], P('shard'), may hold values from -0.625 to 0.625
- gain_ffn: bfloat16 [1536], P('shard'), may hold values from 0.25 to 1.75
- w_gate: bfloat16 [1536, 8960], P('shard'), may hold values from -0.15625 to 0.15625
- w_up: bfloat16 [1536, 8960], P('shard'), may hold values from -0.15625 to 0.15625
- w_down: bfloat16 [8960, 1536], P('shard'), may hold values from -0.0625 to 0.0625
- cotangent: bfloat16 [32, 128, 1536], P(('replica', 'shard')), may hold values from -6 to 6
Outputs:
- out: bfloat16 [32, 128, 1536], P(('replica', 'shard'))
- grad_tokens: bfloat16 [32, 128, 1536], P(('replica', 'shard'))
- grad_gain_attn: float32 [1536], P('shard')
- grad_w_qkv: float32 [1536, 2048], P('shard')
- grad_b_qkv: float32 [2048], P('shard')
- grad_w_out: float32 [1536, 1536], P('shard')
- grad_gain_ffn: float32 [1536], P('shard')
- grad_w_gate: float32 [1536, 8960], P('shard')
- grad_w_up: float32 [1536, 8960], P('shard')
- grad_w_down: float32 [8960, 1536], P('shard')
The draws below stay inside these ranges and needn't reach their ends.
Inputs may be any that keep to these rules, and one draw needn't show every extreme that they name: `segments`: along each sequence the document numbers never fall; a document has 1 to 64 tokens, and one of each sequence has exactly 64.
All inputs are finite; a program needn't handle non-finite values.
Results may differ from the reference program's by a relative error of at most 0.018.
Values may be sent and summed in bfloat16 or wider, within the bound.
A program may use at most 448 MiB of HBM per device.

```python
import math
import jax
import jax.numpy as jnp
import numpy as np
from jax import lax

D = 1536
QUERY_HEADS = 12
KEY_VALUE_HEADS = 2
HEAD_DIMENSION = 128
FF = 8960
L = 128
DOCS = 4
QKV = 2048
DOC_MOST = 64
SEQS = 32


def level_of(stream_key, extent, cuts, low, high):
    def one(dim, parts):
        heights = jax.random.uniform(jax.random.fold_in(jax.random.fold_in(stream_key, 6), dim), (parts,), jnp.float32, low / len(cuts), high / len(cuts))
        return jnp.repeat(jnp.exp(heights), extent[dim] // parts).reshape((-1,) + (1,) * (len(extent) - dim - 1))

    level = one(*cuts[0])
    for cut in cuts[1:]:
        level = level * one(*cut)
    return level


def split_up(number_of, total, most, slope):
    loads = [(1 << 20) // math.isqrt(grade ** slope) + 1 for grade in range(2, number_of + 1)]
    surplus, given = total - most - (number_of - 1), [1] * (number_of - 1)
    while surplus > 0:
        free = [i for i in range(number_of - 1) if given[i] < most]
        whole, left = sum([loads[i] for i in free]), surplus
        for i in free:
            extra = min(most - given[i], max(1, left * loads[i] // whole), surplus)
            given[i] = given[i] + extra
            surplus = surplus - extra
    return np.array([most] + given)


def ragged_sizes(key, count, total, bound, lean):
    if count == 2:
        one = jax.random.randint(key, (), max(1, total - bound), min(bound, total - 1) + 1)
        return jnp.stack([one, total - one])
    lengths = jnp.asarray(split_up(count, total, bound, lean), jnp.int32)
    pairs = (count - 1) // 2
    donor, receiver = lengths[1:1 + 2 * pairs:2], lengths[2:2 + 2 * pairs:2]
    margin = jnp.minimum(donor - 1, bound - receiver)
    moved = jax.random.randint(jax.random.fold_in(key, 1), (pairs,), 0, 1 << 20) % (margin + 1)
    lengths = lengths.at[1:1 + 2 * pairs:2].set(donor - moved).at[2:2 + 2 * pairs:2].set(receiver + moved)
    return lengths[jax.random.permutation(jax.random.fold_in(key, 2), count)]


def centred(stream_key, shape, deviation, most, pieces=(), held_as=jnp.bfloat16):
    loudness = level_of(stream_key, shape, pieces, -0.22, 0.18) if pieces else 1.0
    drawn = jax.random.normal(stream_key, shape, jnp.float32) * deviation * loudness
    return jnp.minimum(jnp.maximum(drawn, -most), most).astype(held_as)


def setup_inputs(seed: int = 0) -> dict:
    keys = jax.random.split(jax.random.key(seed), 12)
    return {
        "tokens": centred(keys[0], (SEQS, L, D), 1.0, 6.0, ((0, 32),)),
        "segments": jax.vmap(lambda own: jnp.searchsorted(jnp.cumsum(ragged_sizes(own, DOCS, L, DOC_MOST, 0)), jnp.arange(L), side="right"))(jax.random.split(keys[1], SEQS)).reshape((SEQS, L)).astype(jnp.int32),
        "gain_attn": jnp.clip(1.0 + 0.15 * jax.random.normal(keys[2], (D,), jnp.float32), 0.25, 1.75).astype(jnp.bfloat16),
        "w_qkv": centred(keys[3], (D, QKV), D ** -0.5, 0.15625, ((0, 8),)),
        "b_qkv": centred(keys[4], (QKV,), 0.5, 3.0, ((0, 8),)),
        "w_out": centred(keys[5], (QUERY_HEADS * HEAD_DIMENSION, D), (QUERY_HEADS * HEAD_DIMENSION // 16) ** -0.5, 0.625, ((0, 8),)),
        "gain_ffn": jnp.clip(1.0 + 0.15 * jax.random.normal(keys[6], (D,), jnp.float32), 0.25, 1.75).astype(jnp.bfloat16),
        "w_gate": centred(keys[7], (D, FF), D ** -0.5, 0.15625, ((0, 8),)),
        "w_up": centred(keys[8], (D, FF), D ** -0.5, 0.15625, ((0, 8),)),
        "w_down": centred(keys[9], (FF, D), FF ** -0.5, 0.0625, ((0, 8),)),
        "cotangent": centred(keys[10], (SEQS, L, D), 1.0, 6.0, ((0, 32),)),
    }


eps_norm = 1e-06
rope_base = 1000000.0

@jax.custom_vjp
def reduced_input(v):
    return lax.optimization_barrier(v.astype(jnp.bfloat16)).astype(jnp.float32)

@jax.custom_vjp
def low_back(v):
    return v

def low_keep(v):
    return (reduced_input(v), None)

def low_pass(kept, grad):
    return (grad,)

def back_keep(v):
    return (v, None)

def back_low(kept, grad):
    return (reduced_input(grad),)
reduced_input.defvjp(low_keep, low_pass)
low_back.defvjp(back_keep, back_low)

def tables(segment_ids, head_size):
    token_length = segment_ids.shape[-1]
    row_index = jnp.arange(token_length, dtype=jnp.int32)
    earlier = lax.optimization_barrier(jnp.sum((segment_ids[..., None, :] < segment_ids[..., :, None]).astype(jnp.int32), axis=-1, dtype=jnp.int32))
    positions = (row_index - earlier).astype(jnp.float32)
    frequencies = jnp.exp(jnp.arange(head_size // 2, dtype=jnp.float32) * (-2.0 * math.log(rope_base) / head_size))
    angles = positions[..., None] * frequencies
    cosine = jnp.concatenate([jnp.cos(angles), jnp.cos(angles)], axis=-1)
    sine_vals = jnp.concatenate([jnp.sin(angles), jnp.sin(angles)], axis=-1)
    allowed = ((segment_ids[..., None, :] == segment_ids[..., :, None]) & (row_index[None, :] <= row_index[:, None])).astype(jnp.int32)
    return (cosine, sine_vals, allowed)

def apply_rotation(values, cosine, sine_vals):
    halfway = values.shape[-1] // 2
    turned = jnp.concatenate([-values[..., halfway:], values[..., :halfway]], axis=-1)
    return values * cosine + turned * sine_vals

def rms_norm(hidden, gain_vec):
    return hidden * lax.rsqrt(lax.optimization_barrier(jnp.mean(hidden * hidden, axis=-1, keepdims=True)) + eps_norm) * gain_vec

def layer(inputs, gain_attn, w_qkv, b_qkv, w_out, gain_ffn, w_gate, w_up, w_down, cosine, sine_vals, allowed):
    highest = lax.Precision.HIGHEST
    query_groups = inputs.shape[0]
    token_length = inputs.shape[1]
    head_dimension = QUERY_HEADS * HEAD_DIMENSION
    key_value_limit = head_dimension + KEY_VALUE_HEADS * HEAD_DIMENSION
    normed_first = reduced_input(rms_norm(inputs, gain_attn))
    joined_projection = low_back(jnp.einsum('gld,de->gle', normed_first, w_qkv, precision=highest) + b_qkv)
    cosine_per_head = cosine[:, :, None, :]
    sine_per_head = sine_vals[:, :, None, :]
    query_rows = apply_rotation(joined_projection[..., :head_dimension].reshape(query_groups, token_length, QUERY_HEADS, HEAD_DIMENSION), cosine_per_head, sine_per_head)
    query_rows = reduced_input(query_rows * HEAD_DIMENSION ** (-0.5)).reshape(query_groups, token_length, KEY_VALUE_HEADS, QUERY_HEADS // KEY_VALUE_HEADS, HEAD_DIMENSION)
    key_rows = reduced_input(apply_rotation(joined_projection[..., head_dimension:key_value_limit].reshape(query_groups, token_length, KEY_VALUE_HEADS, HEAD_DIMENSION), cosine_per_head, sine_per_head))
    value_rows = reduced_input(joined_projection[..., key_value_limit:].reshape(query_groups, token_length, KEY_VALUE_HEADS, HEAD_DIMENSION))
    scores = low_back(jnp.einsum('gikrd,gjkd->gkrij', query_rows, key_rows, precision=highest))
    scores = jnp.where(allowed[:, None, None] != 0, scores, -1e+30)
    largest = lax.optimization_barrier(jnp.max(scores, axis=-1, keepdims=True))
    exponents = jnp.exp(scores - largest)
    soft_probs = exponents / lax.optimization_barrier(jnp.sum(exponents, axis=-1, keepdims=True))
    attended = jnp.einsum('gkrij,gjkd->gikrd', reduced_input(soft_probs), value_rows, precision=highest)
    attended = reduced_input(low_back(attended.reshape(query_groups, token_length, head_dimension)))
    hidden_mid = inputs + low_back(jnp.einsum('gle,ed->gld', attended, w_out, precision=highest))
    normed_second = reduced_input(rms_norm(hidden_mid, gain_ffn))
    gate_vals = low_back(jnp.einsum('gld,df->glf', normed_second, w_gate, precision=highest))
    up_vals = low_back(jnp.einsum('gld,df->glf', normed_second, w_up, precision=highest))
    mixed_hidden = reduced_input(gate_vals * jax.nn.sigmoid(gate_vals) * up_vals)
    return hidden_mid + jnp.einsum('glf,fd->gld', mixed_hidden, w_down, precision=highest)

def reference(tokens, segments, gain_attn, w_qkv, b_qkv, w_out, gain_ffn, w_gate, w_up, w_down, cotangent):
    weights = tuple((weight_arr.astype(jnp.float32) for weight_arr in (gain_attn, w_qkv, b_qkv, w_out, gain_ffn, w_gate, w_up, w_down)))
    token_length = tokens.shape[1]
    model_width = tokens.shape[2]
    token_blocks = tokens.reshape(-1, 8, token_length, model_width)
    segment_blocks = segments.reshape(-1, 8, token_length)
    cot_blocks = cotangent.reshape(-1, 8, token_length, model_width)

    def block_step(totals, block_data):
        token_part, segment_part, cot_part = block_data
        cosine, sine_vals, allowed = tables(segment_part, HEAD_DIMENSION)

        def forward(inputs, *params):
            return layer(inputs, *params, cosine, sine_vals, allowed)
        output, pullback = jax.vjp(forward, token_part.astype(jnp.float32), *weights)
        gradients = pullback(cot_part.astype(jnp.float32))
        totals = tuple((running + part_grad for running, part_grad in zip(totals, gradients[1:])))
        return (totals, (output.astype(jnp.bfloat16), gradients[0].astype(jnp.bfloat16)))
    start_totals = tuple((jnp.zeros(weight_arr.shape, jnp.float32) for weight_arr in weights))
    totals, (outputs, input_grads) = lax.scan(block_step, start_totals, (token_blocks, segment_blocks, cot_blocks))
    out_tokens = outputs.reshape(tokens.shape)
    grad_tokens = input_grads.reshape(tokens.shape)
    return (out_tokens, grad_tokens, totals[0], totals[1], totals[2], totals[3], totals[4], totals[5], totals[6], totals[7])
```

```python
import math

import jax
import jax.numpy as jnp
from jax import lax
from jax.sharding import PartitionSpec as P

QUERY_HEADS = 12
KEY_VALUE_HEADS = 2
HEAD_DIMENSION = 128


eps_norm = 1e-06
rope_base = 1000000.0


def tables(segment_ids, head_size):
    token_length = segment_ids.shape[-1]
    row_index = jnp.arange(token_length, dtype=jnp.int32)
    earlier = jnp.sum(
        (segment_ids[..., None, :] < segment_ids[..., :, None]).astype(jnp.int32),
        axis=-1,
        dtype=jnp.int32,
    )
    positions = (row_index - earlier).astype(jnp.float32)
    frequencies = jnp.exp(
        jnp.arange(head_size // 2, dtype=jnp.float32) * (-2.0 * math.log(rope_base) / head_size)
    )
    angles = positions[..., None] * frequencies
    cosine = jnp.concatenate([jnp.cos(angles), jnp.cos(angles)], axis=-1)
    sine_vals = jnp.concatenate([jnp.sin(angles), jnp.sin(angles)], axis=-1)
    allowed = (
        (segment_ids[..., None, :] == segment_ids[..., :, None])
        & (row_index[None, :] <= row_index[:, None])
    ).astype(jnp.int32)
    return (cosine, sine_vals, allowed)


def apply_rotation(values, cosine, sine_vals):
    halfway = values.shape[-1] // 2
    turned = jnp.concatenate([-values[..., halfway:], values[..., :halfway]], axis=-1)
    return values * cosine + turned * sine_vals


def rotate_back(values, cosine, sine_vals):
    halfway = values.shape[-1] // 2
    shifted = values * sine_vals
    return values * cosine + jnp.concatenate(
        [shifted[..., halfway:], -shifted[..., :halfway]], axis=-1
    )


def norm_forward(hidden, gain_vec):
    rstd_rows = lax.rsqrt(jnp.mean(hidden * hidden, axis=-1, keepdims=True) + eps_norm)
    unit_rows = hidden * rstd_rows
    return (unit_rows * gain_vec, unit_rows, rstd_rows)


def norm_backward(grad_in, gain_vec, unit_rows, rstd_rows):
    inner_grad = grad_in * gain_vec
    return rstd_rows * (
        inner_grad - unit_rows * jnp.mean(inner_grad * unit_rows, axis=-1, keepdims=True)
    )


def column_term(left_side, right_side):
    return jnp.einsum("lf,ld->fd", left_side, right_side, preferred_element_type=jnp.float32)


def to_columns(rows):
    ranks = lax.axis_size("shard")
    depth, width = rows.shape
    split = rows.reshape(depth, ranks, width // ranks).transpose(1, 0, 2)
    return lax.all_to_all(split, "shard", 0, 0, tiled=True).reshape(ranks * depth, width // ranks)


def to_rows(columns):
    ranks, copies = lax.axis_size("shard"), lax.axis_size("replica")
    depth, width = columns.shape
    depth = depth // ranks
    parts = columns.reshape(ranks, copies, depth // copies, width)
    part = lax.psum_scatter(parts, "replica", scatter_dimension=1, tiled=False)
    part = lax.all_to_all(part, "shard", 0, 0, tiled=True)
    part = part.transpose(1, 0, 2).reshape(depth // copies, ranks * width)
    return lax.all_gather(part, "replica", axis=0, tiled=True)


def shards(
    tokens, segments, gain_attn, w_qkv, b_qkv, w_out, gain_ffn, w_gate, w_up, w_down, cotangent
):
    heads_per_group = QUERY_HEADS // KEY_VALUE_HEADS
    head_dimension = QUERY_HEADS * HEAD_DIMENSION
    key_value_limit = head_dimension + KEY_VALUE_HEADS * HEAD_DIMENSION
    logit_scale = HEAD_DIMENSION ** (-0.5)
    token_length = tokens.shape[1]
    full_gain_attn, full_qkv, full_bias, full_out, full_gain_ffn = (
        lax.all_gather(gain_attn, "shard", axis=0, tiled=True),
        lax.all_gather(w_qkv, "shard", axis=0, tiled=True),
        lax.all_gather(b_qkv, "shard", axis=0, tiled=True),
        lax.all_gather(w_out, "shard", axis=0, tiled=True),
        lax.all_gather(gain_ffn, "shard", axis=0, tiled=True),
    )
    gate_columns = to_columns(w_gate)
    up_columns = to_columns(w_up)
    all_cot = lax.all_gather(cotangent[0], "shard", axis=0, tiled=True)
    gain_first = full_gain_attn.astype(jnp.float32)
    gain_second = full_gain_ffn.astype(jnp.float32)
    cosine, sine_vals, allowed = tables(segments[0], HEAD_DIMENSION)
    cosine_per_head = cosine[:, None, :]
    sine_per_head = sine_vals[:, None, :]
    inputs = tokens[0].astype(jnp.float32)
    normed_first, unit_first, rstd_first = norm_forward(inputs, gain_first)
    acts_first = normed_first.astype(jnp.bfloat16)
    joined_projection = jnp.dot(
        acts_first, full_qkv, preferred_element_type=jnp.float32
    ) + full_bias.astype(jnp.float32)
    query_rows = apply_rotation(
        joined_projection[:, :head_dimension].reshape(token_length, QUERY_HEADS, HEAD_DIMENSION),
        cosine_per_head,
        sine_per_head,
    )
    query_reduced = (
        (query_rows * logit_scale)
        .astype(jnp.bfloat16)
        .reshape(token_length, KEY_VALUE_HEADS, heads_per_group, HEAD_DIMENSION)
    )
    k_low = apply_rotation(
        joined_projection[:, head_dimension:key_value_limit].reshape(
            token_length, KEY_VALUE_HEADS, HEAD_DIMENSION
        ),
        cosine_per_head,
        sine_per_head,
    ).astype(jnp.bfloat16)
    value_reduced = (
        joined_projection[:, key_value_limit:]
        .reshape(token_length, KEY_VALUE_HEADS, HEAD_DIMENSION)
        .astype(jnp.bfloat16)
    )
    scores = jnp.einsum("ikrd,jkd->krij", query_reduced, k_low, preferred_element_type=jnp.float32)
    scores = jnp.where(allowed != 0, scores, -1e30)
    largest = jnp.max(scores, axis=-1, keepdims=True)
    exponents = jnp.exp(scores - largest)
    soft_probs = exponents / jnp.sum(exponents, axis=-1, keepdims=True)
    soft_low = soft_probs.astype(jnp.bfloat16)
    attended = jnp.einsum(
        "krij,jkd->ikrd", soft_low, value_reduced, preferred_element_type=jnp.float32
    )
    attended = attended.reshape(token_length, head_dimension).astype(jnp.bfloat16)
    hidden_mid = inputs + jnp.dot(attended, full_out, preferred_element_type=jnp.float32)
    normed_second, unit_second, rstd_second = norm_forward(hidden_mid, gain_second)
    acts_second = normed_second.astype(jnp.bfloat16)
    all_acts = lax.all_gather(acts_second, "shard", axis=0, tiled=True)
    gate_vals = jnp.dot(all_acts, gate_columns, preferred_element_type=jnp.float32)
    up_vals = jnp.dot(all_acts, up_columns, preferred_element_type=jnp.float32)
    sigmoid_gate = jax.nn.sigmoid(gate_vals)
    active = gate_vals * sigmoid_gate
    mixed_hidden = (active * up_vals).astype(jnp.bfloat16)
    d_mixed = jnp.einsum("ld,fd->lf", all_cot, w_down, preferred_element_type=jnp.float32)
    d_active = d_mixed * up_vals
    d_gate = (
        d_active * sigmoid_gate + d_active * gate_vals * sigmoid_gate * (1.0 - sigmoid_gate)
    ).astype(jnp.bfloat16)
    d_up = (d_mixed * active).astype(jnp.bfloat16)
    d_normed_part = jnp.einsum("lf,df->ld", d_gate, gate_columns, preferred_element_type=jnp.float32)
    d_normed_part = d_normed_part + jnp.einsum(
        "lf,df->ld", d_up, up_columns, preferred_element_type=jnp.float32
    )
    d_normed_second = lax.psum_scatter(
        d_normed_part.astype(jnp.bfloat16), "shard", scatter_dimension=0, tiled=True
    ).astype(jnp.float32)
    down_part = jnp.dot(mixed_hidden, w_down, preferred_element_type=jnp.float32)
    result = (
        hidden_mid
        + lax.psum_scatter(
            down_part.astype(jnp.bfloat16), "shard", scatter_dimension=0, tiled=True
        ).astype(jnp.float32)
    ).astype(jnp.bfloat16)
    grad_out = cotangent[0]
    down_grad = column_term(mixed_hidden, all_cot).astype(jnp.bfloat16)
    gate_grad = to_rows(column_term(all_acts, d_gate).astype(jnp.bfloat16))
    up_grad = to_rows(column_term(all_acts, d_up).astype(jnp.bfloat16))
    gain_second_grad = jnp.sum(d_normed_second * unit_second, axis=0)
    d_hidden_mid = grad_out.astype(jnp.float32) + norm_backward(
        d_normed_second, gain_second, unit_second, rstd_second
    )
    d_branch = d_hidden_mid.astype(jnp.bfloat16)
    out_grad_term = jnp.einsum("le,ld->ed", attended, d_branch, preferred_element_type=jnp.float32)
    attended_gradient = jnp.einsum(
        "ld,ed->le", d_branch, full_out, preferred_element_type=jnp.float32
    )
    attended_gradient = attended_gradient.astype(jnp.bfloat16).reshape(
        token_length, KEY_VALUE_HEADS, heads_per_group, HEAD_DIMENSION
    )
    d_probs = jnp.einsum(
        "ikrd,jkd->krij", attended_gradient, value_reduced, preferred_element_type=jnp.float32
    )
    value_gradient = jnp.einsum(
        "krij,ikrd->jkd", soft_low, attended_gradient, preferred_element_type=jnp.float32
    )
    d_scores = soft_probs * (d_probs - jnp.sum(soft_probs * d_probs, axis=-1, keepdims=True))
    d_scores_low = d_scores.astype(jnp.bfloat16)
    d_queries = jnp.einsum(
        "krij,jkd->ikrd", d_scores_low, k_low, preferred_element_type=jnp.float32
    )
    d_queries = rotate_back(
        d_queries.reshape(token_length, QUERY_HEADS, HEAD_DIMENSION) * logit_scale,
        cosine_per_head,
        sine_per_head,
    )
    key_gradient = jnp.einsum(
        "krij,ikrd->jkd", d_scores_low, query_reduced, preferred_element_type=jnp.float32
    )
    key_gradient = rotate_back(key_gradient, cosine_per_head, sine_per_head)
    d_joined = jnp.concatenate(
        [
            d_queries.reshape(token_length, head_dimension),
            key_gradient.reshape(token_length, KEY_VALUE_HEADS * HEAD_DIMENSION),
            value_gradient.reshape(token_length, KEY_VALUE_HEADS * HEAD_DIMENSION),
        ],
        axis=1,
    ).astype(jnp.bfloat16)
    bias_grad_term = jnp.sum(d_joined.astype(jnp.float32), axis=0)
    qkv_grad_term = jnp.einsum(
        "ld,le->de", acts_first, d_joined, preferred_element_type=jnp.float32
    )
    d_normed_first = jnp.einsum("le,de->ld", d_joined, full_qkv, preferred_element_type=jnp.float32)
    gain_first_grad = jnp.sum(d_normed_first * unit_first, axis=0)
    d_inputs = d_hidden_mid + norm_backward(d_normed_first, gain_first, unit_first, rstd_first)
    owned = (
        lax.psum_scatter(
            gain_first_grad.astype(jnp.bfloat16), "shard", scatter_dimension=0, tiled=True
        ).astype(jnp.float32),
        lax.psum_scatter(
            qkv_grad_term.astype(jnp.bfloat16), "shard", scatter_dimension=0, tiled=True
        ).astype(jnp.float32),
        lax.psum_scatter(
            bias_grad_term.astype(jnp.bfloat16), "shard", scatter_dimension=0, tiled=True
        ).astype(jnp.float32),
        lax.psum_scatter(
            out_grad_term.astype(jnp.bfloat16), "shard", scatter_dimension=0, tiled=True
        ).astype(jnp.float32),
        lax.psum_scatter(
            gain_second_grad.astype(jnp.bfloat16), "shard", scatter_dimension=0, tiled=True
        ).astype(jnp.float32),
    )
    summed = (
        lax.psum(owned[0].astype(jnp.bfloat16), "replica").astype(jnp.float32),
        lax.psum(owned[1].astype(jnp.bfloat16), "replica").astype(jnp.float32),
        lax.psum(owned[2].astype(jnp.bfloat16), "replica").astype(jnp.float32),
        lax.psum(owned[3].astype(jnp.bfloat16), "replica").astype(jnp.float32),
        lax.psum(owned[4].astype(jnp.bfloat16), "replica").astype(jnp.float32),
        gate_grad.astype(jnp.float32),
        up_grad.astype(jnp.float32),
        lax.psum(down_grad, "replica").astype(jnp.float32),
    )
    return (
        result[None],
        d_inputs.astype(jnp.bfloat16)[None],
        summed[0],
        summed[1],
        summed[2],
        summed[3],
        summed[4],
        summed[5],
        summed[6],
        summed[7],
    )


def solution(mesh):
    placed = (
        P(("replica", "shard"), None, None),
        P(("replica", "shard"), None),
        P("shard"),
        P("shard", None),
        P("shard"),
        P("shard", None),
        P("shard"),
        P("shard", None),
        P("shard", None),
        P("shard", None),
        P(("replica", "shard"), None, None),
    )
    return jax.shard_map(
        shards,
        mesh=mesh,
        in_specs=placed,
        out_specs=(
            P(("replica", "shard"), None, None),
            P(("replica", "shard"), None, None),
            P("shard"),
            P("shard", None),
            P("shard"),
            P("shard", None),
            P("shard"),
            P("shard", None),
            P("shard", None),
            P("shard", None),
        ),
        check_vma=False,
    )
```

```python
import math

import jax
import jax.numpy as jnp
from jax import lax
from jax.experimental import pallas as pl
from jax.experimental.pallas import tpu as pltpu
from jax.sharding import PartitionSpec as P

MESH = pl.DeviceIdType.MESH
BF, F32 = jnp.bfloat16, jnp.float32

QUERY_HEADS = 12
KEY_VALUE_HEADS = 2
HEAD_DIMENSION = 128


eps_norm = 1e-06
rope_base = 1000000.0


def tables(segment_ids, head_size):
    token_length = segment_ids.shape[-1]
    row_index = jnp.arange(token_length, dtype=jnp.int32)
    earlier = jnp.sum(
        (segment_ids[..., None, :] < segment_ids[..., :, None]).astype(jnp.int32),
        axis=-1,
        dtype=jnp.int32,
    )
    positions = (row_index - earlier).astype(jnp.float32)
    frequencies = jnp.exp(
        jnp.arange(head_size // 2, dtype=jnp.float32) * (-2.0 * math.log(rope_base) / head_size)
    )
    angles = positions[..., None] * frequencies
    cosine = jnp.concatenate([jnp.cos(angles), jnp.cos(angles)], axis=-1)
    sine_vals = jnp.concatenate([jnp.sin(angles), jnp.sin(angles)], axis=-1)
    allowed = (
        (segment_ids[..., None, :] == segment_ids[..., :, None])
        & (row_index[None, :] <= row_index[:, None])
    ).astype(jnp.int32)
    return (cosine, sine_vals, allowed)


def apply_rotation(values, cosine, sine_vals):
    halfway = values.shape[-1] // 2
    turned = jnp.concatenate([-values[..., halfway:], values[..., :halfway]], axis=-1)
    return values * cosine + turned * sine_vals


def rotate_back(values, cosine, sine_vals):
    halfway = values.shape[-1] // 2
    shifted = values * sine_vals
    return values * cosine + jnp.concatenate(
        [shifted[..., halfway:], -shifted[..., :halfway]], axis=-1
    )


def norm_forward(hidden, gain_vec):
    rstd_rows = lax.rsqrt(jnp.mean(hidden * hidden, axis=-1, keepdims=True) + eps_norm)
    unit_rows = hidden * rstd_rows
    return (unit_rows * gain_vec, unit_rows, rstd_rows)


def norm_backward(grad_in, gain_vec, unit_rows, rstd_rows):
    inner_grad = grad_in * gain_vec
    return rstd_rows * (
        inner_grad - unit_rows * jnp.mean(inner_grad * unit_rows, axis=-1, keepdims=True)
    )


def column_term(left_side, right_side):
    return jnp.einsum("lf,ld->fd", left_side, right_side, preferred_element_type=jnp.float32)


def topo():
    r = lax.axis_index("replica"); s = lax.axis_index("shard")
    x, c, z, y = r // 2, r % 2, s // 2, s % 2
    return r, s, x, c, z, y

def rcopy(src, dst, ssem, rsem, dev):
    return pltpu.make_async_remote_copy(src_ref=src, dst_ref=dst, send_sem=ssem, recv_sem=rsem, device_id=dev, device_id_type=MESH)

def greet(devs):
    bar = pltpu.get_barrier_semaphore()
    for d in devs:
        pl.semaphore_signal(bar, inc=1, device_id=d, device_id_type=MESH)
    pl.semaphore_wait(bar, len(devs))

def k1_body(w_ref, g_ref, c_ref, small_ref, W, G, C, S,
            own_rows, own_cols, own_cot, rw, rg, rc, rs, sw, swd, sg, sgd, sc, ss, loc):
    r, s, x, c, z, y = topo()
    cp, xp = (r + 1 - 2 * c, s), ((r + 2) % 4, s)
    rcp, rxp = r + 1 - 2 * c, (r + 2) % 4
    greet([cp, xp] + [(r, (s + k) % 8) for k in range(1, 8)])
    def wq(t, q):
        return W.at[pl.ds(pl.multiple_of(192 * t + 48 * q, 16), 48)]
    def gq(t, q):
        return G.at[pl.ds(pl.multiple_of(192 * t + 48 * q, 16), 48)]
    def cb(t):
        return C.at[pl.ds(pl.multiple_of(128 * t, 128), 128)]
    own_w = w_ref.at[pl.ds(pl.multiple_of(48 * r, 16), 48)]
    yp, up, dn = (r, s + 1 - 2 * y), (r, s + 2), (r, s - 2)
    def plane(src_w, src_c, t, zz, go_up, go_dn):
        def send(dev, d):
            rcopy(src_w, wq(t, r), sw.at[zz, d], rw.at[t, r], dev).start()
            rcopy(src_c, cb(t), sc.at[zz, d], rc.at[t], dev).start()
        if go_up is not None:
            pl.when(go_up)(lambda: send(up, 0))
        if go_dn is not None:
            pl.when(go_dn)(lambda: send(dn, 1))
        send(yp, 2)
    to_vmem = (
        pltpu.make_async_copy(w_ref, own_rows, loc.at[0]),
        pltpu.make_async_copy(g_ref.at[s], own_cols, loc.at[1]),
        pltpu.make_async_copy(c_ref, own_cot, loc.at[2]),
    )
    own = pl.ds(pl.multiple_of(192 * s, 16), 192)
    to_hbm = (
        pltpu.make_async_copy(own_rows, W.at[own], loc.at[3]),
        pltpu.make_async_copy(own_cols, G.at[own], loc.at[4]),
        pltpu.make_async_copy(own_cot, cb(s), loc.at[5]),
    )
    for copy in to_vmem:
        copy.start()
    plane(own_w, c_ref, s, z, z < 3, z > 0)
    for k in range(1, 8):
        t = (s + k) % 8
        rcopy(small_ref, S.at[s], ss.at[t], rs.at[s], (r, t)).start()
        rcopy(g_ref.at[t, pl.ds(pl.multiple_of(48 * r, 16), 48)], gq(s, r), sg.at[t], rg.at[s, r], (r, t)).start()
    S[s] = small_ref[...]
    for near, far in zip(to_vmem, to_hbm):
        near.wait()
        far.start()
    def wait_w(t, q):
        rcopy(wq(t, q), wq(t, q), sw.at[0, 0], rw.at[t, q], cp).wait_recv()
    def wait_g(t, q):
        rcopy(gq(t, q), gq(t, q), sg.at[0], rg.at[t, q], cp).wait_recv()
    def wait_c(t):
        rcopy(cb(t), cb(t), sg.at[0], rc.at[t], cp).wait_recv()
    def share(view, t, sems, rsems):
        rcopy(view(t, r), view(t, r), sems.at[t, 0], rsems.at[t, r], xp).start()
        rcopy(view(t, r), view(t, r), sems.at[t, 1], rsems.at[t, r], cp).start()
    for k in (1, 2, 3):
        def below():
            t = s - 2 * k
            wait_w(t, r); wait_c(t)
            plane(wq(t, r), cb(t), t, z - k, z < 3, None)
            share(wq, t, swd, rw)
        def above():
            t = s + 2 * k
            wait_w(t, r); wait_c(t)
            plane(wq(t, r), cb(t), t, z + k, None, z > 0)
            share(wq, t, swd, rw)
        pl.when(z >= k)(below)
        pl.when(z + k <= 3)(above)
    @pl.loop(0, 4)
    def _(zz):
        t = 2 * zz + 1 - y
        wait_w(t, r)
        share(wq, t, swd, rw)
    @pl.loop(1, 8)
    def _(k):
        t = (s + k) % 8
        wait_g(t, r)
        share(gq, t, sgd, rg)
    @pl.loop(1, 8)
    def _(k):
        t = (s + k) % 8
        wait_w(t, rxp)
        rcopy(wq(t, rxp), wq(t, rxp), swd.at[t, 2], rw.at[t, rxp], cp).start()
    @pl.loop(1, 8)
    def _(k):
        t = (s + k) % 8
        wait_g(t, rxp)
        rcopy(gq(t, rxp), gq(t, rxp), sgd.at[t, 2], rg.at[t, rxp], cp).start()
    @pl.loop(0, 4)
    def _(zz):
        wait_c(2 * zz + 1 - y)
    @pl.loop(1, 8)
    def _(k):
        t = (s + k) % 8
        rcopy(small_ref, S.at[t], ss.at[t], rs.at[t], cp).wait_recv()
        rcopy(small_ref, S.at[t], ss.at[t], rs.at[t], cp).wait_send()
        rcopy(gq(s, r), gq(s, r), sg.at[t], rg.at[s, r], cp).wait_send()
        for q in (rcp, 3 - r):
            wait_w(t, q)
            wait_g(t, q)
        for d in range(3):
            rcopy(wq(t, r), wq(t, r), swd.at[t, d], rw.at[t, r], cp).wait_send()
            rcopy(gq(t, r), gq(t, r), sgd.at[t, d], rg.at[t, r], cp).wait_send()
    def sent(zz, d):
        rcopy(own_w, own_w, sw.at[zz, d], rw.at[s, r], cp).wait_send()
        rcopy(c_ref, c_ref, sc.at[zz, d], rc.at[s], cp).wait_send()
    for zz in range(4):
        sent(zz, 2)
        pl.when((zz <= z) & (z < 3))(lambda: sent(zz, 0))
        pl.when((zz >= z) & (z > 0))(lambda: sent(zz, 1))
    for copy in to_hbm:
        copy.wait()

def k1(w, g, c, small):
    A = pl.BlockSpec(memory_space=pl.ANY)
    V = pl.BlockSpec(memory_space=pltpu.VMEM)
    D = pltpu.SemaphoreType.DMA
    return pl.pallas_call(
        k1_body,
        out_shape=(jax.ShapeDtypeStruct((1536, 3584), jnp.bfloat16), jax.ShapeDtypeStruct((1536, 2304), jnp.bfloat16),
                   jax.ShapeDtypeStruct((1024, 1536), jnp.bfloat16), jax.ShapeDtypeStruct((8, 16, 128), jnp.bfloat16)),
        in_specs=[A, A, A, V], out_specs=(A, A, A, V),
        scratch_shapes=[pltpu.VMEM((192, 3584), BF), pltpu.VMEM((192, 2304), BF), pltpu.VMEM((128, 1536), BF), D((8, 4)), D((8, 4)), D((8,)), D((8,)), D((4, 3)), D((8, 3)), D((8,)), D((8, 3)), D((4, 3)), D((8,)), D((6,))],
        compiler_params=pltpu.CompilerParams(collective_id=0, has_side_effects=True, vmem_limit_bytes=16 << 20), name="gather_weights",
    )(w, g, c, small)


def al(v, m): return pl.multiple_of(v, m)
def dot(a, b): return lax.dot_general(a, b, (((1,), (0,)), ((), ())), preferred_element_type=F32)
def dot_nt(a, b): return lax.dot_general(a, b, (((1,), (1,)), ((), ())), preferred_element_type=F32)

def kb_body(n_ref, c_hbm, g_hbm, d_hbm, DS, OS, OG, OD,
            vG, vD, vC, N, NT, MX, MT, H, PD, PO, YD, YO, ZD, ZO, GD, RCd, RXd, RC, RX,
            rn, syn, szn, ryd, ryo, rzd, rzo, syd, szd, syo, szo,
            scd, rcd, sxd, rxd, sfd, rfd, scg, rcg, sxg, rxg, sag, rag, sfg, loc):
    r, s, x, c, z, y = topo()
    cp, xp, yp = (r + 1 - 2 * c, s), ((r + 2) % 4, s), (r, s + 1 - 2 * y)
    rcp, rxp, rdp = r + 1 - 2 * c, (r + 2) % 4, 3 - r
    greet([cp, xp] + [(r, (s + k) % 8) for k in range(1, 8)])
    def wr(ref, sem): rcopy(ref, ref, loc.at[0], sem, cp).wait_recv()
    def ws(ref, sem): rcopy(ref, ref, sem, loc.at[0], cp).wait_send()
    def line(k):
        return (z + (1 - 2 * (z % 2)) * (k % 2) + (k // 2) * (2 - 4 * (z // 2)))
    def nb(t): return N.at[pl.ds(al(128 * t, 128), 128)]
    loads = [pltpu.make_async_copy(c_hbm, vC, loc.at[1]), pltpu.make_async_copy(g_hbm, vG, loc.at[2]),
             pltpu.make_async_copy(d_hbm, vD, loc.at[3])]
    l0 = pltpu.make_async_copy(n_ref, nb(s), loc.at[4])
    l0.start()
    rcopy(n_ref, nb(s), syn.at[z], rn.at[s], yp).start()
    for k in (1, 2, 3):
        zz = line(k)
        rcopy(n_ref, nb(s), szn.at[zz], rn.at[s], (r, 2 * zz + y)).start()
    for l in loads: l.start()
    l0.wait()
    for l in loads: l.wait()

    def add_d(k):
        zz = line(k)
        t = 2 * zz + y
        wr(YD.at[zz], ryd.at[zz])
        PD[t] = (PD[t].astype(F32) + YD[zz].astype(F32)).astype(BF)
    def send_d(k):
        zz = line(k)
        t = 2 * zz + y
        rcopy(PD.at[t], ZD.at[z], szd.at[zz], rzd.at[z], (r, t)).start()

    @pl.loop(0, 4)
    def _(k):
        zz = line(k)
        @pl.when(k < 3)
        def _():
            zn = line(k + 1)
            t = 2 * zn + y
            wr(nb(t), rn.at[t])
            rcopy(nb(t), nb(t), syn.at[zn], rn.at[t], yp).start()
        to = 2 * zz + 1 - y
        wr(nb(to), rn.at[to])
        rows = pl.ds(al(256 * zz, 256), 256)
        X = N[rows]
        NT[:, rows] = X.T
        Cp = vC[rows]
        for j in range(3):
            ga, ua = pl.ds(384 * j, 384), pl.ds(1152 + 384 * j, 384)
            g = dot(X, vG[:, ga])
            u = dot(X, vG[:, ua])
            dm = dot_nt(Cp, vD[ga])
            sg = jax.nn.sigmoid(g)
            act = g * sg
            du = dm * u
            MX[:, ga] = (act * u).astype(BF)
            H[rows, ga] = (du * sg + du * act * (1.0 - sg)).astype(BF)
            H[rows, ua] = (dm * act).astype(BF)
        for j in range(3):
            co = pl.ds(512 * j, 512)
            d = dot_nt(H[rows], vG[co]).astype(BF)
            PD[2 * zz, :, co] = d[:128]
            PD[2 * zz + 1, :, co] = d[128:]
        rcopy(PD.at[to], YD.at[zz], syd.at[zz], ryd.at[zz], yp).start()
        for j in range(3):
            co = pl.ds(512 * j, 512)
            o = dot(MX[...], vD[:, co]).astype(BF)
            PO[2 * zz, :, co] = o[:128]
            PO[2 * zz + 1, :, co] = o[128:]
        MT[:, rows] = MX[...].T
        @pl.when(k >= 1)
        def _():
            add_d(k - 1)
        @pl.when(k >= 2)
        def _():
            send_d(k - 1)
    for k in range(4):
        zz = line(k)
        to = 2 * zz + 1 - y
        rcopy(PO.at[to], YO.at[zz], syo.at[zz], ryo.at[zz], yp).start()

    def dch(i): return pl.ds(al(288 * i, 16), 288)
    def qc(q): return pl.ds(al(384 * q, 128), 384)
    def d1(i):
        for j in range(3):
            co = pl.ds(512 * j, 512)
            GD[dch(i), co] = dot(MT[dch(i)], vC[:, co]).astype(BF)
        for xx in range(2):
            q = 2 * xx + 1 - c
            rcopy(GD.at[dch(i), qc(q)], RCd.at[xx, dch(i)], scd.at[i, xx], rcd.at[i, xx], cp).start()
    def d2(i):
        for xx in range(2):
            wr(RCd.at[xx, dch(i)], rcd.at[i, xx])
            q = 2 * xx + c
            GD[dch(i), qc(q)] = (GD[dch(i), qc(q)].astype(F32) + RCd[xx, dch(i)].astype(F32)).astype(BF)
        rcopy(GD.at[dch(i), qc(rxp)], RXd.at[dch(i)], sxd.at[i], rxd.at[i], xp).start()
    def d3(i):
        wr(RXd.at[dch(i)], rxd.at[i])
        GD[dch(i), qc(r)] = (GD[dch(i), qc(r)].astype(F32) + RXd[dch(i)].astype(F32)).astype(BF)
        src, dst = GD.at[dch(i), qc(r)], OD.at[r, dch(i)]
        pltpu.make_async_copy(src, dst, sfd.at[i, 3]).start()
        rcopy(src, dst, sfd.at[i, 0], rfd.at[i, r], xp).start()
        rcopy(src, dst, sfd.at[i, 1], rfd.at[i, r], cp).start()
    def d4(i):
        v = OD.at[rxp, dch(i)]
        wr(v, rfd.at[i, rxp])
        rcopy(v, v, sfd.at[i, 2], rfd.at[i, rxp], cp).start()
    @pl.loop(0, 6)
    def _(i):
        pl.when(i < 4)(lambda: d1(i))
        pl.when((i >= 1) & (i < 5))(lambda: d2(i - 1))
        pl.when(i >= 2)(lambda: d3(i - 2))
        @pl.when(i == 1)
        def _():
            add_d(3)
            send_d(3)
    def own(k): return (s + 1 + k) % 8
    def gq(t, q): return pl.ds(al(192 * t + 48 * q, 16), 48)
    def g1(k):
        t = own(k)
        rows = pl.ds(al(192 * t, 16), 192)
        for j in range(3):
            co = pl.ds(768 * j, 768)
            vG[rows, co] = dot(NT[rows], H[:, co]).astype(BF)
        for xx in range(2):
            q = 2 * xx + 1 - c
            rcopy(vG.at[gq(t, q)], RC.at[t, xx], scg.at[t, xx], rcg.at[t, xx], cp).start()
    def g2(k):
        t = own(k)
        for xx in range(2):
            wr(RC.at[t, xx], rcg.at[t, xx])
            q = gq(t, 2 * xx + c)
            vG[q] = (vG[q].astype(F32) + RC[t, xx].astype(F32)).astype(BF)
        rcopy(vG.at[gq(t, rxp)], RX.at[t], sxg.at[t], rxg.at[t], xp).start()
    def g3(k):
        t = own(k)
        wr(RX.at[t], rxg.at[t])
        q = gq(t, r)
        vG[q] = (vG[q].astype(F32) + RX[t].astype(F32)).astype(BF)
        @pl.when(k < 7)
        def _():
            rcopy(vG.at[q], OG.at[r, s], sag.at[t], rag.at[s, r], (r, t)).start()
        @pl.when(k == 7)
        def _():
            pltpu.make_async_copy(vG.at[q], OG.at[r, s], loc.at[5]).start()
    def share(t):
        v = OG.at[r, t]
        rcopy(v, v, sfg.at[t, 0], rag.at[t, r], xp).start()
        rcopy(v, v, sfg.at[t, 1], rag.at[t, r], cp).start()
    def add_o(k):
        zz = line(k)
        t = 2 * zz + y
        wr(YO.at[zz], ryo.at[zz])
        PO[t] = (PO[t].astype(F32) + YO[zz].astype(F32)).astype(BF)
    def send_o(k):
        zz = line(k)
        t = 2 * zz + y
        rcopy(PO.at[t], ZO.at[z], szo.at[zz], rzo.at[z], (r, t)).start()
    @pl.loop(0, 10)
    def _(i):
        pl.when(i < 8)(lambda: g1(i))
        pl.when((i >= 1) & (i < 9))(lambda: g2(i - 1))
        pl.when(i >= 2)(lambda: g3(i - 2))
        pl.when(i < 4)(lambda: d4(i))
        pl.when(i < 4)(lambda: add_o(i))
        pl.when((i >= 1) & (i < 4))(lambda: send_o(i))
    pltpu.make_async_copy(vG.at[gq(s, r)], OG.at[r, s], loc.at[5]).wait()
    share(s)
    @pl.loop(1, 8)
    def _(k):
        t = (s + 8 - k) % 8
        wr(OG.at[r, t], rag.at[t, r])
        share(t)
    def total(P, Z, rz, out):
        acc = P[s].astype(F32)
        for k in (1, 2, 3):
            zz = line(k)
            wr(Z.at[zz], rz.at[zz])
            acc = acc + Z[zz].astype(F32)
        out[...] = acc
    total(PD, ZD, rzd, DS)
    total(PO, ZO, rzo, OS)
    @pl.loop(0, 8)
    def _(k):
        t = (s + 8 - k) % 8
        v = OG.at[rxp, t]
        wr(v, rag.at[t, rxp])
        rcopy(v, v, sfg.at[t, 2], rag.at[t, rxp], cp).start()
    @pl.loop(0, 8)
    def _(t):
        for q in (rcp, rdp):
            wr(OG.at[q, t], rag.at[t, q])
        for d in range(3):
            ws(OG.at[r, t], sfg.at[t, d])
        for xx in range(2):
            ws(RC.at[t, xx], scg.at[t, xx])
        ws(RX.at[t], sxg.at[t])
        @pl.when(t != s)
        def _():
            ws(OG.at[r, s], sag.at[t])
    @pl.loop(0, 4)
    def _(i):
        for q in (rcp, rdp):
            wr(OD.at[q, dch(i)], rfd.at[i, q])
        for d in range(4):
            ws(OD.at[r, dch(i)], sfd.at[i, d])
        for xx in range(2):
            ws(RCd.at[xx, dch(i)], scd.at[i, xx])
        ws(RXd.at[dch(i)], sxd.at[i])
        ws(nb(s), syn.at[i])
        ws(YD.at[i], syd.at[i])
        ws(YO.at[i], syo.at[i])
        @pl.when(i != z)
        def _():
            ws(nb(s), szn.at[i])
            ws(ZD.at[i], szd.at[i])
            ws(ZO.at[i], szo.at[i])

def kb(n2, C, G, Dn):
    A = pl.BlockSpec(memory_space=pl.ANY)
    V = pl.BlockSpec(memory_space=pltpu.VMEM)
    D = pltpu.SemaphoreType.DMA
    sh = lambda a, b=BF: jax.ShapeDtypeStruct(a, b)
    vm = lambda *a: pltpu.VMEM(a, BF)
    return pl.pallas_call(
        kb_body,
        out_shape=(sh((128, 1536), F32), sh((128, 1536), F32), sh((4, 8, 48, 2304)), sh((4, 1152, 384))),
        in_specs=[A] * 4, out_specs=(V, V, A, A),
        scratch_shapes=[vm(1536, 2304), vm(1152, 1536), vm(1024, 1536), vm(1024, 1536), vm(1536, 1024), vm(256, 1152), vm(1152, 1024),
                        vm(1024, 2304), vm(8, 128, 1536), vm(8, 128, 1536)] + [vm(4, 128, 1536)] * 4 +
                       [vm(1152, 1536), vm(2, 1152, 384), vm(1152, 384), vm(8, 2, 48, 2304), vm(8, 48, 2304)] +
                       [D((8,)), D((4,)), D((4,))] + [D((4,))] * 8 +
                       [D((4, 2)), D((4, 2)), D((4,)), D((4,)), D((4, 4)), D((4, 4)),
                        D((8, 2)), D((8, 2)), D((8,)), D((8,)), D((8,)), D((8, 4)), D((8, 3)), D((6,))],
        compiler_params=pltpu.CompilerParams(collective_id=1, has_side_effects=True, vmem_limit_bytes=63 << 20), name="feed_forward",
    )(n2, C, G, Dn)


def k4_body(w_ref, OW, V, RC, RX, Y, Z, scw, rcw, sxw, rxw, syw, ryw, szw, rzw, sfw, rfw, loc):
    r, s, x, c, z, y = topo()
    cp, xp, yp = (r + 1 - 2 * c, s), ((r + 2) % 4, s), (r, s + 1 - 2 * y)
    rcp, rxp, rdp = r + 1 - 2 * c, (r + 2) % 4, 3 - r
    def wr(ref, sem): rcopy(ref, ref, loc.at[0], sem, cp).wait_recv()
    def ws(ref, sem): rcopy(ref, ref, sem, loc.at[0], cp).wait_send()
    load = pltpu.make_async_copy(w_ref, V, loc.at[1])
    load.start()
    greet([cp, xp, yp] + [(r, (s + k) % 8) for k in (2, 4, 6)])
    load.wait()
    def line(k):
        return (z + (1 - 2 * (z % 2)) * (k % 2) + (k // 2) * (2 - 4 * (z // 2)))
    def own(k):
        return 2 * line(3 - k % 4) + (1 - y + (k // 4) * (2 * y - 1))
    def gq(t, q): return pl.ds(al(192 * t + 48 * q, 16), 48)
    def p1(k):
        t = own(k)
        for xx in range(2):
            rcopy(V.at[gq(t, 2 * xx + 1 - c)], RC.at[t, xx], scw.at[t, xx], rcw.at[t, xx], cp).start()
    def p2(k):
        t = own(k)
        for xx in range(2):
            wr(RC.at[t, xx], rcw.at[t, xx])
            q = gq(t, 2 * xx + c)
            V[q] = (V[q].astype(F32) + RC[t, xx].astype(F32)).astype(BF)
        rcopy(V.at[gq(t, rxp)], RX.at[t], sxw.at[t], rxw.at[t], xp).start()
    def p3(k):
        t = own(k)
        wr(RX.at[t], rxw.at[t])
        q = gq(t, r)
        V[q] = (V[q].astype(F32) + RX[t].astype(F32)).astype(BF)
        @pl.when(k < 4)
        def _():
            rcopy(V.at[q], Y.at[t // 2], syw.at[t // 2], ryw.at[t // 2], yp).start()
        @pl.when(k >= 4)
        def _():
            wr(Y.at[t // 2], ryw.at[t // 2])
            V[q] = (V[q].astype(F32) + Y[t // 2].astype(F32)).astype(BF)
        @pl.when((k >= 4) & (k < 7))
        def _():
            rcopy(V.at[q], Z.at[z], szw.at[t // 2], rzw.at[z], (r, t)).start()
    @pl.loop(0, 8)
    def _(k): p1(k)
    @pl.loop(0, 9)
    def _(i):
        pl.when(i < 8)(lambda: p2(i))
        pl.when(i >= 1)(lambda: p3(i - 1))
    acc = V[gq(s, r)].astype(F32)
    for k in (1, 2, 3):
        zz = line(k)
        wr(Z.at[zz], rzw.at[zz])
        acc = acc + Z[zz].astype(F32)
    OW[r] = acc.astype(BF)
    rcopy(OW.at[r], OW.at[r], sfw.at[0], rfw.at[r], xp).start()
    rcopy(OW.at[r], OW.at[r], sfw.at[1], rfw.at[r], cp).start()
    wr(OW.at[rxp], rfw.at[rxp])
    rcopy(OW.at[rxp], OW.at[rxp], sfw.at[2], rfw.at[rxp], cp).start()
    wr(OW.at[rcp], rfw.at[rcp])
    wr(OW.at[rdp], rfw.at[rdp])
    for d in range(3):
        ws(OW.at[r], sfw.at[d])
    @pl.loop(0, 8)
    def _(t):
        for xx in range(2):
            ws(RC.at[t, xx], scw.at[t, xx])
        ws(RX.at[t], sxw.at[t])
    @pl.loop(0, 4)
    def _(i):
        ws(Y.at[i], syw.at[i])
        @pl.when(i != z)
        def _():
            ws(Z.at[i], szw.at[i])

def k4(w):
    A = pl.BlockSpec(memory_space=pl.ANY)
    V = pl.BlockSpec(memory_space=pltpu.VMEM)
    D = pltpu.SemaphoreType.DMA
    vm = lambda *a: pltpu.VMEM(a, BF)
    wide = w.shape[1]
    return pl.pallas_call(
        k4_body,
        out_shape=jax.ShapeDtypeStruct((4, 48, wide), BF),
        in_specs=[A], out_specs=V,
        scratch_shapes=[vm(1536, wide), vm(8, 2, 48, wide), vm(8, 48, wide), vm(4, 48, wide), vm(4, 48, wide),
                        D((8, 2)), D((8, 2)), D((8,)), D((8,)), D((4,)), D((4,)), D((4,)), D((4,)), D((3,)), D((4,)), D((2,))],
        compiler_params=pltpu.CompilerParams(collective_id=2, has_side_effects=True, vmem_limit_bytes=50 << 20), name="attention_gradients",
    )(w)


def to_columns(rows):
    ranks = lax.axis_size("shard")
    depth, width = rows.shape
    split = rows.reshape(depth, ranks, width // ranks).transpose(1, 0, 2)
    return lax.all_to_all(split, "shard", 0, 0, tiled=True).reshape(ranks * depth, width // ranks)


def to_rows(columns):
    ranks, copies = lax.axis_size("shard"), lax.axis_size("replica")
    depth, width = columns.shape
    depth = depth // ranks
    parts = columns.reshape(ranks, copies, depth // copies, width)
    part = lax.psum_scatter(parts, "replica", scatter_dimension=1, tiled=False)
    part = lax.all_to_all(part, "shard", 0, 0, tiled=True)
    part = part.transpose(1, 0, 2).reshape(depth // copies, ranks * width)
    return lax.all_gather(part, "replica", axis=0, tiled=True)


def shards(
    tokens, segments, gain_attn, w_qkv, b_qkv, w_out, gain_ffn, w_gate, w_up, w_down, cotangent
):
    heads_per_group = QUERY_HEADS // KEY_VALUE_HEADS
    head_dimension = QUERY_HEADS * HEAD_DIMENSION
    key_value_limit = head_dimension + KEY_VALUE_HEADS * HEAD_DIMENSION
    logit_scale = HEAD_DIMENSION ** (-0.5)
    token_length = tokens.shape[1]
    full_gain_attn, full_qkv, full_bias, full_out, full_gain_ffn = (
        lax.all_gather(gain_attn, "shard", axis=0, tiled=True),
        lax.all_gather(w_qkv, "shard", axis=0, tiled=True),
        lax.all_gather(b_qkv, "shard", axis=0, tiled=True),
        lax.all_gather(w_out, "shard", axis=0, tiled=True),
        lax.all_gather(gain_ffn, "shard", axis=0, tiled=True),
    )
    gate_columns = to_columns(w_gate)
    up_columns = to_columns(w_up)
    all_cot = lax.all_gather(cotangent[0], "shard", axis=0, tiled=True)
    gain_first = full_gain_attn.astype(jnp.float32)
    gain_second = full_gain_ffn.astype(jnp.float32)
    cosine, sine_vals, allowed = tables(segments[0], HEAD_DIMENSION)
    cosine_per_head = cosine[:, None, :]
    sine_per_head = sine_vals[:, None, :]
    inputs = tokens[0].astype(jnp.float32)
    normed_first, unit_first, rstd_first = norm_forward(inputs, gain_first)
    acts_first = normed_first.astype(jnp.bfloat16)
    joined_projection = jnp.dot(
        acts_first, full_qkv, preferred_element_type=jnp.float32
    ) + full_bias.astype(jnp.float32)
    query_rows = apply_rotation(
        joined_projection[:, :head_dimension].reshape(token_length, QUERY_HEADS, HEAD_DIMENSION),
        cosine_per_head,
        sine_per_head,
    )
    query_reduced = (
        (query_rows * logit_scale)
        .astype(jnp.bfloat16)
        .reshape(token_length, KEY_VALUE_HEADS, heads_per_group, HEAD_DIMENSION)
    )
    k_low = apply_rotation(
        joined_projection[:, head_dimension:key_value_limit].reshape(
            token_length, KEY_VALUE_HEADS, HEAD_DIMENSION
        ),
        cosine_per_head,
        sine_per_head,
    ).astype(jnp.bfloat16)
    value_reduced = (
        joined_projection[:, key_value_limit:]
        .reshape(token_length, KEY_VALUE_HEADS, HEAD_DIMENSION)
        .astype(jnp.bfloat16)
    )
    scores = jnp.einsum("ikrd,jkd->krij", query_reduced, k_low, preferred_element_type=jnp.float32)
    scores = jnp.where(allowed != 0, scores, -1e30)
    largest = jnp.max(scores, axis=-1, keepdims=True)
    exponents = jnp.exp(scores - largest)
    soft_probs = exponents / jnp.sum(exponents, axis=-1, keepdims=True)
    soft_low = soft_probs.astype(jnp.bfloat16)
    attended = jnp.einsum(
        "krij,jkd->ikrd", soft_low, value_reduced, preferred_element_type=jnp.float32
    )
    attended = attended.reshape(token_length, head_dimension).astype(jnp.bfloat16)
    hidden_mid = inputs + jnp.dot(attended, full_out, preferred_element_type=jnp.float32)
    normed_second, unit_second, rstd_second = norm_forward(hidden_mid, gain_second)
    acts_second = normed_second.astype(jnp.bfloat16)
    all_acts = lax.all_gather(acts_second, "shard", axis=0, tiled=True)
    gate_vals = jnp.dot(all_acts, gate_columns, preferred_element_type=jnp.float32)
    up_vals = jnp.dot(all_acts, up_columns, preferred_element_type=jnp.float32)
    sigmoid_gate = jax.nn.sigmoid(gate_vals)
    active = gate_vals * sigmoid_gate
    mixed_hidden = (active * up_vals).astype(jnp.bfloat16)
    d_mixed = jnp.einsum("ld,fd->lf", all_cot, w_down, preferred_element_type=jnp.float32)
    d_active = d_mixed * up_vals
    d_gate = (
        d_active * sigmoid_gate + d_active * gate_vals * sigmoid_gate * (1.0 - sigmoid_gate)
    ).astype(jnp.bfloat16)
    d_up = (d_mixed * active).astype(jnp.bfloat16)
    d_normed_part = jnp.einsum("lf,df->ld", d_gate, gate_columns, preferred_element_type=jnp.float32)
    d_normed_part = d_normed_part + jnp.einsum(
        "lf,df->ld", d_up, up_columns, preferred_element_type=jnp.float32
    )
    d_normed_second = lax.psum_scatter(
        d_normed_part.astype(jnp.bfloat16), "shard", scatter_dimension=0, tiled=True
    ).astype(jnp.float32)
    down_part = jnp.dot(mixed_hidden, w_down, preferred_element_type=jnp.float32)
    result = (
        hidden_mid
        + lax.psum_scatter(
            down_part.astype(jnp.bfloat16), "shard", scatter_dimension=0, tiled=True
        ).astype(jnp.float32)
    ).astype(jnp.bfloat16)
    grad_out = cotangent[0]
    down_grad = column_term(mixed_hidden, all_cot).astype(jnp.bfloat16)
    gate_grad = to_rows(column_term(all_acts, d_gate).astype(jnp.bfloat16))
    up_grad = to_rows(column_term(all_acts, d_up).astype(jnp.bfloat16))
    gain_second_grad = jnp.sum(d_normed_second * unit_second, axis=0)
    d_hidden_mid = grad_out.astype(jnp.float32) + norm_backward(
        d_normed_second, gain_second, unit_second, rstd_second
    )
    d_branch = d_hidden_mid.astype(jnp.bfloat16)
    out_grad_term = jnp.einsum("le,ld->ed", attended, d_branch, preferred_element_type=jnp.float32)
    attended_gradient = jnp.einsum(
        "ld,ed->le", d_branch, full_out, preferred_element_type=jnp.float32
    )
    attended_gradient = attended_gradient.astype(jnp.bfloat16).reshape(
        token_length, KEY_VALUE_HEADS, heads_per_group, HEAD_DIMENSION
    )
    d_probs = jnp.einsum(
        "ikrd,jkd->krij", attended_gradient, value_reduced, preferred_element_type=jnp.float32
    )
    value_gradient = jnp.einsum(
        "krij,ikrd->jkd", soft_low, attended_gradient, preferred_element_type=jnp.float32
    )
    d_scores = soft_probs * (d_probs - jnp.sum(soft_probs * d_probs, axis=-1, keepdims=True))
    d_scores_low = d_scores.astype(jnp.bfloat16)
    d_queries = jnp.einsum(
        "krij,jkd->ikrd", d_scores_low, k_low, preferred_element_type=jnp.float32
    )
    d_queries = rotate_back(
        d_queries.reshape(token_length, QUERY_HEADS, HEAD_DIMENSION) * logit_scale,
        cosine_per_head,
        sine_per_head,
    )
    key_gradient = jnp.einsum(
        "krij,ikrd->jkd", d_scores_low, query_reduced, preferred_element_type=jnp.float32
    )
    key_gradient = rotate_back(key_gradient, cosine_per_head, sine_per_head)
    d_joined = jnp.concatenate(
        [
            d_queries.reshape(token_length, head_dimension),
            key_gradient.reshape(token_length, KEY_VALUE_HEADS * HEAD_DIMENSION),
            value_gradient.reshape(token_length, KEY_VALUE_HEADS * HEAD_DIMENSION),
        ],
        axis=1,
    ).astype(jnp.bfloat16)
    bias_grad_term = jnp.sum(d_joined.astype(jnp.float32), axis=0)
    qkv_grad_term = jnp.einsum(
        "ld,le->de", acts_first, d_joined, preferred_element_type=jnp.float32
    )
    d_normed_first = jnp.einsum("le,de->ld", d_joined, full_qkv, preferred_element_type=jnp.float32)
    gain_first_grad = jnp.sum(d_normed_first * unit_first, axis=0)
    d_inputs = d_hidden_mid + norm_backward(d_normed_first, gain_first, unit_first, rstd_first)
    owned = (
        lax.psum_scatter(
            gain_first_grad.astype(jnp.bfloat16), "shard", scatter_dimension=0, tiled=True
        ).astype(jnp.float32),
        lax.psum_scatter(
            qkv_grad_term.astype(jnp.bfloat16), "shard", scatter_dimension=0, tiled=True
        ).astype(jnp.float32),
        lax.psum_scatter(
            bias_grad_term.astype(jnp.bfloat16), "shard", scatter_dimension=0, tiled=True
        ).astype(jnp.float32),
        lax.psum_scatter(
            out_grad_term.astype(jnp.bfloat16), "shard", scatter_dimension=0, tiled=True
        ).astype(jnp.float32),
        lax.psum_scatter(
            gain_second_grad.astype(jnp.bfloat16), "shard", scatter_dimension=0, tiled=True
        ).astype(jnp.float32),
    )
    summed = (
        lax.psum(owned[0].astype(jnp.bfloat16), "replica").astype(jnp.float32),
        lax.psum(owned[1].astype(jnp.bfloat16), "replica").astype(jnp.float32),
        lax.psum(owned[2].astype(jnp.bfloat16), "replica").astype(jnp.float32),
        lax.psum(owned[3].astype(jnp.bfloat16), "replica").astype(jnp.float32),
        lax.psum(owned[4].astype(jnp.bfloat16), "replica").astype(jnp.float32),
        gate_grad.astype(jnp.float32),
        up_grad.astype(jnp.float32),
        lax.psum(down_grad, "replica").astype(jnp.float32),
    )
    return (
        result[None],
        d_inputs.astype(jnp.bfloat16)[None],
        summed[0],
        summed[1],
        summed[2],
        summed[3],
        summed[4],
        summed[5],
        summed[6],
        summed[7],
    )


def shards_eight(
    tokens, segments, gain_attn, w_qkv, b_qkv, w_out, gain_ffn, w_gate, w_up, w_down, cotangent
):
    heads_per_group = QUERY_HEADS // KEY_VALUE_HEADS
    head_dimension = QUERY_HEADS * HEAD_DIMENSION
    key_value_limit = head_dimension + KEY_VALUE_HEADS * HEAD_DIMENSION
    logit_scale = HEAD_DIMENSION ** (-0.5)
    token_length = tokens.shape[1]
    small = jnp.concatenate([gain_attn, b_qkv, gain_ffn]).reshape(5, 128)
    columns = jnp.concatenate(
        [
            jnp.pad(w.reshape(192, 8, 1120).transpose(1, 0, 2), ((0, 0), (0, 0), (0, 32)))
            for w in (w_gate, w_up)
        ],
        axis=2,
    )
    attn_full, gate_up, all_cot, smalls = k1(
        jnp.concatenate([w_qkv, w_out], axis=1),
        columns,
        cotangent[0],
        jnp.pad(small, ((0, 11), (0, 0))),
    )
    smalls = smalls[:, :5].reshape(8, 640)
    full_gain_attn = smalls[:, :192].reshape(-1)
    full_bias = smalls[:, 192:448].reshape(-1)
    full_gain_ffn = smalls[:, 448:].reshape(-1)
    full_qkv, full_out = attn_full[:, :2048], attn_full[:, 2048:]
    gain_first = full_gain_attn.astype(jnp.float32)
    gain_second = full_gain_ffn.astype(jnp.float32)
    cosine, sine_vals, allowed = tables(segments[0], HEAD_DIMENSION)
    cosine_per_head = cosine[:, None, :]
    sine_per_head = sine_vals[:, None, :]
    inputs = tokens[0].astype(jnp.float32)
    normed_first, unit_first, rstd_first = norm_forward(inputs, gain_first)
    acts_first = normed_first.astype(jnp.bfloat16)
    joined_projection = jnp.dot(
        acts_first, full_qkv, preferred_element_type=jnp.float32
    ) + full_bias.astype(jnp.float32)
    query_rows = apply_rotation(
        joined_projection[:, :head_dimension].reshape(token_length, QUERY_HEADS, HEAD_DIMENSION),
        cosine_per_head,
        sine_per_head,
    )
    query_reduced = (
        (query_rows * logit_scale)
        .astype(jnp.bfloat16)
        .reshape(token_length, KEY_VALUE_HEADS, heads_per_group, HEAD_DIMENSION)
    )
    k_low = apply_rotation(
        joined_projection[:, head_dimension:key_value_limit].reshape(
            token_length, KEY_VALUE_HEADS, HEAD_DIMENSION
        ),
        cosine_per_head,
        sine_per_head,
    ).astype(jnp.bfloat16)
    value_reduced = (
        joined_projection[:, key_value_limit:]
        .reshape(token_length, KEY_VALUE_HEADS, HEAD_DIMENSION)
        .astype(jnp.bfloat16)
    )
    scores = jnp.einsum("ikrd,jkd->krij", query_reduced, k_low, preferred_element_type=jnp.float32)
    scores = jnp.where(allowed != 0, scores, -1e30)
    largest = jnp.max(scores, axis=-1, keepdims=True)
    exponents = jnp.exp(scores - largest)
    soft_probs = exponents / jnp.sum(exponents, axis=-1, keepdims=True)
    soft_low = soft_probs.astype(jnp.bfloat16)
    attended = jnp.einsum(
        "krij,jkd->ikrd", soft_low, value_reduced, preferred_element_type=jnp.float32
    )
    attended = attended.reshape(token_length, head_dimension).astype(jnp.bfloat16)
    hidden_mid = inputs + jnp.dot(attended, full_out, preferred_element_type=jnp.float32)
    normed_second, unit_second, rstd_second = norm_forward(hidden_mid, gain_second)
    acts_second = normed_second.astype(jnp.bfloat16)
    d_normed_second, down_sum, gate_up_rows, down_rows = kb(
        acts_second, all_cot, gate_up, jnp.pad(w_down, ((0, 32), (0, 0)))
    )
    result = (hidden_mid + down_sum).astype(jnp.bfloat16)
    grad_out = cotangent[0]
    gate_up_rows = gate_up_rows.transpose(0, 2, 1, 3).reshape(192, 8, 2304)
    gate_grad = gate_up_rows[:, :, :1120].reshape(192, 8960)
    up_grad = gate_up_rows[:, :, 1152:2272].reshape(192, 8960)
    down_grad = down_rows.transpose(1, 0, 2)[:1120].reshape(1120, 1536)
    gain_second_grad = jnp.sum(d_normed_second * unit_second, axis=0)
    d_hidden_mid = grad_out.astype(jnp.float32) + norm_backward(
        d_normed_second, gain_second, unit_second, rstd_second
    )
    d_branch = d_hidden_mid.astype(jnp.bfloat16)
    out_grad_term = jnp.einsum("le,ld->ed", attended, d_branch, preferred_element_type=jnp.float32)
    attended_gradient = jnp.einsum(
        "ld,ed->le", d_branch, full_out, preferred_element_type=jnp.float32
    )
    attended_gradient = attended_gradient.astype(jnp.bfloat16).reshape(
        token_length, KEY_VALUE_HEADS, heads_per_group, HEAD_DIMENSION
    )
    d_probs = jnp.einsum(
        "ikrd,jkd->krij", attended_gradient, value_reduced, preferred_element_type=jnp.float32
    )
    value_gradient = jnp.einsum(
        "krij,ikrd->jkd", soft_low, attended_gradient, preferred_element_type=jnp.float32
    )
    d_scores = soft_probs * (d_probs - jnp.sum(soft_probs * d_probs, axis=-1, keepdims=True))
    d_scores_low = d_scores.astype(jnp.bfloat16)
    d_queries = jnp.einsum(
        "krij,jkd->ikrd", d_scores_low, k_low, preferred_element_type=jnp.float32
    )
    d_queries = rotate_back(
        d_queries.reshape(token_length, QUERY_HEADS, HEAD_DIMENSION) * logit_scale,
        cosine_per_head,
        sine_per_head,
    )
    key_gradient = jnp.einsum(
        "krij,ikrd->jkd", d_scores_low, query_reduced, preferred_element_type=jnp.float32
    )
    key_gradient = rotate_back(key_gradient, cosine_per_head, sine_per_head)
    d_joined = jnp.concatenate(
        [
            d_queries.reshape(token_length, head_dimension),
            key_gradient.reshape(token_length, KEY_VALUE_HEADS * HEAD_DIMENSION),
            value_gradient.reshape(token_length, KEY_VALUE_HEADS * HEAD_DIMENSION),
        ],
        axis=1,
    ).astype(jnp.bfloat16)
    bias_grad_term = jnp.sum(d_joined.astype(jnp.float32), axis=0)
    qkv_grad_term = jnp.einsum(
        "ld,le->de", acts_first, d_joined, preferred_element_type=jnp.float32
    )
    d_normed_first = jnp.einsum("le,de->ld", d_joined, full_qkv, preferred_element_type=jnp.float32)
    gain_first_grad = jnp.sum(d_normed_first * unit_first, axis=0)
    d_inputs = d_hidden_mid + norm_backward(d_normed_first, gain_first, unit_first, rstd_first)
    small_terms = jnp.concatenate(
        [
            gain_first_grad.reshape(8, 192),
            bias_grad_term.reshape(8, 256),
            gain_second_grad.reshape(8, 192),
        ],
        axis=1,
    )
    small_terms = jnp.pad(small_terms.reshape(8, 5, 128), ((0, 0), (0, 187), (0, 0))).reshape(1536, 128)
    owned = k4(
        jnp.concatenate([t.astype(jnp.bfloat16) for t in (qkv_grad_term, out_grad_term, small_terms)], axis=1)
    ).reshape(192, 3712)
    small_rows = owned[:5, 3584:].reshape(640)
    summed = tuple(
        part.astype(jnp.float32)
        for part in (
            small_rows[:192],
            owned[:, :2048],
            small_rows[192:448],
            owned[:, 2048:3584],
            small_rows[448:],
            gate_grad,
            up_grad,
            down_grad,
        )
    )
    return (
        result[None],
        d_inputs.astype(jnp.bfloat16)[None],
        summed[0],
        summed[1],
        summed[2],
        summed[3],
        summed[4],
        summed[5],
        summed[6],
        summed[7],
    )


def solution(mesh):
    placed = (
        P(("replica", "shard"), None, None),
        P(("replica", "shard"), None),
        P("shard"),
        P("shard", None),
        P("shard"),
        P("shard", None),
        P("shard"),
        P("shard", None),
        P("shard", None),
        P("shard", None),
        P(("replica", "shard"), None, None),
    )
    return jax.shard_map(
        shards_eight if (mesh.shape["replica"], mesh.shape["shard"]) == (4, 8) else shards,
        mesh=mesh,
        in_specs=placed,
        out_specs=(
            P(("replica", "shard"), None, None),
            P(("replica", "shard"), None, None),
            P("shard"),
            P("shard", None),
            P("shard"),
            P("shard", None),
            P("shard"),
            P("shard", None),
            P("shard", None),
            P("shard", None),
        ),
        check_vma=False,
    )
```

```python
import math

import jax
import jax.numpy as jnp
from jax import lax
from jax.experimental import pallas as pl
from jax.experimental.pallas import tpu as pltpu
from jax.sharding import PartitionSpec as P

QUERY_HEADS = 12
KEY_VALUE_HEADS = 2
HEAD_DIMENSION = 128


eps_norm = 1e-06
rope_base = 1000000.0


def tables(segment_ids, head_size):
    token_length = segment_ids.shape[-1]
    row_index = jnp.arange(token_length, dtype=jnp.int32)
    earlier = jnp.sum(
        (segment_ids[..., None, :] < segment_ids[..., :, None]).astype(jnp.int32),
        axis=-1,
        dtype=jnp.int32,
    )
    positions = (row_index - earlier).astype(jnp.float32)
    frequencies = jnp.exp(
        jnp.arange(head_size // 2, dtype=jnp.float32) * (-2.0 * math.log(rope_base) / head_size)
    )
    angles = positions[..., None] * frequencies
    cosine = jnp.concatenate([jnp.cos(angles), jnp.cos(angles)], axis=-1)
    sine_vals = jnp.concatenate([jnp.sin(angles), jnp.sin(angles)], axis=-1)
    allowed = (
        (segment_ids[..., None, :] == segment_ids[..., :, None])
        & (row_index[None, :] <= row_index[:, None])
    ).astype(jnp.int32)
    return (cosine, sine_vals, allowed)


def apply_rotation(values, cosine, sine_vals):
    halfway = values.shape[-1] // 2
    turned = jnp.concatenate([-values[..., halfway:], values[..., :halfway]], axis=-1)
    return values * cosine + turned * sine_vals


def rotate_back(values, cosine, sine_vals):
    halfway = values.shape[-1] // 2
    shifted = values * sine_vals
    return values * cosine + jnp.concatenate(
        [shifted[..., halfway:], -shifted[..., :halfway]], axis=-1
    )


def norm_forward(hidden, gain_vec):
    rstd_rows = lax.rsqrt(jnp.mean(hidden * hidden, axis=-1, keepdims=True) + eps_norm)
    unit_rows = hidden * rstd_rows
    return (unit_rows * gain_vec, unit_rows, rstd_rows)


def norm_backward(grad_in, gain_vec, unit_rows, rstd_rows):
    inner_grad = grad_in * gain_vec
    return rstd_rows * (
        inner_grad - unit_rows * jnp.mean(inner_grad * unit_rows, axis=-1, keepdims=True)
    )


def column_term(left_side, right_side):
    return jnp.einsum("lf,ld->fd", left_side, right_side, preferred_element_type=jnp.float32)


def to_columns(rows):
    ranks = lax.axis_size("shard")
    depth, width = rows.shape
    split = rows.reshape(depth, ranks, width // ranks).transpose(1, 0, 2)
    return lax.all_to_all(split, "shard", 0, 0, tiled=True).reshape(ranks * depth, width // ranks)


def to_rows(columns):
    ranks, copies = lax.axis_size("shard"), lax.axis_size("replica")
    depth, width = columns.shape
    depth = depth // ranks
    parts = columns.reshape(ranks, copies, depth // copies, width)
    part = lax.psum_scatter(parts, "replica", scatter_dimension=1, tiled=False)
    part = lax.all_to_all(part, "shard", 0, 0, tiled=True)
    part = part.transpose(1, 0, 2).reshape(depth // copies, ranks * width)
    return lax.all_gather(part, "replica", axis=0, tiled=True)


def shards(
    tokens, segments, gain_attn, w_qkv, b_qkv, w_out, gain_ffn, w_gate, w_up, w_down, cotangent
):
    heads_per_group = QUERY_HEADS // KEY_VALUE_HEADS
    head_dimension = QUERY_HEADS * HEAD_DIMENSION
    key_value_limit = head_dimension + KEY_VALUE_HEADS * HEAD_DIMENSION
    logit_scale = HEAD_DIMENSION ** (-0.5)
    token_length = tokens.shape[1]
    full_gain_attn, full_qkv, full_bias, full_out, full_gain_ffn = (
        lax.all_gather(gain_attn, "shard", axis=0, tiled=True),
        lax.all_gather(w_qkv, "shard", axis=0, tiled=True),
        lax.all_gather(b_qkv, "shard", axis=0, tiled=True),
        lax.all_gather(w_out, "shard", axis=0, tiled=True),
        lax.all_gather(gain_ffn, "shard", axis=0, tiled=True),
    )
    gate_columns = to_columns(w_gate)
    up_columns = to_columns(w_up)
    all_cot = lax.all_gather(cotangent[0], "shard", axis=0, tiled=True)
    gain_first = full_gain_attn.astype(jnp.float32)
    gain_second = full_gain_ffn.astype(jnp.float32)
    cosine, sine_vals, allowed = tables(segments[0], HEAD_DIMENSION)
    cosine_per_head = cosine[:, None, :]
    sine_per_head = sine_vals[:, None, :]
    inputs = tokens[0].astype(jnp.float32)
    normed_first, unit_first, rstd_first = norm_forward(inputs, gain_first)
    acts_first = normed_first.astype(jnp.bfloat16)
    joined_projection = jnp.dot(
        acts_first, full_qkv, preferred_element_type=jnp.float32
    ) + full_bias.astype(jnp.float32)
    query_rows = apply_rotation(
        joined_projection[:, :head_dimension].reshape(token_length, QUERY_HEADS, HEAD_DIMENSION),
        cosine_per_head,
        sine_per_head,
    )
    query_reduced = (
        (query_rows * logit_scale)
        .astype(jnp.bfloat16)
        .reshape(token_length, KEY_VALUE_HEADS, heads_per_group, HEAD_DIMENSION)
    )
    k_low = apply_rotation(
        joined_projection[:, head_dimension:key_value_limit].reshape(
            token_length, KEY_VALUE_HEADS, HEAD_DIMENSION
        ),
        cosine_per_head,
        sine_per_head,
    ).astype(jnp.bfloat16)
    value_reduced = (
        joined_projection[:, key_value_limit:]
        .reshape(token_length, KEY_VALUE_HEADS, HEAD_DIMENSION)
        .astype(jnp.bfloat16)
    )
    scores = jnp.einsum("ikrd,jkd->krij", query_reduced, k_low, preferred_element_type=jnp.float32)
    scores = jnp.where(allowed != 0, scores, -1e30)
    largest = jnp.max(scores, axis=-1, keepdims=True)
    exponents = jnp.exp(scores - largest)
    soft_probs = exponents / jnp.sum(exponents, axis=-1, keepdims=True)
    soft_low = soft_probs.astype(jnp.bfloat16)
    attended = jnp.einsum(
        "krij,jkd->ikrd", soft_low, value_reduced, preferred_element_type=jnp.float32
    )
    attended = attended.reshape(token_length, head_dimension).astype(jnp.bfloat16)
    hidden_mid = inputs + jnp.dot(attended, full_out, preferred_element_type=jnp.float32)
    normed_second, unit_second, rstd_second = norm_forward(hidden_mid, gain_second)
    acts_second = normed_second.astype(jnp.bfloat16)
    all_acts = lax.all_gather(acts_second, "shard", axis=0, tiled=True)
    gate_vals = jnp.dot(all_acts, gate_columns, preferred_element_type=jnp.float32)
    up_vals = jnp.dot(all_acts, up_columns, preferred_element_type=jnp.float32)
    sigmoid_gate = jax.nn.sigmoid(gate_vals)
    active = gate_vals * sigmoid_gate
    mixed_hidden = (active * up_vals).astype(jnp.bfloat16)
    d_mixed = jnp.einsum("ld,fd->lf", all_cot, w_down, preferred_element_type=jnp.float32)
    d_active = d_mixed * up_vals
    d_gate = (
        d_active * sigmoid_gate + d_active * gate_vals * sigmoid_gate * (1.0 - sigmoid_gate)
    ).astype(jnp.bfloat16)
    d_up = (d_mixed * active).astype(jnp.bfloat16)
    d_normed_part = jnp.einsum("lf,df->ld", d_gate, gate_columns, preferred_element_type=jnp.float32)
    d_normed_part = d_normed_part + jnp.einsum(
        "lf,df->ld", d_up, up_columns, preferred_element_type=jnp.float32
    )
    d_normed_second = lax.psum_scatter(
        d_normed_part.astype(jnp.bfloat16), "shard", scatter_dimension=0, tiled=True
    ).astype(jnp.float32)
    down_part = jnp.dot(mixed_hidden, w_down, preferred_element_type=jnp.float32)
    result = (
        hidden_mid
        + lax.psum_scatter(
            down_part.astype(jnp.bfloat16), "shard", scatter_dimension=0, tiled=True
        ).astype(jnp.float32)
    ).astype(jnp.bfloat16)
    grad_out = cotangent[0]
    down_grad = column_term(mixed_hidden, all_cot).astype(jnp.bfloat16)
    gate_grad = to_rows(column_term(all_acts, d_gate).astype(jnp.bfloat16))
    up_grad = to_rows(column_term(all_acts, d_up).astype(jnp.bfloat16))
    gain_second_grad = jnp.sum(d_normed_second * unit_second, axis=0)
    d_hidden_mid = grad_out.astype(jnp.float32) + norm_backward(
        d_normed_second, gain_second, unit_second, rstd_second
    )
    d_branch = d_hidden_mid.astype(jnp.bfloat16)
    out_grad_term = jnp.einsum("le,ld->ed", attended, d_branch, preferred_element_type=jnp.float32)
    attended_gradient = jnp.einsum(
        "ld,ed->le", d_branch, full_out, preferred_element_type=jnp.float32
    )
    attended_gradient = attended_gradient.astype(jnp.bfloat16).reshape(
        token_length, KEY_VALUE_HEADS, heads_per_group, HEAD_DIMENSION
    )
    d_probs = jnp.einsum(
        "ikrd,jkd->krij", attended_gradient, value_reduced, preferred_element_type=jnp.float32
    )
    value_gradient = jnp.einsum(
        "krij,ikrd->jkd", soft_low, attended_gradient, preferred_element_type=jnp.float32
    )
    d_scores = soft_probs * (d_probs - jnp.sum(soft_probs * d_probs, axis=-1, keepdims=True))
    d_scores_low = d_scores.astype(jnp.bfloat16)
    d_queries = jnp.einsum(
        "krij,jkd->ikrd", d_scores_low, k_low, preferred_element_type=jnp.float32
    )
    d_queries = rotate_back(
        d_queries.reshape(token_length, QUERY_HEADS, HEAD_DIMENSION) * logit_scale,
        cosine_per_head,
        sine_per_head,
    )
    key_gradient = jnp.einsum(
        "krij,ikrd->jkd", d_scores_low, query_reduced, preferred_element_type=jnp.float32
    )
    key_gradient = rotate_back(key_gradient, cosine_per_head, sine_per_head)
    d_joined = jnp.concatenate(
        [
            d_queries.reshape(token_length, head_dimension),
            key_gradient.reshape(token_length, KEY_VALUE_HEADS * HEAD_DIMENSION),
            value_gradient.reshape(token_length, KEY_VALUE_HEADS * HEAD_DIMENSION),
        ],
        axis=1,
    ).astype(jnp.bfloat16)
    bias_grad_term = jnp.sum(d_joined.astype(jnp.float32), axis=0)
    qkv_grad_term = jnp.einsum(
        "ld,le->de", acts_first, d_joined, preferred_element_type=jnp.float32
    )
    d_normed_first = jnp.einsum("le,de->ld", d_joined, full_qkv, preferred_element_type=jnp.float32)
    gain_first_grad = jnp.sum(d_normed_first * unit_first, axis=0)
    d_inputs = d_hidden_mid + norm_backward(d_normed_first, gain_first, unit_first, rstd_first)
    owned = (
        lax.psum_scatter(
            gain_first_grad.astype(jnp.bfloat16), "shard", scatter_dimension=0, tiled=True
        ).astype(jnp.float32),
        lax.psum_scatter(
            qkv_grad_term.astype(jnp.bfloat16), "shard", scatter_dimension=0, tiled=True
        ).astype(jnp.float32),
        lax.psum_scatter(
            bias_grad_term.astype(jnp.bfloat16), "shard", scatter_dimension=0, tiled=True
        ).astype(jnp.float32),
        lax.psum_scatter(
            out_grad_term.astype(jnp.bfloat16), "shard", scatter_dimension=0, tiled=True
        ).astype(jnp.float32),
        lax.psum_scatter(
            gain_second_grad.astype(jnp.bfloat16), "shard", scatter_dimension=0, tiled=True
        ).astype(jnp.float32),
    )
    summed = (
        lax.psum(owned[0].astype(jnp.bfloat16), "replica").astype(jnp.float32),
        lax.psum(owned[1].astype(jnp.bfloat16), "replica").astype(jnp.float32),
        lax.psum(owned[2].astype(jnp.bfloat16), "replica").astype(jnp.float32),
        lax.psum(owned[3].astype(jnp.bfloat16), "replica").astype(jnp.float32),
        lax.psum(owned[4].astype(jnp.bfloat16), "replica").astype(jnp.float32),
        gate_grad.astype(jnp.float32),
        up_grad.astype(jnp.float32),
        lax.psum(down_grad, "replica").astype(jnp.float32),
    )
    return (
        result[None],
        d_inputs.astype(jnp.bfloat16)[None],
        summed[0],
        summed[1],
        summed[2],
        summed[3],
        summed[4],
        summed[5],
        summed[6],
        summed[7],
    )


MESH = pl.DeviceIdType.MESH
BF, F32 = jnp.bfloat16, jnp.float32
HBM = pl.BlockSpec(memory_space=pl.ANY)
VMEM = pl.BlockSpec(memory_space=pltpu.VMEM)
DMA = pltpu.SemaphoreType.DMA


def shaped(*shape, dtype=BF):
    return jax.ShapeDtypeStruct(shape, dtype)


def low(*shape):
    return pltpu.VMEM(shape, BF)


def full(*shape):
    return pltpu.VMEM(shape, F32)


def dot(a, b):
    return lax.dot_general(a, b, (((1,), (0,)), ((), ())), preferred_element_type=F32)


def dot_nt(a, b):
    return lax.dot_general(a, b, (((1,), (1,)), ((), ())), preferred_element_type=F32)


def rows_of(start, size, unit=16):
    return pl.ds(pl.multiple_of(start, unit), size)


def quarter(t, q):
    return rows_of(192 * t + 48 * q, 48)


def send(src, dst, send_sem, recv_sem, device):
    copy = pltpu.make_async_remote_copy(
        src_ref=src, dst_ref=dst, send_sem=send_sem, recv_sem=recv_sem, device_id=device, device_id_type=MESH
    )
    copy.start()


class Place:
    def __init__(self):
        self.r = r = lax.axis_index("replica")
        self.s = s = lax.axis_index("shard")
        self.x, self.c, self.z, self.y = r // 2, r % 2, s // 2, s % 2
        self.rc, self.rx, self.rd = r + 1 - 2 * self.c, (r + 2) % 4, 3 - r
        self.core, self.across, self.side = (self.rc, s), (self.rx, s), (r, s + 1 - 2 * self.y)

    def peer(self, t):
        return (self.r, t)

    def line(self, k):
        return self.z + (1 - 2 * (self.z % 2)) * (k % 2) + (k // 2) * (2 - 4 * (self.z // 2))

    def mine(self, zz):
        return 2 * zz + self.y

    def theirs(self, zz):
        return 2 * zz + 1 - self.y

    def greet(self, steps):
        bar = pltpu.get_barrier_semaphore()
        devices = [self.core, self.across] + [(self.r, (self.s + k) % 8) for k in steps]
        for device in devices:
            pl.semaphore_signal(bar, inc=1, device_id=device, device_id_type=MESH)
        pl.semaphore_wait(bar, len(devices))

    def arrived(self, ref, sem, spare):
        pltpu.make_async_remote_copy(
            src_ref=ref, dst_ref=ref, send_sem=spare, recv_sem=sem, device_id=self.core, device_id_type=MESH
        ).wait_recv()

    def sent(self, ref, sem, spare):
        pltpu.make_async_remote_copy(
            src_ref=ref, dst_ref=ref, send_sem=sem, recv_sem=spare, device_id=self.core, device_id_type=MESH
        ).wait_send()


def inverse_norm(v):
    return lax.rsqrt(jnp.mean(v * v, axis=-1, keepdims=True) + eps_norm)


def gather_body(
    x_ref, cos_ref, sin_ref, allow_ref, small_ref, wq_ref, wo_ref, wg_ref, wu_ref, c_ref,
    WQ_out, WO_out, G, C, gains, queries, keys, values, probs, att, a1, mid, a2,
    WQ, WO, vg, vu, GS, CS, S, bias,
    rq, ro, rg, rc, rs, szq, syq, sdq, szo, syo, sdo, sg, sdg, scz, scy, ss, loc,
):
    p = Place()
    r, s, z = p.r, p.s, p.z
    spare = loc.at[0]
    own = rows_of(192 * s, 192)
    own_c = rows_of(128 * s, 128, 128)
    loads = (
        pltpu.make_async_copy(wq_ref, WQ.at[own], loc.at[1]),
        pltpu.make_async_copy(wo_ref, WO.at[own], loc.at[2]),
        pltpu.make_async_copy(wg_ref, vg, loc.at[3]),
        pltpu.make_async_copy(wu_ref, vu, loc.at[4]),
        pltpu.make_async_copy(c_ref, CS, loc.at[5]),
    )
    for copy in loads:
        copy.start()
    p.greet(range(1, 8))
    S[s] = small_ref[...]
    for k in range(1, 8):
        t = (s + k) % 8
        send(small_ref, S.at[s], ss.at[t], rs.at[s], p.peer(t))

    def in_plane(W, src, sz, sy, rw):
        for k in (1, 2, 3):
            zz = p.line(k)
            send(src, W.at[quarter(s, r)], sz.at[zz], rw.at[s, r], p.peer(p.mine(zz)))
        send(src, W.at[quarter(s, r)], sy.at[z], rw.at[s, r], p.side)

    in_plane(WQ, wq_ref.at[rows_of(48 * r, 48)], szq, syq, rq)
    in_plane(WO, wo_ref.at[rows_of(48 * r, 48)], szo, syo, ro)

    def share(view, t, sems, rsems):
        v = view(t, r)
        send(v, v, sems.at[t, 0], rsems.at[t, r], p.across)
        send(v, v, sems.at[t, 1], rsems.at[t, r], p.core)

    def vq(t, q):
        return WQ.at[quarter(t, q)]

    def vo(t, q):
        return WO.at[quarter(t, q)]

    def gq(t, q):
        return G.at[quarter(t, q)]

    def collect(view, sy, sd, rw):
        @pl.loop(1, 4)
        def _(k):
            zz = p.line(k)
            t = p.mine(zz)
            v = view(t, r)
            p.arrived(v, rw.at[t, r], spare)
            send(v, v, sy.at[zz], rw.at[t, r], p.side)
            share(view, t, sd, rw)

        @pl.loop(0, 4)
        def _(k):
            t = p.theirs(p.line(k))
            p.arrived(view(t, r), rw.at[t, r], spare)
            share(view, t, sd, rw)

    def relay(view, sd, rw):
        @pl.loop(1, 8)
        def _(k):
            t = (s + k) % 8
            v = view(t, p.rx)
            p.arrived(v, rw.at[t, p.rx], spare)
            send(v, v, sd.at[t, 2], rw.at[t, p.rx], p.core)

        @pl.loop(1, 8)
        def _(k):
            t = (s + k) % 8
            p.arrived(view(t, p.rc), rw.at[t, p.rc], spare)
            p.arrived(view(t, p.rd), rw.at[t, p.rd], spare)

    for copy in loads:
        copy.wait()
    zeros = jnp.zeros((192, 32), BF)
    for t in range(8):
        GS[t, :, 0:1120] = vg[:, 1120 * t : 1120 * t + 1120]
        GS[t, :, 1120:1152] = zeros
        GS[t, :, 1152:2272] = vu[:, 1120 * t : 1120 * t + 1120]
        GS[t, :, 2272:2304] = zeros
    collect(vq, syq, sdq, rq)
    for k in range(1, 8):
        t = (s + k) % 8
        send(GS.at[t, rows_of(48 * r, 48)], gq(s, r), sg.at[t], rg.at[s, r], p.peer(t))
    own_out = (
        pltpu.make_async_copy(GS.at[s], G.at[own], loc.at[1]),
        pltpu.make_async_copy(CS, C.at[own_c], loc.at[2]),
    )
    for copy in own_out:
        copy.start()

    def cot_block(t):
        return C.at[rows_of(128 * t, 128, 128)]

    def cot_on(src, t, zz, up, down):
        if up is not None:
            pl.when(up)(lambda: send(src, cot_block(t), scz.at[zz, 0], rc.at[t], p.peer(s + 2)))
        if down is not None:
            pl.when(down)(lambda: send(src, cot_block(t), scz.at[zz, 1], rc.at[t], p.peer(s - 2)))
        send(src, cot_block(t), scy.at[zz], rc.at[t], p.side)

    def cot_step(k):
        def below():
            t = s - 2 * k
            p.arrived(cot_block(t), rc.at[t], spare)
            cot_on(cot_block(t), t, z - k, z < 3, None)

        def above():
            t = s + 2 * k
            p.arrived(cot_block(t), rc.at[t], spare)
            cot_on(cot_block(t), t, z + k, None, z > 0)

        pl.when(z >= k)(below)
        pl.when(z + k <= 3)(above)

    collect(vo, syo, sdo, ro)
    cot_on(CS, s, z, z < 3, z > 0)
    @pl.loop(1, 8)
    def _(k):
        t = (s + k) % 8
        p.arrived(S.at[t], rs.at[t], spare)

    for t in range(8):
        row = S[t, 0:1, :].astype(F32)
        gains[0:1, 192 * t : 192 * t + 192] = row[:, 0:192]
        bias[0:1, 256 * t : 256 * t + 256] = row[:, 256:512]
        gains[1:2, 192 * t : 192 * t + 192] = row[:, 512:704]
    x = x_ref[...].astype(F32)
    a1[...] = (x * inverse_norm(x) * gains[0:1, :]).astype(BF)
    relay(vq, sdq, rq)
    cosine, sine = cos_ref[...], sin_ref[...]
    for j in range(4):
        co = pl.ds(512 * j, 512)
        joined = dot(a1[...], WQ[:, co]) + bias[0:1, co]
        for i in range(4):
            h = 4 * j + i
            u = joined[:, 128 * i : 128 * i + 128]
            if h < 14:
                u = u * cosine + pltpu.roll(u, 64, 1) * sine
            if h < 12:
                queries[h // 6, pl.ds(128 * (h % 6), 128), :] = (u * HEAD_DIMENSION**-0.5).astype(BF)
            elif h < 14:
                keys[h - 12] = u.astype(BF)
            else:
                values[h - 14] = u.astype(BF)
    cot_step(1)
    save = (pltpu.make_async_copy(WQ, WQ_out, loc.at[3]), pltpu.make_async_copy(WO, WO_out, loc.at[4]))
    save[0].start()
    open_to = allow_ref[...] != 0
    for g in range(2):
        scores = dot_nt(queries[g], keys[g]).reshape(6, 128, 128)
        scores = jnp.where(open_to[None], scores, -1e30)
        ex = jnp.exp(scores - jnp.max(scores, axis=-1, keepdims=True))
        soft = (ex / jnp.sum(ex, axis=-1, keepdims=True)).reshape(768, 128)
        probs[g] = soft
        out = dot(soft.astype(BF), values[g]).astype(BF)
        for i in range(6):
            att[:, pl.ds(128 * (6 * g + i), 128)] = out[128 * i : 128 * i + 128]
    relay(vo, sdo, ro)
    save[1].start()
    for j in range(3):
        co = pl.ds(512 * j, 512)
        mid[:, co] = x[:, 512 * j : 512 * j + 512] + dot(att[...], WO[:, co])
    hidden = mid[...]
    a2[...] = (hidden * inverse_norm(hidden) * gains[1:2, :]).astype(BF)

    @pl.loop(1, 8)
    def _(k):
        t = (s + k) % 8
        p.arrived(gq(t, r), rg.at[t, r], spare)
        share(gq, t, sdg, rg)

    cot_step(2)
    cot_step(3)
    relay(gq, sdg, rg)

    @pl.loop(0, 4)
    def _(zz):
        t = p.theirs(zz)
        p.arrived(cot_block(t), rc.at[t], spare)

    @pl.loop(1, 8)
    def _(k):
        t = (s + k) % 8
        p.sent(S.at[t], ss.at[t], spare)
        p.sent(gq(t, r), sg.at[t], spare)
        for d in range(3):
            p.sent(vq(t, r), sdq.at[t, d], spare)
            p.sent(vo(t, r), sdo.at[t, d], spare)
            p.sent(gq(t, r), sdg.at[t, d], spare)

    for zz in range(4):
        p.sent(vq(s, r), syq.at[zz], spare)
        p.sent(vo(s, r), syo.at[zz], spare)
        p.sent(CS, scy.at[zz], spare)

        @pl.when(zz != z)
        def _():
            p.sent(vq(s, r), szq.at[zz], spare)
            p.sent(vo(s, r), szo.at[zz], spare)

        pl.when((zz <= z) & (z < 3))(lambda: p.sent(CS, scz.at[zz, 0], spare))
        pl.when((zz >= z) & (z > 0))(lambda: p.sent(CS, scz.at[zz, 1], spare))
    for copy in own_out + save:
        copy.wait()


def gather_weights(x, cosine, sine, allowed, small, w_qkv, w_out, w_gate, w_up, cot):
    return pl.pallas_call(
        gather_body,
        out_shape=(
            shaped(1536, 2048), shaped(1536, 1536), shaped(1536, 2304), shaped(1024, 1536), shaped(8, 1536, dtype=F32),
            shaped(2, 768, 128), shaped(2, 128, 128), shaped(2, 128, 128), shaped(2, 768, 128, dtype=F32),
            shaped(128, 1536), shaped(128, 1536), shaped(128, 1536, dtype=F32), shaped(128, 1536),
        ),
        in_specs=[VMEM] * 5 + [HBM] * 5,
        out_specs=(HBM,) * 4 + (VMEM,) * 9,
        scratch_shapes=[
            low(1536, 2048), low(1536, 1536), low(192, 8960), low(192, 8960), low(8, 192, 2304), low(128, 1536),
            low(8, 16, 768), full(8, 2048),
            DMA((8, 4)), DMA((8, 4)), DMA((8, 4)), DMA((8,)), DMA((8,)),
            DMA((4,)), DMA((4,)), DMA((8, 3)), DMA((4,)), DMA((4,)), DMA((8, 3)),
            DMA((8,)), DMA((8, 3)), DMA((4, 2)), DMA((4,)), DMA((8,)), DMA((6,)),
        ],
        compiler_params=pltpu.CompilerParams(collective_id=0, has_side_effects=True, vmem_limit_bytes=56 << 20),
        name="gather_and_attend",
    )(x, cosine, sine, allowed, small, w_qkv, w_out, w_gate, w_up, cot)


def feed_body(
    n_ref, c_hbm, g_hbm, d_hbm, DS, PO_out, GQ, OD,
    vG, vD, vC, N, NT, MX, MT, H, PD, PO, YD, ZD, GD, RCd, RXd, RC, RX,
    rn, syn, szn, ryd, rzd, syd, szd, scd, rcd, sxd, rxd, sfd, rfd, scg, rcg, sxg, rxg, lq, loc,
):
    p = Place()
    r, s, c, y, z = p.r, p.s, p.c, p.y, p.z
    spare = loc.at[0]

    def block(t):
        return N.at[rows_of(128 * t, 128, 128)]

    loads = (
        pltpu.make_async_copy(n_ref, block(s), loc.at[1]),
        pltpu.make_async_copy(c_hbm, vC, loc.at[2]),
        pltpu.make_async_copy(g_hbm, vG, loc.at[3]),
        pltpu.make_async_copy(d_hbm, vD.at[0:1120], loc.at[4]),
    )
    for copy in loads:
        copy.start()
    p.greet(range(1, 8))
    send(n_ref, block(s), syn.at[z], rn.at[s], p.side)
    for k in (1, 2, 3):
        zz = p.line(k)
        send(n_ref, block(s), szn.at[zz], rn.at[s], p.peer(p.mine(zz)))
    vD[1120:1152, :] = jnp.zeros((32, 1536), BF)
    for copy in loads:
        copy.wait()

    def add_d(k):
        zz = p.line(k)
        t = p.mine(zz)
        p.arrived(YD.at[zz], ryd.at[zz], spare)
        PD[t] = (PD[t].astype(F32) + YD[zz].astype(F32)).astype(BF)

    def send_d(k):
        zz = p.line(k)
        send(PD.at[p.mine(zz)], ZD.at[z], szd.at[zz], rzd.at[z], p.peer(p.mine(zz)))

    @pl.loop(0, 4)
    def _(k):
        zz = p.line(k)

        @pl.when(k < 3)
        def _():
            zn = p.line(k + 1)
            t = p.mine(zn)
            p.arrived(block(t), rn.at[t], spare)
            send(block(t), block(t), syn.at[zn], rn.at[t], p.side)

        to = p.theirs(zz)
        p.arrived(block(to), rn.at[to], spare)
        rows = rows_of(256 * zz, 256, 256)
        X = N[rows]
        NT[:, rows] = X.T
        cot = vC[rows]
        for j in range(3):
            ga, ua = pl.ds(384 * j, 384), pl.ds(1152 + 384 * j, 384)
            gate = dot(X, vG[:, ga])
            up = dot(X, vG[:, ua])
            d_mixed = dot_nt(cot, vD[ga])
            sg = jax.nn.sigmoid(gate)
            active = gate * sg
            d_active = d_mixed * up
            MX[:, ga] = (active * up).astype(BF)
            H[rows, ga] = (d_active * sg + d_active * active * (1.0 - sg)).astype(BF)
            H[rows, ua] = (d_mixed * active).astype(BF)
        for j in range(3):
            co = pl.ds(512 * j, 512)
            part = dot_nt(H[rows], vG[co]).astype(BF)
            PD[2 * zz, :, co] = part[:128]
            PD[2 * zz + 1, :, co] = part[128:]
        send(PD.at[to], YD.at[zz], syd.at[zz], ryd.at[zz], p.side)
        for j in range(3):
            co = pl.ds(512 * j, 512)
            part = dot(MX[...], vD[:, co]).astype(BF)
            PO[2 * zz, :, co] = part[:128]
            PO[2 * zz + 1, :, co] = part[128:]
        MT[:, rows] = MX[...].T

        @pl.when(k >= 1)
        def _():
            add_d(k - 1)

        @pl.when(k >= 2)
        def _():
            send_d(k - 1)

    save = pltpu.make_async_copy(PO, PO_out, loc.at[1])
    save.start()

    def chunk(i):
        return rows_of(288 * i, 288)

    def cols(q):
        return rows_of(384 * q, 384, 128)

    def down_term(i):
        for j in range(3):
            co = pl.ds(512 * j, 512)
            GD[chunk(i), co] = dot(MT[chunk(i)], vC[:, co]).astype(BF)
        for xx in range(2):
            q = 2 * xx + 1 - c
            send(GD.at[chunk(i), cols(q)], RCd.at[xx, chunk(i)], scd.at[i, xx], rcd.at[i, xx], p.core)

    def down_chip(i):
        for xx in range(2):
            p.arrived(RCd.at[xx, chunk(i)], rcd.at[i, xx], spare)
            q = cols(2 * xx + c)
            GD[chunk(i), q] = (GD[chunk(i), q].astype(F32) + RCd[xx, chunk(i)].astype(F32)).astype(BF)
        send(GD.at[chunk(i), cols(p.rx)], RXd.at[chunk(i)], sxd.at[i], rxd.at[i], p.across)

    def down_whole(i):
        p.arrived(RXd.at[chunk(i)], rxd.at[i], spare)
        q = cols(r)
        GD[chunk(i), q] = (GD[chunk(i), q].astype(F32) + RXd[chunk(i)].astype(F32)).astype(BF)
        src, dst = GD.at[chunk(i), q], OD.at[r, chunk(i)]
        pltpu.make_async_copy(src, dst, sfd.at[i, 3]).start()
        send(src, dst, sfd.at[i, 0], rfd.at[i, r], p.across)
        send(src, dst, sfd.at[i, 1], rfd.at[i, r], p.core)

    def down_relay(i):
        v = OD.at[p.rx, chunk(i)]
        p.arrived(v, rfd.at[i, p.rx], spare)
        send(v, v, sfd.at[i, 2], rfd.at[i, p.rx], p.core)

    @pl.loop(0, 6)
    def _(i):
        pl.when(i < 4)(lambda: down_term(i))
        pl.when((i >= 1) & (i < 5))(lambda: down_chip(i - 1))
        pl.when(i >= 2)(lambda: down_whole(i - 2))

        @pl.when(i == 1)
        def _():
            add_d(3)
            send_d(3)

    def own(k):
        return (s + 1 + k) % 8

    def pair_term(k):
        t = own(k)
        rows = rows_of(192 * t, 192)
        for j in range(3):
            co = pl.ds(768 * j, 768)
            vG[rows, co] = dot(NT[rows], H[:, co]).astype(BF)
        for xx in range(2):
            send(vG.at[quarter(t, 2 * xx + 1 - c)], RC.at[t, xx], scg.at[t, xx], rcg.at[t, xx], p.core)

    def pair_chip(k):
        t = own(k)
        for xx in range(2):
            p.arrived(RC.at[t, xx], rcg.at[t, xx], spare)
            q = quarter(t, 2 * xx + c)
            vG[q] = (vG[q].astype(F32) + RC[t, xx].astype(F32)).astype(BF)
        send(vG.at[quarter(t, p.rx)], RX.at[t], sxg.at[t], rxg.at[t], p.across)

    def pair_whole(k):
        t = own(k)
        p.arrived(RX.at[t], rxg.at[t], spare)
        q = quarter(t, r)
        vG[q] = (vG[q].astype(F32) + RX[t].astype(F32)).astype(BF)
        pltpu.make_async_copy(vG.at[q], GQ.at[t], lq.at[t]).start()

    @pl.loop(0, 10)
    def _(i):
        pl.when(i < 8)(lambda: pair_term(i))
        pl.when((i >= 1) & (i < 9))(lambda: pair_chip(i - 1))
        pl.when(i >= 2)(lambda: pair_whole(i - 2))
        pl.when(i < 4)(lambda: down_relay(i))

    acc = PD[s].astype(F32)
    for k in (1, 2, 3):
        zz = p.line(k)
        p.arrived(ZD.at[zz], rzd.at[zz], spare)
        acc = acc + ZD[zz].astype(F32)
    DS[...] = acc

    @pl.loop(0, 8)
    def _(t):
        for xx in range(2):
            p.sent(RC.at[t, xx], scg.at[t, xx], spare)
        p.sent(RX.at[t], sxg.at[t], spare)
        pltpu.make_async_copy(RX.at[t], GQ.at[t], lq.at[t]).wait()

    @pl.loop(0, 4)
    def _(i):
        for q in (p.rc, p.rd):
            p.arrived(OD.at[q, chunk(i)], rfd.at[i, q], spare)
        for d in range(3):
            p.sent(OD.at[r, chunk(i)], sfd.at[i, d], spare)
        pltpu.make_async_copy(OD.at[r, chunk(i)], OD.at[r, chunk(i)], sfd.at[i, 3]).wait()
        for xx in range(2):
            p.sent(RCd.at[xx, chunk(i)], scd.at[i, xx], spare)
        p.sent(RXd.at[chunk(i)], sxd.at[i], spare)
        p.sent(block(s), syn.at[i], spare)
        p.sent(YD.at[i], syd.at[i], spare)

        @pl.when(i != z)
        def _():
            p.sent(block(s), szn.at[i], spare)
            p.sent(ZD.at[i], szd.at[i], spare)

    save.wait()


def feed_forward(n2, cot, gate_up, w_down):
    return pl.pallas_call(
        feed_body,
        out_shape=(shaped(128, 1536, dtype=F32), shaped(8, 128, 1536), shaped(8, 48, 2304), shaped(4, 1152, 384)),
        in_specs=[HBM] * 4,
        out_specs=(VMEM, HBM, HBM, HBM),
        scratch_shapes=[
            low(1536, 2304), low(1152, 1536), low(1024, 1536), low(1024, 1536), low(1536, 1024), low(256, 1152),
            low(1152, 1024), low(1024, 2304), low(8, 128, 1536), low(8, 128, 1536), low(4, 128, 1536), low(4, 128, 1536),
            low(1152, 1536), low(2, 1152, 384), low(1152, 384), low(8, 2, 48, 2304), low(8, 48, 2304),
            DMA((8,)), DMA((4,)), DMA((4,)), DMA((4,)), DMA((4,)), DMA((4,)), DMA((4,)),
            DMA((4, 2)), DMA((4, 2)), DMA((4,)), DMA((4,)), DMA((4, 4)), DMA((4, 4)),
            DMA((8, 2)), DMA((8, 2)), DMA((8,)), DMA((8,)), DMA((8,)), DMA((5,)),
        ],
        compiler_params=pltpu.CompilerParams(collective_id=1, has_side_effects=True, vmem_limit_bytes=62 << 20),
        name="feed_forward",
    )(n2, cot, gate_up, w_down)


def attend_back_body(
    ds_ref, mid_ref, x_ref, cot_ref, gains, cos_ref, sin_ref, queries, keys, values, probs, att, a1,
    wq_ref, wo_ref, po_ref, gq_ref,
    out_ref, gtok_ref, OG, OWq, OWo,
    vQ, vO, PO, YO, ZO, own_g, dmid, DB, dA, dj, AT, SM, RCq, RXq, Yq, Zq, RCo, Yo, Zo, RXo,
    sa, ra, sf, syo, ryo, szo, rzo, scq, rcq, sxq, rxq, syq, ryq, szq, rzq, sfq, rfq,
    sco, rco, syw, ryw, szw, rzw, sfo, rfo, loc,
):
    p = Place()
    r, s, c, y, z = p.r, p.s, p.c, p.y, p.z
    spare = loc.at[0]
    loads = (
        pltpu.make_async_copy(wo_ref, vO, loc.at[1]),
        pltpu.make_async_copy(wq_ref, vQ.at[:, 0:2048], loc.at[2]),
        pltpu.make_async_copy(po_ref, PO, loc.at[3]),
        pltpu.make_async_copy(gq_ref.at[s], own_g, loc.at[4]),
    )
    for copy in loads:
        copy.start()
    p.greet(range(1, 8))
    for k in range(1, 8):
        t = (s + k) % 8
        send(gq_ref.at[t], OG.at[r, s], sa.at[t], ra.at[s, r], p.peer(t))
    for k in range(4):
        zz = p.line(3 - k)
        send(po_ref.at[p.theirs(zz)], YO.at[zz], syo.at[zz], ryo.at[zz], p.side)

    def share(t):
        v = OG.at[r, t]
        send(v, v, sf.at[t, 0], ra.at[t, r], p.across)
        send(v, v, sf.at[t, 1], ra.at[t, r], p.core)

    def back(w):
        return w * cos_ref[...] - pltpu.roll(w, 64, 1) * sin_ref[...]

    dn, hidden = ds_ref[...], mid_ref[...]
    rstd = inverse_norm(hidden)
    unit = hidden * rstd
    gain_ffn_grad = jnp.sum(dn * unit, axis=0, keepdims=True)
    e = dn * gains[1:2, :]
    dm = cot_ref[...].astype(F32) + rstd * (e - unit * jnp.mean(e * unit, axis=-1, keepdims=True))
    dmid[...] = dm
    DB[...] = dm.astype(BF)
    AT[...] = att[...].T
    for copy in loads:
        copy.wait()
    keep = pltpu.make_async_copy(own_g, OG.at[r, s], loc.at[4])
    keep.start()
    for j in range(3):
        part = dot_nt(DB[...], vO[pl.ds(512 * j, 512)]).astype(BF)
        for i in range(4):
            h = 4 * j + i
            dA[h // 6, pl.ds(128 * (h % 6), 128), :] = part[:, 128 * i : 128 * i + 128]

    def own(k):
        return 2 * p.line(3 - k % 4) + (1 - y + (k // 4) * (2 * y - 1))

    for j in range(3):
        co = pl.ds(512 * j, 512)
        vO[:, co] = dot(AT[...], DB[:, co]).astype(BF)

    @pl.loop(0, 8)
    def _(k):
        t = own(k)
        for xx in range(2):
            send(vO.at[quarter(t, 2 * xx + 1 - c)], RCo.at[t, xx], sco.at[t, xx], rco.at[t, xx], p.core)

    def heads(g):
        grad, soft = dA[g], probs[g]
        d_probs = dot_nt(grad, values[g])
        d_scores = (soft * (d_probs - jnp.sum(soft * d_probs, axis=-1, keepdims=True))).astype(BF)
        d_values = dot(soft.astype(BF).T, grad)
        d_queries = dot(d_scores, keys[g]) * HEAD_DIMENSION**-0.5
        d_keys = dot(d_scores.T, queries[g])
        for i in range(6):
            dj[:, pl.ds(128 * (6 * g + i), 128)] = back(d_queries[128 * i : 128 * i + 128]).astype(BF)
        dj[:, pl.ds(128 * (12 + g), 128)] = back(d_keys).astype(BF)
        dj[:, pl.ds(128 * (14 + g), 128)] = d_values.astype(BF)

    heads(0)

    @pl.loop(0, 8)
    def _(k):
        t = own(k)
        for xx in range(2):
            p.arrived(RCo.at[t, xx], rco.at[t, xx], spare)
            q = quarter(t, 2 * xx + c)
            vO[q] = (vO[q].astype(F32) + RCo[t, xx].astype(F32)).astype(BF)

            @pl.when(k < 4)
            def _():
                send(vO.at[q], Yo.at[t // 2, xx], syw.at[t // 2, xx], ryw.at[t // 2, xx], p.side)

    heads(1)
    joined_grad = dj[...]
    bias_grad = jnp.sum(joined_grad.astype(F32), axis=0, keepdims=True)
    x = x_ref[...].astype(F32)
    rstd = inverse_norm(x)
    unit = x * rstd
    dn1 = jnp.concatenate(
        [dot_nt(joined_grad, vQ[pl.ds(512 * j, 512), 0:2048]) for j in range(3)], axis=1
    )
    gain_attn_grad = jnp.sum(dn1 * unit, axis=0, keepdims=True)
    e = dn1 * gains[0:1, :]
    gtok_ref[...] = (
        dmid[...] + rstd * (e - unit * jnp.mean(e * unit, axis=-1, keepdims=True))
    ).astype(BF)
    SM[...] = jnp.zeros_like(SM)
    for t in range(8):
        SM[t, 0:1, :] = gain_attn_grad[:, 192 * t : 192 * t + 128]
        SM[t, 1:2, 0:64] = gain_attn_grad[:, 192 * t + 128 : 192 * t + 192]
        SM[t, 2:3, :] = bias_grad[:, 256 * t : 256 * t + 128]
        SM[t, 3:4, :] = bias_grad[:, 256 * t + 128 : 256 * t + 256]
        SM[t, 4:5, :] = gain_ffn_grad[:, 192 * t : 192 * t + 128]
        SM[t, 5:6, 0:64] = gain_ffn_grad[:, 192 * t + 128 : 192 * t + 192]
    AT[...] = a1[...].T

    @pl.loop(0, 8)
    def _(k):
        t = own(k)
        rows = rows_of(192 * t, 192)
        for j in range(2):
            co = pl.ds(1024 * j, 1024)
            vQ[rows, co] = dot(AT[rows], dj[:, co]).astype(BF)
        vQ[rows, 2048:2176] = jnp.zeros((192, 128), BF)
        vQ[rows_of(192 * t, 16), 2048:2176] = SM[t].astype(BF)
        for xx in range(2):
            send(vQ.at[quarter(t, 2 * xx + 1 - c)], RCq.at[t, xx], scq.at[t, xx], rcq.at[t, xx], p.core)

    def q_chip(k):
        t = own(k)
        for xx in range(2):
            p.arrived(RCq.at[t, xx], rcq.at[t, xx], spare)
            q = quarter(t, 2 * xx + c)
            vQ[q] = (vQ[q].astype(F32) + RCq[t, xx].astype(F32)).astype(BF)
        send(vQ.at[quarter(t, p.rx)], RXq.at[t], sxq.at[t], rxq.at[t], p.across)

    def q_whole(k):
        t = own(k)
        p.arrived(RXq.at[t], rxq.at[t], spare)
        q = quarter(t, r)
        vQ[q] = (vQ[q].astype(F32) + RXq[t].astype(F32)).astype(BF)

        @pl.when(k < 4)
        def _():
            send(vQ.at[q], Yq.at[t // 2], syq.at[t // 2], ryq.at[t // 2], p.side)

        @pl.when(k >= 4)
        def _():
            p.arrived(Yq.at[t // 2], ryq.at[t // 2], spare)
            vQ[q] = (vQ[q].astype(F32) + Yq[t // 2].astype(F32)).astype(BF)

        @pl.when((k >= 4) & (k < 7))
        def _():
            send(vQ.at[q], Zq.at[z], szq.at[t // 2], rzq.at[z], p.peer(t))

    def out_line(k):
        zz = p.line(3 - k)
        t = p.mine(zz)
        p.arrived(YO.at[zz], ryo.at[zz], spare)
        PO[t] = (PO[t].astype(F32) + YO[zz].astype(F32)).astype(BF)

        @pl.when(k < 3)
        def _():
            send(PO.at[t], ZO.at[z], szo.at[zz], rzo.at[z], p.peer(t))

    def w_line(k):
        zz = p.line(3 - k)
        t = p.mine(zz)
        for xx in range(2):
            p.arrived(Yo.at[zz, xx], ryw.at[zz, xx], spare)
            q = quarter(t, 2 * xx + c)
            vO[q] = (vO[q].astype(F32) + Yo[zz, xx].astype(F32)).astype(BF)

            @pl.when(k < 3)
            def _():
                send(vO.at[q], Zo.at[z, xx], szw.at[zz, xx], rzw.at[z, xx], p.peer(t))

    @pl.loop(0, 8)
    def _(k):
        q_chip(k)
    share_own = pltpu.make_async_copy(own_g, OG.at[r, s], loc.at[4])
    share_own.wait()
    share(s)

    @pl.loop(1, 8)
    def _(k):
        t = (s + 8 - k) % 8
        p.arrived(OG.at[r, t], ra.at[t, r], spare)
        share(t)

    @pl.loop(0, 4)
    def _(k):
        out_line(k)
        w_line(k)

    @pl.loop(0, 8)
    def _(k):
        q_whole(k)
    acc = PO[s].astype(F32) + mid_ref[...]
    for k in (1, 2, 3):
        zz = p.line(k)
        p.arrived(ZO.at[zz], rzo.at[zz], spare)
        acc = acc + ZO[zz].astype(F32)
    out_ref[...] = acc.astype(BF)
    for xx in range(2):
        q = quarter(s, 2 * xx + c)
        acc = vO[q].astype(F32)
        for k in (1, 2, 3):
            zz = p.line(k)
            p.arrived(Zo.at[zz, xx], rzw.at[zz, xx], spare)
            acc = acc + Zo[zz, xx].astype(F32)
        vO[q] = acc.astype(BF)
    send(vO.at[quarter(s, p.rx)], RXo, sfo.at[3], rfo.at[4], p.across)
    acc = vQ[quarter(s, r)].astype(F32)
    for k in (1, 2, 3):
        zz = p.line(k)
        p.arrived(Zq.at[zz], rzq.at[zz], spare)
        acc = acc + Zq[zz].astype(F32)
    OWq[r] = acc.astype(BF)

    def spread(O, sems, rsems):
        send(O.at[r], O.at[r], sems.at[0], rsems.at[r], p.across)
        send(O.at[r], O.at[r], sems.at[1], rsems.at[r], p.core)

    def pass_on(O, sems, rsems):
        v = O.at[p.rx]
        p.arrived(v, rsems.at[p.rx], spare)
        send(v, v, sems.at[2], rsems.at[p.rx], p.core)

    spread(OWq, sfq, rfq)
    p.arrived(RXo, rfo.at[4], spare)
    OWo[r] = (vO[quarter(s, r)].astype(F32) + RXo[...].astype(F32)).astype(BF)
    spread(OWo, sfo, rfo)

    @pl.loop(0, 8)
    def _(k):
        t = (s + 8 - k) % 8
        v = OG.at[p.rx, t]
        p.arrived(v, ra.at[t, p.rx], spare)
        send(v, v, sf.at[t, 2], ra.at[t, p.rx], p.core)

    pass_on(OWq, sfq, rfq)
    pass_on(OWo, sfo, rfo)
    for q in (p.rc, p.rd):
        p.arrived(OWq.at[q], rfq.at[q], spare)
        p.arrived(OWo.at[q], rfo.at[q], spare)
    for d in range(3):
        p.sent(OWq.at[r], sfq.at[d], spare)
        p.sent(OWo.at[r], sfo.at[d], spare)
    p.sent(RXo, sfo.at[3], spare)

    @pl.loop(0, 8)
    def _(t):
        for q in (p.rc, p.rd):
            p.arrived(OG.at[q, t], ra.at[t, q], spare)
        for d in range(3):
            p.sent(OG.at[r, t], sf.at[t, d], spare)
        for xx in range(2):
            p.sent(RCq.at[t, xx], scq.at[t, xx], spare)
            p.sent(RCo.at[t, xx], sco.at[t, xx], spare)
        p.sent(RXq.at[t], sxq.at[t], spare)

        @pl.when(t != s)
        def _():
            p.sent(OG.at[r, s], sa.at[t], spare)

    @pl.loop(0, 4)
    def _(i):
        p.sent(YO.at[i], syo.at[i], spare)
        p.sent(Yq.at[i], syq.at[i], spare)
        for xx in range(2):
            p.sent(Yo.at[i, xx], syw.at[i, xx], spare)

        @pl.when(i != z)
        def _():
            p.sent(ZO.at[i], szo.at[i], spare)
            p.sent(Zq.at[i], szq.at[i], spare)
            for xx in range(2):
                p.sent(Zo.at[i, xx], szw.at[i, xx], spare)


def attend_back(*args):
    return pl.pallas_call(
        attend_back_body,
        out_shape=(
            shaped(128, 1536), shaped(128, 1536), shaped(4, 8, 48, 2304), shaped(4, 48, 2176), shaped(4, 48, 1536),
        ),
        in_specs=[VMEM] * 13 + [HBM] * 4,
        out_specs=(VMEM, VMEM, HBM, VMEM, VMEM),
        scratch_shapes=[
            low(1536, 2176), low(1536, 1536), low(8, 128, 1536), low(4, 128, 1536), low(4, 128, 1536), low(48, 2304),
            full(128, 1536), low(128, 1536), low(2, 768, 128), low(128, 2048), low(1536, 128), full(8, 16, 128),
            low(8, 2, 48, 2176), low(8, 48, 2176), low(4, 48, 2176), low(4, 48, 2176),
            low(8, 2, 48, 1536), low(4, 2, 48, 1536), low(4, 2, 48, 1536), low(48, 1536),
            DMA((8,)), DMA((8, 4)), DMA((8, 3)), DMA((4,)), DMA((4,)), DMA((4,)), DMA((4,)),
            DMA((8, 2)), DMA((8, 2)), DMA((8,)), DMA((8,)), DMA((4,)), DMA((4,)), DMA((4,)), DMA((4,)), DMA((3,)), DMA((4,)),
            DMA((8, 2)), DMA((8, 2)), DMA((4, 2)), DMA((4, 2)), DMA((4, 2)), DMA((4, 2)), DMA((4,)), DMA((5,)), DMA((5,)),
        ],
        compiler_params=pltpu.CompilerParams(collective_id=2, has_side_effects=True, vmem_limit_bytes=58 << 20),
        name="attend_back",
    )(*args)


def widen_body(g_ref, d_ref, q_ref, o_ref, gate, up, down, qkv, out):
    for t in range(8):
        gate[:, 1120 * t : 1120 * t + 1120] = g_ref[0, t, :, 0:1120].astype(F32)
        up[:, 1120 * t : 1120 * t + 1120] = g_ref[0, t, :, 1152:2272].astype(F32)
    down[...] = d_ref[0, 0:1120, :].astype(F32)
    qkv[...] = q_ref[0, :, 0:2048].astype(F32)
    out[...] = o_ref[0].astype(F32)


def widen(g, d, q, o):
    return pl.pallas_call(
        widen_body,
        grid=(4,),
        out_shape=(
            shaped(192, 8960, dtype=F32), shaped(192, 8960, dtype=F32), shaped(1120, 1536, dtype=F32),
            shaped(192, 2048, dtype=F32), shaped(192, 1536, dtype=F32),
        ),
        in_specs=[
            pl.BlockSpec((1, 8, 48, 2304), lambda i: (i, 0, 0, 0)),
            pl.BlockSpec((1, 1152, 384), lambda i: (i, 0, 0)),
            pl.BlockSpec((1, 48, 2176), lambda i: (i, 0, 0)),
            pl.BlockSpec((1, 48, 1536), lambda i: (i, 0, 0)),
        ],
        out_specs=(
            pl.BlockSpec((48, 8960), lambda i: (i, 0)),
            pl.BlockSpec((48, 8960), lambda i: (i, 0)),
            pl.BlockSpec((1120, 384), lambda i: (0, i)),
            pl.BlockSpec((48, 2048), lambda i: (i, 0)),
            pl.BlockSpec((48, 1536), lambda i: (i, 0)),
        ),
        compiler_params=pltpu.CompilerParams(vmem_limit_bytes=48 << 20),
        name="widen",
    )(g, d, q, o)


def shards_eight(
    tokens, segments, gain_attn, w_qkv, b_qkv, w_out, gain_ffn, w_gate, w_up, w_down, cotangent
):
    cosine, sine, allowed = tables(segments[0], HEAD_DIMENSION)
    half = HEAD_DIMENSION // 2
    sine = jnp.concatenate([-sine[:, :half], sine[:, half:]], axis=-1)
    gap = jnp.zeros((64,), BF)
    small = jnp.concatenate([gain_attn, gap, b_qkv, gain_ffn, gap])[None]
    small = jnp.pad(small, ((0, 15), (0, 0)))
    x, cot = tokens[0], cotangent[0]
    WQ, WO, G, C, gains, queries, keys, values, probs, att, a1, mid, a2 = gather_weights(
        x, cosine, sine, allowed, small, w_qkv, w_out, w_gate, w_up, cot
    )
    ds, parts, gate_up, down = feed_forward(a2, C, G, w_down)
    out, grad_tokens, gate_up, qkv, o = attend_back(
        ds, mid, x, cot, gains, cosine, sine, queries, keys, values, probs, att, a1, WQ, WO, parts, gate_up
    )
    gate, up, down, qkv_rows, out_rows = widen(gate_up, down, qkv, o)
    small = qkv[0, 0:6, 2048:].astype(F32).reshape(768)
    return (
        out[None], grad_tokens[None], small[0:192], qkv_rows, small[256:512], out_rows, small[512:704], gate, up, down,
    )


def solution(mesh):
    placed = (
        P(("replica", "shard"), None, None),
        P(("replica", "shard"), None),
        P("shard"),
        P("shard", None),
        P("shard"),
        P("shard", None),
        P("shard"),
        P("shard", None),
        P("shard", None),
        P("shard", None),
        P(("replica", "shard"), None, None),
    )
    return jax.shard_map(
        shards_eight if (mesh.shape["replica"], mesh.shape["shard"]) == (4, 8) else shards,
        mesh=mesh,
        in_specs=placed,
        out_specs=(
            P(("replica", "shard"), None, None),
            P(("replica", "shard"), None, None),
            P("shard"),
            P("shard", None),
            P("shard"),
            P("shard", None),
            P("shard"),
            P("shard", None),
            P("shard", None),
            P("shard", None),
        ),
        check_vma=False,
    )
```

```python
import math

import jax
import jax.numpy as jnp
from jax import lax
from jax.experimental import pallas as pl
from jax.experimental.pallas import tpu as pltpu
from jax.sharding import PartitionSpec as P

QUERY_HEADS = 12
KEY_VALUE_HEADS = 2
HEAD_DIMENSION = 128


eps_norm = 1e-06
rope_base = 1000000.0


def tables(segment_ids, head_size):
    token_length = segment_ids.shape[-1]
    row_index = jnp.arange(token_length, dtype=jnp.int32)
    earlier = jnp.sum(
        (segment_ids[..., None, :] < segment_ids[..., :, None]).astype(jnp.int32),
        axis=-1,
        dtype=jnp.int32,
    )
    positions = (row_index - earlier).astype(jnp.float32)
    frequencies = jnp.exp(
        jnp.arange(head_size // 2, dtype=jnp.float32) * (-2.0 * math.log(rope_base) / head_size)
    )
    angles = positions[..., None] * frequencies
    cosine = jnp.concatenate([jnp.cos(angles), jnp.cos(angles)], axis=-1)
    sine_vals = jnp.concatenate([jnp.sin(angles), jnp.sin(angles)], axis=-1)
    allowed = (
        (segment_ids[..., None, :] == segment_ids[..., :, None])
        & (row_index[None, :] <= row_index[:, None])
    ).astype(jnp.int32)
    return (cosine, sine_vals, allowed)


def apply_rotation(values, cosine, sine_vals):
    halfway = values.shape[-1] // 2
    turned = jnp.concatenate([-values[..., halfway:], values[..., :halfway]], axis=-1)
    return values * cosine + turned * sine_vals


def rotate_back(values, cosine, sine_vals):
    halfway = values.shape[-1] // 2
    shifted = values * sine_vals
    return values * cosine + jnp.concatenate(
        [shifted[..., halfway:], -shifted[..., :halfway]], axis=-1
    )


def norm_forward(hidden, gain_vec):
    rstd_rows = lax.rsqrt(jnp.mean(hidden * hidden, axis=-1, keepdims=True) + eps_norm)
    unit_rows = hidden * rstd_rows
    return (unit_rows * gain_vec, unit_rows, rstd_rows)


def norm_backward(grad_in, gain_vec, unit_rows, rstd_rows):
    inner_grad = grad_in * gain_vec
    return rstd_rows * (
        inner_grad - unit_rows * jnp.mean(inner_grad * unit_rows, axis=-1, keepdims=True)
    )


def column_term(left_side, right_side):
    return jnp.einsum("lf,ld->fd", left_side, right_side, preferred_element_type=jnp.float32)


def to_columns(rows):
    ranks = lax.axis_size("shard")
    depth, width = rows.shape
    split = rows.reshape(depth, ranks, width // ranks).transpose(1, 0, 2)
    return lax.all_to_all(split, "shard", 0, 0, tiled=True).reshape(ranks * depth, width // ranks)


def to_rows(columns):
    ranks, copies = lax.axis_size("shard"), lax.axis_size("replica")
    depth, width = columns.shape
    depth = depth // ranks
    parts = columns.reshape(ranks, copies, depth // copies, width)
    part = lax.psum_scatter(parts, "replica", scatter_dimension=1, tiled=False)
    part = lax.all_to_all(part, "shard", 0, 0, tiled=True)
    part = part.transpose(1, 0, 2).reshape(depth // copies, ranks * width)
    return lax.all_gather(part, "replica", axis=0, tiled=True)


def shards(
    tokens, segments, gain_attn, w_qkv, b_qkv, w_out, gain_ffn, w_gate, w_up, w_down, cotangent
):
    heads_per_group = QUERY_HEADS // KEY_VALUE_HEADS
    head_dimension = QUERY_HEADS * HEAD_DIMENSION
    key_value_limit = head_dimension + KEY_VALUE_HEADS * HEAD_DIMENSION
    logit_scale = HEAD_DIMENSION ** (-0.5)
    token_length = tokens.shape[1]
    full_gain_attn, full_qkv, full_bias, full_out, full_gain_ffn = (
        lax.all_gather(gain_attn, "shard", axis=0, tiled=True),
        lax.all_gather(w_qkv, "shard", axis=0, tiled=True),
        lax.all_gather(b_qkv, "shard", axis=0, tiled=True),
        lax.all_gather(w_out, "shard", axis=0, tiled=True),
        lax.all_gather(gain_ffn, "shard", axis=0, tiled=True),
    )
    gate_columns = to_columns(w_gate)
    up_columns = to_columns(w_up)
    all_cot = lax.all_gather(cotangent[0], "shard", axis=0, tiled=True)
    gain_first = full_gain_attn.astype(jnp.float32)
    gain_second = full_gain_ffn.astype(jnp.float32)
    cosine, sine_vals, allowed = tables(segments[0], HEAD_DIMENSION)
    cosine_per_head = cosine[:, None, :]
    sine_per_head = sine_vals[:, None, :]
    inputs = tokens[0].astype(jnp.float32)
    normed_first, unit_first, rstd_first = norm_forward(inputs, gain_first)
    acts_first = normed_first.astype(jnp.bfloat16)
    joined_projection = jnp.dot(
        acts_first, full_qkv, preferred_element_type=jnp.float32
    ) + full_bias.astype(jnp.float32)
    query_rows = apply_rotation(
        joined_projection[:, :head_dimension].reshape(token_length, QUERY_HEADS, HEAD_DIMENSION),
        cosine_per_head,
        sine_per_head,
    )
    query_reduced = (
        (query_rows * logit_scale)
        .astype(jnp.bfloat16)
        .reshape(token_length, KEY_VALUE_HEADS, heads_per_group, HEAD_DIMENSION)
    )
    k_low = apply_rotation(
        joined_projection[:, head_dimension:key_value_limit].reshape(
            token_length, KEY_VALUE_HEADS, HEAD_DIMENSION
        ),
        cosine_per_head,
        sine_per_head,
    ).astype(jnp.bfloat16)
    value_reduced = (
        joined_projection[:, key_value_limit:]
        .reshape(token_length, KEY_VALUE_HEADS, HEAD_DIMENSION)
        .astype(jnp.bfloat16)
    )
    scores = jnp.einsum("ikrd,jkd->krij", query_reduced, k_low, preferred_element_type=jnp.float32)
    scores = jnp.where(allowed != 0, scores, -1e30)
    largest = jnp.max(scores, axis=-1, keepdims=True)
    exponents = jnp.exp(scores - largest)
    soft_probs = exponents / jnp.sum(exponents, axis=-1, keepdims=True)
    soft_low = soft_probs.astype(jnp.bfloat16)
    attended = jnp.einsum(
        "krij,jkd->ikrd", soft_low, value_reduced, preferred_element_type=jnp.float32
    )
    attended = attended.reshape(token_length, head_dimension).astype(jnp.bfloat16)
    hidden_mid = inputs + jnp.dot(attended, full_out, preferred_element_type=jnp.float32)
    normed_second, unit_second, rstd_second = norm_forward(hidden_mid, gain_second)
    acts_second = normed_second.astype(jnp.bfloat16)
    all_acts = lax.all_gather(acts_second, "shard", axis=0, tiled=True)
    gate_vals = jnp.dot(all_acts, gate_columns, preferred_element_type=jnp.float32)
    up_vals = jnp.dot(all_acts, up_columns, preferred_element_type=jnp.float32)
    sigmoid_gate = jax.nn.sigmoid(gate_vals)
    active = gate_vals * sigmoid_gate
    mixed_hidden = (active * up_vals).astype(jnp.bfloat16)
    d_mixed = jnp.einsum("ld,fd->lf", all_cot, w_down, preferred_element_type=jnp.float32)
    d_active = d_mixed * up_vals
    d_gate = (
        d_active * sigmoid_gate + d_active * gate_vals * sigmoid_gate * (1.0 - sigmoid_gate)
    ).astype(jnp.bfloat16)
    d_up = (d_mixed * active).astype(jnp.bfloat16)
    d_normed_part = jnp.einsum("lf,df->ld", d_gate, gate_columns, preferred_element_type=jnp.float32)
    d_normed_part = d_normed_part + jnp.einsum(
        "lf,df->ld", d_up, up_columns, preferred_element_type=jnp.float32
    )
    d_normed_second = lax.psum_scatter(
        d_normed_part.astype(jnp.bfloat16), "shard", scatter_dimension=0, tiled=True
    ).astype(jnp.float32)
    down_part = jnp.dot(mixed_hidden, w_down, preferred_element_type=jnp.float32)
    result = (
        hidden_mid
        + lax.psum_scatter(
            down_part.astype(jnp.bfloat16), "shard", scatter_dimension=0, tiled=True
        ).astype(jnp.float32)
    ).astype(jnp.bfloat16)
    grad_out = cotangent[0]
    down_grad = column_term(mixed_hidden, all_cot).astype(jnp.bfloat16)
    gate_grad = to_rows(column_term(all_acts, d_gate).astype(jnp.bfloat16))
    up_grad = to_rows(column_term(all_acts, d_up).astype(jnp.bfloat16))
    gain_second_grad = jnp.sum(d_normed_second * unit_second, axis=0)
    d_hidden_mid = grad_out.astype(jnp.float32) + norm_backward(
        d_normed_second, gain_second, unit_second, rstd_second
    )
    d_branch = d_hidden_mid.astype(jnp.bfloat16)
    out_grad_term = jnp.einsum("le,ld->ed", attended, d_branch, preferred_element_type=jnp.float32)
    attended_gradient = jnp.einsum(
        "ld,ed->le", d_branch, full_out, preferred_element_type=jnp.float32
    )
    attended_gradient = attended_gradient.astype(jnp.bfloat16).reshape(
        token_length, KEY_VALUE_HEADS, heads_per_group, HEAD_DIMENSION
    )
    d_probs = jnp.einsum(
        "ikrd,jkd->krij", attended_gradient, value_reduced, preferred_element_type=jnp.float32
    )
    value_gradient = jnp.einsum(
        "krij,ikrd->jkd", soft_low, attended_gradient, preferred_element_type=jnp.float32
    )
    d_scores = soft_probs * (d_probs - jnp.sum(soft_probs * d_probs, axis=-1, keepdims=True))
    d_scores_low = d_scores.astype(jnp.bfloat16)
    d_queries = jnp.einsum(
        "krij,jkd->ikrd", d_scores_low, k_low, preferred_element_type=jnp.float32
    )
    d_queries = rotate_back(
        d_queries.reshape(token_length, QUERY_HEADS, HEAD_DIMENSION) * logit_scale,
        cosine_per_head,
        sine_per_head,
    )
    key_gradient = jnp.einsum(
        "krij,ikrd->jkd", d_scores_low, query_reduced, preferred_element_type=jnp.float32
    )
    key_gradient = rotate_back(key_gradient, cosine_per_head, sine_per_head)
    d_joined = jnp.concatenate(
        [
            d_queries.reshape(token_length, head_dimension),
            key_gradient.reshape(token_length, KEY_VALUE_HEADS * HEAD_DIMENSION),
            value_gradient.reshape(token_length, KEY_VALUE_HEADS * HEAD_DIMENSION),
        ],
        axis=1,
    ).astype(jnp.bfloat16)
    bias_grad_term = jnp.sum(d_joined.astype(jnp.float32), axis=0)
    qkv_grad_term = jnp.einsum(
        "ld,le->de", acts_first, d_joined, preferred_element_type=jnp.float32
    )
    d_normed_first = jnp.einsum("le,de->ld", d_joined, full_qkv, preferred_element_type=jnp.float32)
    gain_first_grad = jnp.sum(d_normed_first * unit_first, axis=0)
    d_inputs = d_hidden_mid + norm_backward(d_normed_first, gain_first, unit_first, rstd_first)
    owned = (
        lax.psum_scatter(
            gain_first_grad.astype(jnp.bfloat16), "shard", scatter_dimension=0, tiled=True
        ).astype(jnp.float32),
        lax.psum_scatter(
            qkv_grad_term.astype(jnp.bfloat16), "shard", scatter_dimension=0, tiled=True
        ).astype(jnp.float32),
        lax.psum_scatter(
            bias_grad_term.astype(jnp.bfloat16), "shard", scatter_dimension=0, tiled=True
        ).astype(jnp.float32),
        lax.psum_scatter(
            out_grad_term.astype(jnp.bfloat16), "shard", scatter_dimension=0, tiled=True
        ).astype(jnp.float32),
        lax.psum_scatter(
            gain_second_grad.astype(jnp.bfloat16), "shard", scatter_dimension=0, tiled=True
        ).astype(jnp.float32),
    )
    summed = (
        lax.psum(owned[0].astype(jnp.bfloat16), "replica").astype(jnp.float32),
        lax.psum(owned[1].astype(jnp.bfloat16), "replica").astype(jnp.float32),
        lax.psum(owned[2].astype(jnp.bfloat16), "replica").astype(jnp.float32),
        lax.psum(owned[3].astype(jnp.bfloat16), "replica").astype(jnp.float32),
        lax.psum(owned[4].astype(jnp.bfloat16), "replica").astype(jnp.float32),
        gate_grad.astype(jnp.float32),
        up_grad.astype(jnp.float32),
        lax.psum(down_grad, "replica").astype(jnp.float32),
    )
    return (
        result[None],
        d_inputs.astype(jnp.bfloat16)[None],
        summed[0],
        summed[1],
        summed[2],
        summed[3],
        summed[4],
        summed[5],
        summed[6],
        summed[7],
    )


MESH = pl.DeviceIdType.MESH
BF, F32 = jnp.bfloat16, jnp.float32
HBM = pl.BlockSpec(memory_space=pl.ANY)
VMEM = pl.BlockSpec(memory_space=pltpu.VMEM)
DMA = pltpu.SemaphoreType.DMA


def shaped(*shape, dtype=BF):
    return jax.ShapeDtypeStruct(shape, dtype)


def low(*shape):
    return pltpu.VMEM(shape, BF)


def full(*shape):
    return pltpu.VMEM(shape, F32)


def dot(a, b):
    return lax.dot_general(a, b, (((1,), (0,)), ((), ())), preferred_element_type=F32)


def dot_nt(a, b):
    return lax.dot_general(a, b, (((1,), (1,)), ((), ())), preferred_element_type=F32)


def rows_of(start, size, unit=16):
    return pl.ds(pl.multiple_of(start, unit), size)


def quarter(t, q):
    return rows_of(192 * t + 48 * q, 48)


def send(src, dst, send_sem, recv_sem, device):
    copy = pltpu.make_async_remote_copy(
        src_ref=src, dst_ref=dst, send_sem=send_sem, recv_sem=recv_sem, device_id=device, device_id_type=MESH
    )
    copy.start()


class Place:
    def __init__(self):
        self.r = r = lax.axis_index("replica")
        self.s = s = lax.axis_index("shard")
        self.x, self.c, self.z, self.y = r // 2, r % 2, s // 2, s % 2
        self.rc, self.rx, self.rd = r + 1 - 2 * self.c, (r + 2) % 4, 3 - r
        self.core, self.across, self.side = (self.rc, s), (self.rx, s), (r, s + 1 - 2 * self.y)

    def peer(self, t):
        return (self.r, t)

    def line(self, k):
        near = self.z + (1 - 2 * (self.z % 2)) * (k % 2)
        far = k + (self.z // 2) * (3 - 2 * k)
        return (1 - k // 2) * near + (k // 2) * far

    def onward(self, zz, copy):
        pl.when((zz <= self.z) & (self.z < 3))(lambda: copy(0, self.peer(self.s + 2)))
        pl.when((zz >= self.z) & (self.z > 0))(lambda: copy(1, self.peer(self.s - 2)))

    def went_onward(self, zz, wait):
        pl.when((zz <= self.z) & (self.z < 3))(lambda: wait(0))
        pl.when((zz >= self.z) & (self.z > 0))(lambda: wait(1))

    def reduce_step(self, zz, add, hand):
        pl.when((zz >= self.z) & (self.z > 0))(lambda: add(zz))
        pl.when((zz < self.z) & (self.z < 3))(lambda: add(zz))
        pl.when((zz == self.z) & (self.z < 3))(lambda: add(4))
        pl.when(zz > self.z)(lambda: hand(zz, self.peer(self.s + 2)))
        pl.when(zz < self.z - 1)(lambda: hand(zz, self.peer(self.s - 2)))
        pl.when(zz == self.z - 1)(lambda: hand(4, self.peer(self.s - 2)))

    def mine(self, zz):
        return 2 * zz + self.y

    def theirs(self, zz):
        return 2 * zz + 1 - self.y

    def greet(self, steps):
        bar = pltpu.get_barrier_semaphore()
        devices = [self.core, self.across] + [(self.r, (self.s + k) % 8) for k in steps]
        for device in devices:
            pl.semaphore_signal(bar, inc=1, device_id=device, device_id_type=MESH)
        pl.semaphore_wait(bar, len(devices))

    def arrived(self, ref, sem, spare):
        pltpu.make_async_remote_copy(
            src_ref=ref, dst_ref=ref, send_sem=spare, recv_sem=sem, device_id=self.core, device_id_type=MESH
        ).wait_recv()

    def sent(self, ref, sem, spare):
        pltpu.make_async_remote_copy(
            src_ref=ref, dst_ref=ref, send_sem=sem, recv_sem=spare, device_id=self.core, device_id_type=MESH
        ).wait_send()


def inverse_norm(v):
    return lax.rsqrt(jnp.mean(v * v, axis=-1, keepdims=True) + eps_norm)


class Gather:
    def __init__(self, p, spare, view, arrivals, along, aside):
        self.p, self.spare, self.view = p, spare, view
        self.arrivals, self.along, self.aside = arrivals, along, aside

    def move(self, src, t, zz):
        p, dst, sem = self.p, self.view(t), self.arrivals(t)
        p.onward(zz, lambda d, device: send(src, dst, self.along.at[zz, d], sem, device))
        send(src, dst, self.aside.at[zz], sem, p.side)

    def start(self, src):
        self.move(src, self.p.s, self.p.z)

    def wait(self, t):
        self.p.arrived(self.view(t), self.arrivals(t), self.spare)

    def step(self, k, then=None):
        zz = self.p.line(k)
        t = self.p.mine(zz)
        self.wait(t)
        self.move(self.view(t), t, zz)
        if then is not None:
            then(t)

    def other(self, k, then=None):
        t = self.p.theirs(self.p.line(k))
        self.wait(t)
        if then is not None:
            then(t)

    def finish(self):
        block = self.view(self.p.s)
        for zz in range(4):
            self.p.sent(block, self.aside.at[zz], self.spare)
            self.p.went_onward(zz, lambda d: self.p.sent(block, self.along.at[zz, d], self.spare))


def gather_body(
    x_ref, cos_ref, sin_ref, allow_ref, small_ref, wq_ref, wo_ref, wg_ref, wu_ref, c_ref,
    WQ_out, WO_out, G, C, gains, queries, keys, values, probs, att, a1, mid, a2,
    WQ, WO, vg, vu, GS, CS, S, bias,
    rq, ro, rg, rc, rs, szq, syq, sdq, szo, syo, sdo, sg, sdg, scz, scy, ss, loc,
):
    p = Place()
    r, s, c, z = p.r, p.s, p.c, p.z
    spare = loc.at[0]
    own = rows_of(192 * s, 192)
    own_c = rows_of(128 * s, 128, 128)
    loads = (
        pltpu.make_async_copy(wq_ref, WQ.at[own], loc.at[1]),
        pltpu.make_async_copy(wo_ref, WO.at[own], loc.at[2]),
        pltpu.make_async_copy(wg_ref, vg, loc.at[3]),
        pltpu.make_async_copy(wu_ref, vu, loc.at[4]),
        pltpu.make_async_copy(c_ref, CS, loc.at[5]),
    )
    for copy in loads:
        copy.start()
    p.greet(range(1, 8))
    S[s] = small_ref[...]

    def vq(t, q):
        return WQ.at[quarter(t, q)]

    def vo(t, h):
        return WO.at[rows_of(192 * t + 96 * h, 96)]

    def gq(t, q):
        return G.at[quarter(t, q)]

    def cot_block(t):
        return C.at[rows_of(128 * t, 128, 128)]

    g_q = Gather(p, spare, lambda t: vq(t, r), lambda t: rq.at[t, r], szq, syq)
    g_o = Gather(p, spare, lambda t: vo(t, c), lambda t: ro.at[t, c], szo, syo)
    g_c = Gather(p, spare, cot_block, lambda t: rc.at[t], scz, scy)
    g_q.start(wq_ref.at[rows_of(48 * r, 48)])
    for k in range(1, 8):
        t = (s + k) % 8
        send(small_ref, S.at[s], ss.at[t], rs.at[s], p.peer(t))

    def share(view, sems, rsems):
        def to_replicas(t):
            v = view(t, r)
            send(v, v, sems.at[t, 0], rsems.at[t, r], p.across)
            send(v, v, sems.at[t, 1], rsems.at[t, r], p.core)

        return to_replicas

    def relay(view, sems, rsems, t):
        v = view(t, p.rx)
        p.arrived(v, rsems.at[t, p.rx], spare)
        send(v, v, sems.at[t, 2], rsems.at[t, p.rx], p.core)

    def from_core(view, rsems):
        @pl.loop(1, 8)
        def _(k):
            t = (s + k) % 8
            p.arrived(view(t, p.rc), rsems.at[t, p.rc], spare)
            p.arrived(view(t, p.rd), rsems.at[t, p.rd], spare)

    share_q, share_g = share(vq, sdq, rq), share(gq, sdg, rg)

    def share_o(t):
        send(vo(t, c), vo(t, c), sdo.at[t], ro.at[t, c], p.core)

    for copy in loads:
        copy.wait()
    zeros = jnp.zeros((192, 32), BF)
    for t in range(8):
        GS[t, :, 0:1120] = vg[:, 1120 * t : 1120 * t + 1120]
        GS[t, :, 1120:1152] = zeros
        GS[t, :, 1152:2272] = vu[:, 1120 * t : 1120 * t + 1120]
        GS[t, :, 2272:2304] = zeros
    g_q.step(1, share_q)
    g_q.other(0, share_q)
    g_q.step(2, share_q)
    g_q.other(1, share_q)
    g_q.step(3, share_q)
    g_o.start(wo_ref.at[rows_of(96 * c, 96)])
    turns = (4, 1, 6, 3, 2, 5, 7)

    def give_g(i):
        t = (s + turns[i]) % 8
        send(GS.at[t, rows_of(48 * r, 48)], gq(s, r), sg.at[t], rg.at[s, r], p.peer(t))

    def take_g(i):
        t = (s + 8 - turns[i]) % 8
        p.arrived(gq(t, r), rg.at[t, r], spare)
        share_g(t)

    own_out = (
        pltpu.make_async_copy(GS.at[s], G.at[own], loc.at[1]),
        pltpu.make_async_copy(CS, C.at[own_c], loc.at[2]),
    )
    for copy in own_out:
        copy.start()
    g_q.other(2, share_q)
    give_g(0)
    g_q.other(3, share_q)
    give_g(1)

    @pl.loop(1, 8)
    def _(k):
        t = (s + k) % 8
        p.arrived(S.at[t], rs.at[t], spare)

    for t in range(8):
        row = S[t, 0:1, :].astype(F32)
        gains[0:1, 192 * t : 192 * t + 192] = row[:, 0:192]
        bias[0:1, 256 * t : 256 * t + 256] = row[:, 256:512]
        gains[1:2, 192 * t : 192 * t + 192] = row[:, 512:704]
    x = x_ref[...].astype(F32)
    a1[...] = (x * inverse_norm(x) * gains[0:1, :]).astype(BF)

    def relay_q(t):
        relay(vq, sdq, rq, t)

    g_o.step(1, share_o)
    give_g(2)
    g_o.other(0, share_o)
    relay_q(p.mine(p.line(1)))
    relay_q(p.theirs(p.line(0)))
    g_o.step(2, share_o)
    give_g(3)
    g_o.other(1, share_o)
    relay_q(p.mine(p.line(2)))
    relay_q(p.theirs(p.line(1)))
    g_o.step(3, share_o)
    give_g(4)
    g_c.start(CS)
    take_g(0)
    take_g(1)
    relay_q(p.mine(p.line(3)))
    relay_q(p.theirs(p.line(2)))
    relay_q(p.theirs(p.line(3)))
    take_g(2)
    give_g(5)
    give_g(6)
    from_core(vq, rq)
    cosine, sine = cos_ref[...], sin_ref[...]
    for j in range(4):
        co = pl.ds(512 * j, 512)
        joined = dot(a1[...], WQ[:, co]) + bias[0:1, co]
        for i in range(4):
            h = 4 * j + i
            u = joined[:, 128 * i : 128 * i + 128]
            if h < 14:
                u = u * cosine + pltpu.roll(u, 64, 1) * sine
            if h < 12:
                queries[h // 6, pl.ds(128 * (h % 6), 128), :] = (u * HEAD_DIMENSION**-0.5).astype(BF)
            elif h < 14:
                keys[h - 12] = u.astype(BF)
            else:
                values[h - 14] = u.astype(BF)
    save = (pltpu.make_async_copy(WQ, WQ_out, loc.at[3]), pltpu.make_async_copy(WO, WO_out, loc.at[4]))
    save[0].start()
    open_to = allow_ref[...] != 0
    for g in range(2):
        scores = dot_nt(queries[g], keys[g]).reshape(6, 128, 128)
        scores = jnp.where(open_to[None], scores, -1e30)
        ex = jnp.exp(scores - jnp.max(scores, axis=-1, keepdims=True))
        soft = (ex / jnp.sum(ex, axis=-1, keepdims=True)).reshape(768, 128)
        probs[g] = soft
        out = dot(soft.astype(BF), values[g]).astype(BF)
        for i in range(6):
            att[:, pl.ds(128 * (6 * g + i), 128)] = out[128 * i : 128 * i + 128]

    for i in (3, 4):
        take_g(i)
    g_o.other(2, share_o)
    g_o.other(3, share_o)

    @pl.loop(1, 8)
    def _(k):
        t = (s + k) % 8
        p.arrived(vo(t, 1 - c), ro.at[t, 1 - c], spare)

    save[1].start()
    for j in range(3):
        co = pl.ds(512 * j, 512)
        mid[:, co] = x[:, 512 * j : 512 * j + 512] + dot(att[...], WO[:, co])
    hidden = mid[...]
    a2[...] = (hidden * inverse_norm(hidden) * gains[1:2, :]).astype(BF)
    g_c.step(1)
    take_g(5)
    g_c.step(2)
    take_g(6)
    g_c.step(3)

    for k in turns:
        relay(gq, sdg, rg, (s + 8 - k) % 8)

    from_core(gq, rg)

    @pl.loop(0, 4)
    def _(k):
        g_c.other(k)

    g_q.finish()
    g_o.finish()
    g_c.finish()

    @pl.loop(1, 8)
    def _(k):
        t = (s + k) % 8
        p.sent(S.at[t], ss.at[t], spare)
        p.sent(gq(t, r), sg.at[t], spare)
        p.sent(vo(t, c), sdo.at[t], spare)
        for d in range(3):
            p.sent(vq(t, r), sdq.at[t, d], spare)
            p.sent(gq(t, r), sdg.at[t, d], spare)

    for copy in own_out + save:
        copy.wait()


def gather_weights(x, cosine, sine, allowed, small, w_qkv, w_out, w_gate, w_up, cot):
    return pl.pallas_call(
        gather_body,
        out_shape=(
            shaped(1536, 2048), shaped(1536, 1536), shaped(1536, 2304), shaped(1024, 1536), shaped(8, 1536, dtype=F32),
            shaped(2, 768, 128), shaped(2, 128, 128), shaped(2, 128, 128), shaped(2, 768, 128, dtype=F32),
            shaped(128, 1536), shaped(128, 1536), shaped(128, 1536, dtype=F32), shaped(128, 1536),
        ),
        in_specs=[VMEM] * 5 + [HBM] * 5,
        out_specs=(HBM,) * 4 + (VMEM,) * 9,
        scratch_shapes=[
            low(1536, 2048), low(1536, 1536), low(192, 8960), low(192, 8960), low(8, 192, 2304), low(128, 1536),
            low(8, 16, 768), full(8, 2048),
            DMA((8, 4)), DMA((8, 2)), DMA((8, 4)), DMA((8,)), DMA((8,)),
            DMA((4, 2)), DMA((4,)), DMA((8, 3)), DMA((4, 2)), DMA((4,)), DMA((8,)),
            DMA((8,)), DMA((8, 3)), DMA((4, 2)), DMA((4,)), DMA((8,)), DMA((6,)),
        ],
        compiler_params=pltpu.CompilerParams(collective_id=0, has_side_effects=True, vmem_limit_bytes=56 << 20),
        name="gather_and_attend",
    )(x, cosine, sine, allowed, small, w_qkv, w_out, w_gate, w_up, cot)


def feed_body(
    n_ref, c_hbm, g_hbm, d_hbm, DS, PO_out, GC, OD,
    vG, vD, vC, N, NT, MX, MT, H, PD, PO, YD, ZD, YO, GD, RCd, RXd, RC, RX,
    rn, syn, szn, ryd, rzd, syd, szd, syo, ryo, scd, rcd, sxd, rxd, sfd, scg, rcg, sx, rx, lq, lo, loc,
):
    p = Place()
    r, s, c, y, z = p.r, p.s, p.c, p.y, p.z
    spare = loc.at[0]

    def block(t):
        return N.at[rows_of(128 * t, 128, 128)]

    loads = (
        pltpu.make_async_copy(n_ref, block(s), loc.at[1]),
        pltpu.make_async_copy(c_hbm, vC, loc.at[2]),
        pltpu.make_async_copy(g_hbm, vG, loc.at[3]),
        pltpu.make_async_copy(d_hbm, vD.at[0:1120], loc.at[4]),
    )
    for copy in loads:
        copy.start()
    p.greet(range(1, 8))
    g_n = Gather(p, spare, block, lambda t: rn.at[t], szn, syn)
    g_n.start(n_ref)
    vD[1120:1152, :] = jnp.zeros((32, 1536), BF)
    for copy in loads:
        copy.wait()

    def side_d(k):
        zz = p.line(k)
        send(PD.at[p.theirs(zz)], YD.at[zz], syd.at[zz], ryd.at[zz], p.side)

    def side_o(k):
        zz = p.line(k)
        send(PO.at[p.theirs(zz)], YO.at[zz], syo.at[zz], ryo.at[zz], p.side)

    def step_d(k):
        zz = p.line(k)
        t = p.mine(zz)

        def add(ref, sem):
            p.arrived(ref, sem, spare)
            PD[t] = (PD[t].astype(F32) + ref[...].astype(F32)).astype(BF)

        add(YD.at[zz], ryd.at[zz])
        p.reduce_step(
            zz,
            lambda slot: add(ZD.at[slot], rzd.at[slot]),
            lambda slot, device: send(PD.at[t], ZD.at[slot], szd.at[zz], rzd.at[slot], device),
        )

    at_end = (z == 0) | (z == 3)

    @pl.loop(0, 4)
    def _(k):
        zz = p.line(k)

        pl.when(k < 3)(lambda: g_n.step(k + 1))
        g_n.other(k)
        rows = rows_of(256 * zz, 256, 256)
        X = N[rows]
        NT[:, rows] = X.T
        cot = vC[rows]
        for j in range(3):
            ga, ua = pl.ds(384 * j, 384), pl.ds(1152 + 384 * j, 384)
            gate = dot(X, vG[:, ga])
            up = dot(X, vG[:, ua])
            d_mixed = dot_nt(cot, vD[ga])
            sg = jax.nn.sigmoid(gate)
            active = gate * sg
            d_active = d_mixed * up
            MX[:, ga] = (active * up).astype(BF)
            H[rows, ga] = (d_active * sg + d_active * active * (1.0 - sg)).astype(BF)
            H[rows, ua] = (d_mixed * active).astype(BF)
        for j in range(3):
            co = pl.ds(512 * j, 512)
            part = dot_nt(H[rows], vG[co]).astype(BF)
            PD[2 * zz, :, co] = part[:128]
            PD[2 * zz + 1, :, co] = part[128:]
        pl.when(k == 3)(lambda: side_d(3))
        for j in range(3):
            co = pl.ds(512 * j, 512)
            part = dot(MX[...], vD[:, co]).astype(BF)
            PO[2 * zz, :, co] = part[:128]
            PO[2 * zz + 1, :, co] = part[128:]
        MT[:, rows] = MX[...].T

        pl.when(k == 2)(lambda: side_o(2))

    side_d(2)
    side_d(1)
    side_d(0)

    def save_o(t, i):
        pltpu.make_async_copy(PO.at[t], PO_out.at[t], lo.at[i]).start()

    def add_o(k):
        zz = p.line(k)
        t = p.mine(zz)
        p.arrived(YO.at[zz], ryo.at[zz], spare)
        PO[t] = (PO[t].astype(F32) + YO[zz].astype(F32)).astype(BF)
        save_o(t, k)

    for k in (0, 1, 3):
        save_o(p.mine(p.line(k)), k)
        save_o(p.theirs(p.line(k)), 4 + k)

    def chunk(i):
        return rows_of(288 * i, 288)

    def cols(q):
        return rows_of(384 * q, 384, 128)

    def down_term(i):
        for j in range(3):
            co = pl.ds(512 * j, 512)
            GD[chunk(i), co] = dot(MT[chunk(i)], vC[:, co]).astype(BF)
        for xx in range(2):
            q = 2 * xx + 1 - c
            send(GD.at[chunk(i), cols(q)], RCd.at[xx, chunk(i)], scd.at[i, xx], rcd.at[i, xx], p.core)

    def down_chip(i):
        for xx in range(2):
            p.arrived(RCd.at[xx, chunk(i)], rcd.at[i, xx], spare)
            q = cols(2 * xx + c)
            GD[chunk(i), q] = (GD[chunk(i), q].astype(F32) + RCd[xx, chunk(i)].astype(F32)).astype(BF)
        send(GD.at[chunk(i), cols(p.rx)], RXd.at[chunk(i)], sxd.at[i], rxd.at[i], p.across)

    def down_whole(i):
        p.arrived(RXd.at[chunk(i)], rxd.at[i], spare)
        q = cols(r)
        GD[chunk(i), q] = (GD[chunk(i), q].astype(F32) + RXd[chunk(i)].astype(F32)).astype(BF)
        pltpu.make_async_copy(GD.at[chunk(i), q], OD.at[chunk(i)], sfd.at[i]).start()

    def pair_term(k):
        t = (s + 1 + k) % 8
        rows = rows_of(192 * t, 192)
        for j in range(3):
            co = pl.ds(768 * j, 768)
            vG[rows, co] = dot(NT[rows], H[:, co]).astype(BF)
        for xx in range(2):
            send(vG.at[quarter(t, 2 * xx + 1 - c)], RC.at[t, xx], scg.at[t, xx], rcg.at[t, xx], p.core)

    def pair_chip(k):
        t = (s + 1 + k) % 8
        for xx in range(2):
            p.arrived(RC.at[t, xx], rcg.at[t, xx], spare)
            q = quarter(t, 2 * xx + c)
            vG[q] = (vG[q].astype(F32) + RC[t, xx].astype(F32)).astype(BF)

            @pl.when(k >= 3)
            def _():
                pltpu.make_async_copy(vG.at[q], GC.at[t, xx], lq.at[t, xx]).start()

        @pl.when(k < 3)
        def _():
            send(vG.at[quarter(t, p.rx)], RX.at[k], sx.at[k], rx.at[k], p.across)

    def pair_whole(k):
        t = (s + 1 + k) % 8
        q = quarter(t, r)
        p.arrived(RX.at[k], rx.at[k], spare)
        vG[q] = (vG[q].astype(F32) + RX[k].astype(F32)).astype(BF)
        pltpu.make_async_copy(vG.at[q], GC.at[t, p.x], lq.at[t, 0]).start()

    @pl.loop(0, 5)
    def _(i):
        pl.when(i < 4)(lambda: down_term(i))
        pl.when(i >= 1)(lambda: down_chip(i - 1))

    @pl.loop(0, 9)
    def _(i):
        pl.when(i < 8)(lambda: pair_term(i))
        pl.when(i >= 1)(lambda: pair_chip(i - 1))

        pl.when((i == 3) & at_end)(lambda: step_d(3))

    pl.when(at_end)(lambda: step_d(2))
    pl.when(jnp.logical_not(at_end))(lambda: step_d(3))

    @pl.loop(0, 4)
    def _(i):
        down_whole(i)

    pl.when(at_end)(lambda: step_d(1))
    pl.when(jnp.logical_not(at_end))(lambda: step_d(2))
    zo = p.line(2)
    to = p.mine(zo)
    p.arrived(YO.at[zo], ryo.at[zo], spare)
    PO[to] = (PO[to].astype(F32) + YO[zo].astype(F32)).astype(BF)
    save_o(to, 2)

    @pl.loop(0, 3)
    def _(k):
        pair_whole(k)

    pl.when(jnp.logical_not(at_end))(lambda: step_d(1))
    step_d(0)
    DS[...] = PD[s].astype(F32)

    @pl.loop(0, 8)
    def _(t):
        for xx in range(2):
            p.sent(RC.at[t, xx], scg.at[t, xx], spare)

            @pl.when(((t + 7 - s) % 8 >= 3) | (xx == 0))
            def _():
                pltpu.make_async_copy(RC.at[t, xx], GC.at[t, xx], lq.at[t, xx]).wait()

    @pl.loop(0, 4)
    def _(i):
        pltpu.make_async_copy(RXd.at[chunk(i)], OD.at[chunk(i)], sfd.at[i]).wait()
        for xx in range(2):
            p.sent(RCd.at[xx, chunk(i)], scd.at[i, xx], spare)
        p.sent(RXd.at[chunk(i)], sxd.at[i], spare)
        p.sent(YD.at[i], syd.at[i], spare)

        @pl.when(i != z)
        def _():
            p.sent(ZD.at[i], szd.at[i], spare)

    g_n.finish()
    p.sent(YO.at[0], syo.at[p.line(2)], spare)
    for k in range(3):
        p.sent(RX.at[k], sx.at[k], spare)
    for i in range(8):
        if i == 6:
            continue
        pltpu.make_async_copy(PO.at[s], PO_out.at[s], lo.at[i]).wait()


def feed_forward(n2, cot, gate_up, w_down):
    return pl.pallas_call(
        feed_body,
        out_shape=(shaped(128, 1536, dtype=F32), shaped(8, 128, 1536), shaped(8, 2, 48, 2304), shaped(1152, 384)),
        in_specs=[HBM] * 4,
        out_specs=(VMEM, HBM, HBM, HBM),
        scratch_shapes=[
            low(1536, 2304), low(1152, 1536), low(1024, 1536), low(1024, 1536), low(1536, 1024), low(256, 1152),
            low(1152, 1024), low(1024, 2304), low(8, 128, 1536), low(8, 128, 1536), low(4, 128, 1536), low(5, 128, 1536), low(4, 128, 1536),
            low(1152, 1536), low(2, 1152, 384), low(1152, 384), low(8, 2, 48, 2304), low(3, 48, 2304),
            DMA((8,)), DMA((4,)), DMA((4, 2)), DMA((4,)), DMA((5,)), DMA((4,)), DMA((4,)), DMA((4,)), DMA((4,)),
            DMA((4, 2)), DMA((4, 2)), DMA((4,)), DMA((4,)), DMA((4,)), DMA((8, 2)), DMA((8, 2)), DMA((3,)), DMA((3,)), DMA((8, 2)), DMA((8,)), DMA((5,)),
        ],
        compiler_params=pltpu.CompilerParams(collective_id=1, has_side_effects=True, vmem_limit_bytes=62 << 20),
        name="feed_forward",
    )(n2, cot, gate_up, w_down)


class RowSums:
    def __init__(self, p, spare, total, chip, side, far, across, out, sems):
        self.p, self.spare, self.total, self.chip, self.side = p, spare, total, chip, side
        self.far, self.across, self.out, self.sems = far, across, out, sems

    def own(self, k):
        p = self.p
        return 2 * p.line(3 - k % 4) + (1 - p.y + (k // 4) * (2 * p.y - 1))

    def to_core(self, t):
        p = self.p
        for xx in range(2):
            send(
                self.total.at[quarter(t, 2 * xx + 1 - p.c)], self.chip.at[t, xx],
                self.sems[0].at[t, xx], self.sems[1].at[t, xx], p.core,
            )

    def add(self, q, ref, sem):
        self.p.arrived(ref, sem, self.spare)
        self.total[q] = (self.total[q].astype(F32) + ref[...].astype(F32)).astype(BF)

    def on_chip(self, k):
        p, t = self.p, self.own(k)
        for xx in range(2):
            q = quarter(t, 2 * xx + p.c)
            self.add(q, self.chip.at[t, xx], self.sems[1].at[t, xx])

    def aside(self, k):
        p, t = self.p, self.own(k)
        for xx in range(2):
            at = t // 2, xx
            q = quarter(t, 2 * xx + p.c)
            send(self.total.at[q], self.side.at[at], self.sems[2].at[at], self.sems[3].at[at], p.side)

    def on_line(self, k):
        p = self.p
        zz = p.line(3 - k)
        t = p.mine(zz)
        for xx in range(2):
            q = quarter(t, 2 * xx + p.c)
            self.add(q, self.side.at[zz, xx], self.sems[3].at[zz, xx])
            p.reduce_step(
                zz,
                lambda slot: self.add(q, self.far.at[slot, xx], self.sems[5].at[slot, xx]),
                lambda slot, device: send(
                    self.total.at[q], self.far.at[slot, xx], self.sems[4].at[zz, xx], self.sems[5].at[slot, xx], device
                ),
            )

    def at_owner(self):
        p = self.p
        send(self.total.at[quarter(p.s, p.rx)], self.across, self.sems[6].at[3], self.sems[7].at[4], p.across)

    def spread(self):
        p = self.p
        p.arrived(self.across, self.sems[7].at[4], self.spare)
        q = quarter(p.s, p.r)
        self.out[p.r] = (self.total[q].astype(F32) + self.across[...].astype(F32)).astype(BF)
        mine = self.out.at[p.r]
        send(mine, mine, self.sems[6].at[0], self.sems[7].at[p.r], p.across)
        send(mine, mine, self.sems[6].at[1], self.sems[7].at[p.r], p.core)

    def pass_on(self):
        p = self.p
        v = self.out.at[p.rx]
        p.arrived(v, self.sems[7].at[p.rx], self.spare)
        send(v, v, self.sems[6].at[2], self.sems[7].at[p.rx], p.core)

    def finish(self):
        p = self.p
        for q in (p.rc, p.rd):
            p.arrived(self.out.at[q], self.sems[7].at[q], self.spare)
        for d in range(3):
            p.sent(self.out.at[p.r], self.sems[6].at[d], self.spare)
        p.sent(self.across, self.sems[6].at[3], self.spare)

        @pl.loop(0, 8)
        def _(t):
            for xx in range(2):
                p.sent(self.chip.at[t, xx], self.sems[0].at[t, xx], self.spare)

        @pl.loop(0, 4)
        def _(i):
            for xx in range(2):
                p.sent(self.side.at[i, xx], self.sems[2].at[i, xx], self.spare)

                @pl.when(i != p.z)
                def _():
                    p.sent(self.far.at[i, xx], self.sems[4].at[i, xx], self.spare)

    @staticmethod
    def buffers(width):
        return [low(8, 2, 48, width), low(4, 2, 48, width), low(5, 2, 48, width), low(48, width)]

    @staticmethod
    def semaphores():
        return [DMA((8, 2)), DMA((8, 2)), DMA((4, 2)), DMA((4, 2)), DMA((4, 2)), DMA((5, 2)), DMA((4,)), DMA((5,))]


def attend_back_body(
    ds_ref, mid_ref, x_ref, cot_ref, gains, cos_ref, sin_ref, queries, keys, values, probs, att, a1,
    wq_ref, wo_ref, po_ref, gc_ref, od_ref,
    out_ref, gtok_ref, OG, OD, OWq, OWo,
    vQ, vO, PO, YO, ZO, GX, RX, DQ, dmid, DB, dA, dj, AT, SM, RCq, Yq, Zq, RXq, RCo, Yo, Zo, RXo,
    sx, rx, sa, ra, sf, sd, rd, syo, ryo, szo, rzo, *sems,
):
    p = Place()
    r, s, c, y, z = p.r, p.s, p.c, p.y, p.z
    loc = sems[-1]
    spare = loc.at[0]
    q_sums = RowSums(p, spare, vQ, RCq, Yq, Zq, RXq, OWq, sems[0:8])
    o_sums = RowSums(p, spare, vO, RCo, Yo, Zo, RXo, OWo, sems[8:16])
    loads = (
        pltpu.make_async_copy(wo_ref, vO, loc.at[1]),
        pltpu.make_async_copy(wq_ref, vQ.at[:, 0:2048], loc.at[2]),
        pltpu.make_async_copy(po_ref, PO, loc.at[3]),
        pltpu.make_async_copy(gc_ref.at[:, p.x], GX, loc.at[4]),
        pltpu.make_async_copy(od_ref, DQ, loc.at[5]),
    )
    for copy in loads:
        copy.start()
    p.greet(range(1, 8))

    def owner(k):
        return (s + 1 + k) % 8

    for k in range(3, 8):
        t = owner(k)
        send(gc_ref.at[t, 1 - p.x], RX.at[t], sx.at[t], rx.at[t], p.across)
    for k in range(3):
        t = owner(k)
        send(gc_ref.at[t, p.x], OG.at[r, s], sa.at[t], ra.at[s, r], p.peer(t))

    def send_out(k):
        zz = p.line(k)
        send(po_ref.at[p.theirs(zz)], YO.at[zz], syo.at[zz], ryo.at[zz], p.side)

    send_out(3)

    def step_out(k):
        zz = p.line(k)
        t = p.mine(zz)

        def add(ref, sem):
            p.arrived(ref, sem, spare)
            PO[t] = (PO[t].astype(F32) + ref[...].astype(F32)).astype(BF)

        if k != 2:
            add(YO.at[zz], ryo.at[zz])
        p.reduce_step(
            zz,
            lambda slot: add(ZO.at[slot], rzo.at[slot]),
            lambda slot, device: send(PO.at[t], ZO.at[slot], szo.at[zz], rzo.at[slot], device),
        )

    def ends(*steps):
        @pl.when((z == 0) | (z == 3))
        def _():
            for f, k in steps:
                f(k)

    def middles(*steps):
        @pl.when((z == 1) | (z == 2))
        def _():
            for f, k in steps:
                f(k)

    def pair_whole(k):
        t = owner(k)
        p.arrived(RX.at[t], rx.at[t], spare)
        GX[t] = (GX[t].astype(F32) + RX[t].astype(F32)).astype(BF)

        @pl.when(k < 7)
        def _():
            send(GX.at[t], OG.at[r, s], sa.at[t], ra.at[s, r], p.peer(t))

        @pl.when(k == 7)
        def _():
            pltpu.make_async_copy(GX.at[t], OG.at[r, s], loc.at[4]).start()

    def share(t):
        v = OG.at[r, t]
        send(v, v, sf.at[t, 0], ra.at[t, r], p.across)
        send(v, v, sf.at[t, 1], ra.at[t, r], p.core)

    def back(w):
        return w * cos_ref[...] - pltpu.roll(w, 64, 1) * sin_ref[...]

    dn, hidden = ds_ref[...], mid_ref[...]
    rstd = inverse_norm(hidden)
    unit = hidden * rstd
    gain_ffn_grad = jnp.sum(dn * unit, axis=0, keepdims=True)
    e = dn * gains[1:2, :]
    dm = cot_ref[...].astype(F32) + rstd * (e - unit * jnp.mean(e * unit, axis=-1, keepdims=True))
    dmid[...] = dm
    DB[...] = dm.astype(BF)
    AT[...] = att[...].T
    for copy in loads:
        copy.wait()
    keep = pltpu.make_async_copy(DQ, OD.at[r], loc.at[5])
    keep.start()
    for j in range(3):
        part = dot_nt(DB[...], vO[pl.ds(512 * j, 512)]).astype(BF)
        for i in range(4):
            h = 4 * j + i
            dA[h // 6, pl.ds(128 * (h % 6), 128), :] = part[:, 128 * i : 128 * i + 128]
    for j in range(3):
        co = pl.ds(512 * j, 512)
        vO[:, co] = dot(AT[...], DB[:, co]).astype(BF)

    @pl.loop(0, 8)
    def _(k):
        o_sums.to_core(o_sums.own(k))

    def heads(g):
        grad, soft = dA[g], probs[g]
        d_probs = dot_nt(grad, values[g])
        d_scores = (soft * (d_probs - jnp.sum(soft * d_probs, axis=-1, keepdims=True))).astype(BF)
        d_values = dot(soft.astype(BF).T, grad)
        d_queries = dot(d_scores, keys[g]) * HEAD_DIMENSION**-0.5
        d_keys = dot(d_scores.T, queries[g])
        for i in range(6):
            dj[:, pl.ds(128 * (6 * g + i), 128)] = back(d_queries[128 * i : 128 * i + 128]).astype(BF)
        dj[:, pl.ds(128 * (12 + g), 128)] = back(d_keys).astype(BF)
        dj[:, pl.ds(128 * (14 + g), 128)] = d_values.astype(BF)

    heads(0)

    @pl.loop(0, 8)
    def _(k):
        o_sums.on_chip(k)

    o_sums.aside(0)
    o_sums.aside(1)
    ends((step_out, 3))

    heads(1)
    joined_grad = dj[...]
    bias_grad = jnp.sum(joined_grad.astype(F32), axis=0, keepdims=True)
    x = x_ref[...].astype(F32)
    rstd = inverse_norm(x)
    unit = x * rstd
    dn1 = jnp.concatenate(
        [dot_nt(joined_grad, vQ[pl.ds(512 * j, 512), 0:2048]) for j in range(3)], axis=1
    )
    gain_attn_grad = jnp.sum(dn1 * unit, axis=0, keepdims=True)
    e = dn1 * gains[0:1, :]
    gtok_ref[...] = (
        dmid[...] + rstd * (e - unit * jnp.mean(e * unit, axis=-1, keepdims=True))
    ).astype(BF)
    SM[...] = jnp.zeros_like(SM)
    for t in range(8):
        SM[t, 0:1, :] = gain_attn_grad[:, 192 * t : 192 * t + 128]
        SM[t, 1:2, 0:64] = gain_attn_grad[:, 192 * t + 128 : 192 * t + 192]
        SM[t, 2:3, :] = bias_grad[:, 256 * t : 256 * t + 128]
        SM[t, 3:4, :] = bias_grad[:, 256 * t + 128 : 256 * t + 256]
        SM[t, 4:5, :] = gain_ffn_grad[:, 192 * t : 192 * t + 128]
        SM[t, 5:6, 0:64] = gain_ffn_grad[:, 192 * t + 128 : 192 * t + 192]
    AT[...] = a1[...].T

    @pl.loop(0, 8)
    def _(k):
        t = q_sums.own(k)
        rows = rows_of(192 * t, 192)
        for j in range(2):
            co = pl.ds(1024 * j, 1024)
            vQ[rows, co] = dot(AT[rows], dj[:, co]).astype(BF)
        vQ[rows, 2048:2176] = jnp.zeros((192, 128), BF)
        vQ[rows_of(192 * t, 16), 2048:2176] = SM[t].astype(BF)
        q_sums.to_core(t)

    @pl.loop(0, 8)
    def _(k):
        q_sums.on_chip(k)


    def take(k):
        t = (s + 8 - k) % 8
        p.arrived(OG.at[r, t], ra.at[t, r], spare)
        share(t)

    o_line, q_line = o_sums.on_line, q_sums.on_line
    o_sums.aside(2)
    o_sums.aside(3)
    ends((step_out, 2), (o_line, 0))
    pair_whole(3)
    pair_whole(4)
    pair_whole(5)
    middles((step_out, 3), (step_out, 2), (o_line, 0))
    pair_whole(6)
    ends((o_line, 1))
    pair_whole(7)
    send(od_ref, OD.at[r], sd.at[0], rd.at[r], p.across)
    send(od_ref, OD.at[r], sd.at[1], rd.at[r], p.core)
    q_sums.aside(0)
    q_sums.aside(1)
    middles((o_line, 1))
    ends((o_line, 2))
    take(1)
    middles((o_line, 2))
    o_line(3)
    o_sums.at_owner()
    q_sums.aside(2)
    q_sums.aside(3)
    take(2)
    take(3)
    ends((q_line, 0))
    take(4)
    middles((q_line, 0))
    ends((q_line, 1))
    o_sums.spread()
    send_out(1)
    take(5)
    middles((q_line, 1))
    ends((q_line, 2))
    send_out(0)
    take(6)
    middles((q_line, 2))
    take(7)
    pltpu.make_async_copy(GX.at[s], OG.at[r, s], loc.at[4]).wait()
    share(s)
    q_line(3)
    q_sums.at_owner()
    step_out(1)
    q_sums.spread()
    step_out(0)
    out_ref[...] = (PO[s].astype(F32) + mid_ref[...]).astype(BF)
    o_sums.pass_on()
    v = OD.at[p.rx]
    p.arrived(v, rd.at[p.rx], spare)
    send(v, v, sd.at[2], rd.at[p.rx], p.core)

    @pl.loop(1, 9)
    def _(k):
        t = (s + 8 - k) % 8
        v = OG.at[p.rx, t]
        p.arrived(v, ra.at[t, p.rx], spare)
        send(v, v, sf.at[t, 2], ra.at[t, p.rx], p.core)

    q_sums.pass_on()
    o_sums.finish()
    q_sums.finish()
    for q in (p.rc, p.rd):
        p.arrived(OD.at[q], rd.at[q], spare)
    for d in range(3):
        p.sent(OD.at[r], sd.at[d], spare)
    keep.wait()

    @pl.loop(0, 8)
    def _(t):
        for q in (p.rc, p.rd):
            p.arrived(OG.at[q, t], ra.at[t, q], spare)
        for d in range(3):
            p.sent(OG.at[r, t], sf.at[t, d], spare)
        pl.when((t + 7 - s) % 8 >= 3)(lambda: p.sent(RX.at[t], sx.at[t], spare))

        @pl.when(t != s)
        def _():
            p.sent(OG.at[r, s], sa.at[t], spare)

    @pl.loop(0, 4)
    def _(i):
        @pl.when(i != z)
        def _():
            p.sent(ZO.at[i], szo.at[i], spare)

    for k in (0, 1, 3):
        p.sent(YO.at[k], syo.at[p.line(k)], spare)


def attend_back(*args):
    return pl.pallas_call(
        attend_back_body,
        out_shape=(
            shaped(128, 1536), shaped(128, 1536), shaped(4, 8, 48, 2304), shaped(4, 1152, 384), shaped(4, 48, 2176),
            shaped(4, 48, 1536),
        ),
        in_specs=[VMEM] * 13 + [HBM] * 5,
        out_specs=(VMEM, VMEM, HBM, HBM, VMEM, VMEM),
        scratch_shapes=[
            low(1536, 2176), low(1536, 1536), low(8, 128, 1536), low(4, 128, 1536), low(5, 128, 1536), low(8, 48, 2304),
            low(8, 48, 2304), low(1152, 384), full(128, 1536), low(128, 1536), low(2, 768, 128), low(128, 2048),
            low(1536, 128), full(8, 16, 128), *RowSums.buffers(2176), *RowSums.buffers(1536),
            DMA((8,)), DMA((8,)), DMA((8,)), DMA((8, 4)), DMA((8, 3)), DMA((3,)), DMA((4,)),
            DMA((4,)), DMA((4,)), DMA((4,)), DMA((5,)), *RowSums.semaphores(), *RowSums.semaphores(), DMA((6,)),
        ],
        compiler_params=pltpu.CompilerParams(collective_id=2, has_side_effects=True, vmem_limit_bytes=60 << 20),
        name="attend_back",
    )(*args)


def widen_body(g_ref, d_ref, q_ref, o_ref, gate, up, down, qkv, out):
    for t in range(8):
        gate[:, 1120 * t : 1120 * t + 1120] = g_ref[0, t, :, 0:1120].astype(F32)
        up[:, 1120 * t : 1120 * t + 1120] = g_ref[0, t, :, 1152:2272].astype(F32)
    down[...] = d_ref[0, 0:1120, :].astype(F32)
    qkv[...] = q_ref[0, :, 0:2048].astype(F32)
    out[...] = o_ref[0].astype(F32)


def widen(g, d, q, o):
    return pl.pallas_call(
        widen_body,
        grid=(4,),
        out_shape=(
            shaped(192, 8960, dtype=F32), shaped(192, 8960, dtype=F32), shaped(1120, 1536, dtype=F32),
            shaped(192, 2048, dtype=F32), shaped(192, 1536, dtype=F32),
        ),
        in_specs=[
            pl.BlockSpec((1, 8, 48, 2304), lambda i: (i, 0, 0, 0)),
            pl.BlockSpec((1, 1152, 384), lambda i: (i, 0, 0)),
            pl.BlockSpec((1, 48, 2176), lambda i: (i, 0, 0)),
            pl.BlockSpec((1, 48, 1536), lambda i: (i, 0, 0)),
        ],
        out_specs=(
            pl.BlockSpec((48, 8960), lambda i: (i, 0)),
            pl.BlockSpec((48, 8960), lambda i: (i, 0)),
            pl.BlockSpec((1120, 384), lambda i: (0, i)),
            pl.BlockSpec((48, 2048), lambda i: (i, 0)),
            pl.BlockSpec((48, 1536), lambda i: (i, 0)),
        ),
        compiler_params=pltpu.CompilerParams(vmem_limit_bytes=48 << 20),
        name="widen",
    )(g, d, q, o)


def shards_eight(
    tokens, segments, gain_attn, w_qkv, b_qkv, w_out, gain_ffn, w_gate, w_up, w_down, cotangent
):
    cosine, sine, allowed = tables(segments[0], HEAD_DIMENSION)
    half = HEAD_DIMENSION // 2
    sine = jnp.concatenate([-sine[:, :half], sine[:, half:]], axis=-1)
    gap = jnp.zeros((64,), BF)
    small = jnp.concatenate([gain_attn, gap, b_qkv, gain_ffn, gap])[None]
    small = jnp.pad(small, ((0, 15), (0, 0)))
    x, cot = tokens[0], cotangent[0]
    WQ, WO, G, C, gains, queries, keys, values, probs, att, a1, mid, a2 = gather_weights(
        x, cosine, sine, allowed, small, w_qkv, w_out, w_gate, w_up, cot
    )
    ds, parts, gate_up, down = feed_forward(a2, C, G, w_down)
    out, grad_tokens, gate_up, down, qkv, o = attend_back(
        ds, mid, x, cot, gains, cosine, sine, queries, keys, values, probs, att, a1, WQ, WO, parts, gate_up, down
    )
    gate, up, down, qkv_rows, out_rows = widen(gate_up, down, qkv, o)
    small = qkv[0, 0:6, 2048:].astype(F32).reshape(768)
    return (
        out[None], grad_tokens[None], small[0:192], qkv_rows, small[256:512], out_rows, small[512:704], gate, up, down,
    )


def solution(mesh):
    placed = (
        P(("replica", "shard"), None, None),
        P(("replica", "shard"), None),
        P("shard"),
        P("shard", None),
        P("shard"),
        P("shard", None),
        P("shard"),
        P("shard", None),
        P("shard", None),
        P("shard", None),
        P(("replica", "shard"), None, None),
    )
    return jax.shard_map(
        shards_eight if (mesh.shape["replica"], mesh.shape["shard"]) == (4, 8) else shards,
        mesh=mesh,
        in_specs=placed,
        out_specs=(
            P(("replica", "shard"), None, None),
            P(("replica", "shard"), None, None),
            P("shard"),
            P("shard", None),
            P("shard"),
            P("shard", None),
            P("shard"),
            P("shard", None),
            P("shard", None),
            P("shard", None),
        ),
        check_vma=False,
    )
```

```python
import math

import jax
import jax.numpy as jnp
from jax import lax
from jax.experimental import pallas as pl
from jax.experimental.pallas import tpu as pltpu
from jax.sharding import PartitionSpec as P

QUERY_HEADS = 12
KEY_VALUE_HEADS = 2
HEAD_DIMENSION = 128


eps_norm = 1e-06
rope_base = 1000000.0


def tables(segment_ids, head_size):
    token_length = segment_ids.shape[-1]
    row_index = jnp.arange(token_length, dtype=jnp.int32)
    earlier = jnp.sum(
        (segment_ids[..., None, :] < segment_ids[..., :, None]).astype(jnp.int32),
        axis=-1,
        dtype=jnp.int32,
    )
    positions = (row_index - earlier).astype(jnp.float32)
    frequencies = jnp.exp(
        jnp.arange(head_size // 2, dtype=jnp.float32) * (-2.0 * math.log(rope_base) / head_size)
    )
    angles = positions[..., None] * frequencies
    cosine = jnp.concatenate([jnp.cos(angles), jnp.cos(angles)], axis=-1)
    sine_vals = jnp.concatenate([jnp.sin(angles), jnp.sin(angles)], axis=-1)
    allowed = (
        (segment_ids[..., None, :] == segment_ids[..., :, None])
        & (row_index[None, :] <= row_index[:, None])
    ).astype(jnp.int32)
    return (cosine, sine_vals, allowed)


def apply_rotation(values, cosine, sine_vals):
    halfway = values.shape[-1] // 2
    turned = jnp.concatenate([-values[..., halfway:], values[..., :halfway]], axis=-1)
    return values * cosine + turned * sine_vals


def rotate_back(values, cosine, sine_vals):
    halfway = values.shape[-1] // 2
    shifted = values * sine_vals
    return values * cosine + jnp.concatenate(
        [shifted[..., halfway:], -shifted[..., :halfway]], axis=-1
    )


def norm_forward(hidden, gain_vec):
    rstd_rows = lax.rsqrt(jnp.mean(hidden * hidden, axis=-1, keepdims=True) + eps_norm)
    unit_rows = hidden * rstd_rows
    return (unit_rows * gain_vec, unit_rows, rstd_rows)


def norm_backward(grad_in, gain_vec, unit_rows, rstd_rows):
    inner_grad = grad_in * gain_vec
    return rstd_rows * (
        inner_grad - unit_rows * jnp.mean(inner_grad * unit_rows, axis=-1, keepdims=True)
    )


def column_term(left_side, right_side):
    return jnp.einsum("lf,ld->fd", left_side, right_side, preferred_element_type=jnp.float32)


def to_columns(rows):
    ranks = lax.axis_size("shard")
    depth, width = rows.shape
    split = rows.reshape(depth, ranks, width // ranks).transpose(1, 0, 2)
    return lax.all_to_all(split, "shard", 0, 0, tiled=True).reshape(ranks * depth, width // ranks)


def to_rows(columns):
    ranks, copies = lax.axis_size("shard"), lax.axis_size("replica")
    depth, width = columns.shape
    depth = depth // ranks
    parts = columns.reshape(ranks, copies, depth // copies, width)
    part = lax.psum_scatter(parts, "replica", scatter_dimension=1, tiled=False)
    part = lax.all_to_all(part, "shard", 0, 0, tiled=True)
    part = part.transpose(1, 0, 2).reshape(depth // copies, ranks * width)
    return lax.all_gather(part, "replica", axis=0, tiled=True)


def shards(
    tokens, segments, gain_attn, w_qkv, b_qkv, w_out, gain_ffn, w_gate, w_up, w_down, cotangent
):
    heads_per_group = QUERY_HEADS // KEY_VALUE_HEADS
    head_dimension = QUERY_HEADS * HEAD_DIMENSION
    key_value_limit = head_dimension + KEY_VALUE_HEADS * HEAD_DIMENSION
    logit_scale = HEAD_DIMENSION ** (-0.5)
    token_length = tokens.shape[1]
    full_gain_attn, full_qkv, full_bias, full_out, full_gain_ffn = (
        lax.all_gather(gain_attn, "shard", axis=0, tiled=True),
        lax.all_gather(w_qkv, "shard", axis=0, tiled=True),
        lax.all_gather(b_qkv, "shard", axis=0, tiled=True),
        lax.all_gather(w_out, "shard", axis=0, tiled=True),
        lax.all_gather(gain_ffn, "shard", axis=0, tiled=True),
    )
    gate_columns = to_columns(w_gate)
    up_columns = to_columns(w_up)
    all_cot = lax.all_gather(cotangent[0], "shard", axis=0, tiled=True)
    gain_first = full_gain_attn.astype(jnp.float32)
    gain_second = full_gain_ffn.astype(jnp.float32)
    cosine, sine_vals, allowed = tables(segments[0], HEAD_DIMENSION)
    cosine_per_head = cosine[:, None, :]
    sine_per_head = sine_vals[:, None, :]
    inputs = tokens[0].astype(jnp.float32)
    normed_first, unit_first, rstd_first = norm_forward(inputs, gain_first)
    acts_first = normed_first.astype(jnp.bfloat16)
    joined_projection = jnp.dot(
        acts_first, full_qkv, preferred_element_type=jnp.float32
    ) + full_bias.astype(jnp.float32)
    query_rows = apply_rotation(
        joined_projection[:, :head_dimension].reshape(token_length, QUERY_HEADS, HEAD_DIMENSION),
        cosine_per_head,
        sine_per_head,
    )
    query_reduced = (
        (query_rows * logit_scale)
        .astype(jnp.bfloat16)
        .reshape(token_length, KEY_VALUE_HEADS, heads_per_group, HEAD_DIMENSION)
    )
    k_low = apply_rotation(
        joined_projection[:, head_dimension:key_value_limit].reshape(
            token_length, KEY_VALUE_HEADS, HEAD_DIMENSION
        ),
        cosine_per_head,
        sine_per_head,
    ).astype(jnp.bfloat16)
    value_reduced = (
        joined_projection[:, key_value_limit:]
        .reshape(token_length, KEY_VALUE_HEADS, HEAD_DIMENSION)
        .astype(jnp.bfloat16)
    )
    scores = jnp.einsum("ikrd,jkd->krij", query_reduced, k_low, preferred_element_type=jnp.float32)
    scores = jnp.where(allowed != 0, scores, -1e30)
    largest = jnp.max(scores, axis=-1, keepdims=True)
    exponents = jnp.exp(scores - largest)
    soft_probs = exponents / jnp.sum(exponents, axis=-1, keepdims=True)
    soft_low = soft_probs.astype(jnp.bfloat16)
    attended = jnp.einsum(
        "krij,jkd->ikrd", soft_low, value_reduced, preferred_element_type=jnp.float32
    )
    attended = attended.reshape(token_length, head_dimension).astype(jnp.bfloat16)
    hidden_mid = inputs + jnp.dot(attended, full_out, preferred_element_type=jnp.float32)
    normed_second, unit_second, rstd_second = norm_forward(hidden_mid, gain_second)
    acts_second = normed_second.astype(jnp.bfloat16)
    all_acts = lax.all_gather(acts_second, "shard", axis=0, tiled=True)
    gate_vals = jnp.dot(all_acts, gate_columns, preferred_element_type=jnp.float32)
    up_vals = jnp.dot(all_acts, up_columns, preferred_element_type=jnp.float32)
    sigmoid_gate = jax.nn.sigmoid(gate_vals)
    active = gate_vals * sigmoid_gate
    mixed_hidden = (active * up_vals).astype(jnp.bfloat16)
    d_mixed = jnp.einsum("ld,fd->lf", all_cot, w_down, preferred_element_type=jnp.float32)
    d_active = d_mixed * up_vals
    d_gate = (
        d_active * sigmoid_gate + d_active * gate_vals * sigmoid_gate * (1.0 - sigmoid_gate)
    ).astype(jnp.bfloat16)
    d_up = (d_mixed * active).astype(jnp.bfloat16)
    d_normed_part = jnp.einsum("lf,df->ld", d_gate, gate_columns, preferred_element_type=jnp.float32)
    d_normed_part = d_normed_part + jnp.einsum(
        "lf,df->ld", d_up, up_columns, preferred_element_type=jnp.float32
    )
    d_normed_second = lax.psum_scatter(
        d_normed_part.astype(jnp.bfloat16), "shard", scatter_dimension=0, tiled=True
    ).astype(jnp.float32)
    down_part = jnp.dot(mixed_hidden, w_down, preferred_element_type=jnp.float32)
    result = (
        hidden_mid
        + lax.psum_scatter(
            down_part.astype(jnp.bfloat16), "shard", scatter_dimension=0, tiled=True
        ).astype(jnp.float32)
    ).astype(jnp.bfloat16)
    grad_out = cotangent[0]
    down_grad = column_term(mixed_hidden, all_cot).astype(jnp.bfloat16)
    gate_grad = to_rows(column_term(all_acts, d_gate).astype(jnp.bfloat16))
    up_grad = to_rows(column_term(all_acts, d_up).astype(jnp.bfloat16))
    gain_second_grad = jnp.sum(d_normed_second * unit_second, axis=0)
    d_hidden_mid = grad_out.astype(jnp.float32) + norm_backward(
        d_normed_second, gain_second, unit_second, rstd_second
    )
    d_branch = d_hidden_mid.astype(jnp.bfloat16)
    out_grad_term = jnp.einsum("le,ld->ed", attended, d_branch, preferred_element_type=jnp.float32)
    attended_gradient = jnp.einsum(
        "ld,ed->le", d_branch, full_out, preferred_element_type=jnp.float32
    )
    attended_gradient = attended_gradient.astype(jnp.bfloat16).reshape(
        token_length, KEY_VALUE_HEADS, heads_per_group, HEAD_DIMENSION
    )
    d_probs = jnp.einsum(
        "ikrd,jkd->krij", attended_gradient, value_reduced, preferred_element_type=jnp.float32
    )
    value_gradient = jnp.einsum(
        "krij,ikrd->jkd", soft_low, attended_gradient, preferred_element_type=jnp.float32
    )
    d_scores = soft_probs * (d_probs - jnp.sum(soft_probs * d_probs, axis=-1, keepdims=True))
    d_scores_low = d_scores.astype(jnp.bfloat16)
    d_queries = jnp.einsum(
        "krij,jkd->ikrd", d_scores_low, k_low, preferred_element_type=jnp.float32
    )
    d_queries = rotate_back(
        d_queries.reshape(token_length, QUERY_HEADS, HEAD_DIMENSION) * logit_scale,
        cosine_per_head,
        sine_per_head,
    )
    key_gradient = jnp.einsum(
        "krij,ikrd->jkd", d_scores_low, query_reduced, preferred_element_type=jnp.float32
    )
    key_gradient = rotate_back(key_gradient, cosine_per_head, sine_per_head)
    d_joined = jnp.concatenate(
        [
            d_queries.reshape(token_length, head_dimension),
            key_gradient.reshape(token_length, KEY_VALUE_HEADS * HEAD_DIMENSION),
            value_gradient.reshape(token_length, KEY_VALUE_HEADS * HEAD_DIMENSION),
        ],
        axis=1,
    ).astype(jnp.bfloat16)
    bias_grad_term = jnp.sum(d_joined.astype(jnp.float32), axis=0)
    qkv_grad_term = jnp.einsum(
        "ld,le->de", acts_first, d_joined, preferred_element_type=jnp.float32
    )
    d_normed_first = jnp.einsum("le,de->ld", d_joined, full_qkv, preferred_element_type=jnp.float32)
    gain_first_grad = jnp.sum(d_normed_first * unit_first, axis=0)
    d_inputs = d_hidden_mid + norm_backward(d_normed_first, gain_first, unit_first, rstd_first)
    owned = (
        lax.psum_scatter(
            gain_first_grad.astype(jnp.bfloat16), "shard", scatter_dimension=0, tiled=True
        ).astype(jnp.float32),
        lax.psum_scatter(
            qkv_grad_term.astype(jnp.bfloat16), "shard", scatter_dimension=0, tiled=True
        ).astype(jnp.float32),
        lax.psum_scatter(
            bias_grad_term.astype(jnp.bfloat16), "shard", scatter_dimension=0, tiled=True
        ).astype(jnp.float32),
        lax.psum_scatter(
            out_grad_term.astype(jnp.bfloat16), "shard", scatter_dimension=0, tiled=True
        ).astype(jnp.float32),
        lax.psum_scatter(
            gain_second_grad.astype(jnp.bfloat16), "shard", scatter_dimension=0, tiled=True
        ).astype(jnp.float32),
    )
    summed = (
        lax.psum(owned[0].astype(jnp.bfloat16), "replica").astype(jnp.float32),
        lax.psum(owned[1].astype(jnp.bfloat16), "replica").astype(jnp.float32),
        lax.psum(owned[2].astype(jnp.bfloat16), "replica").astype(jnp.float32),
        lax.psum(owned[3].astype(jnp.bfloat16), "replica").astype(jnp.float32),
        lax.psum(owned[4].astype(jnp.bfloat16), "replica").astype(jnp.float32),
        gate_grad.astype(jnp.float32),
        up_grad.astype(jnp.float32),
        lax.psum(down_grad, "replica").astype(jnp.float32),
    )
    return (
        result[None],
        d_inputs.astype(jnp.bfloat16)[None],
        summed[0],
        summed[1],
        summed[2],
        summed[3],
        summed[4],
        summed[5],
        summed[6],
        summed[7],
    )


MESH = pl.DeviceIdType.MESH
BF, F32 = jnp.bfloat16, jnp.float32
HBM = pl.BlockSpec(memory_space=pl.ANY)
VMEM = pl.BlockSpec(memory_space=pltpu.VMEM)
DMA = pltpu.SemaphoreType.DMA


def shaped(*shape, dtype=BF):
    return jax.ShapeDtypeStruct(shape, dtype)


def low(*shape):
    return pltpu.VMEM(shape, BF)


def full(*shape):
    return pltpu.VMEM(shape, F32)


def dot(a, b):
    return lax.dot_general(a, b, (((1,), (0,)), ((), ())), preferred_element_type=F32)


def dot_nt(a, b):
    return lax.dot_general(a, b, (((1,), (1,)), ((), ())), preferred_element_type=F32)


def rows_of(start, size, unit=16):
    return pl.ds(pl.multiple_of(start, unit), size)


def quarter(t, q):
    return rows_of(192 * t + 48 * q, 48)


def send(src, dst, send_sem, recv_sem, device):
    copy = pltpu.make_async_remote_copy(
        src_ref=src, dst_ref=dst, send_sem=send_sem, recv_sem=recv_sem, device_id=device, device_id_type=MESH
    )
    copy.start()


class Place:
    def __init__(self):
        self.r = r = lax.axis_index("replica")
        self.s = s = lax.axis_index("shard")
        self.x, self.c, self.z, self.y = r // 2, r % 2, s // 2, s % 2
        self.rc, self.rx, self.rd = r + 1 - 2 * self.c, (r + 2) % 4, 3 - r
        self.core, self.across, self.side = (self.rc, s), (self.rx, s), (r, s + 1 - 2 * self.y)

    def peer(self, t):
        return (self.r, t)

    def line(self, k):
        near = self.z + (1 - 2 * (self.z % 2)) * (k % 2)
        far = k + (self.z // 2) * (3 - 2 * k)
        return (1 - k // 2) * near + (k // 2) * far

    def onward(self, zz, copy):
        pl.when((zz <= self.z) & (self.z < 3))(lambda: copy(0, self.peer(self.s + 2)))
        pl.when((zz >= self.z) & (self.z > 0))(lambda: copy(1, self.peer(self.s - 2)))

    def went_onward(self, zz, wait):
        pl.when((zz <= self.z) & (self.z < 3))(lambda: wait(0))
        pl.when((zz >= self.z) & (self.z > 0))(lambda: wait(1))

    def reduce_step(self, zz, add, hand):
        pl.when((zz >= self.z) & (self.z > 0))(lambda: add(zz))
        pl.when((zz < self.z) & (self.z < 3))(lambda: add(zz))
        pl.when((zz == self.z) & (self.z < 3))(lambda: add(4))
        pl.when(zz > self.z)(lambda: hand(zz, self.peer(self.s + 2)))
        pl.when(zz < self.z - 1)(lambda: hand(zz, self.peer(self.s - 2)))
        pl.when(zz == self.z - 1)(lambda: hand(4, self.peer(self.s - 2)))

    def mine(self, zz):
        return 2 * zz + self.y

    def theirs(self, zz):
        return 2 * zz + 1 - self.y

    def greet(self, steps):
        bar = pltpu.get_barrier_semaphore()
        devices = [self.core, self.across] + [(self.r, (self.s + k) % 8) for k in steps]
        for device in devices:
            pl.semaphore_signal(bar, inc=1, device_id=device, device_id_type=MESH)
        pl.semaphore_wait(bar, len(devices))

    def arrived(self, ref, sem, spare):
        pltpu.make_async_remote_copy(
            src_ref=ref, dst_ref=ref, send_sem=spare, recv_sem=sem, device_id=self.core, device_id_type=MESH
        ).wait_recv()

    def sent(self, ref, sem, spare):
        pltpu.make_async_remote_copy(
            src_ref=ref, dst_ref=ref, send_sem=sem, recv_sem=spare, device_id=self.core, device_id_type=MESH
        ).wait_send()


def inverse_norm(v):
    return lax.rsqrt(jnp.mean(v * v, axis=-1, keepdims=True) + eps_norm)


class Gather:
    def __init__(self, p, spare, view, arrivals, along, aside):
        self.p, self.spare, self.view = p, spare, view
        self.arrivals, self.along, self.aside = arrivals, along, aside

    def move(self, src, t, zz):
        p, dst, sem = self.p, self.view(t), self.arrivals(t)
        p.onward(zz, lambda d, device: send(src, dst, self.along.at[zz, d], sem, device))
        send(src, dst, self.aside.at[zz], sem, p.side)

    def start(self, src):
        self.move(src, self.p.s, self.p.z)

    def wait(self, t):
        self.p.arrived(self.view(t), self.arrivals(t), self.spare)

    def step(self, k, then=None):
        zz = self.p.line(k)
        t = self.p.mine(zz)
        self.wait(t)
        self.move(self.view(t), t, zz)
        if then is not None:
            then(t)

    def other(self, k, then=None):
        t = self.p.theirs(self.p.line(k))
        self.wait(t)
        if then is not None:
            then(t)

    def finish(self):
        block = self.view(self.p.s)
        for zz in range(4):
            self.p.sent(block, self.aside.at[zz], self.spare)
            self.p.went_onward(zz, lambda d: self.p.sent(block, self.along.at[zz, d], self.spare))


def gather_body(
    x_ref, seg_ref, ga_ref, bq_ref, gf_ref, wq_ref, wo_ref, wg_ref, wu_ref, c_ref,
    WQ_out, WO_out, G, C, cos_ref, sin_ref, gains, queries, keys, values, probs, att, a1, mid, a2,
    WQ, WO, vg, vu, GS, CS, S, bias,
    rq, ro, rg, rc, rs, szq, syq, sdq, szo, syo, sdo, sg, sdg, scz, scy, ss, loc,
):
    p = Place()
    r, s, c, z = p.r, p.s, p.c, p.z
    spare = loc.at[0]
    own = rows_of(192 * s, 192)
    own_c = rows_of(128 * s, 128, 128)
    loads = (
        pltpu.make_async_copy(wq_ref, WQ.at[own], loc.at[1]),
        pltpu.make_async_copy(wo_ref, WO.at[own], loc.at[2]),
        pltpu.make_async_copy(wg_ref, vg, loc.at[3]),
        pltpu.make_async_copy(wu_ref, vu, loc.at[4]),
        pltpu.make_async_copy(c_ref, CS, loc.at[5]),
    )
    for copy in loads:
        copy.start()
    p.greet(range(1, 8))
    gap = jnp.zeros((1, 64), F32)
    small = jnp.concatenate(
        [ga_ref[...].astype(F32), gap, bq_ref[...].astype(F32), gf_ref[...].astype(F32), gap], axis=1
    )
    S[s] = jnp.broadcast_to(small, (16, 768)).astype(BF)

    def vq(t, q):
        return WQ.at[quarter(t, q)]

    def vo(t, h):
        return WO.at[rows_of(192 * t + 96 * h, 96)]

    def gq(t, q):
        return G.at[quarter(t, q)]

    def cot_block(t):
        return C.at[rows_of(128 * t, 128, 128)]

    g_q = Gather(p, spare, lambda t: vq(t, r), lambda t: rq.at[t, r], szq, syq)
    g_o = Gather(p, spare, lambda t: vo(t, c), lambda t: ro.at[t, c], szo, syo)
    g_c = Gather(p, spare, cot_block, lambda t: rc.at[t], scz, scy)
    g_q.start(wq_ref.at[rows_of(48 * r, 48)])
    for k in range(1, 8):
        t = (s + k) % 8
        send(S.at[s], S.at[s], ss.at[t], rs.at[s], p.peer(t))

    def share(view, sems, rsems):
        def to_replicas(t):
            v = view(t, r)
            send(v, v, sems.at[t, 0], rsems.at[t, r], p.across)
            send(v, v, sems.at[t, 1], rsems.at[t, r], p.core)

        return to_replicas

    def relay(view, sems, rsems, t):
        v = view(t, p.rx)
        p.arrived(v, rsems.at[t, p.rx], spare)
        send(v, v, sems.at[t, 2], rsems.at[t, p.rx], p.core)

    def from_core(view, rsems):
        @pl.loop(1, 8)
        def _(k):
            t = (s + k) % 8
            p.arrived(view(t, p.rc), rsems.at[t, p.rc], spare)
            p.arrived(view(t, p.rd), rsems.at[t, p.rd], spare)

    share_q, share_g = share(vq, sdq, rq), share(gq, sdg, rg)

    def share_o(t):
        send(vo(t, c), vo(t, c), sdo.at[t], ro.at[t, c], p.core)

    for copy in loads:
        copy.wait()
    zeros = jnp.zeros((192, 32), BF)
    for t in range(8):
        GS[t, :, 0:1120] = vg[:, 1120 * t : 1120 * t + 1120]
        GS[t, :, 1120:1152] = zeros
        GS[t, :, 1152:2272] = vu[:, 1120 * t : 1120 * t + 1120]
        GS[t, :, 2272:2304] = zeros
    across = jnp.broadcast_to(seg_ref[...].astype(F32), (128, 128))
    down = across.T
    row = lax.broadcasted_iota(jnp.int32, (128, 128), 0)
    column = lax.broadcasted_iota(jnp.int32, (128, 128), 1)
    earlier = jnp.sum(jnp.where(across < down, 1.0, 0.0), axis=1, keepdims=True)
    position = row.astype(F32) - earlier
    half = (column - 64 * (column // 64)).astype(F32)
    angle = position * jnp.exp(half * (-2.0 * math.log(rope_base) / HEAD_DIMENSION))
    cos_ref[...] = jnp.cos(angle)
    sin_ref[...] = jnp.where(column < 64, -1.0, 1.0) * jnp.sin(angle)
    open_to = (across == down) & (column <= row)
    g_q.step(1, share_q)
    g_q.other(0, share_q)
    g_q.step(2, share_q)
    g_q.other(1, share_q)
    g_q.step(3, share_q)
    g_o.start(wo_ref.at[rows_of(96 * c, 96)])
    turns = (4, 1, 6, 3, 2, 5, 7)

    def give_g(i):
        t = (s + turns[i]) % 8
        send(GS.at[t, rows_of(48 * r, 48)], gq(s, r), sg.at[t], rg.at[s, r], p.peer(t))

    def take_g(i):
        t = (s + 8 - turns[i]) % 8
        p.arrived(gq(t, r), rg.at[t, r], spare)
        share_g(t)

    own_out = (
        pltpu.make_async_copy(GS.at[s], G.at[own], loc.at[1]),
        pltpu.make_async_copy(CS, C.at[own_c], loc.at[2]),
    )
    for copy in own_out:
        copy.start()
    g_q.other(2, share_q)
    give_g(0)
    g_q.other(3, share_q)
    give_g(1)

    @pl.loop(1, 8)
    def _(k):
        t = (s + k) % 8
        p.arrived(S.at[t], rs.at[t], spare)

    for t in range(8):
        row = S[t, 0:1, :].astype(F32)
        gains[0:1, 192 * t : 192 * t + 192] = row[:, 0:192]
        bias[0:1, 256 * t : 256 * t + 256] = row[:, 256:512]
        gains[1:2, 192 * t : 192 * t + 192] = row[:, 512:704]
    x = x_ref[...].astype(F32)
    a1[...] = (x * inverse_norm(x) * gains[0:1, :]).astype(BF)

    def relay_q(t):
        relay(vq, sdq, rq, t)

    g_o.step(1, share_o)
    give_g(2)
    g_o.other(0, share_o)
    relay_q(p.mine(p.line(1)))
    relay_q(p.theirs(p.line(0)))
    g_o.step(2, share_o)
    give_g(3)
    g_o.other(1, share_o)
    relay_q(p.mine(p.line(2)))
    relay_q(p.theirs(p.line(1)))
    g_o.step(3, share_o)
    give_g(4)
    g_c.start(CS)
    take_g(0)
    take_g(1)
    relay_q(p.mine(p.line(3)))
    relay_q(p.theirs(p.line(2)))
    relay_q(p.theirs(p.line(3)))
    take_g(2)
    give_g(5)
    give_g(6)
    from_core(vq, rq)
    cosine, sine = cos_ref[...], sin_ref[...]
    for j in range(4):
        co = pl.ds(512 * j, 512)
        joined = dot(a1[...], WQ[:, co]) + bias[0:1, co]
        for i in range(4):
            h = 4 * j + i
            u = joined[:, 128 * i : 128 * i + 128]
            if h < 14:
                u = u * cosine + pltpu.roll(u, 64, 1) * sine
            if h < 12:
                queries[h // 6, pl.ds(128 * (h % 6), 128), :] = (u * HEAD_DIMENSION**-0.5).astype(BF)
            elif h < 14:
                keys[h - 12] = u.astype(BF)
            else:
                values[h - 14] = u.astype(BF)
    save = (pltpu.make_async_copy(WQ, WQ_out, loc.at[3]), pltpu.make_async_copy(WO, WO_out, loc.at[4]))
    save[0].start()
    for g in range(2):
        scores = dot_nt(queries[g], keys[g]).reshape(6, 128, 128)
        scores = jnp.where(open_to[None], scores, -1e30)
        ex = jnp.exp(scores - jnp.max(scores, axis=-1, keepdims=True))
        soft = (ex / jnp.sum(ex, axis=-1, keepdims=True)).reshape(768, 128)
        probs[g] = soft
        out = dot(soft.astype(BF), values[g]).astype(BF)
        for i in range(6):
            att[:, pl.ds(128 * (6 * g + i), 128)] = out[128 * i : 128 * i + 128]

    for i in (3, 4):
        take_g(i)
    g_o.other(2, share_o)
    g_o.other(3, share_o)

    @pl.loop(1, 8)
    def _(k):
        t = (s + k) % 8
        p.arrived(vo(t, 1 - c), ro.at[t, 1 - c], spare)

    save[1].start()
    for j in range(3):
        co = pl.ds(512 * j, 512)
        mid[:, co] = x[:, 512 * j : 512 * j + 512] + dot(att[...], WO[:, co])
    hidden = mid[...]
    a2[...] = (hidden * inverse_norm(hidden) * gains[1:2, :]).astype(BF)
    g_c.step(1)
    take_g(5)
    g_c.step(2)
    take_g(6)
    g_c.step(3)

    for k in turns:
        relay(gq, sdg, rg, (s + 8 - k) % 8)

    from_core(gq, rg)

    @pl.loop(0, 4)
    def _(k):
        g_c.other(k)

    g_q.finish()
    g_o.finish()
    g_c.finish()

    @pl.loop(1, 8)
    def _(k):
        t = (s + k) % 8
        p.sent(S.at[t], ss.at[t], spare)
        p.sent(gq(t, r), sg.at[t], spare)
        p.sent(vo(t, c), sdo.at[t], spare)
        for d in range(3):
            p.sent(vq(t, r), sdq.at[t, d], spare)
            p.sent(gq(t, r), sdg.at[t, d], spare)

    for copy in own_out + save:
        copy.wait()


def gather_weights(x, segments, gain_attn, b_qkv, gain_ffn, w_qkv, w_out, w_gate, w_up, cot):
    return pl.pallas_call(
        gather_body,
        out_shape=(
            shaped(1536, 2048), shaped(1536, 1536), shaped(1536, 2304), shaped(1024, 1536), shaped(128, 128, dtype=F32),
            shaped(128, 128, dtype=F32), shaped(8, 1536, dtype=F32), shaped(2, 768, 128), shaped(2, 128, 128), shaped(2, 128, 128), shaped(2, 768, 128, dtype=F32),
            shaped(128, 1536), shaped(128, 1536), shaped(128, 1536, dtype=F32), shaped(128, 1536),
        ),
        in_specs=[VMEM] * 5 + [HBM] * 5,
        out_specs=(HBM,) * 4 + (VMEM,) * 11,
        scratch_shapes=[
            low(1536, 2048), low(1536, 1536), low(192, 8960), low(192, 8960), low(8, 192, 2304), low(128, 1536),
            low(8, 16, 768), full(8, 2048),
            DMA((8, 4)), DMA((8, 2)), DMA((8, 4)), DMA((8,)), DMA((8,)),
            DMA((4, 2)), DMA((4,)), DMA((8, 3)), DMA((4, 2)), DMA((4,)), DMA((8,)),
            DMA((8,)), DMA((8, 3)), DMA((4, 2)), DMA((4,)), DMA((8,)), DMA((6,)),
        ],
        compiler_params=pltpu.CompilerParams(collective_id=0, has_side_effects=True, vmem_limit_bytes=56 << 20),
        name="gather_and_attend",
    )(x, segments, gain_attn, b_qkv, gain_ffn, w_qkv, w_out, w_gate, w_up, cot)


class RowSums:
    def __init__(self, p, spare, total, chip, side, far, across, out, sems, width):
        self.p, self.spare, self.total, self.chip, self.side = p, spare, total, chip, side
        self.far, self.across, self.out, self.sems = far, across, out, sems
        self.width = width

    def part(self, t, q):
        return self.total.at[quarter(t, q), 0 : self.width]

    def slot(self, t, xx):
        return self.chip.at[t, xx, :, 0 : self.width]

    def own(self, k):
        p = self.p
        return 2 * p.line(3 - k % 4) + (1 - p.y + (k // 4) * (2 * p.y - 1))

    def to_core(self, t):
        p = self.p
        for xx in range(2):
            send(
                self.part(t, 2 * xx + 1 - p.c), self.slot(t, xx),
                self.sems[0].at[t, xx], self.sems[1].at[t, xx], p.core,
            )

    def add(self, t, q, ref, sem):
        self.p.arrived(ref, sem, self.spare)
        total = self.part(t, q)
        total[...] = (total[...].astype(F32) + ref[...].astype(F32)).astype(BF)

    def on_chip(self, k):
        p, t = self.p, self.own(k)
        for xx in range(2):
            self.add(t, 2 * xx + p.c, self.slot(t, xx), self.sems[1].at[t, xx])

    def aside(self, k):
        p, t = self.p, self.own(k)
        for xx in range(2):
            at = t // 2, xx
            send(self.part(t, 2 * xx + p.c), self.side.at[at], self.sems[2].at[at], self.sems[3].at[at], p.side)

    def on_line(self, k):
        p = self.p
        zz = p.line(3 - k)
        t = p.mine(zz)
        for xx in range(2):
            q = 2 * xx + p.c
            self.add(t, q, self.side.at[zz, xx], self.sems[3].at[zz, xx])
            p.reduce_step(
                zz,
                lambda slot: self.add(t, q, self.far.at[slot, xx], self.sems[5].at[slot, xx]),
                lambda slot, device: send(
                    self.part(t, q), self.far.at[slot, xx], self.sems[4].at[zz, xx], self.sems[5].at[slot, xx], device
                ),
            )

    def at_owner(self):
        p = self.p
        for xx in range(2):
            send(self.part(p.s, 2 * xx + p.c), self.across.at[xx], self.sems[6].at[xx], self.sems[7].at[xx], p.across)

    def spread(self):
        p = self.p
        for xx in range(2):
            q = 2 * xx + p.c
            p.sent(self.across.at[xx], self.sems[6].at[xx], self.spare)
            self.add(p.s, q, self.across.at[xx], self.sems[7].at[xx])
            total = self.part(p.s, q)
            pltpu.make_async_copy(total, self.out.at[q], self.sems[6].at[4 + xx]).start()
            send(total, self.out.at[q], self.sems[6].at[2 + xx], self.sems[7].at[2 + xx], p.core)

    def finish(self):
        p = self.p
        for xx in range(2):
            q = 2 * xx + 1 - p.c
            p.arrived(self.out.at[q], self.sems[7].at[2 + xx], self.spare)
            p.sent(self.out.at[q], self.sems[6].at[2 + xx], self.spare)
            pltpu.make_async_copy(self.part(p.s, 0), self.out.at[q], self.sems[6].at[4 + xx]).wait()

        @pl.loop(0, 8)
        def _(t):
            for xx in range(2):
                p.sent(self.slot(t, xx), self.sems[0].at[t, xx], self.spare)

        @pl.loop(0, 4)
        def _(i):
            for xx in range(2):
                p.sent(self.side.at[i, xx], self.sems[2].at[i, xx], self.spare)

                @pl.when(i != p.z)
                def _():
                    p.sent(self.far.at[i, xx], self.sems[4].at[i, xx], self.spare)

    @staticmethod
    def buffers(width):
        return [low(8, 2, 48, width), low(4, 2, 48, width), low(5, 2, 48, width), low(2, 48, width)]

    @staticmethod
    def semaphores():
        return [DMA((8, 2)), DMA((8, 2)), DMA((4, 2)), DMA((4, 2)), DMA((4, 2)), DMA((5, 2)), DMA((6,)), DMA((4,))]


def layer_back_body(
    n_ref, c_hbm, g_hbm, d_hbm, wq_hbm, wo_hbm, att_hbm, a1_hbm, x_hbm, cot_hbm,
    mid_ref, gains, cos_ref, sin_ref, queries, keys, values, probs,
    out_ref, gtok_ref, OG, OD, OWq, OWo,
    NC, H, vG, vD, MX, PD, PO, YD, ZD, YO, ZO, RCd, RXd, RC, RX, dmid, dA, dj, AT, SM,
    Yq, Zq, RXq, RCo, Yo, Zo, RXo,
    free, rn, syn, szn, ryd, rzd, syd, szd, syo, ryo, szo, rzo,
    scd, rcd, sxd, rxd, sfd, rfd, scg, rcg, sx, rx, sa, ra, sf, *sems,
):
    p = Place()
    r, s, c, y, z = p.r, p.s, p.c, p.y, p.z
    loc = sems[-1]
    spare = loc.at[0]
    q_sums = RowSums(p, spare, H, RC, Yq, Zq, RXq, OWq, sems[0:8], 2176)
    o_sums = RowSums(p, spare, NC, RCo, Yo, Zo, RXo, OWo, sems[8:16], 1536)

    def block(t):
        return NC.at[rows_of(128 * t, 128, 128)]

    def cot_rows(start, size):
        return rows_of(1024 + start, size, 128)

    loads = (
        pltpu.make_async_copy(n_ref, block(s), loc.at[1]),
        pltpu.make_async_copy(c_hbm, NC.at[1024:2048], loc.at[2]),
        pltpu.make_async_copy(g_hbm, vG, loc.at[3]),
        pltpu.make_async_copy(d_hbm, vD.at[0:1120], loc.at[4]),
    )
    for copy in loads:
        copy.start()
    p.greet(range(1, 8))
    g_n = Gather(p, spare, block, lambda t: rn.at[t], szn, syn)
    g_n.start(n_ref)
    vD[1120:1152, :] = jnp.zeros((32, 1536), BF)
    for copy in loads:
        copy.wait()

    def side(P, Y, ssem, rsem, k):
        zz = p.line(k)
        send(P.at[p.theirs(zz)], Y.at[zz], ssem.at[zz], rsem.at[zz], p.side)

    def side_d(k):
        side(PD, YD, syd, ryd, k)

    def line_step(P, Y, Z, ry, sz, rz, k):
        zz = p.line(k)
        t = p.mine(zz)

        def add(ref, sem):
            p.arrived(ref, sem, spare)
            P[t] = (P[t].astype(F32) + ref[...].astype(F32)).astype(BF)

        add(Y.at[zz], ry.at[zz])
        p.reduce_step(
            zz,
            lambda slot: add(Z.at[slot], rz.at[slot]),
            lambda slot, device: send(P.at[t], Z.at[slot], sz.at[zz], rz.at[slot], device),
        )

    def step_d(k):
        line_step(PD, YD, ZD, ryd, szd, rzd, k)

    def side_o(k):
        side(PO, YO, syo, ryo, k)

    def step_o(k):
        line_step(PO, YO, ZO, ryo, szo, rzo, k)

    at_end = (z == 0) | (z == 3)
    in_middle = (z == 1) | (z == 2)
    g_n.step(1)

    @pl.loop(0, 4)
    def _(k):
        zz = p.line(k)
        pl.when(at_end & (k > 0) & (k < 3))(lambda: g_n.step(k + 1))
        pl.when(in_middle & (k < 2))(lambda: g_n.step(k + 2))
        g_n.other(k)
        rows = rows_of(256 * zz, 256, 256)
        X = NC[rows]
        cot = NC[cot_rows(256 * zz, 256)]
        for j in range(3):
            ga, ua = pl.ds(384 * j, 384), pl.ds(1152 + 384 * j, 384)
            gate = dot(X, vG[:, ga])
            up = dot(X, vG[:, ua])
            d_mixed = dot_nt(cot, vD[ga])
            sg = jax.nn.sigmoid(gate)
            active = gate * sg
            d_active = d_mixed * up
            MX[rows, ga] = (active * up).astype(BF)
            H[rows, ga] = (d_active * sg + d_active * active * (1.0 - sg)).astype(BF)
            H[rows, ua] = (d_mixed * active).astype(BF)
        for j in range(3):
            co = pl.ds(512 * j, 512)
            part = dot_nt(H[rows], vG[co]).astype(BF)
            PD[2 * zz, :, co] = part[:128]
            PD[2 * zz + 1, :, co] = part[128:]
        pl.when(k == 2)(lambda: side_d(1))
        pl.when(k == 3)(lambda: side_d(3))
        for j in range(3):
            co = pl.ds(512 * j, 512)
            part = dot(MX[rows], vD[:, co]).astype(BF)
            PO[2 * zz, :, co] = part[:128]
            PO[2 * zz + 1, :, co] = part[128:]

    side_d(2)
    side_d(0)

    def owner(k):
        return 2 * ((z + 1 + k // 2) % 4) + (k % 2) * (2 * y - 1) + 1 - y

    def pair_chip(k):
        t = owner(k)
        for xx in range(2):
            p.arrived(RC.at[t, xx], rcg.at[t, xx], spare)
            q = quarter(t, 2 * xx + c)
            vG[q] = (vG[q].astype(F32) + RC[t, xx].astype(F32)).astype(BF)
        send(vG.at[quarter(t, p.rx)], RX.at[t], sx.at[t], rx.at[t], p.across)

    @pl.loop(0, 5)
    def _(j):
        @pl.when(j < 4)
        def _():
            pair = (z + 1 + j) % 4
            rows = rows_of(384 * pair, 384, 128)
            X = NC[0:1024, rows].T
            for i in range(3):
                co = pl.ds(768 * i, 768)
                vG[rows, co] = dot(X, H[0:1024, co]).astype(BF)
            for i in range(2):
                t = owner(2 * j + i)
                for xx in range(2):
                    send(vG.at[quarter(t, 2 * xx + 1 - c)], RC.at[t, xx], scg.at[t, xx], rcg.at[t, xx], p.core)

        @pl.when(j > 0)
        def _():
            pair_chip(2 * j - 2)
            pair_chip(2 * j - 1)

    pl.semaphore_signal(free, inc=1, device_id=p.core, device_id_type=MESH)

    def chunk(i):
        return rows_of(384 * i, 384, 128)

    def cols(q):
        return rows_of(384 * q, 384, 128)

    held = (
        pltpu.make_async_copy(wo_hbm, NC.at[0:1536], loc.at[1]),
        pltpu.make_async_copy(wq_hbm, H.at[:, 0:2048], loc.at[2]),
        pltpu.make_async_copy(att_hbm, NC.at[1536:1664], loc.at[3]),
        pltpu.make_async_copy(a1_hbm, NC.at[1664:1792], loc.at[4]),
        pltpu.make_async_copy(x_hbm, NC.at[1792:1920], loc.at[5]),
        pltpu.make_async_copy(cot_hbm, NC.at[1920:2048], loc.at[6]),
    )

    def down_terms():
        @pl.loop(0, 3)
        def _(i):
            X = MX[:, chunk(i)].T
            for j in range(3):
                co = pl.ds(512 * j, 512)
                vD[chunk(i), co] = dot(X, NC[1024:2048, co]).astype(BF)
            for xx in range(2):
                q = 2 * xx + 1 - c
                send(vD.at[chunk(i), cols(q)], RCd.at[xx, chunk(i)], scd.at[i, xx], rcd.at[i, xx], p.core)

        g_n.finish()
        for copy in held:
            copy.start()

        @pl.loop(0, 3)
        def _(i):
            for xx in range(2):
                p.arrived(RCd.at[xx, chunk(i)], rcd.at[i, xx], spare)
                q = cols(2 * xx + c)
                vD[chunk(i), q] = (vD[chunk(i), q].astype(F32) + RCd[xx, chunk(i)].astype(F32)).astype(BF)

    def pair_whole(k):
        t = owner(k)
        q = quarter(t, r)
        p.arrived(RX.at[t], rx.at[t], spare)
        vG[q] = (vG[q].astype(F32) + RX[t].astype(F32)).astype(BF)

        if k < 7:
            send(vG.at[q], OG.at[r, s], sa.at[t], ra.at[s, r], p.peer(t))
        else:
            pltpu.make_async_copy(vG.at[q], OG.at[r, s], loc.at[7]).start()

    def share(t):
        v = OG.at[r, t]
        send(v, v, sf.at[t, 0], ra.at[t, r], p.across)
        send(v, v, sf.at[t, 1], ra.at[t, r], p.core)

    def source(k):
        return 2 * ((z + 3 - k // 2) % 4) + (1 - y if k % 2 == 0 else y)

    def take(k):
        t = source(k)
        if k < 7:
            p.arrived(OG.at[r, t], ra.at[t, r], spare)
        else:
            pltpu.make_async_copy(vG.at[quarter(s, r)], OG.at[r, s], loc.at[7]).wait()
        share(t)

    def relay(k):
        t = source(k)
        v = OG.at[p.rx, t]
        p.arrived(v, ra.at[t, p.rx], spare)
        send(v, v, sf.at[t, 2], ra.at[t, p.rx], p.core)

    def down_across(i):
        send(vD.at[chunk(i), cols(p.rx)], RXd.at[chunk(i)], sxd.at[i], rxd.at[i], p.across)

    def down_whole(i):
        p.arrived(RXd.at[chunk(i)], rxd.at[i], spare)
        q = cols(r)
        vD[chunk(i), q] = (vD[chunk(i), q].astype(F32) + RXd[chunk(i)].astype(F32)).astype(BF)
        src, dst = vD.at[chunk(i), q], OD.at[r, chunk(i)]
        pltpu.make_async_copy(src, dst, sfd.at[i, 3]).start()
        send(src, dst, sfd.at[i, 0], rfd.at[i, r], p.across)
        send(src, dst, sfd.at[i, 1], rfd.at[i, r], p.core)

    def down_relay(i):
        v = OD.at[p.rx, chunk(i)]
        p.arrived(v, rfd.at[i, p.rx], spare)
        send(v, v, sfd.at[i, 2], rfd.at[i, p.rx], p.core)

    def back(w):
        return w * cos_ref[...] - pltpu.roll(w, 64, 1) * sin_ref[...]

    kept = {}

    def attention_out():
        for copy in held:
            copy.wait()
        dn, hidden = PD[s].astype(F32), mid_ref[...]
        rstd = inverse_norm(hidden)
        unit = hidden * rstd
        kept["ffn"] = jnp.sum(dn * unit, axis=0, keepdims=True)
        e = dn * gains[1:2, :]
        dm = NC[1920:2048].astype(F32) + rstd * (e - unit * jnp.mean(e * unit, axis=-1, keepdims=True))
        dmid[...] = dm
        NC[1920:2048] = dm.astype(BF)
        AT[...] = NC[1536:1664].T
        for j in range(3):
            part = dot_nt(NC[1920:2048], NC[pl.ds(512 * j, 512)]).astype(BF)
            for i in range(4):
                h = 4 * j + i
                dA[h // 6, pl.ds(128 * (h % 6), 128), :] = part[:, 128 * i : 128 * i + 128]
        for j in range(3):
            co = pl.ds(512 * j, 512)
            NC[0:1536, co] = dot(AT[...], NC[1920:2048, co]).astype(BF)

        @pl.loop(0, 8)
        def _(k):
            o_sums.to_core(o_sums.own(k))

    def heads(g):
        grad, soft = dA[g], probs[g]
        d_probs = dot_nt(grad, values[g])
        d_scores = (soft * (d_probs - jnp.sum(soft * d_probs, axis=-1, keepdims=True))).astype(BF)
        d_values = dot(soft.astype(BF).T, grad)
        d_queries = dot(d_scores, keys[g]) * HEAD_DIMENSION**-0.5
        d_keys = dot(d_scores.T, queries[g])
        for i in range(6):
            dj[:, pl.ds(128 * (6 * g + i), 128)] = back(d_queries[128 * i : 128 * i + 128]).astype(BF)
        dj[:, pl.ds(128 * (12 + g), 128)] = back(d_keys).astype(BF)
        dj[:, pl.ds(128 * (14 + g), 128)] = d_values.astype(BF)

    def attention_in():
        heads(1)
        joined_grad = dj[...]
        bias_grad = jnp.sum(joined_grad.astype(F32), axis=0, keepdims=True)
        x = NC[1792:1920].astype(F32)
        rstd = inverse_norm(x)
        unit = x * rstd
        dn1 = jnp.concatenate(
            [dot_nt(joined_grad, H[pl.ds(512 * j, 512), 0:2048]) for j in range(3)], axis=1
        )
        gain_attn_grad = jnp.sum(dn1 * unit, axis=0, keepdims=True)
        e = dn1 * gains[0:1, :]
        NC[1792:1920] = (
            dmid[...] + rstd * (e - unit * jnp.mean(e * unit, axis=-1, keepdims=True))
        ).astype(BF)
        pltpu.make_async_copy(NC.at[1792:1920], gtok_ref, loc.at[5]).start()
        SM[...] = jnp.zeros_like(SM)
        ffn = kept["ffn"]
        for t in range(8):
            SM[t, 0:1, :] = gain_attn_grad[:, 192 * t : 192 * t + 128]
            SM[t, 1:2, 0:64] = gain_attn_grad[:, 192 * t + 128 : 192 * t + 192]
            SM[t, 2:3, :] = bias_grad[:, 256 * t : 256 * t + 128]
            SM[t, 3:4, :] = bias_grad[:, 256 * t + 128 : 256 * t + 256]
            SM[t, 4:5, :] = ffn[:, 192 * t : 192 * t + 128]
            SM[t, 5:6, 0:64] = ffn[:, 192 * t + 128 : 192 * t + 192]
        AT[...] = NC[1664:1792].T

    def joined_terms():
        pl.semaphore_wait(free, 1)

        @pl.loop(0, 8)
        def _(k):
            t = q_sums.own(k)
            rows = rows_of(192 * t, 192)
            for j in range(2):
                co = pl.ds(1024 * j, 1024)
                H[rows, co] = dot(AT[rows], dj[:, co]).astype(BF)
            H[rows, 2048:2176] = jnp.zeros((192, 128), BF)
            H[rows_of(192 * t, 16), 2048:2176] = SM[t].astype(BF)
            q_sums.to_core(t)

    def on_chip(sums):
        @pl.loop(0, 8)
        def _(k):
            sums.on_chip(k)

    def finish_out():
        PO[s] = (PO[s].astype(F32) + mid_ref[...]).astype(BF)
        pltpu.make_async_copy(PO.at[s], out_ref, loc.at[6]).start()

    def first_heads():
        heads(0)

    def o_on_chip():
        on_chip(o_sums)

    def q_on_chip():
        on_chip(q_sums)


    @pl.when(in_middle)
    def _():
        side_o(3)
        side_o(1)

    step_d(3)
    down_terms()

    @pl.when(at_end)
    def _():
        side_o(3)
        side_o(1)
        step_d(2)
        step_d(1)
        pair_whole(6)
        step_o(3)
        pair_whole(7)
        pair_whole(5)


    @pl.when(in_middle)
    def _():
        step_d(2)
        step_d(1)
        pair_whole(6)
        pair_whole(7)
        pair_whole(5)
        down_across(0)

    pair_whole(1)
    down_across(1)
    step_d(0)
    attention_out()
    down_across(2)

    @pl.when(at_end)
    def _():
        pair_whole(4)
        pair_whole(3)

    o_on_chip()

    @pl.when(at_end)
    def _():
        down_across(0)
        o_sums.aside(1)
        take(1)
        o_sums.aside(0)
        o_sums.aside(2)


    @pl.when(in_middle)
    def _():
        o_sums.aside(1)
        take(1)
        o_sums.aside(0)
        o_sums.aside(2)
        pair_whole(0)
        take(7)
        take(6)

    first_heads()
    take(5)
    pair_whole(2)

    @pl.when(at_end)
    def _():
        pair_whole(0)
        take(6)


    @pl.when(in_middle)
    def _():
        down_whole(1)

    attention_in()
    joined_terms()

    @pl.when(at_end)
    def _():
        o_sums.aside(3)


    @pl.when(in_middle)
    def _():
        pair_whole(4)
        o_sums.aside(3)
        pair_whole(3)

    down_whole(0)
    relay(5)
    q_on_chip()

    @pl.when(at_end)
    def _():
        q_sums.aside(0)
        o_sums.on_line(0)
        take(4)
        q_sums.aside(1)
        o_sums.on_line(1)
        take(0)
        take(7)
        o_sums.on_line(2)
        q_sums.on_line(0)
        q_sums.aside(2)
        side_o(2)
        down_whole(1)
        take(3)
        down_whole(2)
        q_sums.aside(3)
        relay(4)
        take(2)
        q_sums.on_line(1)
        relay(6)
        down_relay(0)
        q_sums.on_line(2)
        o_sums.on_line(3)
        relay(0)
        side_o(0)
        relay(2)
        down_relay(1)
        relay(3)
        o_sums.at_owner()
        step_o(2)
        relay(7)
        relay(1)
        step_o(1)
        q_sums.on_line(3)
        q_sums.at_owner()
        step_o(0)
        finish_out()
        down_relay(2)
        o_sums.spread()
        q_sums.spread()


    @pl.when(in_middle)
    def _():
        take(4)
        q_sums.aside(1)
        step_o(3)
        o_sums.on_line(0)
        take(0)
        o_sums.on_line(1)
        q_sums.aside(0)
        o_sums.on_line(2)
        q_sums.aside(2)
        down_whole(2)
        q_sums.aside(3)
        q_sums.on_line(0)
        take(2)
        q_sums.on_line(1)
        relay(6)
        relay(2)
        side_o(2)
        down_relay(0)
        o_sums.on_line(3)
        down_relay(1)
        o_sums.at_owner()
        take(3)
        relay(4)
        q_sums.on_line(2)
        down_relay(2)
        o_sums.spread()
        q_sums.on_line(3)
        relay(1)
        step_o(1)
        relay(0)
        relay(3)
        side_o(0)
        q_sums.at_owner()
        step_o(2)
        q_sums.spread()
        relay(7)
        step_o(0)
        finish_out()


    o_sums.finish()
    q_sums.finish()
    pltpu.make_async_copy(NC.at[1792:1920], gtok_ref, loc.at[5]).wait()
    pltpu.make_async_copy(PO.at[s], out_ref, loc.at[6]).wait()

    @pl.loop(0, 3)
    def _(i):
        for q in (p.rc, p.rd):
            p.arrived(OD.at[q, chunk(i)], rfd.at[i, q], spare)
        for d in range(3):
            p.sent(OD.at[r, chunk(i)], sfd.at[i, d], spare)
        pltpu.make_async_copy(OD.at[r, chunk(i)], OD.at[r, chunk(i)], sfd.at[i, 3]).wait()
        for xx in range(2):
            p.sent(RCd.at[xx, chunk(i)], scd.at[i, xx], spare)
        p.sent(RXd.at[chunk(i)], sxd.at[i], spare)

    @pl.loop(0, 8)
    def _(t):
        for q in (p.rc, p.rd):
            p.arrived(OG.at[q, t], ra.at[t, q], spare)
        for d in range(3):
            p.sent(OG.at[r, t], sf.at[t, d], spare)
        for xx in range(2):
            p.sent(RC.at[t, xx], scg.at[t, xx], spare)
        p.sent(RX.at[t], sx.at[t], spare)

        @pl.when(t != s)
        def _():
            p.sent(OG.at[r, s], sa.at[t], spare)

    @pl.loop(0, 4)
    def _(i):
        p.sent(YD.at[i], syd.at[i], spare)
        p.sent(YO.at[i], syo.at[i], spare)

        @pl.when(i != z)
        def _():
            p.sent(ZD.at[i], szd.at[i], spare)
            p.sent(ZO.at[i], szo.at[i], spare)


def layer_back(*args):
    return pl.pallas_call(
        layer_back_body,
        out_shape=(
            shaped(128, 1536), shaped(128, 1536), shaped(4, 8, 48, 2304), shaped(4, 1152, 384), shaped(4, 48, 2176),
            shaped(4, 48, 1536),
        ),
        in_specs=[HBM] * 10 + [VMEM] * 8,
        out_specs=(HBM,) * 6,
        scratch_shapes=[
            low(2048, 1536), low(1536, 2304), low(1536, 2304), low(1152, 1536), low(1024, 1152),
            low(8, 128, 1536), low(8, 128, 1536), low(4, 128, 1536), low(5, 128, 1536), low(4, 128, 1536), low(5, 128, 1536),
            low(2, 1152, 384), low(1152, 384), low(8, 2, 48, 2304), low(8, 48, 2304),
            full(128, 1536), low(2, 768, 128), low(128, 2048), low(1536, 128), full(8, 16, 128),
            *RowSums.buffers(2176)[1:], *RowSums.buffers(1536),
            pltpu.SemaphoreType.REGULAR, DMA((8,)), DMA((4,)), DMA((4, 2)),
            DMA((4,)), DMA((5,)), DMA((4,)), DMA((4,)), DMA((4,)), DMA((4,)), DMA((4,)), DMA((5,)),
            DMA((3, 2)), DMA((3, 2)), DMA((3,)), DMA((3,)), DMA((3, 4)), DMA((3, 4)),
            DMA((8, 2)), DMA((8, 2)), DMA((8,)), DMA((8,)), DMA((8,)), DMA((8, 4)), DMA((8, 3)),
            *RowSums.semaphores(), *RowSums.semaphores(), DMA((8,)),
        ],
        compiler_params=pltpu.CompilerParams(collective_id=1, has_side_effects=True, vmem_limit_bytes=64 << 20),
        name="layer_back",
    )(*args)


def widen_body(g_ref, d_ref, q_ref, o_ref, gate, up, down, qkv, out):
    for t in range(8):
        gate[:, 1120 * t : 1120 * t + 1120] = g_ref[0, t, :, 0:1120].astype(F32)
        up[:, 1120 * t : 1120 * t + 1120] = g_ref[0, t, :, 1152:2272].astype(F32)
    down[...] = d_ref[0, 0:1120, :].astype(F32)
    qkv[...] = q_ref[0, :, 0:2048].astype(F32)
    out[...] = o_ref[0].astype(F32)


def widen(g, d, q, o):
    return pl.pallas_call(
        widen_body,
        grid=(4,),
        out_shape=(
            shaped(192, 8960, dtype=F32), shaped(192, 8960, dtype=F32), shaped(1120, 1536, dtype=F32),
            shaped(192, 2048, dtype=F32), shaped(192, 1536, dtype=F32),
        ),
        in_specs=[
            pl.BlockSpec((1, 8, 48, 2304), lambda i: (i, 0, 0, 0)),
            pl.BlockSpec((1, 1152, 384), lambda i: (i, 0, 0)),
            pl.BlockSpec((1, 48, 2176), lambda i: (i, 0, 0)),
            pl.BlockSpec((1, 48, 1536), lambda i: (i, 0, 0)),
        ],
        out_specs=(
            pl.BlockSpec((48, 8960), lambda i: (i, 0)),
            pl.BlockSpec((48, 8960), lambda i: (i, 0)),
            pl.BlockSpec((1120, 384), lambda i: (0, i)),
            pl.BlockSpec((48, 2048), lambda i: (i, 0)),
            pl.BlockSpec((48, 1536), lambda i: (i, 0)),
        ),
        compiler_params=pltpu.CompilerParams(vmem_limit_bytes=62 << 20),
        name="widen",
    )(g, d, q, o)


def shards_eight(
    tokens, segments, gain_attn, w_qkv, b_qkv, w_out, gain_ffn, w_gate, w_up, w_down, cotangent
):
    x, cot = tokens[0], cotangent[0]
    WQ, WO, G, C, cosine, sine, gains, queries, keys, values, probs, att, a1, mid, a2 = gather_weights(
        x, segments, gain_attn[None], b_qkv[None], gain_ffn[None], w_qkv, w_out, w_gate, w_up, cot
    )
    out, grad_tokens, gate_up, down, qkv, o = layer_back(
        a2, C, G, w_down, WQ, WO, att, a1, x, cot, mid, gains, cosine, sine, queries, keys, values, probs
    )
    gate, up, down, qkv_rows, out_rows = widen(gate_up, down, qkv, o)
    small = qkv[0, 0:6, 2048:].astype(F32).reshape(768)
    return (
        out[None], grad_tokens[None], small[0:192], qkv_rows, small[256:512], out_rows, small[512:704], gate, up, down,
    )


def solution(mesh):
    placed = (
        P(("replica", "shard"), None, None),
        P(("replica", "shard"), None),
        P("shard"),
        P("shard", None),
        P("shard"),
        P("shard", None),
        P("shard"),
        P("shard", None),
        P("shard", None),
        P("shard", None),
        P(("replica", "shard"), None, None),
    )
    return jax.shard_map(
        shards_eight if (mesh.shape["replica"], mesh.shape["shard"]) == (4, 8) else shards,
        mesh=mesh,
        in_specs=placed,
        out_specs=(
            P(("replica", "shard"), None, None),
            P(("replica", "shard"), None, None),
            P("shard"),
            P("shard", None),
            P("shard"),
            P("shard", None),
            P("shard"),
            P("shard", None),
            P("shard", None),
            P("shard", None),
        ),
        check_vma=False,
    )
```

```python
import math

import jax
import jax.numpy as jnp
from jax import lax
from jax.experimental import pallas as pl
from jax.experimental.pallas import tpu as pltpu
from jax.sharding import PartitionSpec as P

QUERY_HEADS = 12
KEY_VALUE_HEADS = 2
HEAD_DIMENSION = 128


eps_norm = 1e-06
rope_base = 1000000.0


def tables(segment_ids, head_size):
    token_length = segment_ids.shape[-1]
    row_index = jnp.arange(token_length, dtype=jnp.int32)
    earlier = jnp.sum(
        (segment_ids[..., None, :] < segment_ids[..., :, None]).astype(jnp.int32),
        axis=-1,
        dtype=jnp.int32,
    )
    positions = (row_index - earlier).astype(jnp.float32)
    frequencies = jnp.exp(
        jnp.arange(head_size // 2, dtype=jnp.float32) * (-2.0 * math.log(rope_base) / head_size)
    )
    angles = positions[..., None] * frequencies
    cosine = jnp.concatenate([jnp.cos(angles), jnp.cos(angles)], axis=-1)
    sine_vals = jnp.concatenate([jnp.sin(angles), jnp.sin(angles)], axis=-1)
    allowed = (
        (segment_ids[..., None, :] == segment_ids[..., :, None])
        & (row_index[None, :] <= row_index[:, None])
    ).astype(jnp.int32)
    return (cosine, sine_vals, allowed)


def apply_rotation(values, cosine, sine_vals):
    halfway = values.shape[-1] // 2
    turned = jnp.concatenate([-values[..., halfway:], values[..., :halfway]], axis=-1)
    return values * cosine + turned * sine_vals


def rotate_back(values, cosine, sine_vals):
    halfway = values.shape[-1] // 2
    shifted = values * sine_vals
    return values * cosine + jnp.concatenate(
        [shifted[..., halfway:], -shifted[..., :halfway]], axis=-1
    )


def norm_forward(hidden, gain_vec):
    rstd_rows = lax.rsqrt(jnp.mean(hidden * hidden, axis=-1, keepdims=True) + eps_norm)
    unit_rows = hidden * rstd_rows
    return (unit_rows * gain_vec, unit_rows, rstd_rows)


def norm_backward(grad_in, gain_vec, unit_rows, rstd_rows):
    inner_grad = grad_in * gain_vec
    return rstd_rows * (
        inner_grad - unit_rows * jnp.mean(inner_grad * unit_rows, axis=-1, keepdims=True)
    )


def column_term(left_side, right_side):
    return jnp.einsum("lf,ld->fd", left_side, right_side, preferred_element_type=jnp.float32)


def to_columns(rows):
    ranks = lax.axis_size("shard")
    depth, width = rows.shape
    split = rows.reshape(depth, ranks, width // ranks).transpose(1, 0, 2)
    return lax.all_to_all(split, "shard", 0, 0, tiled=True).reshape(ranks * depth, width // ranks)


def to_rows(columns):
    ranks, copies = lax.axis_size("shard"), lax.axis_size("replica")
    depth, width = columns.shape
    depth = depth // ranks
    parts = columns.reshape(ranks, copies, depth // copies, width)
    part = lax.psum_scatter(parts, "replica", scatter_dimension=1, tiled=False)
    part = lax.all_to_all(part, "shard", 0, 0, tiled=True)
    part = part.transpose(1, 0, 2).reshape(depth // copies, ranks * width)
    return lax.all_gather(part, "replica", axis=0, tiled=True)


def shards(
    tokens, segments, gain_attn, w_qkv, b_qkv, w_out, gain_ffn, w_gate, w_up, w_down, cotangent
):
    heads_per_group = QUERY_HEADS // KEY_VALUE_HEADS
    head_dimension = QUERY_HEADS * HEAD_DIMENSION
    key_value_limit = head_dimension + KEY_VALUE_HEADS * HEAD_DIMENSION
    logit_scale = HEAD_DIMENSION ** (-0.5)
    token_length = tokens.shape[1]
    full_gain_attn, full_qkv, full_bias, full_out, full_gain_ffn = (
        lax.all_gather(gain_attn, "shard", axis=0, tiled=True),
        lax.all_gather(w_qkv, "shard", axis=0, tiled=True),
        lax.all_gather(b_qkv, "shard", axis=0, tiled=True),
        lax.all_gather(w_out, "shard", axis=0, tiled=True),
        lax.all_gather(gain_ffn, "shard", axis=0, tiled=True),
    )
    gate_columns = to_columns(w_gate)
    up_columns = to_columns(w_up)
    all_cot = lax.all_gather(cotangent[0], "shard", axis=0, tiled=True)
    gain_first = full_gain_attn.astype(jnp.float32)
    gain_second = full_gain_ffn.astype(jnp.float32)
    cosine, sine_vals, allowed = tables(segments[0], HEAD_DIMENSION)
    cosine_per_head = cosine[:, None, :]
    sine_per_head = sine_vals[:, None, :]
    inputs = tokens[0].astype(jnp.float32)
    normed_first, unit_first, rstd_first = norm_forward(inputs, gain_first)
    acts_first = normed_first.astype(jnp.bfloat16)
    joined_projection = jnp.dot(
        acts_first, full_qkv, preferred_element_type=jnp.float32
    ) + full_bias.astype(jnp.float32)
    query_rows = apply_rotation(
        joined_projection[:, :head_dimension].reshape(token_length, QUERY_HEADS, HEAD_DIMENSION),
        cosine_per_head,
        sine_per_head,
    )
    query_reduced = (
        (query_rows * logit_scale)
        .astype(jnp.bfloat16)
        .reshape(token_length, KEY_VALUE_HEADS, heads_per_group, HEAD_DIMENSION)
    )
    k_low = apply_rotation(
        joined_projection[:, head_dimension:key_value_limit].reshape(
            token_length, KEY_VALUE_HEADS, HEAD_DIMENSION
        ),
        cosine_per_head,
        sine_per_head,
    ).astype(jnp.bfloat16)
    value_reduced = (
        joined_projection[:, key_value_limit:]
        .reshape(token_length, KEY_VALUE_HEADS, HEAD_DIMENSION)
        .astype(jnp.bfloat16)
    )
    scores = jnp.einsum("ikrd,jkd->krij", query_reduced, k_low, preferred_element_type=jnp.float32)
    scores = jnp.where(allowed != 0, scores, -1e30)
    largest = jnp.max(scores, axis=-1, keepdims=True)
    exponents = jnp.exp(scores - largest)
    soft_probs = exponents / jnp.sum(exponents, axis=-1, keepdims=True)
    soft_low = soft_probs.astype(jnp.bfloat16)
    attended = jnp.einsum(
        "krij,jkd->ikrd", soft_low, value_reduced, preferred_element_type=jnp.float32
    )
    attended = attended.reshape(token_length, head_dimension).astype(jnp.bfloat16)
    hidden_mid = inputs + jnp.dot(attended, full_out, preferred_element_type=jnp.float32)
    normed_second, unit_second, rstd_second = norm_forward(hidden_mid, gain_second)
    acts_second = normed_second.astype(jnp.bfloat16)
    all_acts = lax.all_gather(acts_second, "shard", axis=0, tiled=True)
    gate_vals = jnp.dot(all_acts, gate_columns, preferred_element_type=jnp.float32)
    up_vals = jnp.dot(all_acts, up_columns, preferred_element_type=jnp.float32)
    sigmoid_gate = jax.nn.sigmoid(gate_vals)
    active = gate_vals * sigmoid_gate
    mixed_hidden = (active * up_vals).astype(jnp.bfloat16)
    d_mixed = jnp.einsum("ld,fd->lf", all_cot, w_down, preferred_element_type=jnp.float32)
    d_active = d_mixed * up_vals
    d_gate = (
        d_active * sigmoid_gate + d_active * gate_vals * sigmoid_gate * (1.0 - sigmoid_gate)
    ).astype(jnp.bfloat16)
    d_up = (d_mixed * active).astype(jnp.bfloat16)
    d_normed_part = jnp.einsum("lf,df->ld", d_gate, gate_columns, preferred_element_type=jnp.float32)
    d_normed_part = d_normed_part + jnp.einsum(
        "lf,df->ld", d_up, up_columns, preferred_element_type=jnp.float32
    )
    d_normed_second = lax.psum_scatter(
        d_normed_part.astype(jnp.bfloat16), "shard", scatter_dimension=0, tiled=True
    ).astype(jnp.float32)
    down_part = jnp.dot(mixed_hidden, w_down, preferred_element_type=jnp.float32)
    result = (
        hidden_mid
        + lax.psum_scatter(
            down_part.astype(jnp.bfloat16), "shard", scatter_dimension=0, tiled=True
        ).astype(jnp.float32)
    ).astype(jnp.bfloat16)
    grad_out = cotangent[0]
    down_grad = column_term(mixed_hidden, all_cot).astype(jnp.bfloat16)
    gate_grad = to_rows(column_term(all_acts, d_gate).astype(jnp.bfloat16))
    up_grad = to_rows(column_term(all_acts, d_up).astype(jnp.bfloat16))
    gain_second_grad = jnp.sum(d_normed_second * unit_second, axis=0)
    d_hidden_mid = grad_out.astype(jnp.float32) + norm_backward(
        d_normed_second, gain_second, unit_second, rstd_second
    )
    d_branch = d_hidden_mid.astype(jnp.bfloat16)
    out_grad_term = jnp.einsum("le,ld->ed", attended, d_branch, preferred_element_type=jnp.float32)
    attended_gradient = jnp.einsum(
        "ld,ed->le", d_branch, full_out, preferred_element_type=jnp.float32
    )
    attended_gradient = attended_gradient.astype(jnp.bfloat16).reshape(
        token_length, KEY_VALUE_HEADS, heads_per_group, HEAD_DIMENSION
    )
    d_probs = jnp.einsum(
        "ikrd,jkd->krij", attended_gradient, value_reduced, preferred_element_type=jnp.float32
    )
    value_gradient = jnp.einsum(
        "krij,ikrd->jkd", soft_low, attended_gradient, preferred_element_type=jnp.float32
    )
    d_scores = soft_probs * (d_probs - jnp.sum(soft_probs * d_probs, axis=-1, keepdims=True))
    d_scores_low = d_scores.astype(jnp.bfloat16)
    d_queries = jnp.einsum(
        "krij,jkd->ikrd", d_scores_low, k_low, preferred_element_type=jnp.float32
    )
    d_queries = rotate_back(
        d_queries.reshape(token_length, QUERY_HEADS, HEAD_DIMENSION) * logit_scale,
        cosine_per_head,
        sine_per_head,
    )
    key_gradient = jnp.einsum(
        "krij,ikrd->jkd", d_scores_low, query_reduced, preferred_element_type=jnp.float32
    )
    key_gradient = rotate_back(key_gradient, cosine_per_head, sine_per_head)
    d_joined = jnp.concatenate(
        [
            d_queries.reshape(token_length, head_dimension),
            key_gradient.reshape(token_length, KEY_VALUE_HEADS * HEAD_DIMENSION),
            value_gradient.reshape(token_length, KEY_VALUE_HEADS * HEAD_DIMENSION),
        ],
        axis=1,
    ).astype(jnp.bfloat16)
    bias_grad_term = jnp.sum(d_joined.astype(jnp.float32), axis=0)
    qkv_grad_term = jnp.einsum(
        "ld,le->de", acts_first, d_joined, preferred_element_type=jnp.float32
    )
    d_normed_first = jnp.einsum("le,de->ld", d_joined, full_qkv, preferred_element_type=jnp.float32)
    gain_first_grad = jnp.sum(d_normed_first * unit_first, axis=0)
    d_inputs = d_hidden_mid + norm_backward(d_normed_first, gain_first, unit_first, rstd_first)
    owned = (
        lax.psum_scatter(
            gain_first_grad.astype(jnp.bfloat16), "shard", scatter_dimension=0, tiled=True
        ).astype(jnp.float32),
        lax.psum_scatter(
            qkv_grad_term.astype(jnp.bfloat16), "shard", scatter_dimension=0, tiled=True
        ).astype(jnp.float32),
        lax.psum_scatter(
            bias_grad_term.astype(jnp.bfloat16), "shard", scatter_dimension=0, tiled=True
        ).astype(jnp.float32),
        lax.psum_scatter(
            out_grad_term.astype(jnp.bfloat16), "shard", scatter_dimension=0, tiled=True
        ).astype(jnp.float32),
        lax.psum_scatter(
            gain_second_grad.astype(jnp.bfloat16), "shard", scatter_dimension=0, tiled=True
        ).astype(jnp.float32),
    )
    summed = (
        lax.psum(owned[0].astype(jnp.bfloat16), "replica").astype(jnp.float32),
        lax.psum(owned[1].astype(jnp.bfloat16), "replica").astype(jnp.float32),
        lax.psum(owned[2].astype(jnp.bfloat16), "replica").astype(jnp.float32),
        lax.psum(owned[3].astype(jnp.bfloat16), "replica").astype(jnp.float32),
        lax.psum(owned[4].astype(jnp.bfloat16), "replica").astype(jnp.float32),
        gate_grad.astype(jnp.float32),
        up_grad.astype(jnp.float32),
        lax.psum(down_grad, "replica").astype(jnp.float32),
    )
    return (
        result[None],
        d_inputs.astype(jnp.bfloat16)[None],
        summed[0],
        summed[1],
        summed[2],
        summed[3],
        summed[4],
        summed[5],
        summed[6],
        summed[7],
    )


MESH = pl.DeviceIdType.MESH
BF, F32 = jnp.bfloat16, jnp.float32
HBM = pl.BlockSpec(memory_space=pl.ANY)
VMEM = pl.BlockSpec(memory_space=pltpu.VMEM)
DMA = pltpu.SemaphoreType.DMA


def shaped(*shape, dtype=BF):
    return jax.ShapeDtypeStruct(shape, dtype)


def low(*shape):
    return pltpu.VMEM(shape, BF)


def full(*shape):
    return pltpu.VMEM(shape, F32)


def dot(a, b):
    return lax.dot_general(a, b, (((1,), (0,)), ((), ())), preferred_element_type=F32)


def dot_nt(a, b):
    return lax.dot_general(a, b, (((1,), (1,)), ((), ())), preferred_element_type=F32)


def rows_of(start, size, unit=16):
    return pl.ds(pl.multiple_of(start, unit), size)


def quarter(t, q):
    return rows_of(192 * t + 48 * q, 48)


def send(src, dst, send_sem, recv_sem, device):
    copy = pltpu.make_async_remote_copy(
        src_ref=src, dst_ref=dst, send_sem=send_sem, recv_sem=recv_sem, device_id=device, device_id_type=MESH
    )
    copy.start()


class Place:
    def __init__(self):
        self.r = r = lax.axis_index("replica")
        self.s = s = lax.axis_index("shard")
        self.x, self.c, self.z, self.y = r // 2, r % 2, s // 2, s % 2
        self.rc, self.rx, self.rd = r + 1 - 2 * self.c, (r + 2) % 4, 3 - r
        self.core, self.across, self.side = (self.rc, s), (self.rx, s), (r, s + 1 - 2 * self.y)

    def peer(self, t):
        return (self.r, t)

    def line(self, k):
        near = self.z + (1 - 2 * (self.z % 2)) * (k % 2)
        far = k + (self.z // 2) * (3 - 2 * k)
        return (1 - k // 2) * near + (k // 2) * far

    def onward(self, zz, copy):
        pl.when((zz <= self.z) & (self.z < 3))(lambda: copy(0, self.peer(self.s + 2)))
        pl.when((zz >= self.z) & (self.z > 0))(lambda: copy(1, self.peer(self.s - 2)))

    def went_onward(self, zz, wait):
        pl.when((zz <= self.z) & (self.z < 3))(lambda: wait(0))
        pl.when((zz >= self.z) & (self.z > 0))(lambda: wait(1))

    def reduce_step(self, zz, add, hand):
        pl.when((zz >= self.z) & (self.z > 0))(lambda: add(zz))
        pl.when((zz < self.z) & (self.z < 3))(lambda: add(zz))
        pl.when((zz == self.z) & (self.z < 3))(lambda: add(4))
        pl.when(zz > self.z)(lambda: hand(zz, self.peer(self.s + 2)))
        pl.when(zz < self.z - 1)(lambda: hand(zz, self.peer(self.s - 2)))
        pl.when(zz == self.z - 1)(lambda: hand(4, self.peer(self.s - 2)))

    def mine(self, zz):
        return 2 * zz + self.y

    def theirs(self, zz):
        return 2 * zz + 1 - self.y

    def greet(self, steps):
        bar = pltpu.get_barrier_semaphore()
        devices = [self.core, self.across] + [(self.r, (self.s + k) % 8) for k in steps]
        for device in devices:
            pl.semaphore_signal(bar, inc=1, device_id=device, device_id_type=MESH)
        pl.semaphore_wait(bar, len(devices))

    def arrived(self, ref, sem, spare):
        pltpu.make_async_remote_copy(
            src_ref=ref, dst_ref=ref, send_sem=spare, recv_sem=sem, device_id=self.core, device_id_type=MESH
        ).wait_recv()

    def sent(self, ref, sem, spare):
        pltpu.make_async_remote_copy(
            src_ref=ref, dst_ref=ref, send_sem=sem, recv_sem=spare, device_id=self.core, device_id_type=MESH
        ).wait_send()


def inverse_norm(v):
    return lax.rsqrt(jnp.mean(v * v, axis=-1, keepdims=True) + eps_norm)


class Gather:
    def __init__(self, p, spare, view, arrivals, along, aside):
        self.p, self.spare, self.view = p, spare, view
        self.arrivals, self.along, self.aside = arrivals, along, aside

    def move(self, src, t, zz):
        p, dst, sem = self.p, self.view(t), self.arrivals(t)
        p.onward(zz, lambda d, device: send(src, dst, self.along.at[zz, d], sem, device))
        send(src, dst, self.aside.at[zz], sem, p.side)

    def start(self, src):
        self.move(src, self.p.s, self.p.z)

    def wait(self, t):
        self.p.arrived(self.view(t), self.arrivals(t), self.spare)

    def step(self, k, then=None):
        zz = self.p.line(k)
        t = self.p.mine(zz)
        self.wait(t)
        self.move(self.view(t), t, zz)
        if then is not None:
            then(t)

    def other(self, k, then=None):
        t = self.p.theirs(self.p.line(k))
        self.wait(t)
        if then is not None:
            then(t)

    def finish(self):
        block = self.view(self.p.s)
        for zz in range(4):
            self.p.sent(block, self.aside.at[zz], self.spare)
            self.p.went_onward(zz, lambda d: self.p.sent(block, self.along.at[zz, d], self.spare))


def gather_body(
    x_ref, seg_ref, ga_ref, bq_ref, gf_ref, wq_ref, wo_ref, wg_ref, wu_ref, c_ref,
    WQ_out, WO_out, G, C, cos_ref, sin_ref, gains, queries, keys, values, probs, att, a1, mid, a2,
    WQ, WO, vg, vu, GS, CS, S, bias,
    rq, ro, rg, rc, rs, szq, syq, sdq, szo, syo, sdo, sg, sdg, scz, scy, ss, loc,
):
    p = Place()
    r, s, c, z = p.r, p.s, p.c, p.z
    spare = loc.at[0]
    own = rows_of(192 * s, 192)
    own_c = rows_of(128 * s, 128, 128)
    loads = (
        pltpu.make_async_copy(wq_ref, WQ.at[own], loc.at[1]),
        pltpu.make_async_copy(wo_ref, WO.at[own], loc.at[2]),
        pltpu.make_async_copy(wg_ref, vg, loc.at[3]),
        pltpu.make_async_copy(wu_ref, vu, loc.at[4]),
        pltpu.make_async_copy(c_ref, CS, loc.at[5]),
    )
    for copy in loads:
        copy.start()
    p.greet(range(1, 8))
    gap = jnp.zeros((1, 64), F32)
    small = jnp.concatenate(
        [ga_ref[...].astype(F32)[None], gap, bq_ref[...].astype(F32)[None], gf_ref[...].astype(F32)[None], gap],
        axis=1,
    )
    S[s] = jnp.broadcast_to(small, (16, 768)).astype(BF)

    def vq(t, q):
        return WQ.at[quarter(t, q)]

    def vo(t, h):
        return WO.at[rows_of(192 * t + 96 * h, 96)]

    def gq(t, q):
        return G.at[quarter(t, q)]

    def cot_block(t):
        return C.at[rows_of(128 * t, 128, 128)]

    g_q = Gather(p, spare, lambda t: vq(t, r), lambda t: rq.at[t, r], szq, syq)
    g_o = Gather(p, spare, lambda t: vo(t, c), lambda t: ro.at[t, c], szo, syo)
    g_c = Gather(p, spare, cot_block, lambda t: rc.at[t], scz, scy)
    g_q.start(wq_ref.at[rows_of(48 * r, 48)])
    for k in range(1, 8):
        t = (s + k) % 8
        send(S.at[s], S.at[s], ss.at[t], rs.at[s], p.peer(t))

    def share(view, sems, rsems):
        def to_replicas(t):
            v = view(t, r)
            send(v, v, sems.at[t, 0], rsems.at[t, r], p.across)
            send(v, v, sems.at[t, 1], rsems.at[t, r], p.core)

        return to_replicas

    def relay(view, sems, rsems, t):
        v = view(t, p.rx)
        p.arrived(v, rsems.at[t, p.rx], spare)
        send(v, v, sems.at[t, 2], rsems.at[t, p.rx], p.core)

    def from_core(view, rsems):
        @pl.loop(1, 8)
        def _(k):
            t = (s + k) % 8
            p.arrived(view(t, p.rc), rsems.at[t, p.rc], spare)
            p.arrived(view(t, p.rd), rsems.at[t, p.rd], spare)

    share_q, share_g = share(vq, sdq, rq), share(gq, sdg, rg)

    def share_o(t):
        send(vo(t, c), vo(t, c), sdo.at[t], ro.at[t, c], p.core)

    for copy in loads:
        copy.wait()
    zeros = jnp.zeros((192, 32), BF)
    for t in range(8):
        GS[t, :, 0:1120] = vg[:, 1120 * t : 1120 * t + 1120]
        GS[t, :, 1120:1152] = zeros
        GS[t, :, 1152:2272] = vu[:, 1120 * t : 1120 * t + 1120]
        GS[t, :, 2272:2304] = zeros
    across = jnp.broadcast_to(seg_ref[...].astype(F32), (128, 128))
    down = across.T
    row = lax.broadcasted_iota(jnp.int32, (128, 128), 0)
    column = lax.broadcasted_iota(jnp.int32, (128, 128), 1)
    earlier = jnp.sum(jnp.where(across < down, 1.0, 0.0), axis=1, keepdims=True)
    position = row.astype(F32) - earlier
    half = (column - 64 * (column // 64)).astype(F32)
    angle = position * jnp.exp(half * (-2.0 * math.log(rope_base) / HEAD_DIMENSION))
    cos_ref[...] = jnp.cos(angle)
    sin_ref[...] = jnp.where(column < 64, -1.0, 1.0) * jnp.sin(angle)
    open_to = (across == down) & (column <= row)
    g_q.step(1, share_q)
    g_q.other(0, share_q)
    g_q.step(2, share_q)
    g_q.other(1, share_q)
    g_q.step(3, share_q)
    g_o.start(wo_ref.at[rows_of(96 * c, 96)])
    turns = (4, 1, 6, 3, 2, 5, 7)

    def give_g(i):
        t = (s + turns[i]) % 8
        send(GS.at[t, rows_of(48 * r, 48)], gq(s, r), sg.at[t], rg.at[s, r], p.peer(t))

    def take_g(i):
        t = (s + 8 - turns[i]) % 8
        p.arrived(gq(t, r), rg.at[t, r], spare)
        share_g(t)

    own_out = (
        pltpu.make_async_copy(GS.at[s], G.at[own], loc.at[1]),
        pltpu.make_async_copy(CS, C.at[own_c], loc.at[2]),
    )
    for copy in own_out:
        copy.start()
    g_q.other(2, share_q)
    give_g(0)
    g_q.other(3, share_q)
    give_g(1)

    @pl.loop(1, 8)
    def _(k):
        t = (s + k) % 8
        p.arrived(S.at[t], rs.at[t], spare)

    for t in range(8):
        row = S[t, 0:1, :].astype(F32)
        gains[0:1, 192 * t : 192 * t + 192] = row[:, 0:192]
        bias[0:1, 256 * t : 256 * t + 256] = row[:, 256:512]
        gains[1:2, 192 * t : 192 * t + 192] = row[:, 512:704]
    x = x_ref[...].astype(F32)
    a1[...] = (x * inverse_norm(x) * gains[0:1, :]).astype(BF)

    def relay_q(t):
        relay(vq, sdq, rq, t)

    g_o.step(1, share_o)
    give_g(2)
    g_o.other(0, share_o)
    relay_q(p.mine(p.line(1)))
    relay_q(p.theirs(p.line(0)))
    g_o.step(2, share_o)
    give_g(3)
    g_o.other(1, share_o)
    relay_q(p.mine(p.line(2)))
    relay_q(p.theirs(p.line(1)))
    g_o.step(3, share_o)
    give_g(4)
    g_c.start(CS)
    take_g(0)
    take_g(1)
    relay_q(p.mine(p.line(3)))
    relay_q(p.theirs(p.line(2)))
    relay_q(p.theirs(p.line(3)))
    take_g(2)
    give_g(5)
    give_g(6)
    from_core(vq, rq)
    cosine, sine = cos_ref[...], sin_ref[...]
    for j in range(4):
        co = pl.ds(512 * j, 512)
        joined = dot(a1[...], WQ[:, co]) + bias[0:1, co]
        for i in range(4):
            h = 4 * j + i
            u = joined[:, 128 * i : 128 * i + 128]
            if h < 14:
                u = u * cosine + pltpu.roll(u, 64, 1) * sine
            if h < 12:
                queries[h // 6, pl.ds(128 * (h % 6), 128), :] = (u * HEAD_DIMENSION**-0.5).astype(BF)
            elif h < 14:
                keys[h - 12] = u.astype(BF)
            else:
                values[h - 14] = u.astype(BF)
    save = (pltpu.make_async_copy(WQ, WQ_out, loc.at[3]), pltpu.make_async_copy(WO, WO_out, loc.at[4]))
    save[0].start()
    for g in range(2):
        scores = dot_nt(queries[g], keys[g]).reshape(6, 128, 128)
        scores = jnp.where(open_to[None], scores, -1e30)
        ex = jnp.exp(scores - jnp.max(scores, axis=-1, keepdims=True))
        soft = (ex / jnp.sum(ex, axis=-1, keepdims=True)).reshape(768, 128)
        probs[g] = soft.astype(BF)
        out = dot(probs[g], values[g]).astype(BF)
        for i in range(6):
            att[:, pl.ds(128 * (6 * g + i), 128)] = out[128 * i : 128 * i + 128]

    for i in (3, 4):
        take_g(i)
    g_o.other(2, share_o)
    g_o.other(3, share_o)

    @pl.loop(1, 8)
    def _(k):
        t = (s + k) % 8
        p.arrived(vo(t, 1 - c), ro.at[t, 1 - c], spare)

    save[1].start()
    for j in range(3):
        co = pl.ds(512 * j, 512)
        mid[:, co] = x[:, 512 * j : 512 * j + 512] + dot(att[...], WO[:, co])
    hidden = mid[...]
    a2[...] = (hidden * inverse_norm(hidden) * gains[1:2, :]).astype(BF)
    g_c.step(1)
    take_g(5)
    g_c.step(2)
    take_g(6)
    g_c.step(3)

    for k in turns:
        relay(gq, sdg, rg, (s + 8 - k) % 8)

    from_core(gq, rg)

    @pl.loop(0, 4)
    def _(k):
        g_c.other(k)

    g_q.finish()
    g_o.finish()
    g_c.finish()

    @pl.loop(1, 8)
    def _(k):
        t = (s + k) % 8
        p.sent(S.at[t], ss.at[t], spare)
        p.sent(gq(t, r), sg.at[t], spare)
        p.sent(vo(t, c), sdo.at[t], spare)
        for d in range(3):
            p.sent(vq(t, r), sdq.at[t, d], spare)
            p.sent(gq(t, r), sdg.at[t, d], spare)

    for copy in own_out + save:
        copy.wait()


def gather_weights(x, segments, gain_attn, b_qkv, gain_ffn, w_qkv, w_out, w_gate, w_up, cot):
    return pl.pallas_call(
        gather_body,
        out_shape=(
            shaped(1536, 2048), shaped(1536, 1536), shaped(1536, 2304), shaped(1024, 1536), shaped(128, 128, dtype=F32),
            shaped(128, 128, dtype=F32), shaped(8, 1536, dtype=F32), shaped(2, 768, 128), shaped(2, 128, 128), shaped(2, 128, 128), shaped(2, 768, 128),
            shaped(128, 1536), shaped(128, 1536), shaped(128, 1536, dtype=F32), shaped(128, 1536),
        ),
        in_specs=[VMEM] * 5 + [HBM] * 5,
        out_specs=(HBM,) * 4 + (VMEM,) * 11,
        scratch_shapes=[
            low(1536, 2048), low(1536, 1536), low(192, 8960), low(192, 8960), low(8, 192, 2304), low(128, 1536),
            low(8, 16, 768), full(8, 2048),
            DMA((8, 4)), DMA((8, 2)), DMA((8, 4)), DMA((8,)), DMA((8,)),
            DMA((4, 2)), DMA((4,)), DMA((8, 3)), DMA((4, 2)), DMA((4,)), DMA((8,)),
            DMA((8,)), DMA((8, 3)), DMA((4, 2)), DMA((4,)), DMA((8,)), DMA((6,)),
        ],
        compiler_params=pltpu.CompilerParams(collective_id=0, has_side_effects=True, vmem_limit_bytes=56 << 20),
        name="gather_and_attend",
    )(x, segments, gain_attn, b_qkv, gain_ffn, w_qkv, w_out, w_gate, w_up, cot)


class RowSums:
    def __init__(self, p, spare, total, chip, side, far, across, out, sems, width):
        self.p, self.spare, self.total, self.chip, self.side = p, spare, total, chip, side
        self.far, self.across, self.out, self.sems = far, across, out, sems
        self.width = width

    def part(self, t, q):
        return self.total.at[quarter(t, q), 0 : self.width]

    def slot(self, t, xx):
        return self.chip.at[t, xx, :, 0 : self.width]

    def own(self, k):
        p = self.p
        return 2 * p.line(3 - k % 4) + (1 - p.y + (k // 4) * (2 * p.y - 1))

    def to_core(self, t):
        p = self.p
        for xx in range(2):
            send(
                self.part(t, 2 * xx + 1 - p.c), self.slot(t, xx),
                self.sems[0].at[t, xx], self.sems[1].at[t, xx], p.core,
            )

    def add(self, t, q, ref, sem):
        self.p.arrived(ref, sem, self.spare)
        total = self.part(t, q)
        total[...] = (total[...].astype(F32) + ref[...].astype(F32)).astype(BF)

    def on_chip(self, k):
        p, t = self.p, self.own(k)
        for xx in range(2):
            self.add(t, 2 * xx + p.c, self.slot(t, xx), self.sems[1].at[t, xx])

    def aside(self, k):
        p, t = self.p, self.own(k)
        for xx in range(2):
            at = t // 2, xx
            send(self.part(t, 2 * xx + p.c), self.side.at[at], self.sems[2].at[at], self.sems[3].at[at], p.side)

    def on_line(self, k):
        p = self.p
        zz = p.line(3 - k)
        t = p.mine(zz)
        for xx in range(2):
            q = 2 * xx + p.c
            self.add(t, q, self.side.at[zz, xx], self.sems[3].at[zz, xx])
            p.reduce_step(
                zz,
                lambda slot: self.add(t, q, self.far.at[slot, xx], self.sems[5].at[slot, xx]),
                lambda slot, device: send(
                    self.part(t, q), self.far.at[slot, xx], self.sems[4].at[zz, xx], self.sems[5].at[slot, xx], device
                ),
            )

    def at_owner(self):
        p = self.p
        for xx in range(2):
            send(self.part(p.s, 2 * xx + p.c), self.across.at[xx], self.sems[6].at[xx], self.sems[7].at[xx], p.across)

    def spread(self):
        p = self.p
        for xx in range(2):
            q = 2 * xx + p.c
            p.sent(self.across.at[xx], self.sems[6].at[xx], self.spare)
            self.add(p.s, q, self.across.at[xx], self.sems[7].at[xx])
            total = self.part(p.s, q)
            pltpu.make_async_copy(total, self.out.at[q], self.sems[6].at[4 + xx]).start()
            send(total, self.out.at[q], self.sems[6].at[2 + xx], self.sems[7].at[2 + xx], p.core)

    def finish(self):
        p = self.p
        for xx in range(2):
            q = 2 * xx + 1 - p.c
            p.arrived(self.out.at[q], self.sems[7].at[2 + xx], self.spare)
            p.sent(self.out.at[q], self.sems[6].at[2 + xx], self.spare)
            pltpu.make_async_copy(self.part(p.s, 0), self.out.at[q], self.sems[6].at[4 + xx]).wait()

        @pl.loop(0, 8)
        def _(t):
            for xx in range(2):
                p.sent(self.slot(t, xx), self.sems[0].at[t, xx], self.spare)

        @pl.loop(0, 4)
        def _(i):
            for xx in range(2):
                p.sent(self.side.at[i, xx], self.sems[2].at[i, xx], self.spare)

                @pl.when(i != p.z)
                def _():
                    p.sent(self.far.at[i, xx], self.sems[4].at[i, xx], self.spare)

    @staticmethod
    def buffers(width):
        return [low(8, 2, 48, width), low(4, 2, 48, width), low(5, 2, 48, width), low(2, 48, width)]

    @staticmethod
    def semaphores():
        return [DMA((8, 2)), DMA((8, 2)), DMA((4, 2)), DMA((4, 2)), DMA((4, 2)), DMA((5, 2)), DMA((6,)), DMA((4,))]


def layer_back_body(
    n_ref, c_hbm, g_hbm, d_hbm, wq_hbm, wo_hbm, att_hbm, a1_hbm, x_hbm, cot_hbm, q_hbm,
    mid_ref, gains, cos_ref, sin_ref, keys, values, probs,
    out_ref, gtok_ref, OG, OD, OWq, OWo,
    NC, H, vG, vD, MX, PD, PO, YD, ZD, YO, ZO, YB, ZB, RCd, RXd, RC, RX, dj, AT, SM,
    Yq, Zq, RXq, RCo, Yo, Zo, RXo,
    free, rn, syn, szn, ryd, rzd, syd, szd, syo, ryo, szo, rzo, syb, ryb, szb, rzb,
    scd, rcd, sxd, rxd, sfd, rfd, scg, rcg, sx, rx, sa, ra, sf, *sems,
):
    p = Place()
    r, s, c, y, z = p.r, p.s, p.c, p.y, p.z
    loc = sems[-1]
    spare = loc.at[0]
    q_sums = RowSums(p, spare, H, RC, Yq, Zq, RXq, OWq, sems[0:8], 2176)
    o_sums = RowSums(p, spare, NC, RCo, Yo, Zo, RXo, OWo, sems[8:16], 1536)

    def block(t):
        return NC.at[rows_of(128 * t, 128, 128)]

    def cot_rows(start, size):
        return rows_of(1024 + start, size, 128)

    loads = (
        pltpu.make_async_copy(n_ref, block(s), loc.at[1]),
        pltpu.make_async_copy(c_hbm, NC.at[1024:2048], loc.at[2]),
        pltpu.make_async_copy(g_hbm, vG, loc.at[3]),
        pltpu.make_async_copy(d_hbm, vD.at[0:1120], loc.at[4]),
    )
    for copy in loads:
        copy.start()
    p.greet(range(1, 8))
    g_n = Gather(p, spare, block, lambda t: rn.at[t], szn, syn)
    g_n.start(n_ref)
    vD[1120:1152, :] = jnp.zeros((32, 1536), BF)
    for copy in loads:
        copy.wait()

    def side(P, Y, ssem, rsem, k):
        zz = p.line(k)
        send(P.at[p.theirs(zz)], Y.at[zz], ssem.at[zz], rsem.at[zz], p.side)

    def side_d(k):
        side(PD, YD, syd, ryd, k)

    def line_step(P, Y, Z, ry, sz, rz, k):
        zz = p.line(k)
        t = p.mine(zz)

        def add(ref, sem):
            p.arrived(ref, sem, spare)
            P[t] = (P[t].astype(F32) + ref[...].astype(F32)).astype(BF)

        add(Y.at[zz], ry.at[zz])
        p.reduce_step(
            zz,
            lambda slot: add(Z.at[slot], rz.at[slot]),
            lambda slot, device: send(P.at[t], Z.at[slot], sz.at[zz], rz.at[slot], device),
        )

    def step_d(k):
        line_step(PD, YD, ZD, ryd, szd, rzd, k)

    def side_oa(k):
        zz = p.line(k)
        send(PO.at[p.theirs(zz), :, 0:768], YO.at[zz], syo.at[zz], ryo.at[zz], p.side)

    def step_oa(k):
        zz = p.line(k)
        half = PO.at[p.mine(zz), :, 0:768]

        def add(ref, sem):
            p.arrived(ref, sem, spare)
            half[...] = (half[...].astype(F32) + ref[...].astype(F32)).astype(BF)

        add(YO.at[zz], ryo.at[zz])
        p.reduce_step(
            zz,
            lambda slot: add(ZO.at[slot], rzo.at[slot]),
            lambda slot, device: send(half, ZO.at[slot], szo.at[zz], rzo.at[slot], device),
        )

    def step_ob(k):
        zz = p.line(k)
        both = PO.at[pl.ds(2 * zz, 2), :, 768:1536]

        def add(slot):
            p.arrived(ZB.at[slot], rzb.at[slot], spare)
            both[...] = (both[...].astype(F32) + ZB[slot].astype(F32)).astype(BF)

        p.reduce_step(
            zz, add, lambda slot, device: send(both, ZB.at[slot], szb.at[zz], rzb.at[slot], device)
        )

    def side_ob():
        send(PO.at[p.theirs(z), :, 768:1536], YB, syb, ryb, p.side)

    at_end = (z == 0) | (z == 3)
    in_middle = (z == 1) | (z == 2)
    g_n.step(1)

    @pl.loop(0, 4)
    def _(k):
        zz = p.line(k)
        pl.when(at_end & (k > 0) & (k < 3))(lambda: g_n.step(k + 1))
        pl.when(in_middle & (k < 2))(lambda: g_n.step(k + 2))
        g_n.other(k)
        rows = rows_of(256 * zz, 256, 256)
        X = NC[rows]
        cot = NC[cot_rows(256 * zz, 256)]
        for j in range(3):
            ga, ua = pl.ds(384 * j, 384), pl.ds(1152 + 384 * j, 384)
            gate = dot(X, vG[:, ga])
            up = dot(X, vG[:, ua])
            d_mixed = dot_nt(cot, vD[ga])
            sg = jax.nn.sigmoid(gate)
            active = gate * sg
            d_active = d_mixed * up
            MX[rows, ga] = (active * up).astype(BF)
            H[rows, ga] = (d_active * sg + d_active * active * (1.0 - sg)).astype(BF)
            H[rows, ua] = (d_mixed * active).astype(BF)
        for j in range(3):
            co = pl.ds(512 * j, 512)
            part = dot_nt(H[rows], vG[co]).astype(BF)
            PD[2 * zz, :, co] = part[:128]
            PD[2 * zz + 1, :, co] = part[128:]
        pl.when(k == 2)(lambda: side_d(1))
        pl.when(k == 3)(lambda: side_d(3))
        for j in range(3):
            co = pl.ds(512 * j, 512)
            part = dot(MX[rows], vD[:, co]).astype(BF)
            PO[2 * zz, :, co] = part[:128]
            PO[2 * zz + 1, :, co] = part[128:]
        pl.when(at_end & (k == 1))(lambda: step_ob(1))
        pl.when(at_end & (k == 2))(lambda: step_ob(2))

    side_d(2)
    side_d(0)

    def owner(k):
        return 2 * ((z + 1 + k // 2) % 4) + (k % 2) * (2 * y - 1) + 1 - y

    def pair_chip(k):
        t = owner(k)
        for xx in range(2):
            p.arrived(RC.at[t, xx], rcg.at[t, xx], spare)
            q = quarter(t, 2 * xx + c)
            vG[q] = (vG[q].astype(F32) + RC[t, xx].astype(F32)).astype(BF)
        send(vG.at[quarter(t, p.rx)], RX.at[t], sx.at[t], rx.at[t], p.across)

    @pl.loop(0, 5)
    def _(j):
        @pl.when(j < 4)
        def _():
            pair = (z + 1 + j) % 4
            rows = rows_of(384 * pair, 384, 128)
            X = NC[0:1024, rows].T
            for i in range(3):
                co = pl.ds(768 * i, 768)
                vG[rows, co] = dot(X, H[0:1024, co]).astype(BF)
            for i in range(2):
                t = owner(2 * j + i)
                for xx in range(2):
                    send(vG.at[quarter(t, 2 * xx + 1 - c)], RC.at[t, xx], scg.at[t, xx], rcg.at[t, xx], p.core)

        @pl.when(j > 0)
        def _():
            pair_chip(2 * j - 2)
            pair_chip(2 * j - 1)

    pl.semaphore_signal(free, inc=1, device_id=p.core, device_id_type=MESH)

    def chunk(i):
        return rows_of(384 * i, 384, 128)

    def cols(q):
        return rows_of(384 * q, 384, 128)

    held = (
        pltpu.make_async_copy(wo_hbm, NC.at[0:1536], loc.at[1]),
        pltpu.make_async_copy(wq_hbm, H.at[:, 0:2048], loc.at[2]),
        pltpu.make_async_copy(att_hbm, NC.at[1536:1664], loc.at[3]),
        pltpu.make_async_copy(a1_hbm, NC.at[1664:1792], loc.at[4]),
        pltpu.make_async_copy(x_hbm, NC.at[1792:1920], loc.at[5]),
        pltpu.make_async_copy(cot_hbm, NC.at[1920:2048], loc.at[6]),
        pltpu.make_async_copy(q_hbm.at[0], MX.at[0:768, 256:384], loc.at[8]),
        pltpu.make_async_copy(q_hbm.at[1], MX.at[0:768, 384:512], loc.at[9]),
    )

    def down_terms():
        @pl.loop(0, 3)
        def _(i):
            X = MX[:, chunk(i)].T
            for j in range(3):
                co = pl.ds(512 * j, 512)
                vD[chunk(i), co] = dot(X, NC[1024:2048, co]).astype(BF)
            for xx in range(2):
                q = 2 * xx + 1 - c
                send(vD.at[chunk(i), cols(q)], RCd.at[xx, chunk(i)], scd.at[i, xx], rcd.at[i, xx], p.core)

        g_n.finish()
        for copy in held:
            copy.start()

        @pl.loop(0, 3)
        def _(i):
            for xx in range(2):
                p.arrived(RCd.at[xx, chunk(i)], rcd.at[i, xx], spare)
                q = cols(2 * xx + c)
                vD[chunk(i), q] = (vD[chunk(i), q].astype(F32) + RCd[xx, chunk(i)].astype(F32)).astype(BF)

    def pair_whole(k):
        t = owner(k)
        q = quarter(t, r)
        p.arrived(RX.at[t], rx.at[t], spare)
        vG[q] = (vG[q].astype(F32) + RX[t].astype(F32)).astype(BF)

        if k < 7:
            send(vG.at[q], OG.at[r, s], sa.at[t], ra.at[s, r], p.peer(t))
        else:
            pltpu.make_async_copy(vG.at[q], OG.at[r, s], loc.at[7]).start()

    def share(t):
        v = OG.at[r, t]
        send(v, v, sf.at[t, 0], ra.at[t, r], p.across)
        send(v, v, sf.at[t, 1], ra.at[t, r], p.core)

    def source(k):
        return 2 * ((z + 3 - k // 2) % 4) + (1 - y if k % 2 == 0 else y)

    def take(k):
        t = source(k)
        if k < 7:
            p.arrived(OG.at[r, t], ra.at[t, r], spare)
        else:
            pltpu.make_async_copy(vG.at[quarter(s, r)], OG.at[r, s], loc.at[7]).wait()
        share(t)

    def relay(k):
        t = source(k)
        v = OG.at[p.rx, t]
        p.arrived(v, ra.at[t, p.rx], spare)
        send(v, v, sf.at[t, 2], ra.at[t, p.rx], p.core)

    def down_across(i):
        send(vD.at[chunk(i), cols(p.rx)], RXd.at[chunk(i)], sxd.at[i], rxd.at[i], p.across)

    def down_whole(i):
        p.arrived(RXd.at[chunk(i)], rxd.at[i], spare)
        q = cols(r)
        vD[chunk(i), q] = (vD[chunk(i), q].astype(F32) + RXd[chunk(i)].astype(F32)).astype(BF)
        src, dst = vD.at[chunk(i), q], OD.at[r, chunk(i)]
        pltpu.make_async_copy(src, dst, sfd.at[i, 3]).start()
        send(src, dst, sfd.at[i, 0], rfd.at[i, r], p.across)
        send(src, dst, sfd.at[i, 1], rfd.at[i, r], p.core)

    def down_relay(i):
        v = OD.at[p.rx, chunk(i)]
        p.arrived(v, rfd.at[i, p.rx], spare)
        send(v, v, sfd.at[i, 2], rfd.at[i, p.rx], p.core)

    def back(w):
        return w * cos_ref[...] - pltpu.roll(w, 64, 1) * sin_ref[...]

    kept = {}

    def attention_out():
        for copy in held:
            copy.wait()
        dn, hidden = PD[s].astype(F32), mid_ref[...]
        rstd = inverse_norm(hidden)
        unit = hidden * rstd
        kept["ffn"] = jnp.sum(dn * unit, axis=0, keepdims=True)
        e = dn * gains[1:2, :]
        dm = NC[1920:2048].astype(F32) + rstd * (e - unit * jnp.mean(e * unit, axis=-1, keepdims=True))
        NC[1920:2048] = dm.astype(BF)
        AT[...] = NC[1536:1664].T
        for j in range(3):
            part = dot_nt(NC[1920:2048], NC[pl.ds(512 * j, 512)]).astype(BF)
            for i in range(4):
                h = 4 * j + i
                MX[pl.ds(128 * (h % 6), 128), pl.ds(128 * (h // 6), 128)] = part[:, 128 * i : 128 * i + 128]
        for j in range(3):
            co = pl.ds(512 * j, 512)
            NC[0:1536, co] = dot(AT[...], NC[1920:2048, co]).astype(BF)

        @pl.loop(0, 8)
        def _(k):
            o_sums.to_core(o_sums.own(k))

    def heads(g):
        grad = MX[0:768, 128 * g : 128 * g + 128]
        query = MX[0:768, 256 + 128 * g : 384 + 128 * g]
        soft = probs[g].astype(F32)
        d_probs = dot_nt(grad, values[g])
        d_scores = (soft * (d_probs - jnp.sum(soft * d_probs, axis=-1, keepdims=True))).astype(BF)
        d_values = dot(probs[g].T, grad)
        d_queries = dot(d_scores, keys[g]) * HEAD_DIMENSION**-0.5
        d_keys = dot(d_scores.T, query)
        for i in range(6):
            dj[:, pl.ds(128 * (6 * g + i), 128)] = back(d_queries[128 * i : 128 * i + 128]).astype(BF)
        dj[:, pl.ds(128 * (12 + g), 128)] = back(d_keys).astype(BF)
        dj[:, pl.ds(128 * (14 + g), 128)] = d_values.astype(BF)

    def attention_in():
        heads(1)
        joined_grad = dj[...]
        bias_grad = jnp.sum(joined_grad.astype(F32), axis=0, keepdims=True)
        x = NC[1792:1920].astype(F32)
        rstd = inverse_norm(x)
        unit = x * rstd
        dn1 = jnp.concatenate(
            [dot_nt(joined_grad, H[pl.ds(512 * j, 512), 0:2048]) for j in range(3)], axis=1
        )
        gain_attn_grad = jnp.sum(dn1 * unit, axis=0, keepdims=True)
        e = dn1 * gains[0:1, :]
        NC[1792:1920] = (
            NC[1920:2048].astype(F32) + rstd * (e - unit * jnp.mean(e * unit, axis=-1, keepdims=True))
        ).astype(BF)
        pltpu.make_async_copy(NC.at[1792:1920], gtok_ref, loc.at[5]).start()
        SM[...] = jnp.zeros_like(SM)
        ffn = kept["ffn"]
        for t in range(8):
            SM[t, 0:1, :] = gain_attn_grad[:, 192 * t : 192 * t + 128]
            SM[t, 1:2, 0:64] = gain_attn_grad[:, 192 * t + 128 : 192 * t + 192]
            SM[t, 2:3, :] = bias_grad[:, 256 * t : 256 * t + 128]
            SM[t, 3:4, :] = bias_grad[:, 256 * t + 128 : 256 * t + 256]
            SM[t, 4:5, :] = ffn[:, 192 * t : 192 * t + 128]
            SM[t, 5:6, 0:64] = ffn[:, 192 * t + 128 : 192 * t + 192]
        AT[...] = NC[1664:1792].T

    def joined_terms():
        pl.semaphore_wait(free, 1)

        @pl.loop(0, 8)
        def _(k):
            t = q_sums.own(k)
            rows = rows_of(192 * t, 192)
            for j in range(2):
                co = pl.ds(1024 * j, 1024)
                H[rows, co] = dot(AT[rows], dj[:, co]).astype(BF)
            H[rows, 2048:2176] = jnp.zeros((192, 128), BF)
            H[rows_of(192 * t, 16), 2048:2176] = SM[t].astype(BF)
            q_sums.to_core(t)

    def on_chip(sums):
        @pl.loop(0, 8)
        def _(k):
            sums.on_chip(k)

    def finish_out():
        p.arrived(YB, ryb, spare)
        PO[s, :, 768:1536] = (PO[s, :, 768:1536].astype(F32) + YB[...].astype(F32)).astype(BF)
        PO[s] = (PO[s].astype(F32) + mid_ref[...]).astype(BF)
        pltpu.make_async_copy(PO.at[s], out_ref, loc.at[6]).start()

    def first_heads():
        heads(0)

    def o_on_chip():
        on_chip(o_sums)

    def q_on_chip():
        on_chip(q_sums)


    @pl.when(at_end)
    def _():
        step_d(3)
        side_oa(3)
        step_d(2)
        side_oa(2)
        side_oa(0)
        step_d(1)
        pair_whole(3)


    @pl.when(in_middle)
    def _():
        side_oa(2)
        side_oa(0)
        step_ob(2)
        step_d(3)
        step_d(2)
        step_d(1)
        pair_whole(6)

    down_terms()

    @pl.when(at_end)
    def _():
        step_ob(3)
        pair_whole(6)
        down_across(1)
        pair_whole(5)
        step_oa(3)
        pair_whole(0)
        down_across(0)
        side_oa(1)


    @pl.when(in_middle)
    def _():
        side_oa(3)
        pair_whole(5)
        down_across(0)
        side_oa(1)
        pair_whole(3)
        take(3)
        pair_whole(1)
        down_across(1)
        pair_whole(2)

    step_d(0)
    attention_out()

    @pl.when(at_end)
    def _():
        down_across(2)

    first_heads()
    attention_in()

    @pl.when(at_end)
    def _():
        pair_whole(4)
        pair_whole(2)

    joined_terms()

    @pl.when(in_middle)
    def _():
        pair_whole(4)

    o_on_chip()

    @pl.when(at_end)
    def _():
        o_sums.aside(2)
        take(3)
        o_sums.aside(0)
        pair_whole(1)
        take(6)


    @pl.when(in_middle)
    def _():
        down_across(2)
        o_sums.aside(2)
        pair_whole(7)
        down_whole(0)
        o_sums.aside(0)
        step_oa(3)
        pair_whole(0)
        take(7)

    q_on_chip()

    @pl.when(at_end)
    def _():
        q_sums.aside(0)
        take(2)
        q_sums.aside(1)
        down_whole(1)
        take(5)
        down_whole(0)
        pair_whole(7)
        o_sums.on_line(0)
        down_whole(2)
        take(1)
        q_sums.aside(2)
        take(7)
        q_sums.on_line(0)
        o_sums.aside(1)
        take(4)
        relay(5)
        q_sums.aside(3)
        q_sums.on_line(1)
        q_sums.on_line(2)
        step_ob(0)
        take(0)
        o_sums.on_line(1)
        o_sums.aside(3)
        q_sums.on_line(3)
        q_sums.at_owner()
        o_sums.on_line(2)
        relay(2)
        relay(3)
        step_oa(2)
        relay(4)
        o_sums.on_line(3)
        o_sums.at_owner()
        q_sums.spread()
        step_oa(1)
        down_relay(2)
        down_relay(0)
        relay(1)
        relay(6)
        relay(7)
        relay(0)
        side_ob()
        down_relay(1)
        step_oa(0)
        finish_out()
        o_sums.spread()


    @pl.when(in_middle)
    def _():
        q_sums.aside(1)
        q_sums.aside(0)
        take(4)
        take(6)
        down_whole(1)
        take(5)
        relay(3)
        step_ob(3)
        take(2)
        take(1)
        q_sums.aside(2)
        o_sums.on_line(0)
        q_sums.aside(3)
        o_sums.aside(1)
        down_whole(2)
        step_ob(1)
        q_sums.on_line(0)
        relay(5)
        o_sums.aside(3)
        q_sums.on_line(1)
        q_sums.on_line(2)
        step_ob(0)
        take(0)
        q_sums.on_line(3)
        q_sums.at_owner()
        relay(4)
        o_sums.on_line(2)
        side_ob()
        relay(2)
        o_sums.on_line(1)
        relay(6)
        o_sums.on_line(3)
        o_sums.at_owner()
        relay(0)
        step_oa(1)
        down_relay(1)
        down_relay(2)
        relay(7)
        down_relay(0)
        q_sums.spread()
        relay(1)
        step_oa(2)
        o_sums.spread()
        step_oa(0)
        finish_out()

    o_sums.finish()
    q_sums.finish()
    pltpu.make_async_copy(NC.at[1792:1920], gtok_ref, loc.at[5]).wait()
    pltpu.make_async_copy(PO.at[s], out_ref, loc.at[6]).wait()

    @pl.loop(0, 3)
    def _(i):
        for q in (p.rc, p.rd):
            p.arrived(OD.at[q, chunk(i)], rfd.at[i, q], spare)
        for d in range(3):
            p.sent(OD.at[r, chunk(i)], sfd.at[i, d], spare)
        pltpu.make_async_copy(OD.at[r, chunk(i)], OD.at[r, chunk(i)], sfd.at[i, 3]).wait()
        for xx in range(2):
            p.sent(RCd.at[xx, chunk(i)], scd.at[i, xx], spare)
        p.sent(RXd.at[chunk(i)], sxd.at[i], spare)

    @pl.loop(0, 8)
    def _(t):
        for q in (p.rc, p.rd):
            p.arrived(OG.at[q, t], ra.at[t, q], spare)
        for d in range(3):
            p.sent(OG.at[r, t], sf.at[t, d], spare)
        for xx in range(2):
            p.sent(RC.at[t, xx], scg.at[t, xx], spare)
        p.sent(RX.at[t], sx.at[t], spare)

        @pl.when(t != s)
        def _():
            p.sent(OG.at[r, s], sa.at[t], spare)

    @pl.loop(0, 4)
    def _(i):
        p.sent(YD.at[i], syd.at[i], spare)
        p.sent(YO.at[i], syo.at[i], spare)

        @pl.when(i != z)
        def _():
            p.sent(ZD.at[i], szd.at[i], spare)
            p.sent(ZO.at[i], szo.at[i], spare)
            p.sent(ZB.at[i], szb.at[i], spare)

    p.sent(YB, syb, spare)


def layer_back(*args):
    return pl.pallas_call(
        layer_back_body,
        out_shape=(
            shaped(128, 1536), shaped(128, 1536), shaped(4, 8, 48, 2304), shaped(4, 1152, 384), shaped(4, 48, 2176),
            shaped(4, 48, 1536),
        ),
        in_specs=[HBM] * 11 + [VMEM] * 7,
        out_specs=(HBM,) * 6,
        scratch_shapes=[
            low(2048, 1536), low(1536, 2304), low(1536, 2304), low(1152, 1536), low(1024, 1152),
            low(8, 128, 1536), low(8, 128, 1536), low(4, 128, 1536), low(5, 128, 1536), low(4, 128, 768), low(5, 128, 768),
            low(128, 768), low(5, 2, 128, 768),
            low(2, 1152, 384), low(1152, 384), low(8, 2, 48, 2304), low(8, 48, 2304),
            low(128, 2048), low(1536, 128), full(8, 16, 128),
            *RowSums.buffers(2176)[1:], *RowSums.buffers(1536),
            pltpu.SemaphoreType.REGULAR, DMA((8,)), DMA((4,)), DMA((4, 2)),
            DMA((4,)), DMA((5,)), DMA((4,)), DMA((4,)), DMA((4,)), DMA((4,)), DMA((4,)), DMA((5,)), DMA, DMA, DMA((4,)), DMA((5,)),
            DMA((3, 2)), DMA((3, 2)), DMA((3,)), DMA((3,)), DMA((3, 4)), DMA((3, 4)),
            DMA((8, 2)), DMA((8, 2)), DMA((8,)), DMA((8,)), DMA((8,)), DMA((8, 4)), DMA((8, 3)),
            *RowSums.semaphores(), *RowSums.semaphores(), DMA((10,)),
        ],
        compiler_params=pltpu.CompilerParams(collective_id=1, has_side_effects=True, vmem_limit_bytes=64 << 20),
        name="layer_back",
    )(*args)


def widen_body(
    g_ref, d_ref, q_ref, o_ref, x_ref, y_ref, gate, up, down, qkv, out, x_out, y_out, ga, bq, gf, narrow
):
    for first, wide in ((0, gate), (1152, up)):
        for t in range(8):
            narrow[:, 1120 * t : 1120 * t + 1120] = g_ref[0, t, :, first : first + 1120]
        wide[...] = narrow[...].astype(F32)
    down[...] = d_ref[0, 0:1120, :].astype(F32)
    qkv[...] = q_ref[0, :, 0:2048].astype(F32)
    out[...] = o_ref[0].astype(F32)
    x_out[...] = x_ref[...]
    y_out[...] = y_ref[...]

    @pl.when(pl.program_id(0) == 0)
    def _():
        small = q_ref[0, 0:16, 2048:2176].astype(F32)
        ga[...] = jnp.concatenate([small[0:1], small[1:2, 0:64]], axis=1)[0]
        bq[...] = jnp.concatenate([small[2:3], small[3:4]], axis=1)[0]
        gf[...] = jnp.concatenate([small[4:5], small[5:6, 0:64]], axis=1)[0]


def widen(g, d, q, o, x, y):
    def rows(size, width):
        return pl.BlockSpec((size, width), lambda i: (i, 0))

    def whole(size):
        return pl.BlockSpec((size,), lambda i: (0,))

    return pl.pallas_call(
        widen_body,
        grid=(4,),
        out_shape=(
            shaped(192, 8960, dtype=F32), shaped(192, 8960, dtype=F32), shaped(1120, 1536, dtype=F32),
            shaped(192, 2048, dtype=F32), shaped(192, 1536, dtype=F32), shaped(128, 1536), shaped(128, 1536),
            shaped(192, dtype=F32), shaped(256, dtype=F32), shaped(192, dtype=F32),
        ),
        in_specs=[
            pl.BlockSpec((1, 8, 48, 2304), lambda i: (i, 0, 0, 0)),
            pl.BlockSpec((1, 1152, 384), lambda i: (i, 0, 0)),
            pl.BlockSpec((1, 48, 2176), lambda i: (i, 0, 0)),
            pl.BlockSpec((1, 48, 1536), lambda i: (i, 0, 0)),
            rows(32, 1536),
            rows(32, 1536),
        ],
        out_specs=(
            rows(48, 8960), rows(48, 8960), pl.BlockSpec((1120, 384), lambda i: (0, i)), rows(48, 2048), rows(48, 1536),
            rows(32, 1536), rows(32, 1536), whole(192), whole(256), whole(192),
        ),
        scratch_shapes=[low(48, 8960)],
        compiler_params=pltpu.CompilerParams(vmem_limit_bytes=62 << 20),
        name="widen",
    )(g, d, q, o, x, y)


def shards_eight(
    tokens, segments, gain_attn, w_qkv, b_qkv, w_out, gain_ffn, w_gate, w_up, w_down, cotangent
):
    x, cot = tokens[0], cotangent[0]
    WQ, WO, G, C, cosine, sine, gains, queries, keys, values, probs, att, a1, mid, a2 = gather_weights(
        x, segments, gain_attn, b_qkv, gain_ffn, w_qkv, w_out, w_gate, w_up, cot
    )
    out, grad_tokens, gate_up, down, qkv, o = layer_back(
        a2, C, G, w_down, WQ, WO, att, a1, x, cot, queries, mid, gains, cosine, sine, keys, values, probs
    )
    gate, up, down, qkv_rows, out_rows, out, grad_tokens, ga, bq, gf = widen(gate_up, down, qkv, o, out, grad_tokens)
    return out[None], grad_tokens[None], ga, qkv_rows, bq, out_rows, gf, gate, up, down


def solution(mesh):
    placed = (
        P(("replica", "shard"), None, None),
        P(("replica", "shard"), None),
        P("shard"),
        P("shard", None),
        P("shard"),
        P("shard", None),
        P("shard"),
        P("shard", None),
        P("shard", None),
        P("shard", None),
        P(("replica", "shard"), None, None),
    )
    return jax.shard_map(
        shards_eight if (mesh.shape["replica"], mesh.shape["shard"]) == (4, 8) else shards,
        mesh=mesh,
        in_specs=placed,
        out_specs=(
            P(("replica", "shard"), None, None),
            P(("replica", "shard"), None, None),
            P("shard"),
            P("shard", None),
            P("shard"),
            P("shard", None),
            P("shard"),
            P("shard", None),
            P("shard", None),
            P("shard", None),
        ),
        check_vma=False,
    )
```

```python
import math

import jax
import jax.numpy as jnp
from jax import lax
from jax.experimental import pallas as pl
from jax.experimental.pallas import tpu as pltpu
from jax.sharding import PartitionSpec as P

QUERY_HEADS = 12
KEY_VALUE_HEADS = 2
HEAD_DIMENSION = 128


eps_norm = 1e-06
rope_base = 1000000.0


def tables(segment_ids, head_size):
    token_length = segment_ids.shape[-1]
    row_index = jnp.arange(token_length, dtype=jnp.int32)
    earlier = jnp.sum(
        (segment_ids[..., None, :] < segment_ids[..., :, None]).astype(jnp.int32),
        axis=-1,
        dtype=jnp.int32,
    )
    positions = (row_index - earlier).astype(jnp.float32)
    frequencies = jnp.exp(
        jnp.arange(head_size // 2, dtype=jnp.float32) * (-2.0 * math.log(rope_base) / head_size)
    )
    angles = positions[..., None] * frequencies
    cosine = jnp.concatenate([jnp.cos(angles), jnp.cos(angles)], axis=-1)
    sine_vals = jnp.concatenate([jnp.sin(angles), jnp.sin(angles)], axis=-1)
    allowed = (
        (segment_ids[..., None, :] == segment_ids[..., :, None])
        & (row_index[None, :] <= row_index[:, None])
    ).astype(jnp.int32)
    return (cosine, sine_vals, allowed)


def apply_rotation(values, cosine, sine_vals):
    halfway = values.shape[-1] // 2
    turned = jnp.concatenate([-values[..., halfway:], values[..., :halfway]], axis=-1)
    return values * cosine + turned * sine_vals


def rotate_back(values, cosine, sine_vals):
    halfway = values.shape[-1] // 2
    shifted = values * sine_vals
    return values * cosine + jnp.concatenate(
        [shifted[..., halfway:], -shifted[..., :halfway]], axis=-1
    )


def norm_forward(hidden, gain_vec):
    rstd_rows = lax.rsqrt(jnp.mean(hidden * hidden, axis=-1, keepdims=True) + eps_norm)
    unit_rows = hidden * rstd_rows
    return (unit_rows * gain_vec, unit_rows, rstd_rows)


def norm_backward(grad_in, gain_vec, unit_rows, rstd_rows):
    inner_grad = grad_in * gain_vec
    return rstd_rows * (
        inner_grad - unit_rows * jnp.mean(inner_grad * unit_rows, axis=-1, keepdims=True)
    )


def column_term(left_side, right_side):
    return jnp.einsum("lf,ld->fd", left_side, right_side, preferred_element_type=jnp.float32)


def to_columns(rows):
    ranks = lax.axis_size("shard")
    depth, width = rows.shape
    split = rows.reshape(depth, ranks, width // ranks).transpose(1, 0, 2)
    return lax.all_to_all(split, "shard", 0, 0, tiled=True).reshape(ranks * depth, width // ranks)


def to_rows(columns):
    ranks, copies = lax.axis_size("shard"), lax.axis_size("replica")
    depth, width = columns.shape
    depth = depth // ranks
    parts = columns.reshape(ranks, copies, depth // copies, width)
    part = lax.psum_scatter(parts, "replica", scatter_dimension=1, tiled=False)
    part = lax.all_to_all(part, "shard", 0, 0, tiled=True)
    part = part.transpose(1, 0, 2).reshape(depth // copies, ranks * width)
    return lax.all_gather(part, "replica", axis=0, tiled=True)


def shards(
    tokens, segments, gain_attn, w_qkv, b_qkv, w_out, gain_ffn, w_gate, w_up, w_down, cotangent
):
    heads_per_group = QUERY_HEADS // KEY_VALUE_HEADS
    head_dimension = QUERY_HEADS * HEAD_DIMENSION
    key_value_limit = head_dimension + KEY_VALUE_HEADS * HEAD_DIMENSION
    logit_scale = HEAD_DIMENSION ** (-0.5)
    token_length = tokens.shape[1]
    full_gain_attn, full_qkv, full_bias, full_out, full_gain_ffn = (
        lax.all_gather(gain_attn, "shard", axis=0, tiled=True),
        lax.all_gather(w_qkv, "shard", axis=0, tiled=True),
        lax.all_gather(b_qkv, "shard", axis=0, tiled=True),
        lax.all_gather(w_out, "shard", axis=0, tiled=True),
        lax.all_gather(gain_ffn, "shard", axis=0, tiled=True),
    )
    gate_columns = to_columns(w_gate)
    up_columns = to_columns(w_up)
    all_cot = lax.all_gather(cotangent[0], "shard", axis=0, tiled=True)
    gain_first = full_gain_attn.astype(jnp.float32)
    gain_second = full_gain_ffn.astype(jnp.float32)
    cosine, sine_vals, allowed = tables(segments[0], HEAD_DIMENSION)
    cosine_per_head = cosine[:, None, :]
    sine_per_head = sine_vals[:, None, :]
    inputs = tokens[0].astype(jnp.float32)
    normed_first, unit_first, rstd_first = norm_forward(inputs, gain_first)
    acts_first = normed_first.astype(jnp.bfloat16)
    joined_projection = jnp.dot(
        acts_first, full_qkv, preferred_element_type=jnp.float32
    ) + full_bias.astype(jnp.float32)
    query_rows = apply_rotation(
        joined_projection[:, :head_dimension].reshape(token_length, QUERY_HEADS, HEAD_DIMENSION),
        cosine_per_head,
        sine_per_head,
    )
    query_reduced = (
        (query_rows * logit_scale)
        .astype(jnp.bfloat16)
        .reshape(token_length, KEY_VALUE_HEADS, heads_per_group, HEAD_DIMENSION)
    )
    k_low = apply_rotation(
        joined_projection[:, head_dimension:key_value_limit].reshape(
            token_length, KEY_VALUE_HEADS, HEAD_DIMENSION
        ),
        cosine_per_head,
        sine_per_head,
    ).astype(jnp.bfloat16)
    value_reduced = (
        joined_projection[:, key_value_limit:]
        .reshape(token_length, KEY_VALUE_HEADS, HEAD_DIMENSION)
        .astype(jnp.bfloat16)
    )
    scores = jnp.einsum("ikrd,jkd->krij", query_reduced, k_low, preferred_element_type=jnp.float32)
    scores = jnp.where(allowed != 0, scores, -1e30)
    largest = jnp.max(scores, axis=-1, keepdims=True)
    exponents = jnp.exp(scores - largest)
    soft_probs = exponents / jnp.sum(exponents, axis=-1, keepdims=True)
    soft_low = soft_probs.astype(jnp.bfloat16)
    attended = jnp.einsum(
        "krij,jkd->ikrd", soft_low, value_reduced, preferred_element_type=jnp.float32
    )
    attended = attended.reshape(token_length, head_dimension).astype(jnp.bfloat16)
    hidden_mid = inputs + jnp.dot(attended, full_out, preferred_element_type=jnp.float32)
    normed_second, unit_second, rstd_second = norm_forward(hidden_mid, gain_second)
    acts_second = normed_second.astype(jnp.bfloat16)
    all_acts = lax.all_gather(acts_second, "shard", axis=0, tiled=True)
    gate_vals = jnp.dot(all_acts, gate_columns, preferred_element_type=jnp.float32)
    up_vals = jnp.dot(all_acts, up_columns, preferred_element_type=jnp.float32)
    sigmoid_gate = jax.nn.sigmoid(gate_vals)
    active = gate_vals * sigmoid_gate
    mixed_hidden = (active * up_vals).astype(jnp.bfloat16)
    d_mixed = jnp.einsum("ld,fd->lf", all_cot, w_down, preferred_element_type=jnp.float32)
    d_active = d_mixed * up_vals
    d_gate = (
        d_active * sigmoid_gate + d_active * gate_vals * sigmoid_gate * (1.0 - sigmoid_gate)
    ).astype(jnp.bfloat16)
    d_up = (d_mixed * active).astype(jnp.bfloat16)
    d_normed_part = jnp.einsum("lf,df->ld", d_gate, gate_columns, preferred_element_type=jnp.float32)
    d_normed_part = d_normed_part + jnp.einsum(
        "lf,df->ld", d_up, up_columns, preferred_element_type=jnp.float32
    )
    d_normed_second = lax.psum_scatter(
        d_normed_part.astype(jnp.bfloat16), "shard", scatter_dimension=0, tiled=True
    ).astype(jnp.float32)
    down_part = jnp.dot(mixed_hidden, w_down, preferred_element_type=jnp.float32)
    result = (
        hidden_mid
        + lax.psum_scatter(
            down_part.astype(jnp.bfloat16), "shard", scatter_dimension=0, tiled=True
        ).astype(jnp.float32)
    ).astype(jnp.bfloat16)
    grad_out = cotangent[0]
    down_grad = column_term(mixed_hidden, all_cot).astype(jnp.bfloat16)
    gate_grad = to_rows(column_term(all_acts, d_gate).astype(jnp.bfloat16))
    up_grad = to_rows(column_term(all_acts, d_up).astype(jnp.bfloat16))
    gain_second_grad = jnp.sum(d_normed_second * unit_second, axis=0)
    d_hidden_mid = grad_out.astype(jnp.float32) + norm_backward(
        d_normed_second, gain_second, unit_second, rstd_second
    )
    d_branch = d_hidden_mid.astype(jnp.bfloat16)
    out_grad_term = jnp.einsum("le,ld->ed", attended, d_branch, preferred_element_type=jnp.float32)
    attended_gradient = jnp.einsum(
        "ld,ed->le", d_branch, full_out, preferred_element_type=jnp.float32
    )
    attended_gradient = attended_gradient.astype(jnp.bfloat16).reshape(
        token_length, KEY_VALUE_HEADS, heads_per_group, HEAD_DIMENSION
    )
    d_probs = jnp.einsum(
        "ikrd,jkd->krij", attended_gradient, value_reduced, preferred_element_type=jnp.float32
    )
    value_gradient = jnp.einsum(
        "krij,ikrd->jkd", soft_low, attended_gradient, preferred_element_type=jnp.float32
    )
    d_scores = soft_probs * (d_probs - jnp.sum(soft_probs * d_probs, axis=-1, keepdims=True))
    d_scores_low = d_scores.astype(jnp.bfloat16)
    d_queries = jnp.einsum(
        "krij,jkd->ikrd", d_scores_low, k_low, preferred_element_type=jnp.float32
    )
    d_queries = rotate_back(
        d_queries.reshape(token_length, QUERY_HEADS, HEAD_DIMENSION) * logit_scale,
        cosine_per_head,
        sine_per_head,
    )
    key_gradient = jnp.einsum(
        "krij,ikrd->jkd", d_scores_low, query_reduced, preferred_element_type=jnp.float32
    )
    key_gradient = rotate_back(key_gradient, cosine_per_head, sine_per_head)
    d_joined = jnp.concatenate(
        [
            d_queries.reshape(token_length, head_dimension),
            key_gradient.reshape(token_length, KEY_VALUE_HEADS * HEAD_DIMENSION),
            value_gradient.reshape(token_length, KEY_VALUE_HEADS * HEAD_DIMENSION),
        ],
        axis=1,
    ).astype(jnp.bfloat16)
    bias_grad_term = jnp.sum(d_joined.astype(jnp.float32), axis=0)
    qkv_grad_term = jnp.einsum(
        "ld,le->de", acts_first, d_joined, preferred_element_type=jnp.float32
    )
    d_normed_first = jnp.einsum("le,de->ld", d_joined, full_qkv, preferred_element_type=jnp.float32)
    gain_first_grad = jnp.sum(d_normed_first * unit_first, axis=0)
    d_inputs = d_hidden_mid + norm_backward(d_normed_first, gain_first, unit_first, rstd_first)
    owned = (
        lax.psum_scatter(
            gain_first_grad.astype(jnp.bfloat16), "shard", scatter_dimension=0, tiled=True
        ).astype(jnp.float32),
        lax.psum_scatter(
            qkv_grad_term.astype(jnp.bfloat16), "shard", scatter_dimension=0, tiled=True
        ).astype(jnp.float32),
        lax.psum_scatter(
            bias_grad_term.astype(jnp.bfloat16), "shard", scatter_dimension=0, tiled=True
        ).astype(jnp.float32),
        lax.psum_scatter(
            out_grad_term.astype(jnp.bfloat16), "shard", scatter_dimension=0, tiled=True
        ).astype(jnp.float32),
        lax.psum_scatter(
            gain_second_grad.astype(jnp.bfloat16), "shard", scatter_dimension=0, tiled=True
        ).astype(jnp.float32),
    )
    summed = (
        lax.psum(owned[0].astype(jnp.bfloat16), "replica").astype(jnp.float32),
        lax.psum(owned[1].astype(jnp.bfloat16), "replica").astype(jnp.float32),
        lax.psum(owned[2].astype(jnp.bfloat16), "replica").astype(jnp.float32),
        lax.psum(owned[3].astype(jnp.bfloat16), "replica").astype(jnp.float32),
        lax.psum(owned[4].astype(jnp.bfloat16), "replica").astype(jnp.float32),
        gate_grad.astype(jnp.float32),
        up_grad.astype(jnp.float32),
        lax.psum(down_grad, "replica").astype(jnp.float32),
    )
    return (
        result[None],
        d_inputs.astype(jnp.bfloat16)[None],
        summed[0],
        summed[1],
        summed[2],
        summed[3],
        summed[4],
        summed[5],
        summed[6],
        summed[7],
    )


MESH = pl.DeviceIdType.MESH
BF, F32 = jnp.bfloat16, jnp.float32
HBM = pl.BlockSpec(memory_space=pl.ANY)
VMEM = pl.BlockSpec(memory_space=pltpu.VMEM)
DMA = pltpu.SemaphoreType.DMA


def shaped(*shape, dtype=BF):
    return jax.ShapeDtypeStruct(shape, dtype)


def low(*shape):
    return pltpu.VMEM(shape, BF)


def full(*shape):
    return pltpu.VMEM(shape, F32)


def dot(a, b):
    return lax.dot_general(a, b, (((1,), (0,)), ((), ())), preferred_element_type=F32)


def dot_nt(a, b):
    return lax.dot_general(a, b, (((1,), (1,)), ((), ())), preferred_element_type=F32)


def rows_of(start, size, unit=16):
    return pl.ds(pl.multiple_of(start, unit), size)


def quarter(t, q):
    return rows_of(192 * t + 48 * q, 48)


def send(src, dst, send_sem, recv_sem, device):
    copy = pltpu.make_async_remote_copy(
        src_ref=src, dst_ref=dst, send_sem=send_sem, recv_sem=recv_sem, device_id=device, device_id_type=MESH
    )
    copy.start()


class Place:
    def __init__(self):
        self.r = r = lax.axis_index("replica")
        self.s = s = lax.axis_index("shard")
        self.x, self.c, self.z, self.y = r // 2, r % 2, s // 2, s % 2
        self.rc, self.rx, self.rd = r + 1 - 2 * self.c, (r + 2) % 4, 3 - r
        self.core, self.across, self.side = (self.rc, s), (self.rx, s), (r, s + 1 - 2 * self.y)

    def peer(self, t):
        return (self.r, t)

    def line(self, k):
        near = self.z + (1 - 2 * (self.z % 2)) * (k % 2)
        far = k + (self.z // 2) * (3 - 2 * k)
        return (1 - k // 2) * near + (k // 2) * far

    def onward(self, zz, copy):
        pl.when((zz <= self.z) & (self.z < 3))(lambda: copy(0, self.peer(self.s + 2)))
        pl.when((zz >= self.z) & (self.z > 0))(lambda: copy(1, self.peer(self.s - 2)))

    def went_onward(self, zz, wait):
        pl.when((zz <= self.z) & (self.z < 3))(lambda: wait(0))
        pl.when((zz >= self.z) & (self.z > 0))(lambda: wait(1))

    def reduce_step(self, zz, add, hand):
        pl.when((zz >= self.z) & (self.z > 0))(lambda: add(zz))
        pl.when((zz < self.z) & (self.z < 3))(lambda: add(zz))
        pl.when((zz == self.z) & (self.z < 3))(lambda: add(4))
        pl.when(zz > self.z)(lambda: hand(zz, self.peer(self.s + 2)))
        pl.when(zz < self.z - 1)(lambda: hand(zz, self.peer(self.s - 2)))
        pl.when(zz == self.z - 1)(lambda: hand(4, self.peer(self.s - 2)))

    def mine(self, zz):
        return 2 * zz + self.y

    def theirs(self, zz):
        return 2 * zz + 1 - self.y

    def greet(self, steps):
        bar = pltpu.get_barrier_semaphore()
        devices = [self.core, self.across] + [(self.r, (self.s + k) % 8) for k in steps]
        for device in devices:
            pl.semaphore_signal(bar, inc=1, device_id=device, device_id_type=MESH)
        pl.semaphore_wait(bar, len(devices))

    def arrived(self, ref, sem, spare):
        pltpu.make_async_remote_copy(
            src_ref=ref, dst_ref=ref, send_sem=spare, recv_sem=sem, device_id=self.core, device_id_type=MESH
        ).wait_recv()

    def sent(self, ref, sem, spare):
        pltpu.make_async_remote_copy(
            src_ref=ref, dst_ref=ref, send_sem=sem, recv_sem=spare, device_id=self.core, device_id_type=MESH
        ).wait_send()


def inverse_norm(v):
    return lax.rsqrt(jnp.mean(v * v, axis=-1, keepdims=True) + eps_norm)


class Gather:
    def __init__(self, p, spare, view, arrivals, along, aside):
        self.p, self.spare, self.view = p, spare, view
        self.arrivals, self.along, self.aside = arrivals, along, aside

    def move(self, src, t, zz):
        p, dst, sem = self.p, self.view(t), self.arrivals(t)
        p.onward(zz, lambda d, device: send(src, dst, self.along.at[zz, d], sem, device))
        send(src, dst, self.aside.at[zz], sem, p.side)

    def start(self, src):
        self.move(src, self.p.s, self.p.z)

    def wait(self, t):
        self.p.arrived(self.view(t), self.arrivals(t), self.spare)

    def step(self, k, then=None):
        zz = self.p.line(k)
        t = self.p.mine(zz)
        self.wait(t)
        self.move(self.view(t), t, zz)
        if then is not None:
            then(t)

    def other(self, k, then=None):
        t = self.p.theirs(self.p.line(k))
        self.wait(t)
        if then is not None:
            then(t)

    def finish(self):
        block = self.view(self.p.s)
        for zz in range(4):
            self.p.sent(block, self.aside.at[zz], self.spare)
            self.p.went_onward(zz, lambda d: self.p.sent(block, self.along.at[zz, d], self.spare))


def gather_body(
    x_ref, seg_ref, ga_ref, bq_ref, gf_ref, wq_ref, wo_ref, wg_ref, wu_ref, c_ref,
    WQ_out, WO_out, G, C, cos_ref, sin_ref, gains, queries, keys, values, probs, att, a1, mid, a2,
    WQ, WO, vg, vu, GS, CS, S, bias,
    rq, ro, rg, rc, rs, szq, syq, sdq, szo, syo, sdo, sg, sdg, scz, scy, ss, loc,
):
    p = Place()
    r, s, c, z = p.r, p.s, p.c, p.z
    spare = loc.at[0]
    own = rows_of(192 * s, 192)
    own_c = rows_of(128 * s, 128, 128)
    loads = (
        pltpu.make_async_copy(wq_ref, WQ.at[own], loc.at[1]),
        pltpu.make_async_copy(wo_ref, WO.at[own], loc.at[2]),
        pltpu.make_async_copy(wg_ref, vg, loc.at[3]),
        pltpu.make_async_copy(wu_ref, vu, loc.at[4]),
        pltpu.make_async_copy(c_ref, CS, loc.at[5]),
    )
    for copy in loads:
        copy.start()
    p.greet(range(1, 8))
    gap = jnp.zeros((1, 64), F32)
    small = jnp.concatenate(
        [ga_ref[...].astype(F32)[None], gap, bq_ref[...].astype(F32)[None], gf_ref[...].astype(F32)[None], gap],
        axis=1,
    )
    S[s] = jnp.broadcast_to(small, (16, 768)).astype(BF)

    def vq(t, q):
        return WQ.at[quarter(t, q)]

    def vo(t, q):
        return WO.at[quarter(t, q)]

    def gq(t, q):
        return G.at[quarter(t, q)]

    def cot_block(t):
        return C.at[rows_of(128 * t, 128, 128)]

    g_q = Gather(p, spare, lambda t: vq(t, r), lambda t: rq.at[t, r], szq, syq)
    g_o = Gather(p, spare, lambda t: vo(t, r), lambda t: ro.at[t, r], szo, syo)
    g_c = Gather(p, spare, cot_block, lambda t: rc.at[t], scz, scy)

    def share(view, sems, rsems):
        def to_replicas(t):
            v = view(t, r)
            send(v, v, sems.at[t, 0], rsems.at[t, r], p.across)
            send(v, v, sems.at[t, 1], rsems.at[t, r], p.core)

        return to_replicas

    def relay(view, sems, rsems, t):
        v = view(t, p.rx)
        p.arrived(v, rsems.at[t, p.rx], spare)
        send(v, v, sems.at[t, 2], rsems.at[t, p.rx], p.core)

    def from_core(view, rsems):
        @pl.loop(1, 8)
        def _(k):
            t = (s + k) % 8
            p.arrived(view(t, p.rc), rsems.at[t, p.rc], spare)
            p.arrived(view(t, p.rd), rsems.at[t, p.rd], spare)

    share_q, share_o, share_g = share(vq, sdq, rq), share(vo, sdo, ro), share(gq, sdg, rg)

    def owner(k):
        return 2 * ((z + 1 + k // 2) % 4) + (p.y if k % 2 else 1 - p.y)

    def source(k):
        return 2 * ((z + 3 - k // 2) % 4) + (p.y if k % 2 else 1 - p.y)

    def along(k):
        return p.mine(p.line(k)) if k < 4 else p.theirs(p.line(k - 4))

    def q_step(k):
        g_q.step(k, share_q)

    def q_other(k):
        g_q.other(k, share_q)

    def q_relay(k):
        relay(vq, sdq, rq, along(k))

    def o_start():
        g_o.start(wo_ref.at[rows_of(48 * r, 48)])

    def o_step(k):
        g_o.step(k, share_o)

    def o_other(k):
        g_o.other(k, share_o)

    def o_relay(k):
        relay(vo, sdo, ro, along(k))

    def c_start():
        g_c.start(CS)

    def give(k):
        t = owner(k)
        send(GS.at[t, rows_of(48 * r, 48)], gq(s, r), sg.at[t], rg.at[s, r], p.peer(t))

    def take(k):
        t = source(k)
        p.arrived(gq(t, r), rg.at[t, r], spare)
        share_g(t)

    def g_relay(k):
        relay(gq, sdg, rg, source(k))

    own_out = (
        pltpu.make_async_copy(GS.at[s], G.at[own], loc.at[1]),
        pltpu.make_async_copy(CS, C.at[own_c], loc.at[2]),
    )
    save = (pltpu.make_async_copy(WQ, WQ_out, loc.at[3]), pltpu.make_async_copy(WO, WO_out, loc.at[4]))
    kept = {}

    def prepare():
        for copy in loads:
            copy.wait()
        zeros = jnp.zeros((192, 32), BF)
        for t in range(8):
            GS[t, :, 0:1120] = vg[:, 1120 * t : 1120 * t + 1120]
            GS[t, :, 1120:1152] = zeros
            GS[t, :, 1152:2272] = vu[:, 1120 * t : 1120 * t + 1120]
            GS[t, :, 2272:2304] = zeros
        for copy in own_out:
            copy.start()
        across = jnp.broadcast_to(seg_ref[...].astype(F32), (128, 128))
        down = across.T
        row = lax.broadcasted_iota(jnp.int32, (128, 128), 0)
        column = lax.broadcasted_iota(jnp.int32, (128, 128), 1)
        earlier = jnp.sum(jnp.where(across < down, 1.0, 0.0), axis=1, keepdims=True)
        position = row.astype(F32) - earlier
        half = (column - 64 * (column // 64)).astype(F32)
        angle = position * jnp.exp(half * (-2.0 * math.log(rope_base) / HEAD_DIMENSION))
        cos_ref[...] = jnp.cos(angle)
        sin_ref[...] = jnp.where(column < 64, -1.0, 1.0) * jnp.sin(angle)
        kept["open"] = (across == down) & (column <= row)

    def first_norm():
        @pl.loop(1, 8)
        def _(k):
            t = (s + k) % 8
            p.arrived(S.at[t], rs.at[t], spare)

        for t in range(8):
            row = S[t, 0:1, :].astype(F32)
            gains[0:1, 192 * t : 192 * t + 192] = row[:, 0:192]
            bias[0:1, 256 * t : 256 * t + 256] = row[:, 256:512]
            gains[1:2, 192 * t : 192 * t + 192] = row[:, 512:704]
        x = x_ref[...].astype(F32)
        a1[...] = (x * inverse_norm(x) * gains[0:1, :]).astype(BF)

    def q_all():
        from_core(vq, rq)

    def o_all():
        from_core(vo, ro)

    def attend():
        cosine, sine = cos_ref[...], sin_ref[...]
        for j in range(4):
            co = pl.ds(512 * j, 512)
            joined = dot(a1[...], WQ[:, co]) + bias[0:1, co]
            for i in range(4):
                h = 4 * j + i
                u = joined[:, 128 * i : 128 * i + 128]
                if h < 14:
                    u = u * cosine + pltpu.roll(u, 64, 1) * sine
                if h < 12:
                    queries[h // 6, pl.ds(128 * (h % 6), 128), :] = (u * HEAD_DIMENSION**-0.5).astype(BF)
                elif h < 14:
                    keys[h - 12] = u.astype(BF)
                else:
                    values[h - 14] = u.astype(BF)
        save[0].start()
        for g in range(2):
            scores = dot_nt(queries[g], keys[g]).reshape(6, 128, 128)
            scores = jnp.where(kept["open"][None], scores, -1e30)
            ex = jnp.exp(scores - jnp.max(scores, axis=-1, keepdims=True))
            soft = (ex / jnp.sum(ex, axis=-1, keepdims=True)).reshape(768, 128)
            probs[g] = soft.astype(BF)
            out = dot(probs[g], values[g]).astype(BF)
            for i in range(6):
                att[:, pl.ds(128 * (6 * g + i), 128)] = out[128 * i : 128 * i + 128]

    def second_norm():
        save[1].start()
        x = x_ref[...].astype(F32)
        for j in range(3):
            co = pl.ds(512 * j, 512)
            mid[:, co] = x[:, 512 * j : 512 * j + 512] + dot(att[...], WO[:, co])
        hidden = mid[...]
        a2[...] = (hidden * inverse_norm(hidden) * gains[1:2, :]).astype(BF)

    at_end = (z == 0) | (z == 3)
    in_middle = (z == 1) | (z == 2)
    g_q.start(wq_ref.at[rows_of(48 * r, 48)])
    for k in range(1, 8):
        t = (s + k) % 8
        send(S.at[s], S.at[s], ss.at[t], rs.at[s], p.peer(t))
    prepare()

    @pl.when(at_end)
    def _():
        q_other(0)
        o_start()
        give(0)
        give(1)
        give(6)
        q_step(1)
        o_other(0)
        c_start()
        o_step(1)
        take(0)
        take(6)
        give(5)
        o_step(2)
        q_relay(4)
        q_other(1)
        q_step(3)


    @pl.when(in_middle)
    def _():
        o_start()
        give(1)
        q_step(1)
        give(0)
        give(6)

    q_step(2)
    first_norm()

    @pl.when(at_end)
    def _():
        o_step(3)
        o_relay(1)
        q_relay(3)
        q_other(3)
        q_relay(1)
        take(5)
        o_other(2)
        take(1)
        q_relay(5)
        o_relay(4)
        o_relay(3)
        give(3)
        q_relay(2)
        q_other(2)
        give(4)
        g_c.step(1)
        give(2)
        g_relay(1)
        o_other(3)
        o_other(1)
        o_relay(7)
        take(4)
        take(2)
        q_relay(6)
        g_c.step(2)
        q_relay(7)
        g_c.step(3)
        o_relay(6)
        g_relay(0)


    @pl.when(in_middle)
    def _():
        q_other(0)
        o_step(1)
        o_step(2)
        q_relay(4)
        q_step(3)
        give(5)
        take(1)
        q_other(1)
        o_step(3)
        o_relay(1)
        o_other(0)
        c_start()
        give(2)
        q_relay(1)
        g_relay(1)
        give(4)
        q_other(3)
        take(5)
        o_other(2)
        g_c.step(1)
        give(3)
        q_relay(5)
        take(0)
        take(6)
        q_relay(3)
        q_other(2)
        g_c.step(2)
        o_other(1)
        q_relay(2)
        o_relay(3)
        o_relay(6)
        g_relay(0)
        o_relay(4)
        q_relay(6)
        q_relay(7)
        take(4)
        o_other(3)
        g_c.step(3)
        g_relay(5)
        take(2)

    q_all()
    g_relay(6)
    attend()
    o_relay(5)

    @pl.when(at_end)
    def _():
        o_relay(2)
        g_relay(5)
        take(3)


    @pl.when(in_middle)
    def _():
        o_relay(7)
        take(3)
        o_relay(2)

    g_relay(2)
    o_all()
    g_relay(4)
    g_relay(3)
    second_norm()
    from_core(gq, rg)

    @pl.loop(0, 4)
    def _(k):
        g_c.other(k)

    g_q.finish()
    g_o.finish()
    g_c.finish()

    @pl.loop(1, 8)
    def _(k):
        t = (s + k) % 8
        p.sent(S.at[t], ss.at[t], spare)
        p.sent(gq(t, r), sg.at[t], spare)
        for d in range(3):
            p.sent(vq(t, r), sdq.at[t, d], spare)
            p.sent(vo(t, r), sdo.at[t, d], spare)
            p.sent(gq(t, r), sdg.at[t, d], spare)

    for copy in own_out + save:
        copy.wait()


def gather_weights(x, segments, gain_attn, b_qkv, gain_ffn, w_qkv, w_out, w_gate, w_up, cot):
    return pl.pallas_call(
        gather_body,
        out_shape=(
            shaped(1536, 2048), shaped(1536, 1536), shaped(1536, 2304), shaped(1024, 1536), shaped(128, 128, dtype=F32),
            shaped(128, 128, dtype=F32), shaped(8, 1536, dtype=F32), shaped(2, 768, 128), shaped(2, 128, 128), shaped(2, 128, 128), shaped(2, 768, 128),
            shaped(128, 1536), shaped(128, 1536), shaped(128, 1536, dtype=F32), shaped(128, 1536),
        ),
        in_specs=[VMEM] * 5 + [HBM] * 5,
        out_specs=(HBM,) * 4 + (VMEM,) * 11,
        scratch_shapes=[
            low(1536, 2048), low(1536, 1536), low(192, 8960), low(192, 8960), low(8, 192, 2304), low(128, 1536),
            low(8, 16, 768), full(8, 2048),
            DMA((8, 4)), DMA((8, 4)), DMA((8, 4)), DMA((8,)), DMA((8,)),
            DMA((4, 2)), DMA((4,)), DMA((8, 3)), DMA((4, 2)), DMA((4,)), DMA((8, 3)),
            DMA((8,)), DMA((8, 3)), DMA((4, 2)), DMA((4,)), DMA((8,)), DMA((6,)),
        ],
        compiler_params=pltpu.CompilerParams(collective_id=0, has_side_effects=True, vmem_limit_bytes=56 << 20),
        name="gather_and_attend",
    )(x, segments, gain_attn, b_qkv, gain_ffn, w_qkv, w_out, w_gate, w_up, cot)


class RowSums:
    def __init__(self, p, spare, total, chip, side, far, across, out, sems, width):
        self.p, self.spare, self.total, self.chip, self.side = p, spare, total, chip, side
        self.far, self.across, self.out, self.sems = far, across, out, sems
        self.width = width

    def part(self, t, q):
        return self.total.at[quarter(t, q), 0 : self.width]

    def slot(self, t, xx):
        return self.chip.at[t, xx, :, 0 : self.width]

    def own(self, k):
        p = self.p
        return 2 * p.line(3 - k % 4) + (1 - p.y + (k // 4) * (2 * p.y - 1))

    def to_core(self, t):
        p = self.p
        for xx in range(2):
            send(
                self.part(t, 2 * xx + 1 - p.c), self.slot(t, xx),
                self.sems[0].at[t, xx], self.sems[1].at[t, xx], p.core,
            )

    def add(self, t, q, ref, sem):
        self.p.arrived(ref, sem, self.spare)
        total = self.part(t, q)
        total[...] = (total[...].astype(F32) + ref[...].astype(F32)).astype(BF)

    def on_chip(self, k):
        p, t = self.p, self.own(k)
        for xx in range(2):
            self.add(t, 2 * xx + p.c, self.slot(t, xx), self.sems[1].at[t, xx])

    def aside(self, k):
        p, t = self.p, self.own(k)
        for xx in range(2):
            at = t // 2, xx
            send(self.part(t, 2 * xx + p.c), self.side.at[at], self.sems[2].at[at], self.sems[3].at[at], p.side)

    def on_line(self, k):
        p = self.p
        zz = p.line(3 - k)
        t = p.mine(zz)
        for xx in range(2):
            q = 2 * xx + p.c
            self.add(t, q, self.side.at[zz, xx], self.sems[3].at[zz, xx])
            p.reduce_step(
                zz,
                lambda slot: self.add(t, q, self.far.at[slot, xx], self.sems[5].at[slot, xx]),
                lambda slot, device: send(
                    self.part(t, q), self.far.at[slot, xx], self.sems[4].at[zz, xx], self.sems[5].at[slot, xx], device
                ),
            )

    def at_owner(self):
        p = self.p
        for xx in range(2):
            send(self.part(p.s, 2 * xx + p.c), self.across.at[xx], self.sems[6].at[xx], self.sems[7].at[xx], p.across)

    def spread(self):
        p = self.p
        for xx in range(2):
            q = 2 * xx + p.c
            p.sent(self.across.at[xx], self.sems[6].at[xx], self.spare)
            self.add(p.s, q, self.across.at[xx], self.sems[7].at[xx])
            total = self.part(p.s, q)
            pltpu.make_async_copy(total, self.out.at[q], self.sems[6].at[4 + xx]).start()
            send(total, self.out.at[q], self.sems[6].at[2 + xx], self.sems[7].at[2 + xx], p.core)

    def finish(self):
        p = self.p
        for xx in range(2):
            q = 2 * xx + 1 - p.c
            p.arrived(self.out.at[q], self.sems[7].at[2 + xx], self.spare)
            p.sent(self.out.at[q], self.sems[6].at[2 + xx], self.spare)
            pltpu.make_async_copy(self.part(p.s, 0), self.out.at[q], self.sems[6].at[4 + xx]).wait()

        @pl.loop(0, 8)
        def _(t):
            for xx in range(2):
                p.sent(self.slot(t, xx), self.sems[0].at[t, xx], self.spare)

        @pl.loop(0, 4)
        def _(i):
            for xx in range(2):
                p.sent(self.side.at[i, xx], self.sems[2].at[i, xx], self.spare)

                @pl.when(i != p.z)
                def _():
                    p.sent(self.far.at[i, xx], self.sems[4].at[i, xx], self.spare)

    @staticmethod
    def buffers(width):
        return [low(8, 2, 48, width), low(4, 2, 48, width), low(5, 2, 48, width), low(2, 48, width)]

    @staticmethod
    def semaphores():
        return [DMA((8, 2)), DMA((8, 2)), DMA((4, 2)), DMA((4, 2)), DMA((4, 2)), DMA((5, 2)), DMA((6,)), DMA((4,))]


def layer_back_body(
    n_ref, c_hbm, g_hbm, d_hbm, wq_hbm, wo_hbm, att_hbm, a1_hbm, x_hbm, cot_hbm, q_hbm,
    mid_ref, gains, cos_ref, sin_ref, keys, values, probs,
    out_ref, gtok_ref, OG, OD, OWq, OWo,
    NC, H, vG, vD, MX, PD, PO, YD, ZD, YO, ZO, YB, ZB, RCd, RXd, RC, RX, dj, AT, SM,
    Yq, Zq, RXq, RCo, Yo, Zo, RXo,
    free, rn, syn, szn, ryd, rzd, syd, szd, syo, ryo, szo, rzo, syb, ryb, szb, rzb,
    scd, rcd, sxd, rxd, sfd, rfd, scg, rcg, sx, rx, sa, ra, sf, *sems,
):
    p = Place()
    r, s, c, y, z = p.r, p.s, p.c, p.y, p.z
    loc = sems[-1]
    spare = loc.at[0]
    q_sums = RowSums(p, spare, H, RC, Yq, Zq, RXq, OWq, sems[0:8], 2176)
    o_sums = RowSums(p, spare, NC, RCo, Yo, Zo, RXo, OWo, sems[8:16], 1536)

    def block(t):
        return NC.at[rows_of(128 * t, 128, 128)]

    def cot_rows(start, size):
        return rows_of(1024 + start, size, 128)

    loads = (
        pltpu.make_async_copy(n_ref, block(s), loc.at[1]),
        pltpu.make_async_copy(c_hbm, NC.at[1024:2048], loc.at[2]),
        pltpu.make_async_copy(g_hbm, vG, loc.at[3]),
        pltpu.make_async_copy(d_hbm, vD.at[0:1120], loc.at[4]),
    )
    for copy in loads:
        copy.start()
    p.greet(range(1, 8))
    g_n = Gather(p, spare, block, lambda t: rn.at[t], szn, syn)
    g_n.start(n_ref)
    vD[1120:1152, :] = jnp.zeros((32, 1536), BF)
    for copy in loads:
        copy.wait()

    def side(P, Y, ssem, rsem, k):
        zz = p.line(k)
        send(P.at[p.theirs(zz)], Y.at[zz], ssem.at[zz], rsem.at[zz], p.side)

    def side_d(k):
        side(PD, YD, syd, ryd, k)

    def line_step(P, Y, Z, ry, sz, rz, k):
        zz = p.line(k)
        t = p.mine(zz)

        def add(ref, sem):
            p.arrived(ref, sem, spare)
            P[t] = (P[t].astype(F32) + ref[...].astype(F32)).astype(BF)

        add(Y.at[zz], ry.at[zz])
        p.reduce_step(
            zz,
            lambda slot: add(Z.at[slot], rz.at[slot]),
            lambda slot, device: send(P.at[t], Z.at[slot], sz.at[zz], rz.at[slot], device),
        )

    def step_d(k):
        line_step(PD, YD, ZD, ryd, szd, rzd, k)

    def side_oa(k):
        zz = p.line(k)
        send(PO.at[p.theirs(zz), :, 0:768], YO.at[zz], syo.at[zz], ryo.at[zz], p.side)

    def step_oa(k):
        zz = p.line(k)
        half = PO.at[p.mine(zz), :, 0:768]

        def add(ref, sem):
            p.arrived(ref, sem, spare)
            half[...] = (half[...].astype(F32) + ref[...].astype(F32)).astype(BF)

        add(YO.at[zz], ryo.at[zz])
        p.reduce_step(
            zz,
            lambda slot: add(ZO.at[slot], rzo.at[slot]),
            lambda slot, device: send(half, ZO.at[slot], szo.at[zz], rzo.at[slot], device),
        )

    def step_ob(k):
        zz = p.line(k)
        both = PO.at[pl.ds(2 * zz, 2), :, 768:1536]

        def add(slot):
            p.arrived(ZB.at[slot], rzb.at[slot], spare)
            both[...] = (both[...].astype(F32) + ZB[slot].astype(F32)).astype(BF)

        p.reduce_step(
            zz, add, lambda slot, device: send(both, ZB.at[slot], szb.at[zz], rzb.at[slot], device)
        )

    def side_ob():
        send(PO.at[p.theirs(z), :, 768:1536], YB, syb, ryb, p.side)

    at_end = (z == 0) | (z == 3)
    in_middle = (z == 1) | (z == 2)
    g_n.step(1)

    @pl.loop(0, 4)
    def _(k):
        zz = p.line(k)
        pl.when(at_end & (k > 0) & (k < 3))(lambda: g_n.step(k + 1))
        pl.when(in_middle & (k < 2))(lambda: g_n.step(k + 2))
        g_n.other(k)
        rows = rows_of(256 * zz, 256, 256)
        X = NC[rows]
        cot = NC[cot_rows(256 * zz, 256)]
        for j in range(3):
            ga, ua = pl.ds(384 * j, 384), pl.ds(1152 + 384 * j, 384)
            gate = dot(X, vG[:, ga])
            up = dot(X, vG[:, ua])
            d_mixed = dot_nt(cot, vD[ga])
            sg = jax.nn.sigmoid(gate)
            active = gate * sg
            d_active = d_mixed * up
            MX[rows, ga] = (active * up).astype(BF)
            H[rows, ga] = (d_active * sg + d_active * active * (1.0 - sg)).astype(BF)
            H[rows, ua] = (d_mixed * active).astype(BF)
        for j in range(3):
            co = pl.ds(512 * j, 512)
            part = dot_nt(H[rows], vG[co]).astype(BF)
            PD[2 * zz, :, co] = part[:128]
            PD[2 * zz + 1, :, co] = part[128:]
        pl.when(k == 2)(lambda: side_d(1))
        pl.when(k == 3)(lambda: side_d(3))
        for j in range(3):
            co = pl.ds(512 * j, 512)
            part = dot(MX[rows], vD[:, co]).astype(BF)
            PO[2 * zz, :, co] = part[:128]
            PO[2 * zz + 1, :, co] = part[128:]
        pl.when(at_end & (k == 1))(lambda: step_ob(1))
        pl.when(at_end & (k == 2))(lambda: step_ob(2))

    side_d(2)
    side_d(0)

    def owner(k):
        return 2 * ((z + 1 + k // 2) % 4) + (k % 2) * (2 * y - 1) + 1 - y

    def pair_chip(k):
        t = owner(k)
        for xx in range(2):
            p.arrived(RC.at[t, xx], rcg.at[t, xx], spare)
            q = quarter(t, 2 * xx + c)
            vG[q] = (vG[q].astype(F32) + RC[t, xx].astype(F32)).astype(BF)
        send(vG.at[quarter(t, p.rx)], RX.at[t], sx.at[t], rx.at[t], p.across)

    @pl.loop(0, 5)
    def _(j):
        @pl.when(j < 4)
        def _():
            pair = (z + 1 + j) % 4
            rows = rows_of(384 * pair, 384, 128)
            X = NC[0:1024, rows].T
            for i in range(3):
                co = pl.ds(768 * i, 768)
                vG[rows, co] = dot(X, H[0:1024, co]).astype(BF)
            for i in range(2):
                t = owner(2 * j + i)
                for xx in range(2):
                    send(vG.at[quarter(t, 2 * xx + 1 - c)], RC.at[t, xx], scg.at[t, xx], rcg.at[t, xx], p.core)

        @pl.when(j > 0)
        def _():
            pair_chip(2 * j - 2)
            pair_chip(2 * j - 1)

    pl.semaphore_signal(free, inc=1, device_id=p.core, device_id_type=MESH)

    def chunk(i):
        return rows_of(384 * i, 384, 128)

    def cols(q):
        return rows_of(384 * q, 384, 128)

    held = (
        pltpu.make_async_copy(wo_hbm, NC.at[0:1536], loc.at[1]),
        pltpu.make_async_copy(wq_hbm, H.at[:, 0:2048], loc.at[2]),
        pltpu.make_async_copy(att_hbm, NC.at[1536:1664], loc.at[3]),
        pltpu.make_async_copy(a1_hbm, NC.at[1664:1792], loc.at[4]),
        pltpu.make_async_copy(x_hbm, NC.at[1792:1920], loc.at[5]),
        pltpu.make_async_copy(cot_hbm, NC.at[1920:2048], loc.at[6]),
        pltpu.make_async_copy(q_hbm.at[0], MX.at[0:768, 256:384], loc.at[8]),
        pltpu.make_async_copy(q_hbm.at[1], MX.at[0:768, 384:512], loc.at[9]),
    )

    def down_terms():
        @pl.loop(0, 3)
        def _(i):
            X = MX[:, chunk(i)].T
            for j in range(3):
                co = pl.ds(512 * j, 512)
                vD[chunk(i), co] = dot(X, NC[1024:2048, co]).astype(BF)
            for xx in range(2):
                q = 2 * xx + 1 - c
                send(vD.at[chunk(i), cols(q)], RCd.at[xx, chunk(i)], scd.at[i, xx], rcd.at[i, xx], p.core)

        g_n.finish()
        for copy in held:
            copy.start()

        @pl.loop(0, 3)
        def _(i):
            for xx in range(2):
                p.arrived(RCd.at[xx, chunk(i)], rcd.at[i, xx], spare)
                q = cols(2 * xx + c)
                vD[chunk(i), q] = (vD[chunk(i), q].astype(F32) + RCd[xx, chunk(i)].astype(F32)).astype(BF)

    def pair_whole(k):
        t = owner(k)
        q = quarter(t, r)
        p.arrived(RX.at[t], rx.at[t], spare)
        vG[q] = (vG[q].astype(F32) + RX[t].astype(F32)).astype(BF)

        if k < 7:
            send(vG.at[q], OG.at[r, s], sa.at[t], ra.at[s, r], p.peer(t))
        else:
            pltpu.make_async_copy(vG.at[q], OG.at[r, s], loc.at[7]).start()

    def share(t):
        v = OG.at[r, t]
        send(v, v, sf.at[t, 0], ra.at[t, r], p.across)
        send(v, v, sf.at[t, 1], ra.at[t, r], p.core)

    def source(k):
        return 2 * ((z + 3 - k // 2) % 4) + (1 - y if k % 2 == 0 else y)

    def take(k):
        t = source(k)
        if k < 7:
            p.arrived(OG.at[r, t], ra.at[t, r], spare)
        else:
            pltpu.make_async_copy(vG.at[quarter(s, r)], OG.at[r, s], loc.at[7]).wait()
        share(t)

    def relay(k):
        t = source(k)
        v = OG.at[p.rx, t]
        p.arrived(v, ra.at[t, p.rx], spare)
        send(v, v, sf.at[t, 2], ra.at[t, p.rx], p.core)

    def down_across(i):
        send(vD.at[chunk(i), cols(p.rx)], RXd.at[chunk(i)], sxd.at[i], rxd.at[i], p.across)

    def down_whole(i):
        p.arrived(RXd.at[chunk(i)], rxd.at[i], spare)
        q = cols(r)
        vD[chunk(i), q] = (vD[chunk(i), q].astype(F32) + RXd[chunk(i)].astype(F32)).astype(BF)
        src, dst = vD.at[chunk(i), q], OD.at[r, chunk(i)]
        pltpu.make_async_copy(src, dst, sfd.at[i, 3]).start()
        send(src, dst, sfd.at[i, 0], rfd.at[i, r], p.across)
        send(src, dst, sfd.at[i, 1], rfd.at[i, r], p.core)

    def down_relay(i):
        v = OD.at[p.rx, chunk(i)]
        p.arrived(v, rfd.at[i, p.rx], spare)
        send(v, v, sfd.at[i, 2], rfd.at[i, p.rx], p.core)

    def back(w):
        return w * cos_ref[...] - pltpu.roll(w, 64, 1) * sin_ref[...]

    kept = {}

    def attention_out():
        for copy in held:
            copy.wait()
        dn, hidden = PD[s].astype(F32), mid_ref[...]
        rstd = inverse_norm(hidden)
        unit = hidden * rstd
        kept["ffn"] = jnp.sum(dn * unit, axis=0, keepdims=True)
        e = dn * gains[1:2, :]
        dm = NC[1920:2048].astype(F32) + rstd * (e - unit * jnp.mean(e * unit, axis=-1, keepdims=True))
        NC[1920:2048] = dm.astype(BF)
        AT[...] = NC[1536:1664].T
        for j in range(3):
            part = dot_nt(NC[1920:2048], NC[pl.ds(512 * j, 512)]).astype(BF)
            for i in range(4):
                h = 4 * j + i
                MX[pl.ds(128 * (h % 6), 128), pl.ds(128 * (h // 6), 128)] = part[:, 128 * i : 128 * i + 128]
        for j in range(3):
            co = pl.ds(512 * j, 512)
            NC[0:1536, co] = dot(AT[...], NC[1920:2048, co]).astype(BF)

        @pl.loop(0, 8)
        def _(k):
            o_sums.to_core(o_sums.own(k))

    def heads(g):
        grad = MX[0:768, 128 * g : 128 * g + 128]
        query = MX[0:768, 256 + 128 * g : 384 + 128 * g]
        soft = probs[g].astype(F32)
        d_probs = dot_nt(grad, values[g])
        d_scores = (soft * (d_probs - jnp.sum(soft * d_probs, axis=-1, keepdims=True))).astype(BF)
        d_values = dot(probs[g].T, grad)
        d_queries = dot(d_scores, keys[g]) * HEAD_DIMENSION**-0.5
        d_keys = dot(d_scores.T, query)
        for i in range(6):
            dj[:, pl.ds(128 * (6 * g + i), 128)] = back(d_queries[128 * i : 128 * i + 128]).astype(BF)
        dj[:, pl.ds(128 * (12 + g), 128)] = back(d_keys).astype(BF)
        dj[:, pl.ds(128 * (14 + g), 128)] = d_values.astype(BF)

    def attention_in():
        heads(1)
        joined_grad = dj[...]
        bias_grad = jnp.sum(joined_grad.astype(F32), axis=0, keepdims=True)
        x = NC[1792:1920].astype(F32)
        rstd = inverse_norm(x)
        unit = x * rstd
        dn1 = jnp.concatenate(
            [dot_nt(joined_grad, H[pl.ds(512 * j, 512), 0:2048]) for j in range(3)], axis=1
        )
        gain_attn_grad = jnp.sum(dn1 * unit, axis=0, keepdims=True)
        e = dn1 * gains[0:1, :]
        NC[1792:1920] = (
            NC[1920:2048].astype(F32) + rstd * (e - unit * jnp.mean(e * unit, axis=-1, keepdims=True))
        ).astype(BF)
        pltpu.make_async_copy(NC.at[1792:1920], gtok_ref, loc.at[5]).start()
        SM[...] = jnp.zeros_like(SM)
        ffn = kept["ffn"]
        for t in range(8):
            SM[t, 0:1, :] = gain_attn_grad[:, 192 * t : 192 * t + 128]
            SM[t, 1:2, 0:64] = gain_attn_grad[:, 192 * t + 128 : 192 * t + 192]
            SM[t, 2:3, :] = bias_grad[:, 256 * t : 256 * t + 128]
            SM[t, 3:4, :] = bias_grad[:, 256 * t + 128 : 256 * t + 256]
            SM[t, 4:5, :] = ffn[:, 192 * t : 192 * t + 128]
            SM[t, 5:6, 0:64] = ffn[:, 192 * t + 128 : 192 * t + 192]
        AT[...] = NC[1664:1792].T

    def joined_terms():
        pl.semaphore_wait(free, 1)

        @pl.loop(0, 8)
        def _(k):
            t = q_sums.own(k)
            rows = rows_of(192 * t, 192)
            for j in range(2):
                co = pl.ds(1024 * j, 1024)
                H[rows, co] = dot(AT[rows], dj[:, co]).astype(BF)
            H[rows, 2048:2176] = jnp.zeros((192, 128), BF)
            H[rows_of(192 * t, 16), 2048:2176] = SM[t].astype(BF)
            q_sums.to_core(t)

    def on_chip(sums):
        @pl.loop(0, 8)
        def _(k):
            sums.on_chip(k)

    def finish_out():
        p.arrived(YB, ryb, spare)
        PO[s, :, 768:1536] = (PO[s, :, 768:1536].astype(F32) + YB[...].astype(F32)).astype(BF)
        PO[s] = (PO[s].astype(F32) + mid_ref[...]).astype(BF)
        pltpu.make_async_copy(PO.at[s], out_ref, loc.at[6]).start()

    def first_heads():
        heads(0)

    def o_on_chip():
        on_chip(o_sums)

    def q_on_chip():
        on_chip(q_sums)


    @pl.when(at_end)
    def _():
        step_d(3)
        side_oa(3)
        step_d(2)
        side_oa(2)
        side_oa(0)
        step_d(1)
        pair_whole(3)


    @pl.when(in_middle)
    def _():
        side_oa(2)
        side_oa(0)
        step_ob(2)
        step_d(3)
        step_d(2)
        step_d(1)
        pair_whole(6)

    down_terms()

    @pl.when(at_end)
    def _():
        step_ob(3)
        pair_whole(6)
        down_across(1)
        pair_whole(5)
        step_oa(3)
        pair_whole(0)
        down_across(0)
        side_oa(1)


    @pl.when(in_middle)
    def _():
        side_oa(3)
        pair_whole(5)
        down_across(0)
        side_oa(1)
        pair_whole(3)
        take(3)
        pair_whole(1)
        down_across(1)
        pair_whole(2)

    step_d(0)
    attention_out()

    @pl.when(at_end)
    def _():
        down_across(2)

    first_heads()
    attention_in()

    @pl.when(at_end)
    def _():
        pair_whole(4)
        pair_whole(2)

    joined_terms()

    @pl.when(in_middle)
    def _():
        pair_whole(4)

    o_on_chip()

    @pl.when(at_end)
    def _():
        o_sums.aside(2)
        take(3)
        o_sums.aside(0)
        pair_whole(1)
        take(6)


    @pl.when(in_middle)
    def _():
        down_across(2)
        o_sums.aside(2)
        pair_whole(7)
        down_whole(0)
        o_sums.aside(0)
        step_oa(3)
        pair_whole(0)
        take(7)

    q_on_chip()

    @pl.when(at_end)
    def _():
        q_sums.aside(0)
        take(2)
        q_sums.aside(1)
        down_whole(1)
        take(5)
        down_whole(0)
        pair_whole(7)
        o_sums.on_line(0)
        down_whole(2)
        take(1)
        q_sums.aside(2)
        take(7)
        q_sums.on_line(0)
        o_sums.aside(1)
        take(4)
        relay(5)
        q_sums.aside(3)
        q_sums.on_line(1)
        q_sums.on_line(2)
        step_ob(0)
        take(0)
        o_sums.on_line(1)
        o_sums.aside(3)
        q_sums.on_line(3)
        q_sums.at_owner()
        o_sums.on_line(2)
        relay(2)
        relay(3)
        step_oa(2)
        relay(4)
        o_sums.on_line(3)
        o_sums.at_owner()
        q_sums.spread()
        step_oa(1)
        down_relay(2)
        down_relay(0)
        relay(1)
        relay(6)
        relay(7)
        relay(0)
        side_ob()
        down_relay(1)
        step_oa(0)
        finish_out()
        o_sums.spread()


    @pl.when(in_middle)
    def _():
        q_sums.aside(1)
        q_sums.aside(0)
        take(4)
        take(6)
        down_whole(1)
        take(5)
        relay(3)
        step_ob(3)
        take(2)
        take(1)
        q_sums.aside(2)
        o_sums.on_line(0)
        q_sums.aside(3)
        o_sums.aside(1)
        down_whole(2)
        step_ob(1)
        q_sums.on_line(0)
        relay(5)
        o_sums.aside(3)
        q_sums.on_line(1)
        q_sums.on_line(2)
        step_ob(0)
        take(0)
        q_sums.on_line(3)
        q_sums.at_owner()
        relay(4)
        o_sums.on_line(2)
        side_ob()
        relay(2)
        o_sums.on_line(1)
        relay(6)
        o_sums.on_line(3)
        o_sums.at_owner()
        relay(0)
        step_oa(1)
        down_relay(1)
        down_relay(2)
        relay(7)
        down_relay(0)
        q_sums.spread()
        relay(1)
        step_oa(2)
        o_sums.spread()
        step_oa(0)
        finish_out()

    o_sums.finish()
    q_sums.finish()
    pltpu.make_async_copy(NC.at[1792:1920], gtok_ref, loc.at[5]).wait()
    pltpu.make_async_copy(PO.at[s], out_ref, loc.at[6]).wait()

    @pl.loop(0, 3)
    def _(i):
        for q in (p.rc, p.rd):
            p.arrived(OD.at[q, chunk(i)], rfd.at[i, q], spare)
        for d in range(3):
            p.sent(OD.at[r, chunk(i)], sfd.at[i, d], spare)
        pltpu.make_async_copy(OD.at[r, chunk(i)], OD.at[r, chunk(i)], sfd.at[i, 3]).wait()
        for xx in range(2):
            p.sent(RCd.at[xx, chunk(i)], scd.at[i, xx], spare)
        p.sent(RXd.at[chunk(i)], sxd.at[i], spare)

    @pl.loop(0, 8)
    def _(t):
        for q in (p.rc, p.rd):
            p.arrived(OG.at[q, t], ra.at[t, q], spare)
        for d in range(3):
            p.sent(OG.at[r, t], sf.at[t, d], spare)
        for xx in range(2):
            p.sent(RC.at[t, xx], scg.at[t, xx], spare)
        p.sent(RX.at[t], sx.at[t], spare)

        @pl.when(t != s)
        def _():
            p.sent(OG.at[r, s], sa.at[t], spare)

    @pl.loop(0, 4)
    def _(i):
        p.sent(YD.at[i], syd.at[i], spare)
        p.sent(YO.at[i], syo.at[i], spare)

        @pl.when(i != z)
        def _():
            p.sent(ZD.at[i], szd.at[i], spare)
            p.sent(ZO.at[i], szo.at[i], spare)
            p.sent(ZB.at[i], szb.at[i], spare)

    p.sent(YB, syb, spare)


def layer_back(*args):
    return pl.pallas_call(
        layer_back_body,
        out_shape=(
            shaped(128, 1536), shaped(128, 1536), shaped(4, 8, 48, 2304), shaped(4, 1152, 384), shaped(4, 48, 2176),
            shaped(4, 48, 1536),
        ),
        in_specs=[HBM] * 11 + [VMEM] * 7,
        out_specs=(HBM,) * 6,
        scratch_shapes=[
            low(2048, 1536), low(1536, 2304), low(1536, 2304), low(1152, 1536), low(1024, 1152),
            low(8, 128, 1536), low(8, 128, 1536), low(4, 128, 1536), low(5, 128, 1536), low(4, 128, 768), low(5, 128, 768),
            low(128, 768), low(5, 2, 128, 768),
            low(2, 1152, 384), low(1152, 384), low(8, 2, 48, 2304), low(8, 48, 2304),
            low(128, 2048), low(1536, 128), full(8, 16, 128),
            *RowSums.buffers(2176)[1:], *RowSums.buffers(1536),
            pltpu.SemaphoreType.REGULAR, DMA((8,)), DMA((4,)), DMA((4, 2)),
            DMA((4,)), DMA((5,)), DMA((4,)), DMA((4,)), DMA((4,)), DMA((4,)), DMA((4,)), DMA((5,)), DMA, DMA, DMA((4,)), DMA((5,)),
            DMA((3, 2)), DMA((3, 2)), DMA((3,)), DMA((3,)), DMA((3, 4)), DMA((3, 4)),
            DMA((8, 2)), DMA((8, 2)), DMA((8,)), DMA((8,)), DMA((8,)), DMA((8, 4)), DMA((8, 3)),
            *RowSums.semaphores(), *RowSums.semaphores(), DMA((10,)),
        ],
        compiler_params=pltpu.CompilerParams(collective_id=1, has_side_effects=True, vmem_limit_bytes=64 << 20),
        name="layer_back",
    )(*args)


def widen_body(
    g_ref, d_ref, q_ref, o_ref, x_ref, y_ref, gate, up, down, qkv, out, x_out, y_out, ga, bq, gf, narrow
):
    for first, wide in ((0, gate), (1152, up)):
        for t in range(8):
            narrow[:, 1120 * t : 1120 * t + 1120] = g_ref[0, t, :, first : first + 1120]
        wide[...] = narrow[...].astype(F32)
    down[...] = d_ref[0, 0:1120, :].astype(F32)
    qkv[...] = q_ref[0, :, 0:2048].astype(F32)
    out[...] = o_ref[0].astype(F32)
    x_out[...] = x_ref[...]
    y_out[...] = y_ref[...]

    @pl.when(pl.program_id(0) == 0)
    def _():
        small = q_ref[0, 0:16, 2048:2176].astype(F32)
        ga[...] = jnp.concatenate([small[0:1], small[1:2, 0:64]], axis=1)[0]
        bq[...] = jnp.concatenate([small[2:3], small[3:4]], axis=1)[0]
        gf[...] = jnp.concatenate([small[4:5], small[5:6, 0:64]], axis=1)[0]


def widen(g, d, q, o, x, y):
    def rows(size, width):
        return pl.BlockSpec((size, width), lambda i: (i, 0))

    def whole(size):
        return pl.BlockSpec((size,), lambda i: (0,))

    return pl.pallas_call(
        widen_body,
        grid=(4,),
        out_shape=(
            shaped(192, 8960, dtype=F32), shaped(192, 8960, dtype=F32), shaped(1120, 1536, dtype=F32),
            shaped(192, 2048, dtype=F32), shaped(192, 1536, dtype=F32), shaped(128, 1536), shaped(128, 1536),
            shaped(192, dtype=F32), shaped(256, dtype=F32), shaped(192, dtype=F32),
        ),
        in_specs=[
            pl.BlockSpec((1, 8, 48, 2304), lambda i: (i, 0, 0, 0)),
            pl.BlockSpec((1, 1152, 384), lambda i: (i, 0, 0)),
            pl.BlockSpec((1, 48, 2176), lambda i: (i, 0, 0)),
            pl.BlockSpec((1, 48, 1536), lambda i: (i, 0, 0)),
            rows(32, 1536),
            rows(32, 1536),
        ],
        out_specs=(
            rows(48, 8960), rows(48, 8960), pl.BlockSpec((1120, 384), lambda i: (0, i)), rows(48, 2048), rows(48, 1536),
            rows(32, 1536), rows(32, 1536), whole(192), whole(256), whole(192),
        ),
        scratch_shapes=[low(48, 8960)],
        compiler_params=pltpu.CompilerParams(vmem_limit_bytes=62 << 20),
        name="widen",
    )(g, d, q, o, x, y)


def shards_eight(
    tokens, segments, gain_attn, w_qkv, b_qkv, w_out, gain_ffn, w_gate, w_up, w_down, cotangent
):
    x, cot = tokens[0], cotangent[0]
    WQ, WO, G, C, cosine, sine, gains, queries, keys, values, probs, att, a1, mid, a2 = gather_weights(
        x, segments, gain_attn, b_qkv, gain_ffn, w_qkv, w_out, w_gate, w_up, cot
    )
    out, grad_tokens, gate_up, down, qkv, o = layer_back(
        a2, C, G, w_down, WQ, WO, att, a1, x, cot, queries, mid, gains, cosine, sine, keys, values, probs
    )
    gate, up, down, qkv_rows, out_rows, out, grad_tokens, ga, bq, gf = widen(gate_up, down, qkv, o, out, grad_tokens)
    return out[None], grad_tokens[None], ga, qkv_rows, bq, out_rows, gf, gate, up, down


def solution(mesh):
    placed = (
        P(("replica", "shard"), None, None),
        P(("replica", "shard"), None),
        P("shard"),
        P("shard", None),
        P("shard"),
        P("shard", None),
        P("shard"),
        P("shard", None),
        P("shard", None),
        P("shard", None),
        P(("replica", "shard"), None, None),
    )
    return jax.shard_map(
        shards_eight if (mesh.shape["replica"], mesh.shape["shard"]) == (4, 8) else shards,
        mesh=mesh,
        in_specs=placed,
        out_specs=(
            P(("replica", "shard"), None, None),
            P(("replica", "shard"), None, None),
            P("shard"),
            P("shard", None),
            P("shard"),
            P("shard", None),
            P("shard"),
            P("shard", None),
            P("shard", None),
            P("shard", None),
        ),
        check_vma=False,
    )
```

```python
import math

import jax
import jax.numpy as jnp
from jax import lax
from jax.experimental import pallas as pl
from jax.experimental.pallas import tpu as pltpu
from jax.sharding import PartitionSpec as P

QUERY_HEADS = 12
KEY_VALUE_HEADS = 2
HEAD_DIMENSION = 128


eps_norm = 1e-06
rope_base = 1000000.0


def tables(segment_ids, head_size):
    token_length = segment_ids.shape[-1]
    row_index = jnp.arange(token_length, dtype=jnp.int32)
    earlier = jnp.sum(
        (segment_ids[..., None, :] < segment_ids[..., :, None]).astype(jnp.int32),
        axis=-1,
        dtype=jnp.int32,
    )
    positions = (row_index - earlier).astype(jnp.float32)
    frequencies = jnp.exp(
        jnp.arange(head_size // 2, dtype=jnp.float32) * (-2.0 * math.log(rope_base) / head_size)
    )
    angles = positions[..., None] * frequencies
    cosine = jnp.concatenate([jnp.cos(angles), jnp.cos(angles)], axis=-1)
    sine_vals = jnp.concatenate([jnp.sin(angles), jnp.sin(angles)], axis=-1)
    allowed = (
        (segment_ids[..., None, :] == segment_ids[..., :, None])
        & (row_index[None, :] <= row_index[:, None])
    ).astype(jnp.int32)
    return (cosine, sine_vals, allowed)


def apply_rotation(values, cosine, sine_vals):
    halfway = values.shape[-1] // 2
    turned = jnp.concatenate([-values[..., halfway:], values[..., :halfway]], axis=-1)
    return values * cosine + turned * sine_vals


def rotate_back(values, cosine, sine_vals):
    halfway = values.shape[-1] // 2
    shifted = values * sine_vals
    return values * cosine + jnp.concatenate(
        [shifted[..., halfway:], -shifted[..., :halfway]], axis=-1
    )


def norm_forward(hidden, gain_vec):
    rstd_rows = lax.rsqrt(jnp.mean(hidden * hidden, axis=-1, keepdims=True) + eps_norm)
    unit_rows = hidden * rstd_rows
    return (unit_rows * gain_vec, unit_rows, rstd_rows)


def norm_backward(grad_in, gain_vec, unit_rows, rstd_rows):
    inner_grad = grad_in * gain_vec
    return rstd_rows * (
        inner_grad - unit_rows * jnp.mean(inner_grad * unit_rows, axis=-1, keepdims=True)
    )


def column_term(left_side, right_side):
    return jnp.einsum("lf,ld->fd", left_side, right_side, preferred_element_type=jnp.float32)


def to_columns(rows):
    ranks = lax.axis_size("shard")
    depth, width = rows.shape
    split = rows.reshape(depth, ranks, width // ranks).transpose(1, 0, 2)
    return lax.all_to_all(split, "shard", 0, 0, tiled=True).reshape(ranks * depth, width // ranks)


def to_rows(columns):
    ranks, copies = lax.axis_size("shard"), lax.axis_size("replica")
    depth, width = columns.shape
    depth = depth // ranks
    parts = columns.reshape(ranks, copies, depth // copies, width)
    part = lax.psum_scatter(parts, "replica", scatter_dimension=1, tiled=False)
    part = lax.all_to_all(part, "shard", 0, 0, tiled=True)
    part = part.transpose(1, 0, 2).reshape(depth // copies, ranks * width)
    return lax.all_gather(part, "replica", axis=0, tiled=True)


def shards(
    tokens, segments, gain_attn, w_qkv, b_qkv, w_out, gain_ffn, w_gate, w_up, w_down, cotangent
):
    heads_per_group = QUERY_HEADS // KEY_VALUE_HEADS
    head_dimension = QUERY_HEADS * HEAD_DIMENSION
    key_value_limit = head_dimension + KEY_VALUE_HEADS * HEAD_DIMENSION
    logit_scale = HEAD_DIMENSION ** (-0.5)
    token_length = tokens.shape[1]
    full_gain_attn, full_qkv, full_bias, full_out, full_gain_ffn = (
        lax.all_gather(gain_attn, "shard", axis=0, tiled=True),
        lax.all_gather(w_qkv, "shard", axis=0, tiled=True),
        lax.all_gather(b_qkv, "shard", axis=0, tiled=True),
        lax.all_gather(w_out, "shard", axis=0, tiled=True),
        lax.all_gather(gain_ffn, "shard", axis=0, tiled=True),
    )
    gate_columns = to_columns(w_gate)
    up_columns = to_columns(w_up)
    all_cot = lax.all_gather(cotangent[0], "shard", axis=0, tiled=True)
    gain_first = full_gain_attn.astype(jnp.float32)
    gain_second = full_gain_ffn.astype(jnp.float32)
    cosine, sine_vals, allowed = tables(segments[0], HEAD_DIMENSION)
    cosine_per_head = cosine[:, None, :]
    sine_per_head = sine_vals[:, None, :]
    inputs = tokens[0].astype(jnp.float32)
    normed_first, unit_first, rstd_first = norm_forward(inputs, gain_first)
    acts_first = normed_first.astype(jnp.bfloat16)
    joined_projection = jnp.dot(
        acts_first, full_qkv, preferred_element_type=jnp.float32
    ) + full_bias.astype(jnp.float32)
    query_rows = apply_rotation(
        joined_projection[:, :head_dimension].reshape(token_length, QUERY_HEADS, HEAD_DIMENSION),
        cosine_per_head,
        sine_per_head,
    )
    query_reduced = (
        (query_rows * logit_scale)
        .astype(jnp.bfloat16)
        .reshape(token_length, KEY_VALUE_HEADS, heads_per_group, HEAD_DIMENSION)
    )
    k_low = apply_rotation(
        joined_projection[:, head_dimension:key_value_limit].reshape(
            token_length, KEY_VALUE_HEADS, HEAD_DIMENSION
        ),
        cosine_per_head,
        sine_per_head,
    ).astype(jnp.bfloat16)
    value_reduced = (
        joined_projection[:, key_value_limit:]
        .reshape(token_length, KEY_VALUE_HEADS, HEAD_DIMENSION)
        .astype(jnp.bfloat16)
    )
    scores = jnp.einsum("ikrd,jkd->krij", query_reduced, k_low, preferred_element_type=jnp.float32)
    scores = jnp.where(allowed != 0, scores, -1e30)
    largest = jnp.max(scores, axis=-1, keepdims=True)
    exponents = jnp.exp(scores - largest)
    soft_probs = exponents / jnp.sum(exponents, axis=-1, keepdims=True)
    soft_low = soft_probs.astype(jnp.bfloat16)
    attended = jnp.einsum(
        "krij,jkd->ikrd", soft_low, value_reduced, preferred_element_type=jnp.float32
    )
    attended = attended.reshape(token_length, head_dimension).astype(jnp.bfloat16)
    hidden_mid = inputs + jnp.dot(attended, full_out, preferred_element_type=jnp.float32)
    normed_second, unit_second, rstd_second = norm_forward(hidden_mid, gain_second)
    acts_second = normed_second.astype(jnp.bfloat16)
    all_acts = lax.all_gather(acts_second, "shard", axis=0, tiled=True)
    gate_vals = jnp.dot(all_acts, gate_columns, preferred_element_type=jnp.float32)
    up_vals = jnp.dot(all_acts, up_columns, preferred_element_type=jnp.float32)
    sigmoid_gate = jax.nn.sigmoid(gate_vals)
    active = gate_vals * sigmoid_gate
    mixed_hidden = (active * up_vals).astype(jnp.bfloat16)
    d_mixed = jnp.einsum("ld,fd->lf", all_cot, w_down, preferred_element_type=jnp.float32)
    d_active = d_mixed * up_vals
    d_gate = (
        d_active * sigmoid_gate + d_active * gate_vals * sigmoid_gate * (1.0 - sigmoid_gate)
    ).astype(jnp.bfloat16)
    d_up = (d_mixed * active).astype(jnp.bfloat16)
    d_normed_part = jnp.einsum("lf,df->ld", d_gate, gate_columns, preferred_element_type=jnp.float32)
    d_normed_part = d_normed_part + jnp.einsum(
        "lf,df->ld", d_up, up_columns, preferred_element_type=jnp.float32
    )
    d_normed_second = lax.psum_scatter(
        d_normed_part.astype(jnp.bfloat16), "shard", scatter_dimension=0, tiled=True
    ).astype(jnp.float32)
    down_part = jnp.dot(mixed_hidden, w_down, preferred_element_type=jnp.float32)
    result = (
        hidden_mid
        + lax.psum_scatter(
            down_part.astype(jnp.bfloat16), "shard", scatter_dimension=0, tiled=True
        ).astype(jnp.float32)
    ).astype(jnp.bfloat16)
    grad_out = cotangent[0]
    down_grad = column_term(mixed_hidden, all_cot).astype(jnp.bfloat16)
    gate_grad = to_rows(column_term(all_acts, d_gate).astype(jnp.bfloat16))
    up_grad = to_rows(column_term(all_acts, d_up).astype(jnp.bfloat16))
    gain_second_grad = jnp.sum(d_normed_second * unit_second, axis=0)
    d_hidden_mid = grad_out.astype(jnp.float32) + norm_backward(
        d_normed_second, gain_second, unit_second, rstd_second
    )
    d_branch = d_hidden_mid.astype(jnp.bfloat16)
    out_grad_term = jnp.einsum("le,ld->ed", attended, d_branch, preferred_element_type=jnp.float32)
    attended_gradient = jnp.einsum(
        "ld,ed->le", d_branch, full_out, preferred_element_type=jnp.float32
    )
    attended_gradient = attended_gradient.astype(jnp.bfloat16).reshape(
        token_length, KEY_VALUE_HEADS, heads_per_group, HEAD_DIMENSION
    )
    d_probs = jnp.einsum(
        "ikrd,jkd->krij", attended_gradient, value_reduced, preferred_element_type=jnp.float32
    )
    value_gradient = jnp.einsum(
        "krij,ikrd->jkd", soft_low, attended_gradient, preferred_element_type=jnp.float32
    )
    d_scores = soft_probs * (d_probs - jnp.sum(soft_probs * d_probs, axis=-1, keepdims=True))
    d_scores_low = d_scores.astype(jnp.bfloat16)
    d_queries = jnp.einsum(
        "krij,jkd->ikrd", d_scores_low, k_low, preferred_element_type=jnp.float32
    )
    d_queries = rotate_back(
        d_queries.reshape(token_length, QUERY_HEADS, HEAD_DIMENSION) * logit_scale,
        cosine_per_head,
        sine_per_head,
    )
    key_gradient = jnp.einsum(
        "krij,ikrd->jkd", d_scores_low, query_reduced, preferred_element_type=jnp.float32
    )
    key_gradient = rotate_back(key_gradient, cosine_per_head, sine_per_head)
    d_joined = jnp.concatenate(
        [
            d_queries.reshape(token_length, head_dimension),
            key_gradient.reshape(token_length, KEY_VALUE_HEADS * HEAD_DIMENSION),
            value_gradient.reshape(token_length, KEY_VALUE_HEADS * HEAD_DIMENSION),
        ],
        axis=1,
    ).astype(jnp.bfloat16)
    bias_grad_term = jnp.sum(d_joined.astype(jnp.float32), axis=0)
    qkv_grad_term = jnp.einsum(
        "ld,le->de", acts_first, d_joined, preferred_element_type=jnp.float32
    )
    d_normed_first = jnp.einsum("le,de->ld", d_joined, full_qkv, preferred_element_type=jnp.float32)
    gain_first_grad = jnp.sum(d_normed_first * unit_first, axis=0)
    d_inputs = d_hidden_mid + norm_backward(d_normed_first, gain_first, unit_first, rstd_first)
    owned = (
        lax.psum_scatter(
            gain_first_grad.astype(jnp.bfloat16), "shard", scatter_dimension=0, tiled=True
        ).astype(jnp.float32),
        lax.psum_scatter(
            qkv_grad_term.astype(jnp.bfloat16), "shard", scatter_dimension=0, tiled=True
        ).astype(jnp.float32),
        lax.psum_scatter(
            bias_grad_term.astype(jnp.bfloat16), "shard", scatter_dimension=0, tiled=True
        ).astype(jnp.float32),
        lax.psum_scatter(
            out_grad_term.astype(jnp.bfloat16), "shard", scatter_dimension=0, tiled=True
        ).astype(jnp.float32),
        lax.psum_scatter(
            gain_second_grad.astype(jnp.bfloat16), "shard", scatter_dimension=0, tiled=True
        ).astype(jnp.float32),
    )
    summed = (
        lax.psum(owned[0].astype(jnp.bfloat16), "replica").astype(jnp.float32),
        lax.psum(owned[1].astype(jnp.bfloat16), "replica").astype(jnp.float32),
        lax.psum(owned[2].astype(jnp.bfloat16), "replica").astype(jnp.float32),
        lax.psum(owned[3].astype(jnp.bfloat16), "replica").astype(jnp.float32),
        lax.psum(owned[4].astype(jnp.bfloat16), "replica").astype(jnp.float32),
        gate_grad.astype(jnp.float32),
        up_grad.astype(jnp.float32),
        lax.psum(down_grad, "replica").astype(jnp.float32),
    )
    return (
        result[None],
        d_inputs.astype(jnp.bfloat16)[None],
        summed[0],
        summed[1],
        summed[2],
        summed[3],
        summed[4],
        summed[5],
        summed[6],
        summed[7],
    )


MESH = pl.DeviceIdType.MESH
BF, F32 = jnp.bfloat16, jnp.float32
HBM = pl.BlockSpec(memory_space=pl.ANY)
VMEM = pl.BlockSpec(memory_space=pltpu.VMEM)
DMA = pltpu.SemaphoreType.DMA


def shaped(*shape, dtype=BF):
    return jax.ShapeDtypeStruct(shape, dtype)


def low(*shape):
    return pltpu.VMEM(shape, BF)


def full(*shape):
    return pltpu.VMEM(shape, F32)


def dot(a, b):
    return lax.dot_general(a, b, (((1,), (0,)), ((), ())), preferred_element_type=F32)


def dot_nt(a, b):
    return lax.dot_general(a, b, (((1,), (1,)), ((), ())), preferred_element_type=F32)


def rows_of(start, size, unit=16):
    return pl.ds(pl.multiple_of(start, unit), size)


def quarter(t, q):
    return rows_of(192 * t + 48 * q, 48)


def send(src, dst, send_sem, recv_sem, device):
    copy = pltpu.make_async_remote_copy(
        src_ref=src, dst_ref=dst, send_sem=send_sem, recv_sem=recv_sem, device_id=device, device_id_type=MESH
    )
    copy.start()


class Place:
    def __init__(self):
        self.r = r = lax.axis_index("replica")
        self.s = s = lax.axis_index("shard")
        self.x, self.c, self.z, self.y = r // 2, r % 2, s // 2, s % 2
        self.rc, self.rx, self.rd = r + 1 - 2 * self.c, (r + 2) % 4, 3 - r
        self.core, self.across, self.side = (self.rc, s), (self.rx, s), (r, s + 1 - 2 * self.y)

    def peer(self, t):
        return (self.r, t)

    def line(self, k):
        near = self.z + (1 - 2 * (self.z % 2)) * (k % 2)
        far = k + (self.z // 2) * (3 - 2 * k)
        return (1 - k // 2) * near + (k // 2) * far

    def onward(self, zz, copy):
        pl.when((zz <= self.z) & (self.z < 3))(lambda: copy(0, self.peer(self.s + 2)))
        pl.when((zz >= self.z) & (self.z > 0))(lambda: copy(1, self.peer(self.s - 2)))

    def went_onward(self, zz, wait):
        pl.when((zz <= self.z) & (self.z < 3))(lambda: wait(0))
        pl.when((zz >= self.z) & (self.z > 0))(lambda: wait(1))

    def reduce_step(self, zz, add, hand):
        pl.when((zz >= self.z) & (self.z > 0))(lambda: add(zz))
        pl.when((zz < self.z) & (self.z < 3))(lambda: add(zz))
        pl.when((zz == self.z) & (self.z < 3))(lambda: add(4))
        pl.when(zz > self.z)(lambda: hand(zz, self.peer(self.s + 2)))
        pl.when(zz < self.z - 1)(lambda: hand(zz, self.peer(self.s - 2)))
        pl.when(zz == self.z - 1)(lambda: hand(4, self.peer(self.s - 2)))

    def mine(self, zz):
        return 2 * zz + self.y

    def theirs(self, zz):
        return 2 * zz + 1 - self.y

    def greet(self, steps):
        bar = pltpu.get_barrier_semaphore()
        devices = [self.core, self.across] + [(self.r, (self.s + k) % 8) for k in steps]
        for device in devices:
            pl.semaphore_signal(bar, inc=1, device_id=device, device_id_type=MESH)
        pl.semaphore_wait(bar, len(devices))

    def arrived(self, ref, sem, spare):
        pltpu.make_async_remote_copy(
            src_ref=ref, dst_ref=ref, send_sem=spare, recv_sem=sem, device_id=self.core, device_id_type=MESH
        ).wait_recv()

    def sent(self, ref, sem, spare):
        pltpu.make_async_remote_copy(
            src_ref=ref, dst_ref=ref, send_sem=sem, recv_sem=spare, device_id=self.core, device_id_type=MESH
        ).wait_send()


def inverse_norm(v):
    return lax.rsqrt(jnp.mean(v * v, axis=-1, keepdims=True) + eps_norm)


class Gather:
    def __init__(self, p, spare, view, arrivals, along, aside):
        self.p, self.spare, self.view = p, spare, view
        self.arrivals, self.along, self.aside = arrivals, along, aside

    def move(self, src, t, zz):
        p, dst, sem = self.p, self.view(t), self.arrivals(t)
        p.onward(zz, lambda d, device: send(src, dst, self.along.at[zz, d], sem, device))
        send(src, dst, self.aside.at[zz], sem, p.side)

    def start(self, src):
        self.move(src, self.p.s, self.p.z)

    def wait(self, t):
        self.p.arrived(self.view(t), self.arrivals(t), self.spare)

    def step(self, k, then=None):
        zz = self.p.line(k)
        t = self.p.mine(zz)
        self.wait(t)
        self.move(self.view(t), t, zz)
        if then is not None:
            then(t)

    def other(self, k, then=None):
        t = self.p.theirs(self.p.line(k))
        self.wait(t)
        if then is not None:
            then(t)

    def finish(self):
        block = self.view(self.p.s)
        for zz in range(4):
            self.p.sent(block, self.aside.at[zz], self.spare)
            self.p.went_onward(zz, lambda d: self.p.sent(block, self.along.at[zz, d], self.spare))


def gather_body(
    x_ref, seg_ref, ga_ref, bq_ref, gf_ref, wq_ref, wo_ref, wg_ref, wu_ref, c_ref,
    WQ_out, WO_out, G, C, cos_out, sin_out, gains_out, q_out, k_out, v_out, p_out, att_out, a1_out, mid_out, a2_out,
    WQ, WO, vg, vu, GS, CS, S, bias, cos_ref, sin_ref, gains, queries, keys, values, probs, att, a1, mid, a2,
    rq, ro, rg, rc, rs, szq, syq, sdq, szo, syo, sdo, sg, sdg, scz, scy, ss, loc, written,
):
    p = Place()
    r, s, c, z = p.r, p.s, p.c, p.z
    spare = loc.at[0]
    own = rows_of(192 * s, 192)
    own_c = rows_of(128 * s, 128, 128)
    loads = (
        pltpu.make_async_copy(wq_ref, WQ.at[own], loc.at[1]),
        pltpu.make_async_copy(wo_ref, WO.at[own], loc.at[2]),
        pltpu.make_async_copy(wg_ref, vg, loc.at[3]),
        pltpu.make_async_copy(wu_ref, vu, loc.at[4]),
        pltpu.make_async_copy(c_ref, CS, loc.at[5]),
    )
    for copy in loads:
        copy.start()
    p.greet(range(1, 8))
    gap = jnp.zeros((1, 64), F32)
    small = jnp.concatenate(
        [ga_ref[...].astype(F32)[None], gap, bq_ref[...].astype(F32)[None], gf_ref[...].astype(F32)[None], gap],
        axis=1,
    )
    S[s] = jnp.broadcast_to(small, (16, 768)).astype(BF)

    def vq(t, q):
        return WQ.at[quarter(t, q)]

    def vo(t, q):
        return WO.at[quarter(t, q)]

    def gq(t, q):
        return G.at[quarter(t, q)]

    def cot_block(t):
        return C.at[rows_of(128 * t, 128, 128)]

    g_q = Gather(p, spare, lambda t: vq(t, r), lambda t: rq.at[t, r], szq, syq)
    g_o = Gather(p, spare, lambda t: vo(t, r), lambda t: ro.at[t, r], szo, syo)
    g_c = Gather(p, spare, cot_block, lambda t: rc.at[t], scz, scy)

    def share(view, sems, rsems):
        def to_replicas(t):
            v = view(t, r)
            send(v, v, sems.at[t, 0], rsems.at[t, r], p.across)
            send(v, v, sems.at[t, 1], rsems.at[t, r], p.core)

        return to_replicas

    def relay(view, sems, rsems, t):
        v = view(t, p.rx)
        p.arrived(v, rsems.at[t, p.rx], spare)
        send(v, v, sems.at[t, 2], rsems.at[t, p.rx], p.core)

    def from_core(view, rsems):
        @pl.loop(1, 8)
        def _(k):
            t = (s + k) % 8
            p.arrived(view(t, p.rc), rsems.at[t, p.rc], spare)
            p.arrived(view(t, p.rd), rsems.at[t, p.rd], spare)

    share_q, share_o, share_g = share(vq, sdq, rq), share(vo, sdo, ro), share(gq, sdg, rg)

    def owner(k):
        return 2 * ((z + 1 + k // 2) % 4) + (p.y if k % 2 else 1 - p.y)

    def source(k):
        return 2 * ((z + 3 - k // 2) % 4) + (p.y if k % 2 else 1 - p.y)

    def along(k):
        return p.mine(p.line(k)) if k < 4 else p.theirs(p.line(k - 4))

    def q_step(k):
        g_q.step(k, share_q)

    def q_other(k):
        g_q.other(k, share_q)

    def q_relay(k):
        relay(vq, sdq, rq, along(k))

    def o_start():
        g_o.start(wo_ref.at[rows_of(48 * r, 48)])

    def o_step(k):
        g_o.step(k, share_o)

    def o_other(k):
        g_o.other(k, share_o)

    def o_relay(k):
        relay(vo, sdo, ro, along(k))

    def c_start():
        g_c.start(CS)

    def give(k):
        t = owner(k)
        send(GS.at[t, rows_of(48 * r, 48)], gq(s, r), sg.at[t], rg.at[s, r], p.peer(t))

    def take(k):
        t = source(k)
        p.arrived(gq(t, r), rg.at[t, r], spare)
        share_g(t)

    def g_relay(k):
        relay(gq, sdg, rg, source(k))

    own_out = (
        pltpu.make_async_copy(GS.at[s], G.at[own], loc.at[1]),
        pltpu.make_async_copy(CS, C.at[own_c], loc.at[2]),
    )
    save = (pltpu.make_async_copy(WQ, WQ_out, loc.at[3]), pltpu.make_async_copy(WO, WO_out, loc.at[4]))
    results = tuple(
        pltpu.make_async_copy(ref, out, written.at[i])
        for i, (ref, out) in enumerate(
            (
                (cos_ref, cos_out), (sin_ref, sin_out), (gains, gains_out), (a1, a1_out), (queries, q_out), (keys, k_out),
                (values, v_out), (probs, p_out), (att, att_out), (mid, mid_out), (a2, a2_out),
            )
        )
    )
    kept = {}

    def prepare():
        for copy in loads:
            copy.wait()
        zeros = jnp.zeros((192, 32), BF)
        for t in range(8):
            GS[t, :, 0:1120] = vg[:, 1120 * t : 1120 * t + 1120]
            GS[t, :, 1120:1152] = zeros
            GS[t, :, 1152:2272] = vu[:, 1120 * t : 1120 * t + 1120]
            GS[t, :, 2272:2304] = zeros
        for copy in own_out:
            copy.start()
        across = jnp.broadcast_to(seg_ref[...].astype(F32), (128, 128))
        down = across.T
        row = lax.broadcasted_iota(jnp.int32, (128, 128), 0)
        column = lax.broadcasted_iota(jnp.int32, (128, 128), 1)
        earlier = jnp.sum(jnp.where(across < down, 1.0, 0.0), axis=1, keepdims=True)
        position = row.astype(F32) - earlier
        half = (column - 64 * (column // 64)).astype(F32)
        angle = position * jnp.exp(half * (-2.0 * math.log(rope_base) / HEAD_DIMENSION))
        cos_ref[...] = jnp.cos(angle)
        sin_ref[...] = jnp.where(column < 64, -1.0, 1.0) * jnp.sin(angle)
        kept["open"] = (across == down) & (column <= row)

    def first_norm():
        @pl.loop(1, 8)
        def _(k):
            t = (s + k) % 8
            p.arrived(S.at[t], rs.at[t], spare)

        for t in range(8):
            row = S[t, 0:1, :].astype(F32)
            gains[0:1, 192 * t : 192 * t + 192] = row[:, 0:192]
            bias[0:1, 256 * t : 256 * t + 256] = row[:, 256:512]
            gains[1:2, 192 * t : 192 * t + 192] = row[:, 512:704]
        x = x_ref[...].astype(F32)
        a1[...] = (x * inverse_norm(x) * gains[0:1, :]).astype(BF)

    def q_all():
        from_core(vq, rq)

    def o_all():
        from_core(vo, ro)

    def attend():
        cosine, sine = cos_ref[...], sin_ref[...]
        for j in range(4):
            co = pl.ds(512 * j, 512)
            joined = dot(a1[...], WQ[:, co]) + bias[0:1, co]
            for i in range(4):
                h = 4 * j + i
                u = joined[:, 128 * i : 128 * i + 128]
                if h < 14:
                    u = u * cosine + pltpu.roll(u, 64, 1) * sine
                if h < 12:
                    queries[h // 6, pl.ds(128 * (h % 6), 128), :] = (u * HEAD_DIMENSION**-0.5).astype(BF)
                elif h < 14:
                    keys[h - 12] = u.astype(BF)
                else:
                    values[h - 14] = u.astype(BF)
        save[0].start()
        for g in range(2):
            scores = dot_nt(queries[g], keys[g]).reshape(6, 128, 128)
            scores = jnp.where(kept["open"][None], scores, -1e30)
            ex = jnp.exp(scores - jnp.max(scores, axis=-1, keepdims=True))
            soft = (ex / jnp.sum(ex, axis=-1, keepdims=True)).reshape(768, 128)
            probs[g] = soft.astype(BF)
            out = dot(probs[g], values[g]).astype(BF)
            for i in range(6):
                att[:, pl.ds(128 * (6 * g + i), 128)] = out[128 * i : 128 * i + 128]
        for copy in results[0:9]:
            copy.start()

    def second_norm():
        save[1].start()
        x = x_ref[...].astype(F32)
        for j in range(3):
            co = pl.ds(512 * j, 512)
            mid[:, co] = x[:, 512 * j : 512 * j + 512] + dot(att[...], WO[:, co])
        hidden = mid[...]
        a2[...] = (hidden * inverse_norm(hidden) * gains[1:2, :]).astype(BF)
        for copy in results[9:11]:
            copy.start()

    at_end = (z == 0) | (z == 3)
    in_middle = (z == 1) | (z == 2)
    g_q.start(wq_ref.at[rows_of(48 * r, 48)])
    for k in range(1, 8):
        t = (s + k) % 8
        send(S.at[s], S.at[s], ss.at[t], rs.at[s], p.peer(t))
    prepare()

    @pl.when(at_end)
    def _():
        q_other(0)
        o_start()
        give(0)
        give(1)
        give(6)
        q_step(1)
        o_other(0)
        c_start()
        o_step(1)
        take(0)
        take(6)
        give(5)
        o_step(2)
        q_relay(4)
        q_other(1)
        q_step(3)


    @pl.when(in_middle)
    def _():
        o_start()
        give(1)
        q_step(1)
        give(0)
        give(6)

    q_step(2)
    first_norm()

    @pl.when(at_end)
    def _():
        o_step(3)
        o_relay(1)
        q_relay(3)
        q_other(3)
        q_relay(1)
        take(5)
        o_other(2)
        take(1)
        q_relay(5)
        o_relay(4)
        o_relay(3)
        give(3)
        q_relay(2)
        q_other(2)
        give(4)
        g_c.step(1)
        give(2)
        g_relay(1)
        o_other(3)
        o_other(1)
        o_relay(7)
        take(4)
        take(2)
        q_relay(6)
        g_c.step(2)
        q_relay(7)
        g_c.step(3)
        o_relay(6)
        g_relay(0)


    @pl.when(in_middle)
    def _():
        q_other(0)
        o_step(1)
        o_step(2)
        q_relay(4)
        q_step(3)
        give(5)
        take(1)
        q_other(1)
        o_step(3)
        o_relay(1)
        o_other(0)
        c_start()
        give(2)
        q_relay(1)
        g_relay(1)
        give(4)
        q_other(3)
        take(5)
        o_other(2)
        g_c.step(1)
        give(3)
        q_relay(5)
        take(0)
        take(6)
        q_relay(3)
        q_other(2)
        g_c.step(2)
        o_other(1)
        q_relay(2)
        o_relay(3)
        o_relay(6)
        g_relay(0)
        o_relay(4)
        q_relay(6)
        q_relay(7)
        take(4)
        o_other(3)
        g_c.step(3)
        g_relay(5)
        take(2)

    q_all()
    g_relay(6)
    attend()
    o_relay(5)

    @pl.when(at_end)
    def _():
        o_relay(2)
        g_relay(5)
        take(3)


    @pl.when(in_middle)
    def _():
        o_relay(7)
        take(3)
        o_relay(2)

    g_relay(2)
    o_all()
    g_relay(4)
    g_relay(3)
    second_norm()
    from_core(gq, rg)

    @pl.loop(0, 4)
    def _(k):
        g_c.other(k)

    g_q.finish()
    g_o.finish()
    g_c.finish()

    @pl.loop(1, 8)
    def _(k):
        t = (s + k) % 8
        p.sent(S.at[t], ss.at[t], spare)
        p.sent(gq(t, r), sg.at[t], spare)
        for d in range(3):
            p.sent(vq(t, r), sdq.at[t, d], spare)
            p.sent(vo(t, r), sdo.at[t, d], spare)
            p.sent(gq(t, r), sdg.at[t, d], spare)

    for copy in own_out + save + results:
        copy.wait()


def gather_weights(x, segments, gain_attn, b_qkv, gain_ffn, w_qkv, w_out, w_gate, w_up, cot):
    return pl.pallas_call(
        gather_body,
        out_shape=(
            shaped(1536, 2048), shaped(1536, 1536), shaped(1536, 2304), shaped(1024, 1536), shaped(128, 128, dtype=F32),
            shaped(128, 128, dtype=F32), shaped(8, 1536, dtype=F32), shaped(2, 768, 128), shaped(2, 128, 128), shaped(2, 128, 128), shaped(2, 768, 128),
            shaped(128, 1536), shaped(128, 1536), shaped(128, 1536, dtype=F32), shaped(128, 1536),
        ),
        in_specs=[VMEM] * 5 + [HBM] * 5,
        out_specs=(HBM,) * 15,
        scratch_shapes=[
            low(1536, 2048), low(1536, 1536), low(192, 8960), low(192, 8960), low(8, 192, 2304), low(128, 1536),
            low(8, 16, 768), full(8, 2048), full(128, 128), full(128, 128), full(8, 1536), low(2, 768, 128), low(2, 128, 128),
            low(2, 128, 128), low(2, 768, 128), low(128, 1536), low(128, 1536), full(128, 1536), low(128, 1536),
            DMA((8, 4)), DMA((8, 4)), DMA((8, 4)), DMA((8,)), DMA((8,)),
            DMA((4, 2)), DMA((4,)), DMA((8, 3)), DMA((4, 2)), DMA((4,)), DMA((8, 3)),
            DMA((8,)), DMA((8, 3)), DMA((4, 2)), DMA((4,)), DMA((8,)), DMA((6,)), DMA((11,)),
        ],
        compiler_params=pltpu.CompilerParams(collective_id=0, has_side_effects=True, vmem_limit_bytes=56 << 20),
        name="gather_and_attend",
    )(x, segments, gain_attn, b_qkv, gain_ffn, w_qkv, w_out, w_gate, w_up, cot)


class RowSums:
    def __init__(self, p, spare, total, chip, side, far, across, out, sems, width):
        self.p, self.spare, self.total, self.chip, self.side = p, spare, total, chip, side
        self.far, self.across, self.out, self.sems = far, across, out, sems
        self.width = width

    def part(self, t, q):
        return self.total.at[quarter(t, q), 0 : self.width]

    def slot(self, t, xx):
        return self.chip.at[t, xx, :, 0 : self.width]

    def own(self, k):
        p = self.p
        return 2 * p.line(3 - k % 4) + (1 - p.y + (k // 4) * (2 * p.y - 1))

    def to_core(self, t):
        p = self.p
        for xx in range(2):
            send(
                self.part(t, 2 * xx + 1 - p.c), self.slot(t, xx),
                self.sems[0].at[t, xx], self.sems[1].at[t, xx], p.core,
            )

    def add(self, t, q, ref, sem):
        self.p.arrived(ref, sem, self.spare)
        total = self.part(t, q)
        total[...] = (total[...].astype(F32) + ref[...].astype(F32)).astype(BF)

    def on_chip(self, k):
        p, t = self.p, self.own(k)
        for xx in range(2):
            self.add(t, 2 * xx + p.c, self.slot(t, xx), self.sems[1].at[t, xx])

    def aside(self, k):
        p, t = self.p, self.own(k)
        for xx in range(2):
            at = t // 2, xx
            send(self.part(t, 2 * xx + p.c), self.side.at[at], self.sems[2].at[at], self.sems[3].at[at], p.side)

    def on_line(self, k):
        p = self.p
        zz = p.line(3 - k)
        t = p.mine(zz)
        for xx in range(2):
            q = 2 * xx + p.c
            self.add(t, q, self.side.at[zz, xx], self.sems[3].at[zz, xx])
            p.reduce_step(
                zz,
                lambda slot: self.add(t, q, self.far.at[slot, xx], self.sems[5].at[slot, xx]),
                lambda slot, device: send(
                    self.part(t, q), self.far.at[slot, xx], self.sems[4].at[zz, xx], self.sems[5].at[slot, xx], device
                ),
            )

    def at_owner(self):
        p = self.p
        for xx in range(2):
            send(self.part(p.s, 2 * xx + p.c), self.across.at[xx], self.sems[6].at[xx], self.sems[7].at[xx], p.across)

    def spread(self):
        p = self.p
        for xx in range(2):
            q = 2 * xx + p.c
            p.sent(self.across.at[xx], self.sems[6].at[xx], self.spare)
            self.add(p.s, q, self.across.at[xx], self.sems[7].at[xx])
            total = self.part(p.s, q)
            pltpu.make_async_copy(total, self.out.at[q], self.sems[6].at[4 + xx]).start()
            send(total, self.out.at[q], self.sems[6].at[2 + xx], self.sems[7].at[2 + xx], p.core)

    def finish(self):
        p = self.p
        for xx in range(2):
            q = 2 * xx + 1 - p.c
            p.arrived(self.out.at[q], self.sems[7].at[2 + xx], self.spare)
            p.sent(self.out.at[q], self.sems[6].at[2 + xx], self.spare)
            pltpu.make_async_copy(self.part(p.s, 0), self.out.at[q], self.sems[6].at[4 + xx]).wait()

        @pl.loop(0, 8)
        def _(t):
            for xx in range(2):
                p.sent(self.slot(t, xx), self.sems[0].at[t, xx], self.spare)

        @pl.loop(0, 4)
        def _(i):
            for xx in range(2):
                p.sent(self.side.at[i, xx], self.sems[2].at[i, xx], self.spare)

                @pl.when(i != p.z)
                def _():
                    p.sent(self.far.at[i, xx], self.sems[4].at[i, xx], self.spare)

    @staticmethod
    def buffers(width):
        return [low(8, 2, 48, width), low(4, 2, 48, width), low(5, 2, 48, width), low(2, 48, width)]

    @staticmethod
    def semaphores():
        return [DMA((8, 2)), DMA((8, 2)), DMA((4, 2)), DMA((4, 2)), DMA((4, 2)), DMA((5, 2)), DMA((6,)), DMA((4,))]


def layer_back_body(
    n_ref, c_hbm, g_hbm, d_hbm, wq_hbm, wo_hbm, att_hbm, a1_hbm, x_hbm, cot_hbm, q_hbm,
    mid_hbm, gains_hbm, cos_hbm, sin_hbm, k_hbm, v_hbm, p_hbm,
    out_ref, gtok_ref, OG, OD, OWq, OWo,
    NC, H, vG, vD, MX, PD, PO, YD, ZD, YO, ZO, YB, ZB, RCd, RXd, RC, RX, dj, AT, SM, mid_ref, gains, cos_ref, sin_ref, keys, values, probs,
    Yq, Zq, RXq, RCo, Yo, Zo, RXo,
    free, rn, syn, szn, ryd, rzd, syd, szd, syo, ryo, szo, rzo, syb, ryb, szb, rzb,
    scd, rcd, sxd, rxd, sfd, rfd, scg, rcg, sx, rx, sa, ra, sf, *sems,
):
    p = Place()
    r, s, c, y, z = p.r, p.s, p.c, p.y, p.z
    loc = sems[-1]
    spare = loc.at[0]
    q_sums = RowSums(p, spare, H, RC, Yq, Zq, RXq, OWq, sems[0:8], 2176)
    o_sums = RowSums(p, spare, NC, RCo, Yo, Zo, RXo, OWo, sems[8:16], 1536)

    def block(t):
        return NC.at[rows_of(128 * t, 128, 128)]

    def cot_rows(start, size):
        return rows_of(1024 + start, size, 128)

    loads = (
        pltpu.make_async_copy(n_ref, block(s), loc.at[1]),
        pltpu.make_async_copy(c_hbm, NC.at[1024:2048], loc.at[2]),
        pltpu.make_async_copy(g_hbm, vG, loc.at[3]),
        pltpu.make_async_copy(d_hbm, vD.at[0:1120], loc.at[4]),
    )
    for copy in loads:
        copy.start()
    p.greet(range(1, 8))
    g_n = Gather(p, spare, block, lambda t: rn.at[t], szn, syn)
    g_n.start(n_ref)
    vD[1120:1152, :] = jnp.zeros((32, 1536), BF)
    for copy in loads:
        copy.wait()

    def side(P, Y, ssem, rsem, k):
        zz = p.line(k)
        send(P.at[p.theirs(zz)], Y.at[zz], ssem.at[zz], rsem.at[zz], p.side)

    def side_d(k):
        side(PD, YD, syd, ryd, k)

    def line_step(P, Y, Z, ry, sz, rz, k):
        zz = p.line(k)
        t = p.mine(zz)

        def add(ref, sem):
            p.arrived(ref, sem, spare)
            P[t] = (P[t].astype(F32) + ref[...].astype(F32)).astype(BF)

        add(Y.at[zz], ry.at[zz])
        p.reduce_step(
            zz,
            lambda slot: add(Z.at[slot], rz.at[slot]),
            lambda slot, device: send(P.at[t], Z.at[slot], sz.at[zz], rz.at[slot], device),
        )

    def step_d(k):
        line_step(PD, YD, ZD, ryd, szd, rzd, k)

    def side_oa(k):
        zz = p.line(k)
        send(PO.at[p.theirs(zz), :, 0:768], YO.at[zz], syo.at[zz], ryo.at[zz], p.side)

    def step_oa(k):
        zz = p.line(k)
        half = PO.at[p.mine(zz), :, 0:768]

        def add(ref, sem):
            p.arrived(ref, sem, spare)
            half[...] = (half[...].astype(F32) + ref[...].astype(F32)).astype(BF)

        add(YO.at[zz], ryo.at[zz])
        p.reduce_step(
            zz,
            lambda slot: add(ZO.at[slot], rzo.at[slot]),
            lambda slot, device: send(half, ZO.at[slot], szo.at[zz], rzo.at[slot], device),
        )

    def step_ob(k):
        zz = p.line(k)
        both = PO.at[pl.ds(2 * zz, 2), :, 768:1536]

        def add(slot):
            p.arrived(ZB.at[slot], rzb.at[slot], spare)
            both[...] = (both[...].astype(F32) + ZB[slot].astype(F32)).astype(BF)

        p.reduce_step(
            zz, add, lambda slot, device: send(both, ZB.at[slot], szb.at[zz], rzb.at[slot], device)
        )

    def side_ob():
        send(PO.at[p.theirs(z), :, 768:1536], YB, syb, ryb, p.side)

    at_end = (z == 0) | (z == 3)
    in_middle = (z == 1) | (z == 2)
    g_n.step(1)

    @pl.loop(0, 4)
    def _(k):
        zz = p.line(k)
        pl.when(at_end & (k > 0) & (k < 3))(lambda: g_n.step(k + 1))
        pl.when(in_middle & (k < 2))(lambda: g_n.step(k + 2))
        g_n.other(k)
        rows = rows_of(256 * zz, 256, 256)
        X = NC[rows]
        cot = NC[cot_rows(256 * zz, 256)]
        for j in range(3):
            ga, ua = pl.ds(384 * j, 384), pl.ds(1152 + 384 * j, 384)
            gate = dot(X, vG[:, ga])
            up = dot(X, vG[:, ua])
            d_mixed = dot_nt(cot, vD[ga])
            sg = jax.nn.sigmoid(gate)
            active = gate * sg
            d_active = d_mixed * up
            MX[rows, ga] = (active * up).astype(BF)
            H[rows, ga] = (d_active * sg + d_active * active * (1.0 - sg)).astype(BF)
            H[rows, ua] = (d_mixed * active).astype(BF)
        for j in range(3):
            co = pl.ds(512 * j, 512)
            part = dot_nt(H[rows], vG[co]).astype(BF)
            PD[2 * zz, :, co] = part[:128]
            PD[2 * zz + 1, :, co] = part[128:]
        pl.when(k == 2)(lambda: side_d(1))
        pl.when(k == 3)(lambda: side_d(3))
        for j in range(3):
            co = pl.ds(512 * j, 512)
            part = dot(MX[rows], vD[:, co]).astype(BF)
            PO[2 * zz, :, co] = part[:128]
            PO[2 * zz + 1, :, co] = part[128:]
        pl.when(at_end & (k == 1))(lambda: step_ob(1))
        pl.when(at_end & (k == 2))(lambda: step_ob(2))

    side_d(2)
    side_d(0)

    def owner(k):
        return 2 * ((z + 1 + k // 2) % 4) + (k % 2) * (2 * y - 1) + 1 - y

    def pair_chip(k):
        t = owner(k)
        for xx in range(2):
            p.arrived(RC.at[t, xx], rcg.at[t, xx], spare)
            q = quarter(t, 2 * xx + c)
            vG[q] = (vG[q].astype(F32) + RC[t, xx].astype(F32)).astype(BF)
        send(vG.at[quarter(t, p.rx)], RX.at[t], sx.at[t], rx.at[t], p.across)

    @pl.loop(0, 5)
    def _(j):
        @pl.when(j < 4)
        def _():
            pair = (z + 1 + j) % 4
            rows = rows_of(384 * pair, 384, 128)
            X = NC[0:1024, rows].T
            for i in range(3):
                co = pl.ds(768 * i, 768)
                vG[rows, co] = dot(X, H[0:1024, co]).astype(BF)
            for i in range(2):
                t = owner(2 * j + i)
                for xx in range(2):
                    send(vG.at[quarter(t, 2 * xx + 1 - c)], RC.at[t, xx], scg.at[t, xx], rcg.at[t, xx], p.core)

        @pl.when(j > 0)
        def _():
            pair_chip(2 * j - 2)
            pair_chip(2 * j - 1)

    pl.semaphore_signal(free, inc=1, device_id=p.core, device_id_type=MESH)

    def chunk(i):
        return rows_of(384 * i, 384, 128)

    def cols(q):
        return rows_of(384 * q, 384, 128)

    held = (
        pltpu.make_async_copy(wo_hbm, NC.at[0:1536], loc.at[1]),
        pltpu.make_async_copy(wq_hbm, H.at[:, 0:2048], loc.at[2]),
        pltpu.make_async_copy(att_hbm, NC.at[1536:1664], loc.at[3]),
        pltpu.make_async_copy(a1_hbm, NC.at[1664:1792], loc.at[4]),
        pltpu.make_async_copy(x_hbm, NC.at[1792:1920], loc.at[5]),
        pltpu.make_async_copy(cot_hbm, NC.at[1920:2048], loc.at[6]),
        pltpu.make_async_copy(q_hbm.at[0], MX.at[0:768, 256:384], loc.at[8]),
        pltpu.make_async_copy(q_hbm.at[1], MX.at[0:768, 384:512], loc.at[9]),
        pltpu.make_async_copy(mid_hbm, mid_ref, loc.at[10]),
        pltpu.make_async_copy(gains_hbm, gains, loc.at[11]),
        pltpu.make_async_copy(cos_hbm, cos_ref, loc.at[12]),
        pltpu.make_async_copy(sin_hbm, sin_ref, loc.at[13]),
        pltpu.make_async_copy(k_hbm, keys, loc.at[14]),
        pltpu.make_async_copy(v_hbm, values, loc.at[15]),
        pltpu.make_async_copy(p_hbm, probs, loc.at[16]),
    )

    def down_terms():
        @pl.loop(0, 3)
        def _(i):
            X = MX[:, chunk(i)].T
            for j in range(3):
                co = pl.ds(512 * j, 512)
                vD[chunk(i), co] = dot(X, NC[1024:2048, co]).astype(BF)
            for xx in range(2):
                q = 2 * xx + 1 - c
                send(vD.at[chunk(i), cols(q)], RCd.at[xx, chunk(i)], scd.at[i, xx], rcd.at[i, xx], p.core)

        g_n.finish()
        for copy in held:
            copy.start()

        @pl.loop(0, 3)
        def _(i):
            for xx in range(2):
                p.arrived(RCd.at[xx, chunk(i)], rcd.at[i, xx], spare)
                q = cols(2 * xx + c)
                vD[chunk(i), q] = (vD[chunk(i), q].astype(F32) + RCd[xx, chunk(i)].astype(F32)).astype(BF)

    def pair_whole(k):
        t = owner(k)
        q = quarter(t, r)
        p.arrived(RX.at[t], rx.at[t], spare)
        vG[q] = (vG[q].astype(F32) + RX[t].astype(F32)).astype(BF)

        if k < 7:
            send(vG.at[q], OG.at[r, s], sa.at[t], ra.at[s, r], p.peer(t))
        else:
            pltpu.make_async_copy(vG.at[q], OG.at[r, s], loc.at[7]).start()

    def share(t):
        v = OG.at[r, t]
        send(v, v, sf.at[t, 0], ra.at[t, r], p.across)
        send(v, v, sf.at[t, 1], ra.at[t, r], p.core)

    def source(k):
        return 2 * ((z + 3 - k // 2) % 4) + (1 - y if k % 2 == 0 else y)

    def take(k):
        t = source(k)
        if k < 7:
            p.arrived(OG.at[r, t], ra.at[t, r], spare)
        else:
            pltpu.make_async_copy(vG.at[quarter(s, r)], OG.at[r, s], loc.at[7]).wait()
        share(t)

    def relay(k):
        t = source(k)
        v = OG.at[p.rx, t]
        p.arrived(v, ra.at[t, p.rx], spare)
        send(v, v, sf.at[t, 2], ra.at[t, p.rx], p.core)

    def down_across(i):
        send(vD.at[chunk(i), cols(p.rx)], RXd.at[chunk(i)], sxd.at[i], rxd.at[i], p.across)

    def down_whole(i):
        p.arrived(RXd.at[chunk(i)], rxd.at[i], spare)
        q = cols(r)
        vD[chunk(i), q] = (vD[chunk(i), q].astype(F32) + RXd[chunk(i)].astype(F32)).astype(BF)
        src, dst = vD.at[chunk(i), q], OD.at[r, chunk(i)]
        pltpu.make_async_copy(src, dst, sfd.at[i, 3]).start()
        send(src, dst, sfd.at[i, 0], rfd.at[i, r], p.across)
        send(src, dst, sfd.at[i, 1], rfd.at[i, r], p.core)

    def down_relay(i):
        v = OD.at[p.rx, chunk(i)]
        p.arrived(v, rfd.at[i, p.rx], spare)
        send(v, v, sfd.at[i, 2], rfd.at[i, p.rx], p.core)

    def back(w):
        return w * cos_ref[...] - pltpu.roll(w, 64, 1) * sin_ref[...]

    kept = {}

    def attention_out():
        for copy in held:
            copy.wait()
        dn, hidden = PD[s].astype(F32), mid_ref[...]
        rstd = inverse_norm(hidden)
        unit = hidden * rstd
        kept["ffn"] = jnp.sum(dn * unit, axis=0, keepdims=True)
        e = dn * gains[1:2, :]
        dm = NC[1920:2048].astype(F32) + rstd * (e - unit * jnp.mean(e * unit, axis=-1, keepdims=True))
        NC[1920:2048] = dm.astype(BF)
        AT[...] = NC[1536:1664].T
        for j in range(3):
            part = dot_nt(NC[1920:2048], NC[pl.ds(512 * j, 512)]).astype(BF)
            for i in range(4):
                h = 4 * j + i
                MX[pl.ds(128 * (h % 6), 128), pl.ds(128 * (h // 6), 128)] = part[:, 128 * i : 128 * i + 128]
        for j in range(3):
            co = pl.ds(512 * j, 512)
            NC[0:1536, co] = dot(AT[...], NC[1920:2048, co]).astype(BF)

        @pl.loop(0, 8)
        def _(k):
            o_sums.to_core(o_sums.own(k))

    def heads(g):
        grad = MX[0:768, 128 * g : 128 * g + 128]
        query = MX[0:768, 256 + 128 * g : 384 + 128 * g]
        soft = probs[g].astype(F32)
        d_probs = dot_nt(grad, values[g])
        d_scores = (soft * (d_probs - jnp.sum(soft * d_probs, axis=-1, keepdims=True))).astype(BF)
        d_values = dot(probs[g].T, grad)
        d_queries = dot(d_scores, keys[g]) * HEAD_DIMENSION**-0.5
        d_keys = dot(d_scores.T, query)
        for i in range(6):
            dj[:, pl.ds(128 * (6 * g + i), 128)] = back(d_queries[128 * i : 128 * i + 128]).astype(BF)
        dj[:, pl.ds(128 * (12 + g), 128)] = back(d_keys).astype(BF)
        dj[:, pl.ds(128 * (14 + g), 128)] = d_values.astype(BF)

    def attention_in():
        heads(1)
        joined_grad = dj[...]
        bias_grad = jnp.sum(joined_grad.astype(F32), axis=0, keepdims=True)
        x = NC[1792:1920].astype(F32)
        rstd = inverse_norm(x)
        unit = x * rstd
        dn1 = jnp.concatenate(
            [dot_nt(joined_grad, H[pl.ds(512 * j, 512), 0:2048]) for j in range(3)], axis=1
        )
        gain_attn_grad = jnp.sum(dn1 * unit, axis=0, keepdims=True)
        e = dn1 * gains[0:1, :]
        NC[1792:1920] = (
            NC[1920:2048].astype(F32) + rstd * (e - unit * jnp.mean(e * unit, axis=-1, keepdims=True))
        ).astype(BF)
        pltpu.make_async_copy(NC.at[1792:1920], gtok_ref, loc.at[5]).start()
        SM[...] = jnp.zeros_like(SM)
        ffn = kept["ffn"]
        for t in range(8):
            SM[t, 0:1, :] = gain_attn_grad[:, 192 * t : 192 * t + 128]
            SM[t, 1:2, 0:64] = gain_attn_grad[:, 192 * t + 128 : 192 * t + 192]
            SM[t, 2:3, :] = bias_grad[:, 256 * t : 256 * t + 128]
            SM[t, 3:4, :] = bias_grad[:, 256 * t + 128 : 256 * t + 256]
            SM[t, 4:5, :] = ffn[:, 192 * t : 192 * t + 128]
            SM[t, 5:6, 0:64] = ffn[:, 192 * t + 128 : 192 * t + 192]
        AT[...] = NC[1664:1792].T

    def joined_terms():
        pl.semaphore_wait(free, 1)

        @pl.loop(0, 8)
        def _(k):
            t = q_sums.own(k)
            rows = rows_of(192 * t, 192)
            for j in range(2):
                co = pl.ds(1024 * j, 1024)
                H[rows, co] = dot(AT[rows], dj[:, co]).astype(BF)
            H[rows, 2048:2176] = jnp.zeros((192, 128), BF)
            H[rows_of(192 * t, 16), 2048:2176] = SM[t].astype(BF)
            q_sums.to_core(t)

    def on_chip(sums):
        @pl.loop(0, 8)
        def _(k):
            sums.on_chip(k)

    def finish_out():
        p.arrived(YB, ryb, spare)
        PO[s, :, 768:1536] = (PO[s, :, 768:1536].astype(F32) + YB[...].astype(F32)).astype(BF)
        PO[s] = (PO[s].astype(F32) + mid_ref[...]).astype(BF)
        pltpu.make_async_copy(PO.at[s], out_ref, loc.at[6]).start()

    def first_heads():
        heads(0)

    def o_on_chip():
        on_chip(o_sums)

    def q_on_chip():
        on_chip(q_sums)


    @pl.when(at_end)
    def _():
        step_d(3)
        side_oa(3)
        step_d(2)
        side_oa(2)
        side_oa(0)
        step_d(1)
        pair_whole(3)


    @pl.when(in_middle)
    def _():
        side_oa(2)
        side_oa(0)
        step_ob(2)
        step_d(3)
        step_d(2)
        step_d(1)
        pair_whole(6)

    down_terms()

    @pl.when(at_end)
    def _():
        step_ob(3)
        pair_whole(6)
        down_across(1)
        pair_whole(5)
        step_oa(3)
        pair_whole(0)
        down_across(0)
        side_oa(1)


    @pl.when(in_middle)
    def _():
        side_oa(3)
        pair_whole(5)
        down_across(0)
        side_oa(1)
        pair_whole(3)
        take(3)
        pair_whole(1)
        down_across(1)
        pair_whole(2)

    step_d(0)
    attention_out()

    @pl.when(at_end)
    def _():
        down_across(2)

    first_heads()
    attention_in()

    @pl.when(at_end)
    def _():
        pair_whole(4)
        pair_whole(2)

    joined_terms()

    @pl.when(in_middle)
    def _():
        pair_whole(4)

    o_on_chip()

    @pl.when(at_end)
    def _():
        o_sums.aside(2)
        take(3)
        o_sums.aside(0)
        pair_whole(1)
        take(6)


    @pl.when(in_middle)
    def _():
        down_across(2)
        o_sums.aside(2)
        pair_whole(7)
        down_whole(0)
        o_sums.aside(0)
        step_oa(3)
        pair_whole(0)
        take(7)

    q_on_chip()

    @pl.when(at_end)
    def _():
        q_sums.aside(0)
        take(2)
        q_sums.aside(1)
        down_whole(1)
        take(5)
        down_whole(0)
        pair_whole(7)
        o_sums.on_line(0)
        down_whole(2)
        take(1)
        q_sums.aside(2)
        take(7)
        q_sums.on_line(0)
        o_sums.aside(1)
        take(4)
        relay(5)
        q_sums.aside(3)
        q_sums.on_line(1)
        q_sums.on_line(2)
        step_ob(0)
        take(0)
        o_sums.on_line(1)
        o_sums.aside(3)
        q_sums.on_line(3)
        q_sums.at_owner()
        o_sums.on_line(2)
        relay(2)
        relay(3)
        step_oa(2)
        relay(4)
        o_sums.on_line(3)
        o_sums.at_owner()
        q_sums.spread()
        step_oa(1)
        down_relay(2)
        down_relay(0)
        relay(1)
        relay(6)
        relay(7)
        relay(0)
        side_ob()
        down_relay(1)
        step_oa(0)
        finish_out()
        o_sums.spread()


    @pl.when(in_middle)
    def _():
        q_sums.aside(1)
        q_sums.aside(0)
        take(4)
        take(6)
        down_whole(1)
        take(5)
        relay(3)
        step_ob(3)
        take(2)
        take(1)
        q_sums.aside(2)
        o_sums.on_line(0)
        q_sums.aside(3)
        o_sums.aside(1)
        down_whole(2)
        step_ob(1)
        q_sums.on_line(0)
        relay(5)
        o_sums.aside(3)
        q_sums.on_line(1)
        q_sums.on_line(2)
        step_ob(0)
        take(0)
        q_sums.on_line(3)
        q_sums.at_owner()
        relay(4)
        o_sums.on_line(2)
        side_ob()
        relay(2)
        o_sums.on_line(1)
        relay(6)
        o_sums.on_line(3)
        o_sums.at_owner()
        relay(0)
        step_oa(1)
        down_relay(1)
        down_relay(2)
        relay(7)
        down_relay(0)
        q_sums.spread()
        relay(1)
        step_oa(2)
        o_sums.spread()
        step_oa(0)
        finish_out()

    o_sums.finish()
    q_sums.finish()
    pltpu.make_async_copy(NC.at[1792:1920], gtok_ref, loc.at[5]).wait()
    pltpu.make_async_copy(PO.at[s], out_ref, loc.at[6]).wait()

    @pl.loop(0, 3)
    def _(i):
        for q in (p.rc, p.rd):
            p.arrived(OD.at[q, chunk(i)], rfd.at[i, q], spare)
        for d in range(3):
            p.sent(OD.at[r, chunk(i)], sfd.at[i, d], spare)
        pltpu.make_async_copy(OD.at[r, chunk(i)], OD.at[r, chunk(i)], sfd.at[i, 3]).wait()
        for xx in range(2):
            p.sent(RCd.at[xx, chunk(i)], scd.at[i, xx], spare)
        p.sent(RXd.at[chunk(i)], sxd.at[i], spare)

    @pl.loop(0, 8)
    def _(t):
        for q in (p.rc, p.rd):
            p.arrived(OG.at[q, t], ra.at[t, q], spare)
        for d in range(3):
            p.sent(OG.at[r, t], sf.at[t, d], spare)
        for xx in range(2):
            p.sent(RC.at[t, xx], scg.at[t, xx], spare)
        p.sent(RX.at[t], sx.at[t], spare)

        @pl.when(t != s)
        def _():
            p.sent(OG.at[r, s], sa.at[t], spare)

    @pl.loop(0, 4)
    def _(i):
        p.sent(YD.at[i], syd.at[i], spare)
        p.sent(YO.at[i], syo.at[i], spare)

        @pl.when(i != z)
        def _():
            p.sent(ZD.at[i], szd.at[i], spare)
            p.sent(ZO.at[i], szo.at[i], spare)
            p.sent(ZB.at[i], szb.at[i], spare)

    p.sent(YB, syb, spare)


def layer_back(*args):
    return pl.pallas_call(
        layer_back_body,
        out_shape=(
            shaped(128, 1536), shaped(128, 1536), shaped(4, 8, 48, 2304), shaped(4, 1152, 384), shaped(4, 48, 2176),
            shaped(4, 48, 1536),
        ),
        in_specs=[HBM] * 18,
        out_specs=(HBM,) * 6,
        scratch_shapes=[
            low(2048, 1536), low(1536, 2304), low(1536, 2304), low(1152, 1536), low(1024, 1152),
            low(8, 128, 1536), low(8, 128, 1536), low(4, 128, 1536), low(5, 128, 1536), low(4, 128, 768), low(5, 128, 768),
            low(128, 768), low(5, 2, 128, 768),
            low(2, 1152, 384), low(1152, 384), low(8, 2, 48, 2304), low(8, 48, 2304),
            low(128, 2048), low(1536, 128), full(8, 16, 128), full(128, 1536), full(8, 1536), full(128, 128), full(128, 128),
            low(2, 128, 128), low(2, 128, 128), low(2, 768, 128),
            *RowSums.buffers(2176)[1:], *RowSums.buffers(1536),
            pltpu.SemaphoreType.REGULAR, DMA((8,)), DMA((4,)), DMA((4, 2)),
            DMA((4,)), DMA((5,)), DMA((4,)), DMA((4,)), DMA((4,)), DMA((4,)), DMA((4,)), DMA((5,)), DMA, DMA, DMA((4,)), DMA((5,)),
            DMA((3, 2)), DMA((3, 2)), DMA((3,)), DMA((3,)), DMA((3, 4)), DMA((3, 4)),
            DMA((8, 2)), DMA((8, 2)), DMA((8,)), DMA((8,)), DMA((8,)), DMA((8, 4)), DMA((8, 3)),
            *RowSums.semaphores(), *RowSums.semaphores(), DMA((17,)),
        ],
        compiler_params=pltpu.CompilerParams(collective_id=1, has_side_effects=True, vmem_limit_bytes=64 << 20),
        name="layer_back",
    )(*args)


def widen_body(
    g_ref, d_ref, q_ref, o_ref, x_ref, y_ref, gate, up, down, qkv, out, x_out, y_out, ga, bq, gf, narrow
):
    for first, wide in ((0, gate), (1152, up)):
        for t in range(8):
            narrow[:, 1120 * t : 1120 * t + 1120] = g_ref[0, t, :, first : first + 1120]
        wide[...] = narrow[...].astype(F32)
    down[...] = d_ref[0, 0:1120, :].astype(F32)
    qkv[...] = q_ref[0, :, 0:2048].astype(F32)
    out[...] = o_ref[0].astype(F32)
    x_out[...] = x_ref[...]
    y_out[...] = y_ref[...]

    @pl.when(pl.program_id(0) == 0)
    def _():
        small = q_ref[0, 0:16, 2048:2176].astype(F32)
        ga[...] = jnp.concatenate([small[0:1], small[1:2, 0:64]], axis=1)[0]
        bq[...] = jnp.concatenate([small[2:3], small[3:4]], axis=1)[0]
        gf[...] = jnp.concatenate([small[4:5], small[5:6, 0:64]], axis=1)[0]


def widen(g, d, q, o, x, y):
    def rows(size, width):
        return pl.BlockSpec((size, width), lambda i: (i, 0))

    def whole(size):
        return pl.BlockSpec((size,), lambda i: (0,))

    return pl.pallas_call(
        widen_body,
        grid=(4,),
        out_shape=(
            shaped(192, 8960, dtype=F32), shaped(192, 8960, dtype=F32), shaped(1120, 1536, dtype=F32),
            shaped(192, 2048, dtype=F32), shaped(192, 1536, dtype=F32), shaped(128, 1536), shaped(128, 1536),
            shaped(192, dtype=F32), shaped(256, dtype=F32), shaped(192, dtype=F32),
        ),
        in_specs=[
            pl.BlockSpec((1, 8, 48, 2304), lambda i: (i, 0, 0, 0)),
            pl.BlockSpec((1, 1152, 384), lambda i: (i, 0, 0)),
            pl.BlockSpec((1, 48, 2176), lambda i: (i, 0, 0)),
            pl.BlockSpec((1, 48, 1536), lambda i: (i, 0, 0)),
            rows(32, 1536),
            rows(32, 1536),
        ],
        out_specs=(
            rows(48, 8960), rows(48, 8960), pl.BlockSpec((1120, 384), lambda i: (0, i)), rows(48, 2048), rows(48, 1536),
            rows(32, 1536), rows(32, 1536), whole(192), whole(256), whole(192),
        ),
        scratch_shapes=[low(48, 8960)],
        compiler_params=pltpu.CompilerParams(vmem_limit_bytes=62 << 20),
        name="widen",
    )(g, d, q, o, x, y)


def shards_eight(
    tokens, segments, gain_attn, w_qkv, b_qkv, w_out, gain_ffn, w_gate, w_up, w_down, cotangent
):
    x, cot = tokens[0], cotangent[0]
    WQ, WO, G, C, cosine, sine, gains, queries, keys, values, probs, att, a1, mid, a2 = gather_weights(
        x, segments, gain_attn, b_qkv, gain_ffn, w_qkv, w_out, w_gate, w_up, cot
    )
    out, grad_tokens, gate_up, down, qkv, o = layer_back(
        a2, C, G, w_down, WQ, WO, att, a1, x, cot, queries, mid, gains, cosine, sine, keys, values, probs
    )
    gate, up, down, qkv_rows, out_rows, out, grad_tokens, ga, bq, gf = widen(gate_up, down, qkv, o, out, grad_tokens)
    return out[None], grad_tokens[None], ga, qkv_rows, bq, out_rows, gf, gate, up, down


def solution(mesh):
    placed = (
        P(("replica", "shard"), None, None),
        P(("replica", "shard"), None),
        P("shard"),
        P("shard", None),
        P("shard"),
        P("shard", None),
        P("shard"),
        P("shard", None),
        P("shard", None),
        P("shard", None),
        P(("replica", "shard"), None, None),
    )
    return jax.shard_map(
        shards_eight if (mesh.shape["replica"], mesh.shape["shard"]) == (4, 8) else shards,
        mesh=mesh,
        in_specs=placed,
        out_specs=(
            P(("replica", "shard"), None, None),
            P(("replica", "shard"), None, None),
            P("shard"),
            P("shard", None),
            P("shard"),
            P("shard", None),
            P("shard"),
            P("shard", None),
            P("shard", None),
            P("shard", None),
        ),
        check_vma=False,
    )
```

```python
import math

import jax
import jax.numpy as jnp
from jax import lax
from jax.experimental import pallas as pl
from jax.experimental.pallas import tpu as pltpu
from jax.sharding import PartitionSpec as P

QUERY_HEADS = 12
KEY_VALUE_HEADS = 2
HEAD_DIMENSION = 128


eps_norm = 1e-06
rope_base = 1000000.0


def tables(segment_ids, head_size):
    token_length = segment_ids.shape[-1]
    row_index = jnp.arange(token_length, dtype=jnp.int32)
    earlier = jnp.sum(
        (segment_ids[..., None, :] < segment_ids[..., :, None]).astype(jnp.int32),
        axis=-1,
        dtype=jnp.int32,
    )
    positions = (row_index - earlier).astype(jnp.float32)
    frequencies = jnp.exp(
        jnp.arange(head_size // 2, dtype=jnp.float32) * (-2.0 * math.log(rope_base) / head_size)
    )
    angles = positions[..., None] * frequencies
    cosine = jnp.concatenate([jnp.cos(angles), jnp.cos(angles)], axis=-1)
    sine_vals = jnp.concatenate([jnp.sin(angles), jnp.sin(angles)], axis=-1)
    allowed = (
        (segment_ids[..., None, :] == segment_ids[..., :, None])
        & (row_index[None, :] <= row_index[:, None])
    ).astype(jnp.int32)
    return (cosine, sine_vals, allowed)


def apply_rotation(values, cosine, sine_vals):
    halfway = values.shape[-1] // 2
    turned = jnp.concatenate([-values[..., halfway:], values[..., :halfway]], axis=-1)
    return values * cosine + turned * sine_vals


def rotate_back(values, cosine, sine_vals):
    halfway = values.shape[-1] // 2
    shifted = values * sine_vals
    return values * cosine + jnp.concatenate(
        [shifted[..., halfway:], -shifted[..., :halfway]], axis=-1
    )


def norm_forward(hidden, gain_vec):
    rstd_rows = lax.rsqrt(jnp.mean(hidden * hidden, axis=-1, keepdims=True) + eps_norm)
    unit_rows = hidden * rstd_rows
    return (unit_rows * gain_vec, unit_rows, rstd_rows)


def norm_backward(grad_in, gain_vec, unit_rows, rstd_rows):
    inner_grad = grad_in * gain_vec
    return rstd_rows * (
        inner_grad - unit_rows * jnp.mean(inner_grad * unit_rows, axis=-1, keepdims=True)
    )


def column_term(left_side, right_side):
    return jnp.einsum("lf,ld->fd", left_side, right_side, preferred_element_type=jnp.float32)


def to_columns(rows):
    ranks = lax.axis_size("shard")
    depth, width = rows.shape
    split = rows.reshape(depth, ranks, width // ranks).transpose(1, 0, 2)
    return lax.all_to_all(split, "shard", 0, 0, tiled=True).reshape(ranks * depth, width // ranks)


def to_rows(columns):
    ranks, copies = lax.axis_size("shard"), lax.axis_size("replica")
    depth, width = columns.shape
    depth = depth // ranks
    parts = columns.reshape(ranks, copies, depth // copies, width)
    part = lax.psum_scatter(parts, "replica", scatter_dimension=1, tiled=False)
    part = lax.all_to_all(part, "shard", 0, 0, tiled=True)
    part = part.transpose(1, 0, 2).reshape(depth // copies, ranks * width)
    return lax.all_gather(part, "replica", axis=0, tiled=True)


def shards(
    tokens, segments, gain_attn, w_qkv, b_qkv, w_out, gain_ffn, w_gate, w_up, w_down, cotangent
):
    heads_per_group = QUERY_HEADS // KEY_VALUE_HEADS
    head_dimension = QUERY_HEADS * HEAD_DIMENSION
    key_value_limit = head_dimension + KEY_VALUE_HEADS * HEAD_DIMENSION
    logit_scale = HEAD_DIMENSION ** (-0.5)
    token_length = tokens.shape[1]
    full_gain_attn, full_qkv, full_bias, full_out, full_gain_ffn = (
        lax.all_gather(gain_attn, "shard", axis=0, tiled=True),
        lax.all_gather(w_qkv, "shard", axis=0, tiled=True),
        lax.all_gather(b_qkv, "shard", axis=0, tiled=True),
        lax.all_gather(w_out, "shard", axis=0, tiled=True),
        lax.all_gather(gain_ffn, "shard", axis=0, tiled=True),
    )
    gate_columns = to_columns(w_gate)
    up_columns = to_columns(w_up)
    all_cot = lax.all_gather(cotangent[0], "shard", axis=0, tiled=True)
    gain_first = full_gain_attn.astype(jnp.float32)
    gain_second = full_gain_ffn.astype(jnp.float32)
    cosine, sine_vals, allowed = tables(segments[0], HEAD_DIMENSION)
    cosine_per_head = cosine[:, None, :]
    sine_per_head = sine_vals[:, None, :]
    inputs = tokens[0].astype(jnp.float32)
    normed_first, unit_first, rstd_first = norm_forward(inputs, gain_first)
    acts_first = normed_first.astype(jnp.bfloat16)
    joined_projection = jnp.dot(
        acts_first, full_qkv, preferred_element_type=jnp.float32
    ) + full_bias.astype(jnp.float32)
    query_rows = apply_rotation(
        joined_projection[:, :head_dimension].reshape(token_length, QUERY_HEADS, HEAD_DIMENSION),
        cosine_per_head,
        sine_per_head,
    )
    query_reduced = (
        (query_rows * logit_scale)
        .astype(jnp.bfloat16)
        .reshape(token_length, KEY_VALUE_HEADS, heads_per_group, HEAD_DIMENSION)
    )
    k_low = apply_rotation(
        joined_projection[:, head_dimension:key_value_limit].reshape(
            token_length, KEY_VALUE_HEADS, HEAD_DIMENSION
        ),
        cosine_per_head,
        sine_per_head,
    ).astype(jnp.bfloat16)
    value_reduced = (
        joined_projection[:, key_value_limit:]
        .reshape(token_length, KEY_VALUE_HEADS, HEAD_DIMENSION)
        .astype(jnp.bfloat16)
    )
    scores = jnp.einsum("ikrd,jkd->krij", query_reduced, k_low, preferred_element_type=jnp.float32)
    scores = jnp.where(allowed != 0, scores, -1e30)
    largest = jnp.max(scores, axis=-1, keepdims=True)
    exponents = jnp.exp(scores - largest)
    soft_probs = exponents / jnp.sum(exponents, axis=-1, keepdims=True)
    soft_low = soft_probs.astype(jnp.bfloat16)
    attended = jnp.einsum(
        "krij,jkd->ikrd", soft_low, value_reduced, preferred_element_type=jnp.float32
    )
    attended = attended.reshape(token_length, head_dimension).astype(jnp.bfloat16)
    hidden_mid = inputs + jnp.dot(attended, full_out, preferred_element_type=jnp.float32)
    normed_second, unit_second, rstd_second = norm_forward(hidden_mid, gain_second)
    acts_second = normed_second.astype(jnp.bfloat16)
    all_acts = lax.all_gather(acts_second, "shard", axis=0, tiled=True)
    gate_vals = jnp.dot(all_acts, gate_columns, preferred_element_type=jnp.float32)
    up_vals = jnp.dot(all_acts, up_columns, preferred_element_type=jnp.float32)
    sigmoid_gate = jax.nn.sigmoid(gate_vals)
    active = gate_vals * sigmoid_gate
    mixed_hidden = (active * up_vals).astype(jnp.bfloat16)
    d_mixed = jnp.einsum("ld,fd->lf", all_cot, w_down, preferred_element_type=jnp.float32)
    d_active = d_mixed * up_vals
    d_gate = (
        d_active * sigmoid_gate + d_active * gate_vals * sigmoid_gate * (1.0 - sigmoid_gate)
    ).astype(jnp.bfloat16)
    d_up = (d_mixed * active).astype(jnp.bfloat16)
    d_normed_part = jnp.einsum("lf,df->ld", d_gate, gate_columns, preferred_element_type=jnp.float32)
    d_normed_part = d_normed_part + jnp.einsum(
        "lf,df->ld", d_up, up_columns, preferred_element_type=jnp.float32
    )
    d_normed_second = lax.psum_scatter(
        d_normed_part.astype(jnp.bfloat16), "shard", scatter_dimension=0, tiled=True
    ).astype(jnp.float32)
    down_part = jnp.dot(mixed_hidden, w_down, preferred_element_type=jnp.float32)
    result = (
        hidden_mid
        + lax.psum_scatter(
            down_part.astype(jnp.bfloat16), "shard", scatter_dimension=0, tiled=True
        ).astype(jnp.float32)
    ).astype(jnp.bfloat16)
    grad_out = cotangent[0]
    down_grad = column_term(mixed_hidden, all_cot).astype(jnp.bfloat16)
    gate_grad = to_rows(column_term(all_acts, d_gate).astype(jnp.bfloat16))
    up_grad = to_rows(column_term(all_acts, d_up).astype(jnp.bfloat16))
    gain_second_grad = jnp.sum(d_normed_second * unit_second, axis=0)
    d_hidden_mid = grad_out.astype(jnp.float32) + norm_backward(
        d_normed_second, gain_second, unit_second, rstd_second
    )
    d_branch = d_hidden_mid.astype(jnp.bfloat16)
    out_grad_term = jnp.einsum("le,ld->ed", attended, d_branch, preferred_element_type=jnp.float32)
    attended_gradient = jnp.einsum(
        "ld,ed->le", d_branch, full_out, preferred_element_type=jnp.float32
    )
    attended_gradient = attended_gradient.astype(jnp.bfloat16).reshape(
        token_length, KEY_VALUE_HEADS, heads_per_group, HEAD_DIMENSION
    )
    d_probs = jnp.einsum(
        "ikrd,jkd->krij", attended_gradient, value_reduced, preferred_element_type=jnp.float32
    )
    value_gradient = jnp.einsum(
        "krij,ikrd->jkd", soft_low, attended_gradient, preferred_element_type=jnp.float32
    )
    d_scores = soft_probs * (d_probs - jnp.sum(soft_probs * d_probs, axis=-1, keepdims=True))
    d_scores_low = d_scores.astype(jnp.bfloat16)
    d_queries = jnp.einsum(
        "krij,jkd->ikrd", d_scores_low, k_low, preferred_element_type=jnp.float32
    )
    d_queries = rotate_back(
        d_queries.reshape(token_length, QUERY_HEADS, HEAD_DIMENSION) * logit_scale,
        cosine_per_head,
        sine_per_head,
    )
    key_gradient = jnp.einsum(
        "krij,ikrd->jkd", d_scores_low, query_reduced, preferred_element_type=jnp.float32
    )
    key_gradient = rotate_back(key_gradient, cosine_per_head, sine_per_head)
    d_joined = jnp.concatenate(
        [
            d_queries.reshape(token_length, head_dimension),
            key_gradient.reshape(token_length, KEY_VALUE_HEADS * HEAD_DIMENSION),
            value_gradient.reshape(token_length, KEY_VALUE_HEADS * HEAD_DIMENSION),
        ],
        axis=1,
    ).astype(jnp.bfloat16)
    bias_grad_term = jnp.sum(d_joined.astype(jnp.float32), axis=0)
    qkv_grad_term = jnp.einsum(
        "ld,le->de", acts_first, d_joined, preferred_element_type=jnp.float32
    )
    d_normed_first = jnp.einsum("le,de->ld", d_joined, full_qkv, preferred_element_type=jnp.float32)
    gain_first_grad = jnp.sum(d_normed_first * unit_first, axis=0)
    d_inputs = d_hidden_mid + norm_backward(d_normed_first, gain_first, unit_first, rstd_first)
    owned = (
        lax.psum_scatter(
            gain_first_grad.astype(jnp.bfloat16), "shard", scatter_dimension=0, tiled=True
        ).astype(jnp.float32),
        lax.psum_scatter(
            qkv_grad_term.astype(jnp.bfloat16), "shard", scatter_dimension=0, tiled=True
        ).astype(jnp.float32),
        lax.psum_scatter(
            bias_grad_term.astype(jnp.bfloat16), "shard", scatter_dimension=0, tiled=True
        ).astype(jnp.float32),
        lax.psum_scatter(
            out_grad_term.astype(jnp.bfloat16), "shard", scatter_dimension=0, tiled=True
        ).astype(jnp.float32),
        lax.psum_scatter(
            gain_second_grad.astype(jnp.bfloat16), "shard", scatter_dimension=0, tiled=True
        ).astype(jnp.float32),
    )
    summed = (
        lax.psum(owned[0].astype(jnp.bfloat16), "replica").astype(jnp.float32),
        lax.psum(owned[1].astype(jnp.bfloat16), "replica").astype(jnp.float32),
        lax.psum(owned[2].astype(jnp.bfloat16), "replica").astype(jnp.float32),
        lax.psum(owned[3].astype(jnp.bfloat16), "replica").astype(jnp.float32),
        lax.psum(owned[4].astype(jnp.bfloat16), "replica").astype(jnp.float32),
        gate_grad.astype(jnp.float32),
        up_grad.astype(jnp.float32),
        lax.psum(down_grad, "replica").astype(jnp.float32),
    )
    return (
        result[None],
        d_inputs.astype(jnp.bfloat16)[None],
        summed[0],
        summed[1],
        summed[2],
        summed[3],
        summed[4],
        summed[5],
        summed[6],
        summed[7],
    )


MESH = pl.DeviceIdType.MESH
BF, F32 = jnp.bfloat16, jnp.float32
HBM = pl.BlockSpec(memory_space=pl.ANY)
VMEM = pl.BlockSpec(memory_space=pltpu.VMEM)
DMA = pltpu.SemaphoreType.DMA


def shaped(*shape, dtype=BF):
    return jax.ShapeDtypeStruct(shape, dtype)


def low(*shape):
    return pltpu.VMEM(shape, BF)


def full(*shape):
    return pltpu.VMEM(shape, F32)


def dot(a, b):
    return lax.dot_general(a, b, (((1,), (0,)), ((), ())), preferred_element_type=F32)


def dot_nt(a, b):
    return lax.dot_general(a, b, (((1,), (1,)), ((), ())), preferred_element_type=F32)


def rows_of(start, size, unit=16):
    return pl.ds(pl.multiple_of(start, unit), size)


def quarter(t, q):
    return rows_of(192 * t + 48 * q, 48)


def send(src, dst, send_sem, recv_sem, device):
    copy = pltpu.make_async_remote_copy(
        src_ref=src, dst_ref=dst, send_sem=send_sem, recv_sem=recv_sem, device_id=device, device_id_type=MESH
    )
    copy.start()


class Place:
    def __init__(self):
        self.r = r = lax.axis_index("replica")
        self.s = s = lax.axis_index("shard")
        self.x, self.c, self.z, self.y = r // 2, r % 2, s // 2, s % 2
        self.rc, self.rx, self.rd = r + 1 - 2 * self.c, (r + 2) % 4, 3 - r
        self.core, self.across, self.side = (self.rc, s), (self.rx, s), (r, s + 1 - 2 * self.y)

    def peer(self, t):
        return (self.r, t)

    def line(self, k):
        near = self.z + (1 - 2 * (self.z % 2)) * (k % 2)
        far = k + (self.z // 2) * (3 - 2 * k)
        return (1 - k // 2) * near + (k // 2) * far

    def onward(self, zz, copy):
        pl.when((zz <= self.z) & (self.z < 3))(lambda: copy(0, self.peer(self.s + 2)))
        pl.when((zz >= self.z) & (self.z > 0))(lambda: copy(1, self.peer(self.s - 2)))

    def went_onward(self, zz, wait):
        pl.when((zz <= self.z) & (self.z < 3))(lambda: wait(0))
        pl.when((zz >= self.z) & (self.z > 0))(lambda: wait(1))

    def reduce_step(self, zz, add, hand):
        pl.when((zz >= self.z) & (self.z > 0))(lambda: add(zz))
        pl.when((zz < self.z) & (self.z < 3))(lambda: add(zz))
        pl.when((zz == self.z) & (self.z < 3))(lambda: add(4))
        pl.when(zz > self.z)(lambda: hand(zz, self.peer(self.s + 2)))
        pl.when(zz < self.z - 1)(lambda: hand(zz, self.peer(self.s - 2)))
        pl.when(zz == self.z - 1)(lambda: hand(4, self.peer(self.s - 2)))

    def mine(self, zz):
        return 2 * zz + self.y

    def theirs(self, zz):
        return 2 * zz + 1 - self.y

    def greet(self, steps):
        bar = pltpu.get_barrier_semaphore()
        devices = [self.core, self.across] + [(self.r, (self.s + k) % 8) for k in steps]
        for device in devices:
            pl.semaphore_signal(bar, inc=1, device_id=device, device_id_type=MESH)
        pl.semaphore_wait(bar, len(devices))

    def arrived(self, ref, sem, spare):
        pltpu.make_async_remote_copy(
            src_ref=ref, dst_ref=ref, send_sem=spare, recv_sem=sem, device_id=self.core, device_id_type=MESH
        ).wait_recv()

    def sent(self, ref, sem, spare):
        pltpu.make_async_remote_copy(
            src_ref=ref, dst_ref=ref, send_sem=sem, recv_sem=spare, device_id=self.core, device_id_type=MESH
        ).wait_send()


def inverse_norm(v):
    return lax.rsqrt(jnp.mean(v * v, axis=-1, keepdims=True) + eps_norm)


class Gather:
    def __init__(self, p, spare, view, arrivals, along, aside):
        self.p, self.spare, self.view = p, spare, view
        self.arrivals, self.along, self.aside = arrivals, along, aside

    def move(self, src, t, zz):
        p, dst, sem = self.p, self.view(t), self.arrivals(t)
        p.onward(zz, lambda d, device: send(src, dst, self.along.at[zz, d], sem, device))
        send(src, dst, self.aside.at[zz], sem, p.side)

    def start(self, src):
        self.move(src, self.p.s, self.p.z)

    def wait(self, t):
        self.p.arrived(self.view(t), self.arrivals(t), self.spare)

    def step(self, k, then=None):
        zz = self.p.line(k)
        t = self.p.mine(zz)
        self.wait(t)
        self.move(self.view(t), t, zz)
        if then is not None:
            then(t)

    def other(self, k, then=None):
        t = self.p.theirs(self.p.line(k))
        self.wait(t)
        if then is not None:
            then(t)

    def finish(self):
        block = self.view(self.p.s)
        for zz in range(4):
            self.p.sent(block, self.aside.at[zz], self.spare)
            self.p.went_onward(zz, lambda d: self.p.sent(block, self.along.at[zz, d], self.spare))


def gather_body(
    x_ref, seg_ref, ga_ref, bq_ref, gf_ref, wq_ref, wo_ref, wg_ref, wu_ref, c_ref,
    WQ_out, WO_out, G, C, cos_out, sin_out, gains_out, q_out, k_out, v_out, p_out, att_out, a1_out, mid_out, a2_out,
    WQ, WO, vg, vu, GS, CS, S, bias, cos_ref, sin_ref, gains, queries, keys, values, probs, att, a1, mid, a2,
    rq, ro, rg, rc, rs, szq, syq, sdq, szo, syo, sdo, sg, sdg, scz, scy, ss, loc, written,
):
    p = Place()
    r, s, c, z = p.r, p.s, p.c, p.z
    spare = loc.at[0]
    own = rows_of(192 * s, 192)
    own_c = rows_of(128 * s, 128, 128)
    loads = (
        pltpu.make_async_copy(wq_ref, WQ.at[own], loc.at[1]),
        pltpu.make_async_copy(wo_ref, WO.at[own], loc.at[2]),
        pltpu.make_async_copy(wg_ref, vg, loc.at[3]),
        pltpu.make_async_copy(wu_ref, vu, loc.at[4]),
        pltpu.make_async_copy(c_ref, CS, loc.at[5]),
    )
    for copy in loads:
        copy.start()
    p.greet(range(1, 8))
    gap = jnp.zeros((1, 64), F32)
    small = jnp.concatenate(
        [ga_ref[...].astype(F32)[None], gap, bq_ref[...].astype(F32)[None], gf_ref[...].astype(F32)[None], gap],
        axis=1,
    )
    S[s] = jnp.broadcast_to(small, (16, 768)).astype(BF)

    def vq(t, q):
        return WQ.at[quarter(t, q)]

    def vo(t, q):
        return WO.at[quarter(t, q)]

    def gq(t, q):
        return G.at[quarter(t, q)]

    def cot_block(t):
        return C.at[rows_of(128 * t, 128, 128)]

    g_q = Gather(p, spare, lambda t: vq(t, r), lambda t: rq.at[t, r], szq, syq)
    g_o = Gather(p, spare, lambda t: vo(t, r), lambda t: ro.at[t, r], szo, syo)
    g_c = Gather(p, spare, cot_block, lambda t: rc.at[t], scz, scy)

    def share(view, sems, rsems):
        def to_replicas(t):
            v = view(t, r)
            send(v, v, sems.at[t, 0], rsems.at[t, r], p.across)
            send(v, v, sems.at[t, 1], rsems.at[t, r], p.core)

        return to_replicas

    def relay(view, sems, rsems, t):
        v = view(t, p.rx)
        p.arrived(v, rsems.at[t, p.rx], spare)
        send(v, v, sems.at[t, 2], rsems.at[t, p.rx], p.core)

    def from_core(view, rsems):
        @pl.loop(1, 8)
        def _(k):
            t = (s + k) % 8
            p.arrived(view(t, p.rc), rsems.at[t, p.rc], spare)
            p.arrived(view(t, p.rd), rsems.at[t, p.rd], spare)

    share_q, share_o, share_g = share(vq, sdq, rq), share(vo, sdo, ro), share(gq, sdg, rg)

    def owner(k):
        return 2 * ((z + 1 + k // 2) % 4) + (p.y if k % 2 else 1 - p.y)

    def source(k):
        return 2 * ((z + 3 - k // 2) % 4) + (p.y if k % 2 else 1 - p.y)

    def along(k):
        return p.mine(p.line(k)) if k < 4 else p.theirs(p.line(k - 4))

    def q_step(k):
        g_q.step(k, share_q)

    def q_other(k):
        g_q.other(k, share_q)

    def q_relay(k):
        relay(vq, sdq, rq, along(k))

    def o_start():
        g_o.start(wo_ref.at[rows_of(48 * r, 48)])

    def o_step(k):
        g_o.step(k, share_o)

    def o_other(k):
        g_o.other(k, share_o)

    def o_relay(k):
        relay(vo, sdo, ro, along(k))

    def c_start():
        g_c.start(CS)

    def give(k):
        t = owner(k)
        send(GS.at[t, rows_of(48 * r, 48)], gq(s, r), sg.at[t], rg.at[s, r], p.peer(t))

    def take(k):
        t = source(k)
        p.arrived(gq(t, r), rg.at[t, r], spare)
        share_g(t)

    def g_relay(k):
        relay(gq, sdg, rg, source(k))

    own_out = (
        pltpu.make_async_copy(GS.at[s], G.at[own], loc.at[1]),
        pltpu.make_async_copy(CS, C.at[own_c], loc.at[2]),
    )
    save = (pltpu.make_async_copy(WQ, WQ_out, loc.at[3]), pltpu.make_async_copy(WO, WO_out, loc.at[4]))
    results = tuple(
        pltpu.make_async_copy(ref, out, written.at[i])
        for i, (ref, out) in enumerate(
            (
                (cos_ref, cos_out), (sin_ref, sin_out), (gains, gains_out), (a1, a1_out), (queries, q_out), (keys, k_out),
                (values, v_out), (probs, p_out), (att, att_out), (mid, mid_out), (a2, a2_out),
            )
        )
    )
    kept = {}

    def prepare():
        for copy in loads:
            copy.wait()
        zeros = jnp.zeros((192, 32), BF)
        for t in range(8):
            GS[t, :, 0:1120] = vg[:, 1120 * t : 1120 * t + 1120]
            GS[t, :, 1120:1152] = zeros
            GS[t, :, 1152:2272] = vu[:, 1120 * t : 1120 * t + 1120]
            GS[t, :, 2272:2304] = zeros
        for copy in own_out:
            copy.start()
        across = jnp.broadcast_to(seg_ref[...].astype(F32), (128, 128))
        down = across.T
        row = lax.broadcasted_iota(jnp.int32, (128, 128), 0)
        column = lax.broadcasted_iota(jnp.int32, (128, 128), 1)
        earlier = jnp.sum(jnp.where(across < down, 1.0, 0.0), axis=1, keepdims=True)
        position = row.astype(F32) - earlier
        half = (column - 64 * (column // 64)).astype(F32)
        angle = position * jnp.exp(half * (-2.0 * math.log(rope_base) / HEAD_DIMENSION))
        cos_ref[...] = jnp.cos(angle)
        sin_ref[...] = jnp.where(column < 64, -1.0, 1.0) * jnp.sin(angle)
        kept["open"] = (across == down) & (column <= row)

    def first_norm():
        @pl.loop(1, 8)
        def _(k):
            t = (s + k) % 8
            p.arrived(S.at[t], rs.at[t], spare)

        for t in range(8):
            row = S[t, 0:1, :].astype(F32)
            gains[0:1, 192 * t : 192 * t + 192] = row[:, 0:192]
            bias[0:1, 256 * t : 256 * t + 256] = row[:, 256:512]
            gains[1:2, 192 * t : 192 * t + 192] = row[:, 512:704]
        x = x_ref[...].astype(F32)
        a1[...] = (x * inverse_norm(x) * gains[0:1, :]).astype(BF)

    def q_all():
        from_core(vq, rq)

    def o_all():
        from_core(vo, ro)

    def attend():
        cosine, sine = cos_ref[...], sin_ref[...]
        for j in range(4):
            co = pl.ds(512 * j, 512)
            joined = dot(a1[...], WQ[:, co]) + bias[0:1, co]
            for i in range(4):
                h = 4 * j + i
                u = joined[:, 128 * i : 128 * i + 128]
                if h < 14:
                    u = u * cosine + pltpu.roll(u, 64, 1) * sine
                if h < 12:
                    queries[h // 6, pl.ds(128 * (h % 6), 128), :] = (u * HEAD_DIMENSION**-0.5).astype(BF)
                elif h < 14:
                    keys[h - 12] = u.astype(BF)
                else:
                    values[h - 14] = u.astype(BF)
        save[0].start()
        for g in range(2):
            scores = dot_nt(queries[g], keys[g]).reshape(6, 128, 128)
            scores = jnp.where(kept["open"][None], scores, -1e30)
            ex = jnp.exp(scores - jnp.max(scores, axis=-1, keepdims=True))
            soft = (ex / jnp.sum(ex, axis=-1, keepdims=True)).reshape(768, 128)
            probs[g] = soft.astype(BF)
            out = dot(probs[g], values[g]).astype(BF)
            for i in range(6):
                att[:, pl.ds(128 * (6 * g + i), 128)] = out[128 * i : 128 * i + 128]
        for copy in results[0:9]:
            copy.start()

    def second_norm():
        save[1].start()
        x = x_ref[...].astype(F32)
        for j in range(3):
            co = pl.ds(512 * j, 512)
            mid[:, co] = x[:, 512 * j : 512 * j + 512] + dot(att[...], WO[:, co])
        hidden = mid[...]
        a2[...] = (hidden * inverse_norm(hidden) * gains[1:2, :]).astype(BF)
        for copy in results[9:11]:
            copy.start()

    at_end = (z == 0) | (z == 3)
    in_middle = (z == 1) | (z == 2)
    g_q.start(wq_ref.at[rows_of(48 * r, 48)])
    for k in range(1, 8):
        t = (s + k) % 8
        send(S.at[s], S.at[s], ss.at[t], rs.at[s], p.peer(t))
    prepare()

    @pl.when(at_end)
    def _():
        q_other(0)
        o_start()
        give(0)
        give(1)
        give(6)
        q_step(1)
        o_other(0)
        c_start()
        o_step(1)
        take(0)
        take(6)
        give(5)
        o_step(2)
        q_relay(4)
        q_other(1)
        q_step(3)


    @pl.when(in_middle)
    def _():
        o_start()
        give(1)
        q_step(1)
        give(0)
        give(6)

    q_step(2)
    first_norm()

    @pl.when(at_end)
    def _():
        o_step(3)
        o_relay(1)
        q_relay(3)
        q_other(3)
        q_relay(1)
        take(5)
        o_other(2)
        take(1)
        q_relay(5)
        o_relay(4)
        o_relay(3)
        give(3)
        q_relay(2)
        q_other(2)
        give(4)
        g_c.step(1)
        give(2)
        g_relay(1)
        o_other(3)
        o_other(1)
        o_relay(7)
        take(4)
        take(2)
        q_relay(6)
        g_c.step(2)
        q_relay(7)
        g_c.step(3)
        o_relay(6)
        g_relay(0)


    @pl.when(in_middle)
    def _():
        q_other(0)
        o_step(1)
        o_step(2)
        q_relay(4)
        q_step(3)
        give(5)
        take(1)
        q_other(1)
        o_step(3)
        o_relay(1)
        o_other(0)
        c_start()
        give(2)
        q_relay(1)
        g_relay(1)
        give(4)
        q_other(3)
        take(5)
        o_other(2)
        g_c.step(1)
        give(3)
        q_relay(5)
        take(0)
        take(6)
        q_relay(3)
        q_other(2)
        g_c.step(2)
        o_other(1)
        q_relay(2)
        o_relay(3)
        o_relay(6)
        g_relay(0)
        o_relay(4)
        q_relay(6)
        q_relay(7)
        take(4)
        o_other(3)
        g_c.step(3)
        g_relay(5)
        take(2)

    q_all()
    g_relay(6)
    attend()
    o_relay(5)

    @pl.when(at_end)
    def _():
        o_relay(2)
        g_relay(5)
        take(3)


    @pl.when(in_middle)
    def _():
        o_relay(7)
        take(3)
        o_relay(2)

    g_relay(2)
    o_all()
    g_relay(4)
    g_relay(3)
    second_norm()
    from_core(gq, rg)

    @pl.loop(0, 4)
    def _(k):
        g_c.other(k)

    g_q.finish()
    g_o.finish()
    g_c.finish()

    @pl.loop(1, 8)
    def _(k):
        t = (s + k) % 8
        p.sent(S.at[t], ss.at[t], spare)
        p.sent(gq(t, r), sg.at[t], spare)
        for d in range(3):
            p.sent(vq(t, r), sdq.at[t, d], spare)
            p.sent(vo(t, r), sdo.at[t, d], spare)
            p.sent(gq(t, r), sdg.at[t, d], spare)

    for copy in own_out + save + results:
        copy.wait()


def gather_weights(x, segments, gain_attn, b_qkv, gain_ffn, w_qkv, w_out, w_gate, w_up, cot):
    return pl.pallas_call(
        gather_body,
        out_shape=(
            shaped(1536, 2048), shaped(1536, 1536), shaped(1536, 2304), shaped(1024, 1536), shaped(128, 128, dtype=F32),
            shaped(128, 128, dtype=F32), shaped(8, 1536, dtype=F32), shaped(2, 768, 128), shaped(2, 128, 128), shaped(2, 128, 128), shaped(2, 768, 128),
            shaped(128, 1536), shaped(128, 1536), shaped(128, 1536, dtype=F32), shaped(128, 1536),
        ),
        in_specs=[VMEM] * 5 + [HBM] * 5,
        out_specs=(HBM,) * 15,
        scratch_shapes=[
            low(1536, 2048), low(1536, 1536), low(192, 8960), low(192, 8960), low(8, 192, 2304), low(128, 1536),
            low(8, 16, 768), full(8, 2048), full(128, 128), full(128, 128), full(8, 1536), low(2, 768, 128), low(2, 128, 128),
            low(2, 128, 128), low(2, 768, 128), low(128, 1536), low(128, 1536), full(128, 1536), low(128, 1536),
            DMA((8, 4)), DMA((8, 4)), DMA((8, 4)), DMA((8,)), DMA((8,)),
            DMA((4, 2)), DMA((4,)), DMA((8, 3)), DMA((4, 2)), DMA((4,)), DMA((8, 3)),
            DMA((8,)), DMA((8, 3)), DMA((4, 2)), DMA((4,)), DMA((8,)), DMA((6,)), DMA((11,)),
        ],
        compiler_params=pltpu.CompilerParams(collective_id=0, has_side_effects=True, vmem_limit_bytes=56 << 20),
        name="gather_and_attend",
    )(x, segments, gain_attn, b_qkv, gain_ffn, w_qkv, w_out, w_gate, w_up, cot)


class RowSums:
    def __init__(self, p, spare, total, chip, side, far, across, out, sems, width):
        self.p, self.spare, self.total, self.chip, self.side = p, spare, total, chip, side
        self.far, self.across, self.out, self.sems = far, across, out, sems
        self.width = width

    def part(self, t, q):
        return self.total.at[quarter(t, q), 0 : self.width]

    def slot(self, t, xx):
        return self.chip.at[t, xx, :, 0 : self.width]

    def own(self, k):
        p = self.p
        return 2 * p.line(3 - k % 4) + (1 - p.y + (k // 4) * (2 * p.y - 1))

    def to_core(self, t):
        p = self.p
        for xx in range(2):
            send(
                self.part(t, 2 * xx + 1 - p.c), self.slot(t, xx),
                self.sems[0].at[t, xx], self.sems[1].at[t, xx], p.core,
            )

    def add(self, t, q, ref, sem):
        self.p.arrived(ref, sem, self.spare)
        total = self.part(t, q)
        total[...] = (total[...].astype(F32) + ref[...].astype(F32)).astype(BF)

    def on_chip(self, k):
        p, t = self.p, self.own(k)
        for xx in range(2):
            self.add(t, 2 * xx + p.c, self.slot(t, xx), self.sems[1].at[t, xx])

    def aside(self, k):
        p, t = self.p, self.own(k)
        for xx in range(2):
            at = t // 2, xx
            send(self.part(t, 2 * xx + p.c), self.side.at[at], self.sems[2].at[at], self.sems[3].at[at], p.side)

    def on_line(self, k):
        p = self.p
        zz = p.line(3 - k)
        t = p.mine(zz)
        for xx in range(2):
            q = 2 * xx + p.c
            self.add(t, q, self.side.at[zz, xx], self.sems[3].at[zz, xx])
            p.reduce_step(
                zz,
                lambda slot: self.add(t, q, self.far.at[slot, xx], self.sems[5].at[slot, xx]),
                lambda slot, device: send(
                    self.part(t, q), self.far.at[slot, xx], self.sems[4].at[zz, xx], self.sems[5].at[slot, xx], device
                ),
            )

    def at_owner(self):
        p = self.p
        for xx in range(2):
            send(self.part(p.s, 2 * xx + p.c), self.across.at[xx], self.sems[6].at[xx], self.sems[7].at[xx], p.across)

    def spread(self):
        p = self.p
        for xx in range(2):
            q = 2 * xx + p.c
            p.sent(self.across.at[xx], self.sems[6].at[xx], self.spare)
            self.add(p.s, q, self.across.at[xx], self.sems[7].at[xx])
            total = self.part(p.s, q)
            pltpu.make_async_copy(total, self.out.at[q], self.sems[6].at[4 + xx]).start()
            send(total, self.out.at[q], self.sems[6].at[2 + xx], self.sems[7].at[2 + xx], p.core)

    def finish(self):
        p = self.p
        for xx in range(2):
            q = 2 * xx + 1 - p.c
            p.arrived(self.out.at[q], self.sems[7].at[2 + xx], self.spare)
            p.sent(self.out.at[q], self.sems[6].at[2 + xx], self.spare)
            pltpu.make_async_copy(self.part(p.s, 0), self.out.at[q], self.sems[6].at[4 + xx]).wait()

        @pl.loop(0, 8)
        def _(t):
            for xx in range(2):
                p.sent(self.slot(t, xx), self.sems[0].at[t, xx], self.spare)

        @pl.loop(0, 4)
        def _(i):
            for xx in range(2):
                p.sent(self.side.at[i, xx], self.sems[2].at[i, xx], self.spare)

                @pl.when(i != p.z)
                def _():
                    p.sent(self.far.at[i, xx], self.sems[4].at[i, xx], self.spare)

    @staticmethod
    def buffers(width):
        return [low(8, 2, 48, width), low(4, 2, 48, width), low(5, 2, 48, width), low(2, 48, width)]

    @staticmethod
    def semaphores():
        return [DMA((8, 2)), DMA((8, 2)), DMA((4, 2)), DMA((4, 2)), DMA((4, 2)), DMA((5, 2)), DMA((6,)), DMA((4,))]


def layer_back_body(
    n_ref, c_hbm, g_hbm, d_hbm, wq_hbm, wo_hbm, att_hbm, a1_hbm, x_hbm, cot_hbm, q_hbm,
    mid_hbm, gains_hbm, cos_hbm, sin_hbm, k_hbm, v_hbm, p_hbm,
    out_ref, gtok_ref, OG, OD, OWq, OWo,
    NC, H, vG, vD, MX, PD, PO, YD, ZD, YO, ZO, YB, ZB, RCd, RXd, RC, RX, dj, AT, SM, mid_ref, gains, cos_ref, sin_ref, keys, values, probs,
    Yq, Zq, RXq, RCo, Yo, Zo, RXo,
    free, rn, syn, szn, ryd, rzd, syd, szd, syo, ryo, szo, rzo, syb, ryb, szb, rzb,
    scd, rcd, sxd, rxd, sfd, rfd, scg, rcg, sx, rx, sa, ra, sf, *sems,
):
    p = Place()
    r, s, c, y, z = p.r, p.s, p.c, p.y, p.z
    loc = sems[-1]
    spare = loc.at[0]
    q_sums = RowSums(p, spare, H, RC, Yq, Zq, RXq, OWq, sems[0:8], 2176)
    o_sums = RowSums(p, spare, NC, RCo, Yo, Zo, RXo, OWo, sems[8:16], 1536)

    def block(t):
        return NC.at[rows_of(128 * t, 128, 128)]

    def cot_rows(start, size):
        return rows_of(1024 + start, size, 128)

    loads = (
        pltpu.make_async_copy(n_ref, block(s), loc.at[1]),
        pltpu.make_async_copy(c_hbm, NC.at[1024:2048], loc.at[2]),
        pltpu.make_async_copy(g_hbm, vG, loc.at[3]),
        pltpu.make_async_copy(d_hbm, vD.at[0:1120], loc.at[4]),
    )
    for copy in loads:
        copy.start()
    p.greet(range(1, 8))
    g_n = Gather(p, spare, block, lambda t: rn.at[t], szn, syn)
    g_n.start(n_ref)
    vD[1120:1152, :] = jnp.zeros((32, 1536), BF)
    for copy in loads:
        copy.wait()

    def side(P, Y, ssem, rsem, k):
        zz = p.line(k)
        send(P.at[p.theirs(zz)], Y.at[zz], ssem.at[zz], rsem.at[zz], p.side)

    def side_d(k):
        side(PD, YD, syd, ryd, k)

    def line_step(P, Y, Z, ry, sz, rz, k):
        zz = p.line(k)
        t = p.mine(zz)

        def add(ref, sem):
            p.arrived(ref, sem, spare)
            P[t] = (P[t].astype(F32) + ref[...].astype(F32)).astype(BF)

        add(Y.at[zz], ry.at[zz])
        p.reduce_step(
            zz,
            lambda slot: add(Z.at[slot], rz.at[slot]),
            lambda slot, device: send(P.at[t], Z.at[slot], sz.at[zz], rz.at[slot], device),
        )

    def step_d(k):
        line_step(PD, YD, ZD, ryd, szd, rzd, k)

    def side_oa(k):
        zz = p.line(k)
        send(PO.at[p.theirs(zz), :, 0:768], YO.at[zz], syo.at[zz], ryo.at[zz], p.side)

    def step_oa(k):
        zz = p.line(k)
        half = PO.at[p.mine(zz), :, 0:768]

        def add(ref, sem):
            p.arrived(ref, sem, spare)
            half[...] = (half[...].astype(F32) + ref[...].astype(F32)).astype(BF)

        add(YO.at[zz], ryo.at[zz])
        p.reduce_step(
            zz,
            lambda slot: add(ZO.at[slot], rzo.at[slot]),
            lambda slot, device: send(half, ZO.at[slot], szo.at[zz], rzo.at[slot], device),
        )

    def step_ob(k):
        zz = p.line(k)
        both = PO.at[pl.ds(2 * zz, 2), :, 768:1536]

        def add(slot):
            p.arrived(ZB.at[slot], rzb.at[slot], spare)
            both[...] = (both[...].astype(F32) + ZB[slot].astype(F32)).astype(BF)

        p.reduce_step(
            zz, add, lambda slot, device: send(both, ZB.at[slot], szb.at[zz], rzb.at[slot], device)
        )

    def side_ob():
        send(PO.at[p.theirs(z), :, 768:1536], YB, syb, ryb, p.side)

    at_end = (z == 0) | (z == 3)
    in_middle = (z == 1) | (z == 2)
    g_n.step(1)

    @pl.loop(0, 4)
    def _(k):
        zz = p.line(k)
        pl.when(at_end & (k > 0) & (k < 3))(lambda: g_n.step(k + 1))
        pl.when(in_middle & (k < 2))(lambda: g_n.step(k + 2))
        g_n.other(k)
        rows = rows_of(256 * zz, 256, 256)
        X = NC[rows]
        cot = NC[cot_rows(256 * zz, 256)]
        for j in range(3):
            ga, ua = pl.ds(384 * j, 384), pl.ds(1152 + 384 * j, 384)
            gate = dot(X, vG[:, ga])
            up = dot(X, vG[:, ua])
            d_mixed = dot_nt(cot, vD[ga])
            sg = jax.nn.sigmoid(gate)
            active = gate * sg
            d_active = d_mixed * up
            MX[rows, ga] = (active * up).astype(BF)
            H[rows, ga] = (d_active * sg + d_active * active * (1.0 - sg)).astype(BF)
            H[rows, ua] = (d_mixed * active).astype(BF)
        for j in range(3):
            co = pl.ds(512 * j, 512)
            part = dot_nt(H[rows], vG[co]).astype(BF)
            PD[2 * zz, :, co] = part[:128]
            PD[2 * zz + 1, :, co] = part[128:]
        pl.when(k == 2)(lambda: side_d(1))
        pl.when(k == 3)(lambda: side_d(3))
        for j in range(3):
            co = pl.ds(512 * j, 512)
            part = dot(MX[rows], vD[:, co]).astype(BF)
            PO[2 * zz, :, co] = part[:128]
            PO[2 * zz + 1, :, co] = part[128:]
        pl.when(at_end & (k == 1))(lambda: step_ob(1))
        pl.when(at_end & (k == 2))(lambda: step_ob(2))

    side_d(2)
    side_d(0)

    def owner(k):
        return 2 * ((z + 1 + k // 2) % 4) + (k % 2) * (2 * y - 1) + 1 - y

    def pair_chip(k):
        t = owner(k)
        for xx in range(2):
            p.arrived(RC.at[t, xx], rcg.at[t, xx], spare)
            q = quarter(t, 2 * xx + c)
            vG[q] = (vG[q].astype(F32) + RC[t, xx].astype(F32)).astype(BF)
        send(vG.at[quarter(t, p.rx)], RX.at[t], sx.at[t], rx.at[t], p.across)

    @pl.loop(0, 5)
    def _(j):
        pl.when(at_end & (j == 2))(lambda: step_d(3))

        @pl.when(j < 4)
        def _():
            pair = (z + 1 + j) % 4
            rows = rows_of(384 * pair, 384, 128)
            X = NC[0:1024, rows].T
            for i in range(3):
                co = pl.ds(768 * i, 768)
                vG[rows, co] = dot(X, H[0:1024, co]).astype(BF)
            for i in range(2):
                t = owner(2 * j + i)
                for xx in range(2):
                    send(vG.at[quarter(t, 2 * xx + 1 - c)], RC.at[t, xx], scg.at[t, xx], rcg.at[t, xx], p.core)

        @pl.when(j > 0)
        def _():
            pair_chip(2 * j - 2)
            pair_chip(2 * j - 1)

    pl.semaphore_signal(free, inc=1, device_id=p.core, device_id_type=MESH)

    def chunk(i):
        return rows_of(384 * i, 384, 128)

    def cols(q):
        return rows_of(384 * q, 384, 128)

    held = (
        pltpu.make_async_copy(wo_hbm, NC.at[0:1536], loc.at[1]),
        pltpu.make_async_copy(wq_hbm, H.at[:, 0:2048], loc.at[2]),
        pltpu.make_async_copy(att_hbm, NC.at[1536:1664], loc.at[3]),
        pltpu.make_async_copy(a1_hbm, NC.at[1664:1792], loc.at[4]),
        pltpu.make_async_copy(x_hbm, NC.at[1792:1920], loc.at[5]),
        pltpu.make_async_copy(cot_hbm, NC.at[1920:2048], loc.at[6]),
        pltpu.make_async_copy(q_hbm.at[0], MX.at[0:768, 256:384], loc.at[8]),
        pltpu.make_async_copy(q_hbm.at[1], MX.at[0:768, 384:512], loc.at[9]),
        pltpu.make_async_copy(mid_hbm, mid_ref, loc.at[10]),
        pltpu.make_async_copy(gains_hbm, gains, loc.at[11]),
        pltpu.make_async_copy(cos_hbm, cos_ref, loc.at[12]),
        pltpu.make_async_copy(sin_hbm, sin_ref, loc.at[13]),
        pltpu.make_async_copy(k_hbm, keys, loc.at[14]),
        pltpu.make_async_copy(v_hbm, values, loc.at[15]),
        pltpu.make_async_copy(p_hbm, probs, loc.at[16]),
    )

    def down_terms():
        @pl.loop(0, 3)
        def _(i):
            X = MX[:, chunk(i)].T
            for j in range(3):
                co = pl.ds(512 * j, 512)
                vD[chunk(i), co] = dot(X, NC[1024:2048, co]).astype(BF)
            for xx in range(2):
                q = 2 * xx + 1 - c
                send(vD.at[chunk(i), cols(q)], RCd.at[xx, chunk(i)], scd.at[i, xx], rcd.at[i, xx], p.core)

        g_n.finish()
        for copy in held:
            copy.start()

        @pl.loop(0, 3)
        def _(i):
            for xx in range(2):
                p.arrived(RCd.at[xx, chunk(i)], rcd.at[i, xx], spare)
                q = cols(2 * xx + c)
                vD[chunk(i), q] = (vD[chunk(i), q].astype(F32) + RCd[xx, chunk(i)].astype(F32)).astype(BF)

    def pair_whole(k):
        t = owner(k)
        q = quarter(t, r)
        p.arrived(RX.at[t], rx.at[t], spare)
        vG[q] = (vG[q].astype(F32) + RX[t].astype(F32)).astype(BF)

        if k < 7:
            send(vG.at[q], OG.at[r, s], sa.at[t], ra.at[s, r], p.peer(t))
        else:
            pltpu.make_async_copy(vG.at[q], OG.at[r, s], loc.at[7]).start()

    def share(t):
        v = OG.at[r, t]
        send(v, v, sf.at[t, 0], ra.at[t, r], p.across)
        send(v, v, sf.at[t, 1], ra.at[t, r], p.core)

    def source(k):
        return 2 * ((z + 3 - k // 2) % 4) + (1 - y if k % 2 == 0 else y)

    def take(k):
        t = source(k)
        if k < 7:
            p.arrived(OG.at[r, t], ra.at[t, r], spare)
        else:
            pltpu.make_async_copy(vG.at[quarter(s, r)], OG.at[r, s], loc.at[7]).wait()
        share(t)

    def relay(k):
        t = source(k)
        v = OG.at[p.rx, t]
        p.arrived(v, ra.at[t, p.rx], spare)
        send(v, v, sf.at[t, 2], ra.at[t, p.rx], p.core)

    def down_across(i):
        send(vD.at[chunk(i), cols(p.rx)], RXd.at[chunk(i)], sxd.at[i], rxd.at[i], p.across)

    def down_whole(i):
        p.arrived(RXd.at[chunk(i)], rxd.at[i], spare)
        q = cols(r)
        vD[chunk(i), q] = (vD[chunk(i), q].astype(F32) + RXd[chunk(i)].astype(F32)).astype(BF)
        src, dst = vD.at[chunk(i), q], OD.at[r, chunk(i)]
        pltpu.make_async_copy(src, dst, sfd.at[i, 3]).start()
        send(src, dst, sfd.at[i, 0], rfd.at[i, r], p.across)
        send(src, dst, sfd.at[i, 1], rfd.at[i, r], p.core)

    def down_relay(i):
        v = OD.at[p.rx, chunk(i)]
        p.arrived(v, rfd.at[i, p.rx], spare)
        send(v, v, sfd.at[i, 2], rfd.at[i, p.rx], p.core)

    def back(w):
        return w * cos_ref[...] - pltpu.roll(w, 64, 1) * sin_ref[...]

    kept = {}

    def attention_out():
        for copy in held:
            copy.wait()
        dn, hidden = PD[s].astype(F32), mid_ref[...]
        rstd = inverse_norm(hidden)
        unit = hidden * rstd
        kept["ffn"] = jnp.sum(dn * unit, axis=0, keepdims=True)
        e = dn * gains[1:2, :]
        dm = NC[1920:2048].astype(F32) + rstd * (e - unit * jnp.mean(e * unit, axis=-1, keepdims=True))
        NC[1920:2048] = dm.astype(BF)
        AT[...] = NC[1536:1664].T
        for j in range(3):
            part = dot_nt(NC[1920:2048], NC[pl.ds(512 * j, 512)]).astype(BF)
            for i in range(4):
                h = 4 * j + i
                MX[pl.ds(128 * (h % 6), 128), pl.ds(128 * (h // 6), 128)] = part[:, 128 * i : 128 * i + 128]
        for j in range(3):
            co = pl.ds(512 * j, 512)
            NC[0:1536, co] = dot(AT[...], NC[1920:2048, co]).astype(BF)

        @pl.loop(0, 8)
        def _(k):
            o_sums.to_core(o_sums.own(k))

    def heads(g):
        grad = MX[0:768, 128 * g : 128 * g + 128]
        query = MX[0:768, 256 + 128 * g : 384 + 128 * g]
        soft = probs[g].astype(F32)
        d_probs = dot_nt(grad, values[g])
        d_scores = (soft * (d_probs - jnp.sum(soft * d_probs, axis=-1, keepdims=True))).astype(BF)
        d_values = dot(probs[g].T, grad)
        d_queries = dot(d_scores, keys[g]) * HEAD_DIMENSION**-0.5
        d_keys = dot(d_scores.T, query)
        for i in range(6):
            dj[:, pl.ds(128 * (6 * g + i), 128)] = back(d_queries[128 * i : 128 * i + 128]).astype(BF)
        dj[:, pl.ds(128 * (12 + g), 128)] = back(d_keys).astype(BF)
        dj[:, pl.ds(128 * (14 + g), 128)] = d_values.astype(BF)

    def attention_in():
        heads(1)
        joined_grad = dj[...]
        bias_grad = jnp.sum(joined_grad.astype(F32), axis=0, keepdims=True)
        x = NC[1792:1920].astype(F32)
        rstd = inverse_norm(x)
        unit = x * rstd
        dn1 = jnp.concatenate(
            [dot_nt(joined_grad, H[pl.ds(512 * j, 512), 0:2048]) for j in range(3)], axis=1
        )
        gain_attn_grad = jnp.sum(dn1 * unit, axis=0, keepdims=True)
        e = dn1 * gains[0:1, :]
        NC[1792:1920] = (
            NC[1920:2048].astype(F32) + rstd * (e - unit * jnp.mean(e * unit, axis=-1, keepdims=True))
        ).astype(BF)
        pltpu.make_async_copy(NC.at[1792:1920], gtok_ref, loc.at[5]).start()
        SM[...] = jnp.zeros_like(SM)
        ffn = kept["ffn"]
        for t in range(8):
            SM[t, 0:1, :] = gain_attn_grad[:, 192 * t : 192 * t + 128]
            SM[t, 1:2, 0:64] = gain_attn_grad[:, 192 * t + 128 : 192 * t + 192]
            SM[t, 2:3, :] = bias_grad[:, 256 * t : 256 * t + 128]
            SM[t, 3:4, :] = bias_grad[:, 256 * t + 128 : 256 * t + 256]
            SM[t, 4:5, :] = ffn[:, 192 * t : 192 * t + 128]
            SM[t, 5:6, 0:64] = ffn[:, 192 * t + 128 : 192 * t + 192]
        AT[...] = NC[1664:1792].T

    def joined_terms():
        pl.semaphore_wait(free, 1)

        @pl.loop(0, 8)
        def _(k):
            t = q_sums.own(k)
            rows = rows_of(192 * t, 192)
            for j in range(2):
                co = pl.ds(1024 * j, 1024)
                H[rows, co] = dot(AT[rows], dj[:, co]).astype(BF)
            H[rows, 2048:2176] = jnp.zeros((192, 128), BF)
            H[rows_of(192 * t, 16), 2048:2176] = SM[t].astype(BF)
            q_sums.to_core(t)

    def on_chip(sums):
        @pl.loop(0, 8)
        def _(k):
            sums.on_chip(k)

    def finish_out():
        p.arrived(YB, ryb, spare)
        PO[s, :, 768:1536] = (PO[s, :, 768:1536].astype(F32) + YB[...].astype(F32)).astype(BF)
        PO[s] = (PO[s].astype(F32) + mid_ref[...]).astype(BF)
        pltpu.make_async_copy(PO.at[s], out_ref, loc.at[6]).start()

    def first_heads():
        heads(0)

    def o_on_chip():
        on_chip(o_sums)

    def q_on_chip():
        on_chip(q_sums)

    side_oa(3)

    @pl.when(at_end)
    def _():
        step_d(2)
        side_oa(2)
        side_oa(0)
        step_d(1)
        pair_whole(3)


    @pl.when(in_middle)
    def _():
        side_oa(2)
        side_oa(0)
        step_ob(2)
        step_d(3)
        step_d(2)
        step_d(1)
        pair_whole(6)

    down_terms()
    pair_whole(5)

    @pl.when(at_end)
    def _():
        step_ob(3)
        pair_whole(6)
        down_across(1)
        step_oa(3)
        pair_whole(0)
        down_across(0)
        side_oa(1)


    @pl.when(in_middle)
    def _():
        down_across(0)
        side_oa(1)
        pair_whole(3)
        down_across(1)

    pair_whole(2)
    step_d(0)
    attention_out()

    @pl.when(at_end)
    def _():
        down_across(2)

    first_heads()

    @pl.when(in_middle)
    def _():
        pair_whole(1)
        take(3)

    attention_in()

    @pl.when(in_middle)
    def _():
        pair_whole(4)

    joined_terms()
    o_on_chip()

    @pl.when(at_end)
    def _():
        o_sums.aside(0)
        pair_whole(1)
        take(3)
        pair_whole(4)
        take(6)


    @pl.when(in_middle)
    def _():
        down_across(2)
        o_sums.aside(2)
        pair_whole(7)
        down_whole(0)
        o_sums.aside(0)
        step_oa(3)
        pair_whole(0)
        take(7)

    q_on_chip()

    @pl.when(at_end)
    def _():
        o_sums.aside(2)
        q_sums.aside(0)
        take(2)
        q_sums.aside(1)
        down_whole(1)
        take(5)
        pair_whole(7)
        o_sums.on_line(0)
        down_whole(2)
        take(1)
        q_sums.aside(2)
        take(7)
        q_sums.on_line(0)
        o_sums.aside(1)
        take(4)
        q_sums.on_line(1)
        relay(5)
        q_sums.aside(3)
        down_whole(0)
        q_sums.on_line(2)
        take(0)
        o_sums.on_line(1)
        o_sums.aside(3)
        q_sums.on_line(3)
        q_sums.at_owner()
        o_sums.on_line(2)
        relay(2)
        relay(3)
        step_oa(2)
        relay(4)
        o_sums.on_line(3)
        o_sums.at_owner()
        step_ob(0)
        q_sums.spread()
        step_oa(1)
        down_relay(2)
        down_relay(0)
        relay(1)
        relay(6)
        relay(7)
        relay(0)
        side_ob()
        down_relay(1)
        step_oa(0)
        finish_out()
        o_sums.spread()


    @pl.when(in_middle)
    def _():
        q_sums.aside(1)
        q_sums.aside(0)
        take(4)
        take(6)
        down_whole(1)
        take(5)
        relay(3)
        step_ob(3)
        take(2)
        take(1)
        q_sums.aside(2)
        o_sums.on_line(0)
        q_sums.aside(3)
        o_sums.aside(1)
        down_whole(2)
        step_ob(1)
        q_sums.on_line(0)
        relay(5)
        o_sums.aside(3)
        q_sums.on_line(1)
        q_sums.on_line(2)
        step_ob(0)
        take(0)
        q_sums.on_line(3)
        q_sums.at_owner()
        relay(4)
        relay(2)
        o_sums.on_line(2)
        side_ob()
        o_sums.on_line(1)
        relay(6)
        relay(7)
        o_sums.on_line(3)
        o_sums.at_owner()
        relay(0)
        step_oa(1)
        down_relay(1)
        down_relay(2)
        down_relay(0)
        q_sums.spread()
        relay(1)
        step_oa(2)
        o_sums.spread()
        step_oa(0)
        finish_out()

    o_sums.finish()
    q_sums.finish()
    pltpu.make_async_copy(NC.at[1792:1920], gtok_ref, loc.at[5]).wait()
    pltpu.make_async_copy(PO.at[s], out_ref, loc.at[6]).wait()

    @pl.loop(0, 3)
    def _(i):
        for q in (p.rc, p.rd):
            p.arrived(OD.at[q, chunk(i)], rfd.at[i, q], spare)
        for d in range(3):
            p.sent(OD.at[r, chunk(i)], sfd.at[i, d], spare)
        pltpu.make_async_copy(OD.at[r, chunk(i)], OD.at[r, chunk(i)], sfd.at[i, 3]).wait()
        for xx in range(2):
            p.sent(RCd.at[xx, chunk(i)], scd.at[i, xx], spare)
        p.sent(RXd.at[chunk(i)], sxd.at[i], spare)

    @pl.loop(0, 8)
    def _(t):
        for q in (p.rc, p.rd):
            p.arrived(OG.at[q, t], ra.at[t, q], spare)
        for d in range(3):
            p.sent(OG.at[r, t], sf.at[t, d], spare)
        for xx in range(2):
            p.sent(RC.at[t, xx], scg.at[t, xx], spare)
        p.sent(RX.at[t], sx.at[t], spare)

        @pl.when(t != s)
        def _():
            p.sent(OG.at[r, s], sa.at[t], spare)

    @pl.loop(0, 4)
    def _(i):
        p.sent(YD.at[i], syd.at[i], spare)
        p.sent(YO.at[i], syo.at[i], spare)

        @pl.when(i != z)
        def _():
            p.sent(ZD.at[i], szd.at[i], spare)
            p.sent(ZO.at[i], szo.at[i], spare)
            p.sent(ZB.at[i], szb.at[i], spare)

    p.sent(YB, syb, spare)


def layer_back(*args):
    return pl.pallas_call(
        layer_back_body,
        out_shape=(
            shaped(128, 1536), shaped(128, 1536), shaped(4, 8, 48, 2304), shaped(4, 1152, 384), shaped(4, 48, 2176),
            shaped(4, 48, 1536),
        ),
        in_specs=[HBM] * 18,
        out_specs=(HBM,) * 6,
        scratch_shapes=[
            low(2048, 1536), low(1536, 2304), low(1536, 2304), low(1152, 1536), low(1024, 1152),
            low(8, 128, 1536), low(8, 128, 1536), low(4, 128, 1536), low(5, 128, 1536), low(4, 128, 768), low(5, 128, 768),
            low(128, 768), low(5, 2, 128, 768),
            low(2, 1152, 384), low(1152, 384), low(8, 2, 48, 2304), low(8, 48, 2304),
            low(128, 2048), low(1536, 128), full(8, 16, 128), full(128, 1536), full(8, 1536), full(128, 128), full(128, 128),
            low(2, 128, 128), low(2, 128, 128), low(2, 768, 128),
            *RowSums.buffers(2176)[1:], *RowSums.buffers(1536),
            pltpu.SemaphoreType.REGULAR, DMA((8,)), DMA((4,)), DMA((4, 2)),
            DMA((4,)), DMA((5,)), DMA((4,)), DMA((4,)), DMA((4,)), DMA((4,)), DMA((4,)), DMA((5,)), DMA, DMA, DMA((4,)), DMA((5,)),
            DMA((3, 2)), DMA((3, 2)), DMA((3,)), DMA((3,)), DMA((3, 4)), DMA((3, 4)),
            DMA((8, 2)), DMA((8, 2)), DMA((8,)), DMA((8,)), DMA((8,)), DMA((8, 4)), DMA((8, 3)),
            *RowSums.semaphores(), *RowSums.semaphores(), DMA((17,)),
        ],
        compiler_params=pltpu.CompilerParams(collective_id=1, has_side_effects=True, vmem_limit_bytes=64 << 20),
        name="layer_back",
    )(*args)


def widen_body(
    g_ref, d_ref, q_ref, o_ref, x_ref, y_ref, gate, up, down, qkv, out, x_out, y_out, ga, bq, gf, narrow
):
    for first, wide in ((0, gate), (1152, up)):
        for t in range(8):
            narrow[:, 1120 * t : 1120 * t + 1120] = g_ref[0, t, :, first : first + 1120]
        wide[...] = narrow[...].astype(F32)
    down[...] = d_ref[0, 0:1120, :].astype(F32)
    qkv[...] = q_ref[0, :, 0:2048].astype(F32)
    out[...] = o_ref[0].astype(F32)
    x_out[...] = x_ref[...]
    y_out[...] = y_ref[...]

    @pl.when(pl.program_id(0) == 0)
    def _():
        small = q_ref[0, 0:16, 2048:2176].astype(F32)
        ga[...] = jnp.concatenate([small[0:1], small[1:2, 0:64]], axis=1)[0]
        bq[...] = jnp.concatenate([small[2:3], small[3:4]], axis=1)[0]
        gf[...] = jnp.concatenate([small[4:5], small[5:6, 0:64]], axis=1)[0]


def widen(g, d, q, o, x, y):
    def rows(size, width):
        return pl.BlockSpec((size, width), lambda i: (i, 0))

    def whole(size):
        return pl.BlockSpec((size,), lambda i: (0,))

    return pl.pallas_call(
        widen_body,
        grid=(4,),
        out_shape=(
            shaped(192, 8960, dtype=F32), shaped(192, 8960, dtype=F32), shaped(1120, 1536, dtype=F32),
            shaped(192, 2048, dtype=F32), shaped(192, 1536, dtype=F32), shaped(128, 1536), shaped(128, 1536),
            shaped(192, dtype=F32), shaped(256, dtype=F32), shaped(192, dtype=F32),
        ),
        in_specs=[
            pl.BlockSpec((1, 8, 48, 2304), lambda i: (i, 0, 0, 0)),
            pl.BlockSpec((1, 1152, 384), lambda i: (i, 0, 0)),
            pl.BlockSpec((1, 48, 2176), lambda i: (i, 0, 0)),
            pl.BlockSpec((1, 48, 1536), lambda i: (i, 0, 0)),
            rows(32, 1536),
            rows(32, 1536),
        ],
        out_specs=(
            rows(48, 8960), rows(48, 8960), pl.BlockSpec((1120, 384), lambda i: (0, i)), rows(48, 2048), rows(48, 1536),
            rows(32, 1536), rows(32, 1536), whole(192), whole(256), whole(192),
        ),
        scratch_shapes=[low(48, 8960)],
        compiler_params=pltpu.CompilerParams(vmem_limit_bytes=62 << 20),
        name="widen",
    )(g, d, q, o, x, y)


def shards_eight(
    tokens, segments, gain_attn, w_qkv, b_qkv, w_out, gain_ffn, w_gate, w_up, w_down, cotangent
):
    x, cot = tokens[0], cotangent[0]
    WQ, WO, G, C, cosine, sine, gains, queries, keys, values, probs, att, a1, mid, a2 = gather_weights(
        x, segments, gain_attn, b_qkv, gain_ffn, w_qkv, w_out, w_gate, w_up, cot
    )
    out, grad_tokens, gate_up, down, qkv, o = layer_back(
        a2, C, G, w_down, WQ, WO, att, a1, x, cot, queries, mid, gains, cosine, sine, keys, values, probs
    )
    gate, up, down, qkv_rows, out_rows, out, grad_tokens, ga, bq, gf = widen(gate_up, down, qkv, o, out, grad_tokens)
    return out[None], grad_tokens[None], ga, qkv_rows, bq, out_rows, gf, gate, up, down


def solution(mesh):
    placed = (
        P(("replica", "shard"), None, None),
        P(("replica", "shard"), None),
        P("shard"),
        P("shard", None),
        P("shard"),
        P("shard", None),
        P("shard"),
        P("shard", None),
        P("shard", None),
        P("shard", None),
        P(("replica", "shard"), None, None),
    )
    return jax.shard_map(
        shards_eight if (mesh.shape["replica"], mesh.shape["shard"]) == (4, 8) else shards,
        mesh=mesh,
        in_specs=placed,
        out_specs=(
            P(("replica", "shard"), None, None),
            P(("replica", "shard"), None, None),
            P("shard"),
            P("shard", None),
            P("shard"),
            P("shard", None),
            P("shard"),
            P("shard", None),
            P("shard", None),
            P("shard", None),
        ),
        check_vma=False,
    )
```
